32 devices in a mesh: grp: 2 (over y), src: 8 (over z, x), tgt: 2 (over core).
Axes of the slice: x: 2, y: 2, z: 4, core: 2. Of those that a mesh axis runs over, the one named last changes fastest.
Arguments:
- source_feat: float32 [256, 64, 128], P(('grp', 'src')), parts along dimension 0, may hold values from -1.2 to 1.2
- target_feat: float32 [32, 64, 128], P(('grp', 'src', 'tgt')), parts along dimension 0, may hold values from -1.2 to 1.2
- log_mass_src: float32 [256, 128], P(('grp', 'src')), parts along dimension 0, may hold values from -3 to 3
- log_mass_tgt: float32 [32, 128], P(('grp', 'src', 'tgt')), parts along dimension 0, may hold values from -3 to 3
- potential_tgt: float32 [32, 128], P(('grp', 'src', 'tgt')), parts along dimension 0, may hold values from -6 to 152
- support: int32 [256, 2, 8], P(('grp', 'src'), 'tgt'), parts along dimension 0, may hold values from 0 to 7, as said below
- counts: int32 [256, 2], P(('grp', 'src'), 'tgt'), parts along dimension 0, may hold values from 1 to 8, as said below
Outputs:
- potential_src: float32 [256, 128], P(('grp', 'src')), parts along dimension 0
- potential_new: float32 [32, 128], P(('grp', 'src', 'tgt')), parts along dimension 0
The draws below stay inside these ranges and needn't reach their ends.
There are 2 independent parts, one for each index of `grp`. The reference program is written for one: setup_inputs(seed, part) draws one part's arguments, and reference() takes and returns one part's arrays. A program takes and returns all parts, laid end to end along the dimension named above; each array names one. Nothing has to cross between parts.
Inputs may be any that keep to these rules, and one draw needn't show every extreme that they name: `support`: within one list the first counts entries are distinct; unused entries are also valid indices and are ignored; every target block of a shard is named within the used entries of some source block row. `counts`: the source block rows of one index of src share a load level, so some devices use far more slots than others; some list is full in every draw.
All inputs are finite; a program needn't handle non-finite values.
Results may differ from the reference program's by a relative error of at most 0.000096.
Values sent between devices are 32-bit elements; how exact they have to be, the bound alone decides.
No kernel may reach another device: no remote copies, remote signals or barrier semaphores. Data moves between devices by JAX's collectives and lax.ppermute only.
A program may use at most 64 MiB of HBM per device.

```python
import math
import jax
import jax.numpy as jnp
from jax import lax

F = 64
BLOCK = 128
KT = 8
RB = 16
NSB = 128
TBD = 8
NTB = 16


def feature_draw(key, shape):
    second = jax.random.fold_in(key, 1)
    values = 0.3 * jax.random.normal(second, shape)
    return jnp.clip(values, -1.2, 1.2).astype(jnp.float32)


def draw_source_feat(key, part):
    return feature_draw(jax.random.fold_in(key, 11), (NSB, F, BLOCK))


def draw_target_feat(key, part):
    return feature_draw(jax.random.fold_in(key, 23), (NTB, F, BLOCK))


def draw_potential_tgt(key, part):
    first = jax.random.fold_in(jax.random.fold_in(key, 71), 0)
    values = jnp.clip(jax.random.normal(first, (NTB, BLOCK)), -6.0, 6.0)
    return values.astype(jnp.float32)


def draw_support(key, part):
    shards = NTB // TBD
    lists = NSB * shards
    keys = jax.random.split(jax.random.fold_in(key, 37), lists)
    offsets = jax.vmap(lambda single: jax.random.permutation(single, TBD - 1))(keys) + 1
    slot_offsets = jnp.concatenate([jnp.zeros((lists, 1), jnp.int32), offsets[:, :KT - 1].astype(jnp.int32)], axis=1)
    base_rows = jnp.arange(lists, dtype=jnp.int32) // shards % TBD
    chosen = (base_rows[:, None] + slot_offsets) % TBD
    return chosen.reshape(NSB, shards, KT).astype(jnp.int32)


def draw_counts(key, part):
    shards = NTB // TBD
    first, second = jax.random.split(jax.random.fold_in(key, 53))
    levels = jax.random.randint(first, (NSB // RB,), 1, KT + 1)
    level_rows = jnp.repeat(levels, RB)
    drawn = jax.random.randint(second, (NSB, shards), 1, KT + 1)
    drawn = jnp.minimum(drawn, level_rows[:, None])
    drawn = drawn.at[0, 0].set(KT)
    return drawn.astype(jnp.int32)


def block_levels(rng, shape, cuts, least, high):
    def one(dim, shards_of):
        heights = jax.random.uniform(jax.random.fold_in(jax.random.fold_in(rng, 6), dim), (shards_of,), jnp.float32, least / len(cuts), high / len(cuts))
        return jnp.repeat(jnp.exp(heights), shape[dim] // shards_of).reshape((-1,) + (1,) * (len(shape) - dim - 1))

    factor_of = one(*cuts[0])
    for cut in cuts[1:]:
        factor_of = factor_of * one(*cut)
    return factor_of


def setup_inputs(seed: int = 0, part: int = 0) -> dict:
    seeds = jax.random.split(jax.random.key(seed), 8)
    own_keys = jax.random.split(jax.random.fold_in(seeds[7], part), 8)
    source_feat = draw_source_feat(jax.random.fold_in(jax.random.fold_in(seeds[7], part), 71), part)
    target_feat = draw_target_feat(jax.random.fold_in(jax.random.fold_in(seeds[7], part), 71), part)
    log_mass_src = jnp.clip(jax.random.uniform(own_keys[2], (NSB, BLOCK), jnp.float32, -3.0, 3.0) * block_levels(own_keys[2], (NSB, BLOCK), ((0, 8),), -0.4, 0.0), -3.0, 3.0)
    log_mass_tgt = jnp.clip(jax.random.uniform(own_keys[3], (NTB, BLOCK), jnp.float32, -3.0, 3.0) * block_levels(own_keys[3], (NTB, BLOCK), ((0, 16),), -0.4, 0.0), -3.0, 3.0)
    potential_tgt = draw_potential_tgt(jax.random.fold_in(jax.random.fold_in(seeds[7], part), 71), part)
    support = draw_support(jax.random.fold_in(jax.random.fold_in(seeds[7], part), 71), part)
    counts = draw_counts(jax.random.fold_in(jax.random.fold_in(seeds[7], part), 71), part)
    return {"source_feat": source_feat, "target_feat": target_feat, "log_mass_src": log_mass_src, "log_mass_tgt": log_mass_tgt, "potential_tgt": potential_tgt, "support": support, "counts": counts}


entropic = 0.5
very_low = -1.0e30


def cost_tiles(source_blk, source_sq, target_blk, target_sq):
    cross = jnp.einsum("...fi,...fj->...ij", source_blk, target_blk, precision=lax.Precision.HIGHEST)
    return source_sq[..., :, None] + target_sq[..., None, :] - 2.0 * cross


def row_stats(cost, mass_tgt, poten_tgt, usable):
    scores = mass_tgt[..., None, :] + (poten_tgt[..., None, :] - cost) / entropic
    scores = jnp.where(usable[..., None, None], scores, very_low)
    peak = jnp.max(scores, axis=(1, 3))
    total = jnp.sum(jnp.exp(scores - peak[:, None, :, None]), axis=(1, 3))
    return peak, total


def column_stats(cost, mass_src, poten_src, usable):
    scores = mass_src[:, None, :, None] + (poten_src[:, None, :, None] - cost) / entropic
    peak = jnp.max(scores, axis=2)
    total = jnp.sum(jnp.exp(scores - peak[:, :, None, :]), axis=2)
    peak = jnp.where(usable[..., None], peak, very_low)
    total = jnp.where(usable[..., None], total, 0.0)
    return peak, total


def segment_merge(peaks, totals, seg_ids, segments):
    best = jax.ops.segment_max(peaks, seg_ids, num_segments=segments + 1)
    best = jnp.maximum(best, very_low)
    summed = jax.ops.segment_sum(totals * jnp.exp(peaks - best[seg_ids]), seg_ids, num_segments=segments + 1)
    return best[:segments], summed[:segments]


def reference(source_feat, target_feat, log_mass_src, log_mass_tgt, potential_tgt, support, counts):
    shards = NTB // TBD

    def regroup(array):
        split = array.reshape((TBD, shards) + array.shape[1:])
        return jnp.swapaxes(split, 0, 1).reshape((NTB,) + array.shape[1:])

    target_all = regroup(target_feat)
    mass_all = regroup(log_mass_tgt)
    poten_all = regroup(potential_tgt)
    target_sq = jnp.sum(target_all * target_all, axis=1)
    source_sq = jnp.sum(source_feat * source_feat, axis=1)
    offsets = (jnp.arange(shards, dtype=jnp.int32) * TBD)[None, :, None]
    block_ids = (support + offsets).reshape(NSB, shards * KT)
    usable = (jnp.arange(KT, dtype=jnp.int32)[None, None, :] < counts[:, :, None]).reshape(NSB, shards * KT)
    width = math.gcd(NSB, 8)

    def grouped(array):
        return array.reshape((NSB // width, width) + array.shape[1:])

    def row_pass(items):
        source_blk, source_nrm, ids_here, use_here = items
        cost = cost_tiles(source_blk[:, None], source_nrm[:, None], target_all[ids_here], target_sq[ids_here])
        return row_stats(cost, mass_all[ids_here], poten_all[ids_here], use_here)

    peak, total = lax.map(row_pass, (grouped(source_feat), grouped(source_sq), grouped(block_ids), grouped(usable)))
    potential_src = (-entropic * (peak + jnp.log(total))).reshape(NSB, BLOCK)

    def column_pass(items):
        source_blk, source_nrm, mass_here, poten_here, ids_here, use_here = items
        cost = cost_tiles(source_blk[:, None], source_nrm[:, None], target_all[ids_here], target_sq[ids_here])
        return column_stats(cost, mass_here, poten_here, use_here)

    peaks, totals = lax.map(column_pass, (grouped(source_feat), grouped(source_sq), grouped(log_mass_src), grouped(potential_src), grouped(block_ids), grouped(usable)))
    seg_ids = jnp.where(usable, block_ids, NTB).reshape(-1)
    best, summed = segment_merge(peaks.reshape(-1, BLOCK), totals.reshape(-1, BLOCK), seg_ids, NTB)
    updated = -entropic * (best + jnp.log(summed))
    potential_new = jnp.swapaxes(updated.reshape(shards, TBD, BLOCK), 0, 1).reshape(NTB, BLOCK)
    return potential_src, potential_new
```

```python
import functools
import math

import jax
import jax.numpy as jnp
from jax import lax
from jax.experimental import pallas as pl
from jax.experimental.pallas import tpu as pltpu
from jax.sharding import PartitionSpec as P

entropic = 0.5
very_low = -1e30
log2e = 1.0 / math.log(2.0)
ln2 = math.log(2.0)
least_sum = 1e-28

VM = pl.BlockSpec(memory_space=pltpu.VMEM)
PARAMS = pltpu.CompilerParams(vmem_limit_bytes=40 * 2**20)


def in_vmem(shape, dtype):
    return pltpu.VMEM(shape, dtype)


def pieces(values):
    high = values.astype(jnp.bfloat16).astype(jnp.float32)
    rest = values - high
    mid = rest.astype(jnp.bfloat16).astype(jnp.float32)
    low = (rest - mid).astype(jnp.bfloat16).astype(jnp.float32)
    return high, mid, low


def target_weight(mass, poten):
    return (mass + poten / entropic) * log2e


def pack_kernel(feat_ref, mass_ref, poten_ref, out_ref):
    feat = feat_ref[0]
    depth = feat.shape[0]
    weight = target_weight(mass_ref[...], poten_ref[...])
    norm = jnp.sum(feat * feat, axis=0, keepdims=True)
    bias = weight - (log2e / entropic) * norm
    out_ref[:depth, :] = feat * (2.0 * log2e / entropic)
    out_ref[depth:, :] = jnp.broadcast_to(bias, (out_ref.shape[0] - depth, feat.shape[1]))


def source_kernel(shards, feat_ref, support_ref, counts_ref, wide_ref, norm_ref, mask_ref):
    rows, depth, cells = feat_ref.shape
    one = jnp.ones((2 * depth, 2 * cells), jnp.bfloat16)
    for pair in range(rows // 2):
        for half in range(2):
            feat = feat_ref[2 * pair + half]
            norm_ref[2 * pair + half : 2 * pair + half + 1, :] = jnp.sum(feat * feat, axis=0, keepdims=True)
            high, mid, low = pieces(feat)
            lanes = slice(half * cells, (half + 1) * cells)
            top = jnp.concatenate([high, mid], axis=0).astype(jnp.bfloat16)
            wide_ref[pair, 0 : 2 * depth, lanes] = top
            wide_ref[pair, 2 * depth : 4 * depth, lanes] = top
            wide_ref[pair, 4 * depth : 6 * depth, lanes] = jnp.concatenate([low, high], axis=0).astype(jnp.bfloat16)
        wide_ref[pair, 6 * depth : 8 * depth, :] = one
    support = support_ref[...]
    used = lax.broadcasted_iota(jnp.int32, support.shape, 1) < counts_ref[...]
    me = lax.axis_index("src")
    for step in range(shards):
        block = lax.rem(me + step, shards)
        hit = jnp.where(used & (support == block), 0.0, very_low)
        mask_ref[step] = jnp.broadcast_to(jnp.max(hit, axis=1, keepdims=True), (rows, cells))


def row_kernel(shards, *refs):
    packs = refs[:shards]
    wide_ref, mask_ref, exps_ref, tall_ref, peak_ref, rowsum_ref, total_ref = refs[shards:]
    pairs, _, both = wide_ref.shape
    cells = both // 2
    depth = cells // 2
    lane = lax.broadcasted_iota(jnp.int32, (cells, cells), 1)
    biases = jnp.concatenate([pack[depth : depth + 1, :] for pack in packs], axis=0)
    bias_pieces = jnp.concatenate(list(pieces(biases)), axis=0)
    padded = jnp.concatenate([bias_pieces, jnp.zeros((cells - 3 * shards, cells), jnp.float32)], axis=0)
    bias_lanes = padded.T
    for step, pack in enumerate(packs):
        feat = pack[:depth, :]
        turned = jnp.concatenate([feat, feat], axis=0).T
        high, mid, low = pieces(turned)
        own = jnp.where(lax.rem(lane, shards) == step, bias_lanes, 0.0)
        rows = slice(step * cells, (step + 1) * cells)
        tall_ref[rows, 0:cells] = high.astype(jnp.bfloat16)
        tall_ref[rows, cells : 2 * cells] = mid.astype(jnp.bfloat16)
        tall_ref[rows, 2 * cells : 3 * cells] = jnp.where(lane < depth, high, low).astype(jnp.bfloat16)
        tall_ref[rows, 3 * cells : 4 * cells] = own.astype(jnp.bfloat16)

    def body(pair, carry):
        weights = wide_ref[pair]
        for step in range(shards):
            rows = slice(step * cells, (step + 1) * cells)
            score = jnp.dot(tall_ref[rows, :], weights, preferred_element_type=jnp.float32)
            peak = jnp.max(score, axis=0, keepdims=True)
            exps = jnp.exp2(score - peak)
            exps_ref[pair, rows, :] = exps
            total = jnp.sum(exps, axis=0, keepdims=True)
            for half in range(2):
                lanes = slice(half * cells, (half + 1) * cells)
                peak_ref[step, pl.ds(2 * pair + half, 1), :] = peak[:, lanes]
                total_ref[step, pl.ds(2 * pair + half, 1), :] = total[:, lanes]
        return carry

    lax.fori_loop(0, pairs, body, 0)
    masked = [peak_ref[step] + mask_ref[step] for step in range(shards)]
    top = functools.reduce(jnp.maximum, masked)
    summed = sum(total_ref[step] * jnp.exp2(masked[step] - top) for step in range(shards))
    for step in range(shards):
        peak_ref[step] = masked[step]
    rowsum_ref[...] = top + jnp.log2(summed)


def lane_sums(values):
    ones = jnp.ones((8, values.shape[1]), jnp.bfloat16)
    parts = [
        lax.dot_general(ones, part.astype(jnp.bfloat16), (((1,), (1,)), ((), ())), preferred_element_type=jnp.float32)
        for part in pieces(values)
    ]
    return sum(parts)[0:1, :]


def column_kernel(shards, *refs):
    ins, rest = refs[:9], refs[9:]
    exps_ref, tall_ref, wide_ref, peak_ref, mask_ref, own_ref, other_ref, mass_ref, norm_ref = ins
    poten_ref, outs = rest[0], rest[1 : 1 + shards]
    weight_ref, acc_ref, shift_ref = rest[1 + shards :]
    pairs, _, both = wide_ref.shape
    cells = both // 2
    own, other = own_ref[...], other_ref[...]
    top = jnp.maximum(own, other)
    whole = top + jnp.log2(jnp.exp2(own - top) + jnp.exp2(other - top))
    poten_ref[...] = norm_ref[...] - (entropic * ln2) * whole
    shift = mass_ref[...] * log2e - whole
    shift_ref[...] = shift
    for step in range(shards):
        weight_ref[step] = jnp.exp2(peak_ref[step] + shift)
    for step in range(shards):
        rows = slice(step * cells, (step + 1) * cells)
        acc = jnp.zeros((cells, cells), jnp.float32)
        for pair in range(pairs):
            acc = acc + exps_ref[pair, rows, :cells] * weight_ref[step, 2 * pair : 2 * pair + 1, :]
            acc = acc + exps_ref[pair, rows, cells:] * weight_ref[step, 2 * pair + 1 : 2 * pair + 2, :]
        acc_ref[rows, :] = acc
    sums = lane_sums(acc_ref[...])
    worst = jnp.full((1, cells), 1.0, jnp.float32)
    for step in range(shards):
        used = jnp.max(mask_ref[step], axis=0, keepdims=True) > 0.5 * very_low
        here = sums[:, step * cells : (step + 1) * cells]
        outs[step][...] = jnp.where(used, jnp.log2(here), very_low)
        worst = jnp.minimum(worst, jnp.where(used, here, 1.0))

    @pl.when(jnp.min(worst) < least_sum)
    def _():
        acc_ref[...] = jnp.full(acc_ref.shape, very_low, jnp.float32)

        def exponents(pair, step):
            score = jnp.dot(
                tall_ref[pl.ds(pl.multiple_of(step * cells, cells), cells), :],
                wide_ref[pair],
                preferred_element_type=jnp.float32,
            )
            add = shift_ref[pl.ds(2 * pair, 2), :] + mask_ref[step, pl.ds(2 * pair, 2), :]
            return score[:, :cells] + add[0:1, :], score[:, cells:] + add[1:2, :]

        def highest(index, carry):
            pair, step = index // shards, lax.rem(index, shards)
            rows = pl.ds(pl.multiple_of(step * cells, cells), cells)
            first, second = exponents(pair, step)
            acc_ref[rows, :] = jnp.maximum(acc_ref[rows, :], jnp.maximum(first, second))
            return carry

        lax.fori_loop(0, pairs * shards, highest, 0)

        def total(step, carry):
            rows = pl.ds(pl.multiple_of(step * cells, cells), cells)
            peak = jnp.max(acc_ref[rows, :], axis=1, keepdims=True)

            def add(pair, sums):
                first, second = exponents(pair, step)
                return sums + jnp.exp2(first - peak) + jnp.exp2(second - peak)

            sums = lax.fori_loop(0, pairs, add, jnp.zeros((cells, cells), jnp.float32))
            along = jnp.broadcast_to(peak, (cells, cells)).T
            acc_ref[rows, :] = along[0:1, :] + jnp.log2(lane_sums(sums)) + jnp.zeros((cells, 1), jnp.float32)
            return carry

        lax.fori_loop(0, shards, total, 0)
        for step in range(shards):
            used = jnp.max(mask_ref[step], axis=0, keepdims=True) > 0.5 * very_low
            outs[step][...] = jnp.where(used, acc_ref[step * cells : step * cells + 1, :], very_low)


def merge_kernel(shards, *refs):
    parts, (mass_ref, poten_ref, out_ref) = refs[:shards], refs[shards:]
    values = jnp.concatenate([part[...] for part in parts], axis=0)
    top = jnp.max(values, axis=0, keepdims=True)
    whole = top + jnp.log2(jnp.sum(jnp.exp2(values - top), axis=0, keepdims=True))
    out_ref[...] = -(entropic * ln2) * (whole - target_weight(mass_ref[...], poten_ref[...]))


def f32(*shape):
    return jax.ShapeDtypeStruct(shape, jnp.float32)


def dense_device(
    source_feat, target_feat, log_mass_src, log_mass_tgt, potential_tgt, support, counts
):
    shards = lax.axis_size("src")
    rows, depth, cells = source_feat.shape
    pairs, wide = rows // 2, 2 * cells

    def call(kernel, count, out_shape, scratch=()):
        many = isinstance(out_shape, (list, tuple))
        return pl.pallas_call(
            kernel,
            in_specs=[VM] * count,
            out_specs=[VM] * len(out_shape) if many else VM,
            out_shape=out_shape,
            scratch_shapes=list(scratch),
            compiler_params=PARAMS,
        )

    pack = call(pack_kernel, 3, f32(depth + 8, cells))(target_feat, log_mass_tgt, potential_tgt)

    def shifted(array, step):
        return lax.ppermute(array, "src", [(i, (i + step) % shards) for i in range(shards)])

    packs = [pack] + [shifted(pack, shards - step) for step in range(1, shards)]
    wide_feat, norm, mask = call(
        functools.partial(source_kernel, shards),
        3,
        [in_vmem((pairs, 8 * depth, wide), jnp.bfloat16), f32(rows, cells), f32(shards, rows, cells)],
    )(source_feat, support[:, 0, :], counts)
    exps, tall, peaks, own = call(
        functools.partial(row_kernel, shards),
        shards + 2,
        [
            in_vmem((pairs, shards * cells, wide), jnp.float32),
            in_vmem((shards * cells, 8 * depth), jnp.bfloat16),
            f32(shards, rows, cells),
            f32(rows, cells),
        ],
        [pltpu.VMEM((shards, rows, cells), jnp.float32)],
    )(*packs, wide_feat, mask)
    other = lax.ppermute(own, "tgt", [(0, 1), (1, 0)])
    potential_src, *columns = call(
        functools.partial(column_kernel, shards),
        9,
        [f32(rows, cells)] + [f32(1, cells)] * shards,
        [
            pltpu.VMEM((shards, rows, cells), jnp.float32),
            pltpu.VMEM((shards * cells, cells), jnp.float32),
            pltpu.VMEM((rows, cells), jnp.float32),
        ],
    )(exps, tall, wide_feat, peaks, mask, own, other, log_mass_src, norm)
    arrived = [columns[0]] + [shifted(columns[step], step) for step in range(1, shards)]
    potential_new = call(functools.partial(merge_kernel, shards), shards + 2, f32(1, cells))(
        *arrived, log_mass_tgt, potential_tgt
    )
    return potential_src, potential_new


def merged(part, axis, combine):
    gathered = jax.tree.map(lambda a: lax.all_gather(a, axis), part)

    def take(source):
        return jax.tree.map(lambda a: lax.dynamic_index_in_dim(a, source, 0, False), gathered)

    return lax.fori_loop(
        1, lax.axis_size(axis), lambda source, state: combine(state, take(source)), take(0)
    )


def cost_tiles(source_blk, source_sq, target_blk, target_sq):
    cross = jnp.einsum(
        "...fi,...fj->...ij", source_blk, target_blk, precision=lax.Precision.HIGHEST
    )
    return source_sq[..., :, None] + target_sq[..., None, :] - 2.0 * cross


def row_stats(cost, mass_tgt, poten_tgt, usable):
    scores = mass_tgt[..., None, :] + (poten_tgt[..., None, :] - cost) / entropic
    scores = jnp.where(usable[..., None, None], scores, very_low)
    peak = jnp.max(scores, axis=(1, 3))
    total = jnp.sum(jnp.exp(scores - peak[:, None, :, None]), axis=(1, 3))
    return (peak, total)


def column_stats(cost, mass_src, poten_src, usable):
    scores = mass_src[:, None, :, None] + (poten_src[:, None, :, None] - cost) / entropic
    peak = jnp.max(scores, axis=2)
    total = jnp.sum(jnp.exp(scores - peak[:, :, None, :]), axis=2)
    peak = jnp.where(usable[..., None], peak, very_low)
    total = jnp.where(usable[..., None], total, 0.0)
    return (peak, total)


def merge_pair(first_pair, second_pair):
    first_peak, first_total = first_pair
    second_peak, second_total = second_pair
    highest = jnp.maximum(first_peak, second_peak)
    summed = first_total * jnp.exp(first_peak - highest) + second_total * jnp.exp(
        second_peak - highest
    )
    return (highest, summed)


def segment_merge(peaks, totals, seg_ids, segments):
    best = jax.ops.segment_max(peaks, seg_ids, num_segments=segments + 1)
    best = jnp.maximum(best, very_low)
    summed = jax.ops.segment_sum(
        totals * jnp.exp(peaks - best[seg_ids]), seg_ids, num_segments=segments + 1
    )
    return (best[:segments], summed[:segments])


def general_device(
    source_feat, target_feat, log_mass_src, log_mass_tgt, potential_tgt, support, counts
):
    target_all, mass_all, poten_all = (
        lax.all_gather(target_feat, "src", axis=0, tiled=True),
        lax.all_gather(log_mass_tgt, "src", axis=0, tiled=True),
        lax.all_gather(potential_tgt, "src", axis=0, tiled=True),
    )
    blocks = target_all.shape[0]
    rows_here = source_feat.shape[0]
    slots_here = support.shape[2]
    cells = source_feat.shape[2]
    indices = support[:, 0, :]
    limits = counts[:, 0]
    usable = jnp.arange(slots_here, dtype=jnp.int32)[None, :] < limits[:, None]
    source_sq = jnp.sum(source_feat * source_feat, axis=1)
    target_sq = jnp.sum(target_all * target_all, axis=1)
    width = math.gcd(rows_here, 4)

    def grouped(array):
        return array.reshape((rows_here // width, width) + array.shape[1:])

    def row_pass(items):
        source_blk, source_nrm, ids_here, use_here = items
        cost = cost_tiles(
            source_blk[:, None], source_nrm[:, None], target_all[ids_here], target_sq[ids_here]
        )
        return row_stats(cost, mass_all[ids_here], poten_all[ids_here], use_here)

    peak, total = lax.map(
        row_pass, (grouped(source_feat), grouped(source_sq), grouped(indices), grouped(usable))
    )
    peak = peak.reshape(rows_here, cells)
    total = total.reshape(rows_here, cells)
    peak_all, total_all = merged((peak, total), "tgt", merge_pair)
    potential_src = -entropic * (peak_all + jnp.log(total_all))

    def column_pass(items):
        source_blk, source_nrm, mass_here, poten_here, ids_here, use_here = items
        cost = cost_tiles(
            source_blk[:, None], source_nrm[:, None], target_all[ids_here], target_sq[ids_here]
        )
        return column_stats(cost, mass_here, poten_here, use_here)

    peaks, totals = lax.map(
        column_pass,
        (
            grouped(source_feat),
            grouped(source_sq),
            grouped(log_mass_src),
            grouped(potential_src),
            grouped(indices),
            grouped(usable),
        ),
    )
    seg_ids = jnp.where(usable, indices, blocks).reshape(-1)
    best, summed = segment_merge(
        peaks.reshape(-1, cells), totals.reshape(-1, cells), seg_ids, blocks
    )
    share = blocks // lax.axis_size("src")
    own_start = lax.axis_index("src") * share
    highest = lax.pmax(best, "src")
    whole = lax.psum(summed * jnp.exp(best - highest), "src")
    own_peak = lax.dynamic_slice_in_dim(highest, own_start, share, 0)
    own_total = lax.dynamic_slice_in_dim(whole, own_start, share, 0)
    potential_new = -entropic * (own_peak + jnp.log(own_total))
    return (potential_src, potential_new)


def per_device(source_feat, target_feat, *others):
    shards = lax.axis_size("src")
    rows, depth, cells = source_feat.shape
    few = shards == 8 and target_feat.shape[0] == 1 and lax.axis_size("tgt") == 2
    if few and rows % 2 == 0 and cells == 128 and depth == 64:
        return dense_device(source_feat, target_feat, *others)
    return general_device(source_feat, target_feat, *others)


def solution(mesh):
    in_specs = (
        P(("grp", "src"), None, None),
        P(("grp", "src", "tgt"), None, None),
        P(("grp", "src"), None),
        P(("grp", "src", "tgt"), None),
        P(("grp", "src", "tgt"), None),
        P(("grp", "src"), "tgt", None),
        P(("grp", "src"), "tgt"),
    )
    out_specs = (P(("grp", "src"), None), P(("grp", "src", "tgt"), None))
    return jax.shard_map(
        per_device, mesh=mesh, in_specs=in_specs, out_specs=out_specs, check_vma=False
    )
```

```python
import functools
import math

import jax
import jax.numpy as jnp
from jax import lax
from jax.experimental import pallas as pl
from jax.experimental.pallas import tpu as pltpu
from jax.sharding import PartitionSpec as P

entropic = 0.5
very_low = -1e30
log2e = 1.0 / math.log(2.0)
ln2 = math.log(2.0)
least_sum = 1e-28

VM = pl.BlockSpec(memory_space=pltpu.VMEM)
PARAMS = pltpu.CompilerParams(vmem_limit_bytes=40 * 2**20)


def in_vmem(shape, dtype):
    return pltpu.VMEM(shape, dtype)


def pieces(values):
    high = values.astype(jnp.bfloat16).astype(jnp.float32)
    rest = values - high
    mid = rest.astype(jnp.bfloat16).astype(jnp.float32)
    low = (rest - mid).astype(jnp.bfloat16).astype(jnp.float32)
    return high, mid, low


def target_weight(mass, poten):
    return (mass + poten / entropic) * log2e


def entry_kernel(shards, *refs):
    hbm, outs, held, sems = refs[:7], refs[7:13], refs[13:20], refs[20]
    send_ref, wide_ref, norm_ref, mask_ref, own_ref, mass_out_ref = outs
    feat_ref, target_ref, mass_ref, tmass_ref, tpoten_ref, support_ref, counts_ref = held
    copies = [pltpu.make_async_copy(src, dst, sems.at[i]) for i, (src, dst) in enumerate(zip(hbm, held))]
    for copy in copies[1:] + copies[:1]:
        copy.start()
    for copy in copies[1:]:
        copy.wait()
    target = target_ref[0]
    depth, cells = target.shape
    weight = target_weight(tmass_ref[...], tpoten_ref[...])
    norm = jnp.sum(target * target, axis=0, keepdims=True)
    bias = weight - (log2e / entropic) * norm
    scaled = target * (2.0 * log2e / entropic)
    below = jnp.broadcast_to(bias, (send_ref.shape[1] - depth, cells))
    for step in range(shards):
        send_ref[step, :depth, :] = scaled
        send_ref[step, depth:, :] = below
    own_ref[...] = weight
    mass_out_ref[...] = mass_ref[...]
    support = support_ref[...]
    slots, rows = support.shape
    used = lax.broadcasted_iota(jnp.int32, support.shape, 0) < counts_ref[...]
    hits = [
        jnp.max(jnp.where(used & (support == block), 0.0, very_low), axis=0, keepdims=True)
        for block in range(shards)
    ]
    hits = jnp.concatenate(hits + [jnp.zeros((cells - shards, rows), jnp.float32)], axis=0)
    hits = jnp.concatenate([hits, jnp.zeros((cells, cells - rows), jnp.float32)], axis=1).T
    for block in range(shards):
        mask_ref[block] = jnp.broadcast_to(hits[:rows, block : block + 1], (rows, cells))
    copies[0].wait()
    one = jnp.ones((2 * depth, 2 * cells), jnp.bfloat16)
    for pair in range(rows // 2):
        for half in range(2):
            feat = feat_ref[2 * pair + half]
            norm_ref[2 * pair + half : 2 * pair + half + 1, :] = jnp.sum(feat * feat, axis=0, keepdims=True)
            high, mid, low = pieces(feat)
            lanes = slice(half * cells, (half + 1) * cells)
            top = jnp.concatenate([high, mid], axis=0).astype(jnp.bfloat16)
            wide_ref[pair, 0 : 2 * depth, lanes] = top
            wide_ref[pair, 2 * depth : 4 * depth, lanes] = top
            wide_ref[pair, 4 * depth : 6 * depth, lanes] = jnp.concatenate([low, high], axis=0).astype(jnp.bfloat16)
        wide_ref[pair, 6 * depth : 8 * depth, :] = one


def row_kernel(shards, *refs):
    packs_ref, wide_ref, mask_ref, exps_ref, tall_ref, peak_ref, rowsum_ref, total_ref = refs
    packs = [packs_ref.at[step] for step in range(shards)]
    pairs, _, both = wide_ref.shape
    cells = both // 2
    depth = cells // 2
    lane = lax.broadcasted_iota(jnp.int32, (cells, cells), 1)
    biases = jnp.concatenate([pack[depth : depth + 1, :] for pack in packs], axis=0)
    bias_pieces = jnp.concatenate(list(pieces(biases)), axis=0)
    padded = jnp.concatenate([bias_pieces, jnp.zeros((cells - 3 * shards, cells), jnp.float32)], axis=0)
    bias_lanes = padded.T
    for step, pack in enumerate(packs):
        feat = pack[:depth, :]
        turned = jnp.concatenate([feat, feat], axis=0).T
        high, mid, low = pieces(turned)
        own = jnp.where(lax.rem(lane, shards) == step, bias_lanes, 0.0)
        rows = slice(step * cells, (step + 1) * cells)
        tall_ref[rows, 0:cells] = high.astype(jnp.bfloat16)
        tall_ref[rows, cells : 2 * cells] = mid.astype(jnp.bfloat16)
        tall_ref[rows, 2 * cells : 3 * cells] = jnp.where(lane < depth, high, low).astype(jnp.bfloat16)
        tall_ref[rows, 3 * cells : 4 * cells] = own.astype(jnp.bfloat16)

    def body(pair, carry):
        weights = wide_ref[pair]
        for step in range(shards):
            rows = slice(step * cells, (step + 1) * cells)
            score = jnp.dot(tall_ref[rows, :], weights, preferred_element_type=jnp.float32)
            peak = jnp.max(score, axis=0, keepdims=True)
            exps = jnp.exp2(score - peak)
            exps_ref[pair, rows, :] = exps
            total = jnp.sum(exps, axis=0, keepdims=True)
            for half in range(2):
                lanes = slice(half * cells, (half + 1) * cells)
                peak_ref[step, pl.ds(2 * pair + half, 1), :] = peak[:, lanes]
                total_ref[step, pl.ds(2 * pair + half, 1), :] = total[:, lanes]
        return carry

    lax.fori_loop(0, pairs, body, 0)
    masked = [peak_ref[step] + mask_ref[step] for step in range(shards)]
    top = functools.reduce(jnp.maximum, masked)
    summed = sum(total_ref[step] * jnp.exp2(masked[step] - top) for step in range(shards))
    for step in range(shards):
        peak_ref[step] = masked[step]
    rowsum_ref[...] = top + jnp.log2(summed)


def lane_sums(values):
    ones = jnp.ones((8, values.shape[1]), jnp.bfloat16)
    parts = [
        lax.dot_general(ones, part.astype(jnp.bfloat16), (((1,), (1,)), ((), ())), preferred_element_type=jnp.float32)
        for part in pieces(values)
    ]
    return sum(parts)[0:1, :]


def column_kernel(shards, *refs):
    ins, rest = refs[:9], refs[9:]
    exps_ref, tall_ref, wide_ref, peak_ref, mask_ref, own_ref, other_ref, mass_ref, norm_ref = ins
    poten_ref, sums_ref, weight_ref, acc_ref, shift_ref = rest
    pairs, _, both = wide_ref.shape
    cells = both // 2
    own, other = own_ref[...], other_ref[...]
    top = jnp.maximum(own, other)
    whole = top + jnp.log2(jnp.exp2(own - top) + jnp.exp2(other - top))
    poten_ref[...] = norm_ref[...] - (entropic * ln2) * whole
    shift = mass_ref[...] * log2e - whole
    shift_ref[...] = shift
    for step in range(shards):
        weight_ref[step] = jnp.exp2(peak_ref[step] + shift)
    for step in range(shards):
        rows = slice(step * cells, (step + 1) * cells)
        acc = jnp.zeros((cells, cells), jnp.float32)
        for pair in range(pairs):
            acc = acc + exps_ref[pair, rows, :cells] * weight_ref[step, 2 * pair : 2 * pair + 1, :]
            acc = acc + exps_ref[pair, rows, cells:] * weight_ref[step, 2 * pair + 1 : 2 * pair + 2, :]
        acc_ref[rows, :] = acc
    sums = lane_sums(acc_ref[...])
    worst = jnp.full((1, cells), 1.0, jnp.float32)
    for step in range(shards):
        used = jnp.max(mask_ref[step], axis=0, keepdims=True) > 0.5 * very_low
        here = sums[:, step * cells : (step + 1) * cells]
        sums_ref[step] = jnp.where(used, jnp.log2(here), very_low)
        worst = jnp.minimum(worst, jnp.where(used, here, 1.0))

    @pl.when(jnp.min(worst) < least_sum)
    def _():
        acc_ref[...] = jnp.full(acc_ref.shape, very_low, jnp.float32)

        def exponents(pair, step):
            score = jnp.dot(
                tall_ref[pl.ds(pl.multiple_of(step * cells, cells), cells), :],
                wide_ref[pair],
                preferred_element_type=jnp.float32,
            )
            add = shift_ref[pl.ds(2 * pair, 2), :] + mask_ref[step, pl.ds(2 * pair, 2), :]
            return score[:, :cells] + add[0:1, :], score[:, cells:] + add[1:2, :]

        def highest(index, carry):
            pair, step = index // shards, lax.rem(index, shards)
            rows = pl.ds(pl.multiple_of(step * cells, cells), cells)
            first, second = exponents(pair, step)
            acc_ref[rows, :] = jnp.maximum(acc_ref[rows, :], jnp.maximum(first, second))
            return carry

        lax.fori_loop(0, pairs * shards, highest, 0)

        def total(step, carry):
            rows = pl.ds(pl.multiple_of(step * cells, cells), cells)
            peak = jnp.max(acc_ref[rows, :], axis=1, keepdims=True)

            def add(pair, sums):
                first, second = exponents(pair, step)
                return sums + jnp.exp2(first - peak) + jnp.exp2(second - peak)

            sums = lax.fori_loop(0, pairs, add, jnp.zeros((cells, cells), jnp.float32))
            along = jnp.broadcast_to(peak, (cells, cells)).T
            acc_ref[rows, :] = along[0:1, :] + jnp.log2(lane_sums(sums)) + jnp.zeros((cells, 1), jnp.float32)
            return carry

        lax.fori_loop(0, shards, total, 0)
        for step in range(shards):
            used = jnp.max(mask_ref[step], axis=0, keepdims=True) > 0.5 * very_low
            sums_ref[step] = jnp.where(used, acc_ref[step * cells : step * cells + 1, :], very_low)


def merge_kernel(values_ref, weight_ref, out_ref):
    values = values_ref[...]
    top = jnp.max(values, axis=0)
    whole = top + jnp.log2(jnp.sum(jnp.exp2(values - top), axis=0))
    out_ref[...] = -(entropic * ln2) * (whole - weight_ref[...])


def f32(*shape):
    return jax.ShapeDtypeStruct(shape, jnp.float32)


def dense_device(
    source_feat, target_feat, log_mass_src, log_mass_tgt, potential_tgt, support, counts
):
    shards = lax.axis_size("src")
    rows, depth, cells = source_feat.shape
    pairs, wide = rows // 2, 2 * cells

    def call(kernel, ins, out_shape, scratch=()):
        many = isinstance(out_shape, list)
        return pl.pallas_call(
            kernel,
            in_specs=ins,
            out_specs=[VM] * len(out_shape) if many else VM,
            out_shape=out_shape,
            scratch_shapes=list(scratch),
            compiler_params=PARAMS,
        )

    args = [source_feat, target_feat, log_mass_src, log_mass_tgt, potential_tgt, support[:, 0, :].T, counts.T]
    args = [pltpu.with_memory_space_constraint(arg, pltpu.HBM) for arg in args]
    send, wide_feat, norm, mask, weight, mass = call(
        functools.partial(entry_kernel, shards),
        [pl.BlockSpec(memory_space=pltpu.HBM)] * len(args),
        [
            in_vmem((shards, depth + 8, cells), jnp.float32),
            in_vmem((pairs, 8 * depth, wide), jnp.bfloat16),
            in_vmem((rows, cells), jnp.float32),
            in_vmem((shards, rows, cells), jnp.float32),
            in_vmem((1, cells), jnp.float32),
            in_vmem((rows, cells), jnp.float32),
        ],
        [pltpu.VMEM(arg.shape, arg.dtype) for arg in args] + [pltpu.SemaphoreType.DMA((len(args),))],
    )(*args)
    packs = lax.all_to_all(send, "src", 0, 0)
    exps, tall, peaks, own = call(
        functools.partial(row_kernel, shards),
        [VM] * 3,
        [
            in_vmem((pairs, shards * cells, wide), jnp.float32),
            in_vmem((shards * cells, 8 * depth), jnp.bfloat16),
            in_vmem((shards, rows, cells), jnp.float32),
            in_vmem((rows, cells), jnp.float32),
        ],
        [pltpu.VMEM((shards, rows, cells), jnp.float32)],
    )(packs, wide_feat, mask)
    other = lax.ppermute(own, "tgt", [(0, 1), (1, 0)])
    potential_src, columns = call(
        functools.partial(column_kernel, shards),
        [VM] * 9,
        [f32(rows, cells), in_vmem((shards, 1, cells), jnp.float32)],
        [
            pltpu.VMEM((shards, rows, cells), jnp.float32),
            pltpu.VMEM((shards * cells, cells), jnp.float32),
            pltpu.VMEM((rows, cells), jnp.float32),
        ],
    )(exps, tall, wide_feat, peaks, mask, own, other, mass, norm)
    arrived = lax.all_to_all(columns, "src", 0, 0)
    potential_new = call(merge_kernel, [VM] * 2, f32(1, cells))(arrived, weight)
    return potential_src, potential_new


def merged(part, axis, combine):
    gathered = jax.tree.map(lambda a: lax.all_gather(a, axis), part)

    def take(source):
        return jax.tree.map(lambda a: lax.dynamic_index_in_dim(a, source, 0, False), gathered)

    return lax.fori_loop(
        1, lax.axis_size(axis), lambda source, state: combine(state, take(source)), take(0)
    )


def cost_tiles(source_blk, source_sq, target_blk, target_sq):
    cross = jnp.einsum(
        "...fi,...fj->...ij", source_blk, target_blk, precision=lax.Precision.HIGHEST
    )
    return source_sq[..., :, None] + target_sq[..., None, :] - 2.0 * cross


def row_stats(cost, mass_tgt, poten_tgt, usable):
    scores = mass_tgt[..., None, :] + (poten_tgt[..., None, :] - cost) / entropic
    scores = jnp.where(usable[..., None, None], scores, very_low)
    peak = jnp.max(scores, axis=(1, 3))
    total = jnp.sum(jnp.exp(scores - peak[:, None, :, None]), axis=(1, 3))
    return (peak, total)


def column_stats(cost, mass_src, poten_src, usable):
    scores = mass_src[:, None, :, None] + (poten_src[:, None, :, None] - cost) / entropic
    peak = jnp.max(scores, axis=2)
    total = jnp.sum(jnp.exp(scores - peak[:, :, None, :]), axis=2)
    peak = jnp.where(usable[..., None], peak, very_low)
    total = jnp.where(usable[..., None], total, 0.0)
    return (peak, total)


def merge_pair(first_pair, second_pair):
    first_peak, first_total = first_pair
    second_peak, second_total = second_pair
    highest = jnp.maximum(first_peak, second_peak)
    summed = first_total * jnp.exp(first_peak - highest) + second_total * jnp.exp(
        second_peak - highest
    )
    return (highest, summed)


def segment_merge(peaks, totals, seg_ids, segments):
    best = jax.ops.segment_max(peaks, seg_ids, num_segments=segments + 1)
    best = jnp.maximum(best, very_low)
    summed = jax.ops.segment_sum(
        totals * jnp.exp(peaks - best[seg_ids]), seg_ids, num_segments=segments + 1
    )
    return (best[:segments], summed[:segments])


def general_device(
    source_feat, target_feat, log_mass_src, log_mass_tgt, potential_tgt, support, counts
):
    target_all, mass_all, poten_all = (
        lax.all_gather(target_feat, "src", axis=0, tiled=True),
        lax.all_gather(log_mass_tgt, "src", axis=0, tiled=True),
        lax.all_gather(potential_tgt, "src", axis=0, tiled=True),
    )
    blocks = target_all.shape[0]
    rows_here = source_feat.shape[0]
    slots_here = support.shape[2]
    cells = source_feat.shape[2]
    indices = support[:, 0, :]
    limits = counts[:, 0]
    usable = jnp.arange(slots_here, dtype=jnp.int32)[None, :] < limits[:, None]
    source_sq = jnp.sum(source_feat * source_feat, axis=1)
    target_sq = jnp.sum(target_all * target_all, axis=1)
    width = math.gcd(rows_here, 4)

    def grouped(array):
        return array.reshape((rows_here // width, width) + array.shape[1:])

    def row_pass(items):
        source_blk, source_nrm, ids_here, use_here = items
        cost = cost_tiles(
            source_blk[:, None], source_nrm[:, None], target_all[ids_here], target_sq[ids_here]
        )
        return row_stats(cost, mass_all[ids_here], poten_all[ids_here], use_here)

    peak, total = lax.map(
        row_pass, (grouped(source_feat), grouped(source_sq), grouped(indices), grouped(usable))
    )
    peak = peak.reshape(rows_here, cells)
    total = total.reshape(rows_here, cells)
    peak_all, total_all = merged((peak, total), "tgt", merge_pair)
    potential_src = -entropic * (peak_all + jnp.log(total_all))

    def column_pass(items):
        source_blk, source_nrm, mass_here, poten_here, ids_here, use_here = items
        cost = cost_tiles(
            source_blk[:, None], source_nrm[:, None], target_all[ids_here], target_sq[ids_here]
        )
        return column_stats(cost, mass_here, poten_here, use_here)

    peaks, totals = lax.map(
        column_pass,
        (
            grouped(source_feat),
            grouped(source_sq),
            grouped(log_mass_src),
            grouped(potential_src),
            grouped(indices),
            grouped(usable),
        ),
    )
    seg_ids = jnp.where(usable, indices, blocks).reshape(-1)
    best, summed = segment_merge(
        peaks.reshape(-1, cells), totals.reshape(-1, cells), seg_ids, blocks
    )
    share = blocks // lax.axis_size("src")
    own_start = lax.axis_index("src") * share
    highest = lax.pmax(best, "src")
    whole = lax.psum(summed * jnp.exp(best - highest), "src")
    own_peak = lax.dynamic_slice_in_dim(highest, own_start, share, 0)
    own_total = lax.dynamic_slice_in_dim(whole, own_start, share, 0)
    potential_new = -entropic * (own_peak + jnp.log(own_total))
    return (potential_src, potential_new)


def per_device(source_feat, target_feat, *others):
    shards = lax.axis_size("src")
    rows, depth, cells = source_feat.shape
    few = shards == 8 and target_feat.shape[0] == 1 and lax.axis_size("tgt") == 2
    if few and rows % 2 == 0 and cells == 128 and depth == 64:
        return dense_device(source_feat, target_feat, *others)
    return general_device(source_feat, target_feat, *others)


def solution(mesh):
    in_specs = (
        P(("grp", "src"), None, None),
        P(("grp", "src", "tgt"), None, None),
        P(("grp", "src"), None),
        P(("grp", "src", "tgt"), None),
        P(("grp", "src", "tgt"), None),
        P(("grp", "src"), "tgt", None),
        P(("grp", "src"), "tgt"),
    )
    out_specs = (P(("grp", "src"), None), P(("grp", "src", "tgt"), None))
    return jax.shard_map(
        per_device, mesh=mesh, in_specs=in_specs, out_specs=out_specs, check_vma=False
    )
```

```python
import functools
import math

import jax
import jax.numpy as jnp
from jax import lax
from jax.experimental import pallas as pl
from jax.experimental.pallas import tpu as pltpu
from jax.sharding import PartitionSpec as P

entropic = 0.5
very_low = -1e30
log2e = 1.0 / math.log(2.0)
ln2 = math.log(2.0)
least_sum = 1e-28

VM = pl.BlockSpec(memory_space=pltpu.VMEM)
PARAMS = pltpu.CompilerParams(vmem_limit_bytes=40 * 2**20)


def in_vmem(shape, dtype):
    return pltpu.VMEM(shape, dtype)


def pieces(values):
    high = values.astype(jnp.bfloat16).astype(jnp.float32)
    rest = values - high
    mid = rest.astype(jnp.bfloat16).astype(jnp.float32)
    low = (rest - mid).astype(jnp.bfloat16).astype(jnp.float32)
    return high, mid, low


def target_weight(mass, poten):
    return (mass + poten / entropic) * log2e


def entry_kernel(shards, *refs):
    hbm, outs, held, sems = refs[:7], refs[7:13], refs[13:20], refs[20]
    send_ref, wide_ref, norm_ref, mask_ref, own_ref, mass_out_ref = outs
    feat_ref, target_ref, mass_ref, tmass_ref, tpoten_ref, support_ref, counts_ref = held
    copies = [pltpu.make_async_copy(src, dst, sems.at[i]) for i, (src, dst) in enumerate(zip(hbm, held))]
    for copy in copies[1:] + copies[:1]:
        copy.start()
    for copy in copies[1:]:
        copy.wait()
    target = target_ref[0]
    depth, cells = target.shape
    weight = target_weight(tmass_ref[...], tpoten_ref[...])
    norm = jnp.sum(target * target, axis=0, keepdims=True)
    bias = weight - (log2e / entropic) * norm
    scaled = target * (2.0 * log2e / entropic)
    below = jnp.broadcast_to(bias, (send_ref.shape[1] - depth, cells))
    send_ref[0, :depth, :] = scaled
    send_ref[0, depth:, :] = below
    own_ref[...] = weight
    mass_out_ref[...] = mass_ref[...]
    support = support_ref[...]
    slots, rows = support.shape
    used = lax.broadcasted_iota(jnp.int32, support.shape, 0) < counts_ref[...]
    hits = [
        jnp.max(jnp.where(used & (support == block), 0.0, very_low), axis=0, keepdims=True)
        for block in block_order(shards)
    ]
    hits = jnp.concatenate(hits + [jnp.zeros((cells - shards, rows), jnp.float32)], axis=0)
    hits = jnp.concatenate([hits, jnp.zeros((cells, cells - rows), jnp.float32)], axis=1).T
    for block in range(shards):
        mask_ref[block] = jnp.broadcast_to(hits[:rows, block : block + 1], (rows, cells))
    copies[0].wait()
    one = jnp.ones((2 * depth, 2 * cells), jnp.bfloat16)
    for pair in range(rows // 2):
        for half in range(2):
            feat = feat_ref[2 * pair + half]
            norm_ref[2 * pair + half : 2 * pair + half + 1, :] = jnp.sum(feat * feat, axis=0, keepdims=True)
            high, mid, low = pieces(feat)
            lanes = slice(half * cells, (half + 1) * cells)
            top = jnp.concatenate([high, mid], axis=0).astype(jnp.bfloat16)
            wide_ref[pair, 0 : 2 * depth, lanes] = top
            wide_ref[pair, 2 * depth : 4 * depth, lanes] = top
            wide_ref[pair, 4 * depth : 6 * depth, lanes] = jnp.concatenate([low, high], axis=0).astype(jnp.bfloat16)
        wide_ref[pair, 6 * depth : 8 * depth, :] = one


def row_kernel(shards, *refs):
    packs_ref, wide_ref, mask_ref, exps_ref, tall_ref, peak_ref, rowsum_ref, total_ref = refs
    packs = [packs_ref.at[step] for step in range(shards)]
    pairs, _, both = wide_ref.shape
    cells = both // 2
    depth = cells // 2
    lane = lax.broadcasted_iota(jnp.int32, (cells, cells), 1)
    biases = jnp.concatenate([pack[depth : depth + 1, :] for pack in packs], axis=0)
    bias_pieces = jnp.concatenate(list(pieces(biases)), axis=0)
    padded = jnp.concatenate([bias_pieces, jnp.zeros((cells - 3 * shards, cells), jnp.float32)], axis=0)
    bias_lanes = padded.T
    for step, pack in enumerate(packs):
        feat = pack[:depth, :]
        turned = jnp.concatenate([feat, feat], axis=0).T
        high, mid, low = pieces(turned)
        own = jnp.where(lax.rem(lane, shards) == step, bias_lanes, 0.0)
        rows = slice(step * cells, (step + 1) * cells)
        tall_ref[rows, 0:cells] = high.astype(jnp.bfloat16)
        tall_ref[rows, cells : 2 * cells] = mid.astype(jnp.bfloat16)
        tall_ref[rows, 2 * cells : 3 * cells] = jnp.where(lane < depth, high, low).astype(jnp.bfloat16)
        tall_ref[rows, 3 * cells : 4 * cells] = own.astype(jnp.bfloat16)

    def body(pair, carry):
        weights = wide_ref[pair]
        for step in range(shards):
            rows = slice(step * cells, (step + 1) * cells)
            score = jnp.dot(tall_ref[rows, :], weights, preferred_element_type=jnp.float32)
            peak = jnp.max(score, axis=0, keepdims=True)
            exps = jnp.exp2(score - peak)
            exps_ref[pair, rows, :] = exps
            total = jnp.sum(exps, axis=0, keepdims=True)
            for half in range(2):
                lanes = slice(half * cells, (half + 1) * cells)
                peak_ref[step, pl.ds(2 * pair + half, 1), :] = peak[:, lanes]
                total_ref[step, pl.ds(2 * pair + half, 1), :] = total[:, lanes]
        return carry

    lax.fori_loop(0, pairs, body, 0)
    masked = [peak_ref[step] + mask_ref[step] for step in range(shards)]
    top = functools.reduce(jnp.maximum, masked)
    summed = sum(total_ref[step] * jnp.exp2(masked[step] - top) for step in range(shards))
    for step in range(shards):
        peak_ref[step] = masked[step]
    rowsum_ref[...] = top + jnp.log2(summed)


def lane_sums(values):
    ones = jnp.ones((8, values.shape[1]), jnp.bfloat16)
    parts = [
        lax.dot_general(ones, part.astype(jnp.bfloat16), (((1,), (1,)), ((), ())), preferred_element_type=jnp.float32)
        for part in pieces(values)
    ]
    return sum(parts)[0:1, :]


def column_kernel(shards, *refs):
    ins, rest = refs[:9], refs[9:]
    exps_ref, tall_ref, wide_ref, peak_ref, mask_ref, own_ref, other_ref, mass_ref, norm_ref = ins
    poten_ref, sums_ref, weight_ref, acc_ref, shift_ref = rest
    pairs, _, both = wide_ref.shape
    cells = both // 2
    own, other = own_ref[...], other_ref[...]
    top = jnp.maximum(own, other)
    whole = top + jnp.log2(jnp.exp2(own - top) + jnp.exp2(other - top))
    poten_ref[...] = norm_ref[...] - (entropic * ln2) * whole
    shift = mass_ref[...] * log2e - whole
    shift_ref[...] = shift
    for step in range(shards):
        weight_ref[step] = jnp.exp2(peak_ref[step] + shift)
    for step in range(shards):
        rows = slice(step * cells, (step + 1) * cells)
        acc = jnp.zeros((cells, cells), jnp.float32)
        for pair in range(pairs):
            acc = acc + exps_ref[pair, rows, :cells] * weight_ref[step, 2 * pair : 2 * pair + 1, :]
            acc = acc + exps_ref[pair, rows, cells:] * weight_ref[step, 2 * pair + 1 : 2 * pair + 2, :]
        acc_ref[rows, :] = acc
    sums = lane_sums(acc_ref[...])
    worst = jnp.full((1, cells), 1.0, jnp.float32)
    for step in range(shards):
        used = jnp.max(mask_ref[step], axis=0, keepdims=True) > 0.5 * very_low
        here = sums[:, step * cells : (step + 1) * cells]
        sums_ref[step] = jnp.where(used, jnp.log2(here), very_low)
        worst = jnp.minimum(worst, jnp.where(used, here, 1.0))

    @pl.when(jnp.min(worst) < least_sum)
    def _():
        acc_ref[...] = jnp.full(acc_ref.shape, very_low, jnp.float32)

        def exponents(pair, step):
            score = jnp.dot(
                tall_ref[pl.ds(pl.multiple_of(step * cells, cells), cells), :],
                wide_ref[pair],
                preferred_element_type=jnp.float32,
            )
            add = shift_ref[pl.ds(2 * pair, 2), :] + mask_ref[step, pl.ds(2 * pair, 2), :]
            return score[:, :cells] + add[0:1, :], score[:, cells:] + add[1:2, :]

        def highest(index, carry):
            pair, step = index // shards, lax.rem(index, shards)
            rows = pl.ds(pl.multiple_of(step * cells, cells), cells)
            first, second = exponents(pair, step)
            acc_ref[rows, :] = jnp.maximum(acc_ref[rows, :], jnp.maximum(first, second))
            return carry

        lax.fori_loop(0, pairs * shards, highest, 0)

        def total(step, carry):
            rows = pl.ds(pl.multiple_of(step * cells, cells), cells)
            peak = jnp.max(acc_ref[rows, :], axis=1, keepdims=True)

            def add(pair, sums):
                first, second = exponents(pair, step)
                return sums + jnp.exp2(first - peak) + jnp.exp2(second - peak)

            sums = lax.fori_loop(0, pairs, add, jnp.zeros((cells, cells), jnp.float32))
            along = jnp.broadcast_to(peak, (cells, cells)).T
            acc_ref[rows, :] = along[0:1, :] + jnp.log2(lane_sums(sums)) + jnp.zeros((cells, 1), jnp.float32)
            return carry

        lax.fori_loop(0, shards, total, 0)
        for step in range(shards):
            used = jnp.max(mask_ref[step], axis=0, keepdims=True) > 0.5 * very_low
            sums_ref[step] = jnp.where(used, acc_ref[step * cells : step * cells + 1, :], very_low)


def merge_kernel(shards, values_ref, weight_ref, out_ref):
    me = lax.axis_index("src")
    order = block_order(shards)
    values = values_ref[:, 0]
    for place in range(1, shards):
        values = jnp.where(me == order[place], values_ref[:, place], values)
    top = jnp.max(values, axis=0)
    whole = top + jnp.log2(jnp.sum(jnp.exp2(values - top), axis=0))
    out_ref[...] = -(entropic * ln2) * (whole - weight_ref[...])


def block_order(shards):
    bits = shards.bit_length() - 1
    return [sum(((place >> bit) & 1) << (bits - 1 - bit) for bit in range(bits)) for place in range(shards)]


def pair_gather(array):
    shards = lax.axis_size("src")
    apart = shards // 2
    while apart:
        pairs = [[i, i + apart] for i in range(shards) if not i & apart]
        array = lax.all_gather(array, "src", axis=0, tiled=True, axis_index_groups=pairs)
        apart //= 2
    return array


def f32(*shape):
    return jax.ShapeDtypeStruct(shape, jnp.float32)


def dense_device(
    source_feat, target_feat, log_mass_src, log_mass_tgt, potential_tgt, support, counts
):
    shards = lax.axis_size("src")
    rows, depth, cells = source_feat.shape
    pairs, wide = rows // 2, 2 * cells

    def call(kernel, ins, out_shape, scratch=()):
        many = isinstance(out_shape, list)
        return pl.pallas_call(
            kernel,
            in_specs=ins,
            out_specs=[VM] * len(out_shape) if many else VM,
            out_shape=out_shape,
            scratch_shapes=list(scratch),
            compiler_params=PARAMS,
        )

    args = [source_feat, target_feat, log_mass_src, log_mass_tgt, potential_tgt, support[:, 0, :].T, counts.T]
    args = [pltpu.with_memory_space_constraint(arg, pltpu.HBM) for arg in args]
    send, wide_feat, norm, mask, weight, mass = call(
        functools.partial(entry_kernel, shards),
        [pl.BlockSpec(memory_space=pltpu.HBM)] * len(args),
        [
            in_vmem((1, depth + 8, cells), jnp.float32),
            in_vmem((pairs, 8 * depth, wide), jnp.bfloat16),
            in_vmem((rows, cells), jnp.float32),
            in_vmem((shards, rows, cells), jnp.float32),
            in_vmem((1, cells), jnp.float32),
            in_vmem((rows, cells), jnp.float32),
        ],
        [pltpu.VMEM(arg.shape, arg.dtype) for arg in args] + [pltpu.SemaphoreType.DMA((len(args),))],
    )(*args)
    packs = pair_gather(send)
    exps, tall, peaks, own = call(
        functools.partial(row_kernel, shards),
        [VM] * 3,
        [
            in_vmem((pairs, shards * cells, wide), jnp.float32),
            in_vmem((shards * cells, 8 * depth), jnp.bfloat16),
            in_vmem((shards, rows, cells), jnp.float32),
            in_vmem((rows, cells), jnp.float32),
        ],
        [pltpu.VMEM((shards, rows, cells), jnp.float32)],
    )(packs, wide_feat, mask)
    other = lax.ppermute(own, "tgt", [(0, 1), (1, 0)])
    potential_src, columns = call(
        functools.partial(column_kernel, shards),
        [VM] * 9,
        [f32(rows, cells), in_vmem((shards, 1, cells), jnp.float32)],
        [
            pltpu.VMEM((shards, rows, cells), jnp.float32),
            pltpu.VMEM((shards * cells, cells), jnp.float32),
            pltpu.VMEM((rows, cells), jnp.float32),
        ],
    )(exps, tall, wide_feat, peaks, mask, own, other, mass, norm)
    arrived = pair_gather(columns[None])
    potential_new = call(functools.partial(merge_kernel, shards), [VM] * 2, f32(1, cells))(arrived, weight)
    return potential_src, potential_new


def merged(part, axis, combine):
    gathered = jax.tree.map(lambda a: lax.all_gather(a, axis), part)

    def take(source):
        return jax.tree.map(lambda a: lax.dynamic_index_in_dim(a, source, 0, False), gathered)

    return lax.fori_loop(
        1, lax.axis_size(axis), lambda source, state: combine(state, take(source)), take(0)
    )


def cost_tiles(source_blk, source_sq, target_blk, target_sq):
    cross = jnp.einsum(
        "...fi,...fj->...ij", source_blk, target_blk, precision=lax.Precision.HIGHEST
    )
    return source_sq[..., :, None] + target_sq[..., None, :] - 2.0 * cross


def row_stats(cost, mass_tgt, poten_tgt, usable):
    scores = mass_tgt[..., None, :] + (poten_tgt[..., None, :] - cost) / entropic
    scores = jnp.where(usable[..., None, None], scores, very_low)
    peak = jnp.max(scores, axis=(1, 3))
    total = jnp.sum(jnp.exp(scores - peak[:, None, :, None]), axis=(1, 3))
    return (peak, total)


def column_stats(cost, mass_src, poten_src, usable):
    scores = mass_src[:, None, :, None] + (poten_src[:, None, :, None] - cost) / entropic
    peak = jnp.max(scores, axis=2)
    total = jnp.sum(jnp.exp(scores - peak[:, :, None, :]), axis=2)
    peak = jnp.where(usable[..., None], peak, very_low)
    total = jnp.where(usable[..., None], total, 0.0)
    return (peak, total)


def merge_pair(first_pair, second_pair):
    first_peak, first_total = first_pair
    second_peak, second_total = second_pair
    highest = jnp.maximum(first_peak, second_peak)
    summed = first_total * jnp.exp(first_peak - highest) + second_total * jnp.exp(
        second_peak - highest
    )
    return (highest, summed)


def segment_merge(peaks, totals, seg_ids, segments):
    best = jax.ops.segment_max(peaks, seg_ids, num_segments=segments + 1)
    best = jnp.maximum(best, very_low)
    summed = jax.ops.segment_sum(
        totals * jnp.exp(peaks - best[seg_ids]), seg_ids, num_segments=segments + 1
    )
    return (best[:segments], summed[:segments])


def general_device(
    source_feat, target_feat, log_mass_src, log_mass_tgt, potential_tgt, support, counts
):
    target_all, mass_all, poten_all = (
        lax.all_gather(target_feat, "src", axis=0, tiled=True),
        lax.all_gather(log_mass_tgt, "src", axis=0, tiled=True),
        lax.all_gather(potential_tgt, "src", axis=0, tiled=True),
    )
    blocks = target_all.shape[0]
    rows_here = source_feat.shape[0]
    slots_here = support.shape[2]
    cells = source_feat.shape[2]
    indices = support[:, 0, :]
    limits = counts[:, 0]
    usable = jnp.arange(slots_here, dtype=jnp.int32)[None, :] < limits[:, None]
    source_sq = jnp.sum(source_feat * source_feat, axis=1)
    target_sq = jnp.sum(target_all * target_all, axis=1)
    width = math.gcd(rows_here, 4)

    def grouped(array):
        return array.reshape((rows_here // width, width) + array.shape[1:])

    def row_pass(items):
        source_blk, source_nrm, ids_here, use_here = items
        cost = cost_tiles(
            source_blk[:, None], source_nrm[:, None], target_all[ids_here], target_sq[ids_here]
        )
        return row_stats(cost, mass_all[ids_here], poten_all[ids_here], use_here)

    peak, total = lax.map(
        row_pass, (grouped(source_feat), grouped(source_sq), grouped(indices), grouped(usable))
    )
    peak = peak.reshape(rows_here, cells)
    total = total.reshape(rows_here, cells)
    peak_all, total_all = merged((peak, total), "tgt", merge_pair)
    potential_src = -entropic * (peak_all + jnp.log(total_all))

    def column_pass(items):
        source_blk, source_nrm, mass_here, poten_here, ids_here, use_here = items
        cost = cost_tiles(
            source_blk[:, None], source_nrm[:, None], target_all[ids_here], target_sq[ids_here]
        )
        return column_stats(cost, mass_here, poten_here, use_here)

    peaks, totals = lax.map(
        column_pass,
        (
            grouped(source_feat),
            grouped(source_sq),
            grouped(log_mass_src),
            grouped(potential_src),
            grouped(indices),
            grouped(usable),
        ),
    )
    seg_ids = jnp.where(usable, indices, blocks).reshape(-1)
    best, summed = segment_merge(
        peaks.reshape(-1, cells), totals.reshape(-1, cells), seg_ids, blocks
    )
    share = blocks // lax.axis_size("src")
    own_start = lax.axis_index("src") * share
    highest = lax.pmax(best, "src")
    whole = lax.psum(summed * jnp.exp(best - highest), "src")
    own_peak = lax.dynamic_slice_in_dim(highest, own_start, share, 0)
    own_total = lax.dynamic_slice_in_dim(whole, own_start, share, 0)
    potential_new = -entropic * (own_peak + jnp.log(own_total))
    return (potential_src, potential_new)


def per_device(source_feat, target_feat, *others):
    shards = lax.axis_size("src")
    rows, depth, cells = source_feat.shape
    few = shards == 8 and target_feat.shape[0] == 1 and lax.axis_size("tgt") == 2
    if few and rows % 2 == 0 and cells == 128 and depth == 64:
        return dense_device(source_feat, target_feat, *others)
    return general_device(source_feat, target_feat, *others)


def solution(mesh):
    in_specs = (
        P(("grp", "src"), None, None),
        P(("grp", "src", "tgt"), None, None),
        P(("grp", "src"), None),
        P(("grp", "src", "tgt"), None),
        P(("grp", "src", "tgt"), None),
        P(("grp", "src"), "tgt", None),
        P(("grp", "src"), "tgt"),
    )
    out_specs = (P(("grp", "src"), None), P(("grp", "src", "tgt"), None))
    return jax.shard_map(
        per_device, mesh=mesh, in_specs=in_specs, out_specs=out_specs, check_vma=False
    )
```

```python
import functools
import math

import jax
import jax.numpy as jnp
from jax import lax
from jax.experimental import pallas as pl
from jax.experimental.pallas import tpu as pltpu
from jax.sharding import PartitionSpec as P

entropic = 0.5
very_low = -1e30
log2e = 1.0 / math.log(2.0)
ln2 = math.log(2.0)
least_sum = 1e-28

VM = pl.BlockSpec(memory_space=pltpu.VMEM)
PARAMS = pltpu.CompilerParams(vmem_limit_bytes=40 * 2**20)


def in_vmem(shape, dtype):
    return pltpu.VMEM(shape, dtype)


def pieces(values):
    high = values.astype(jnp.bfloat16).astype(jnp.float32)
    rest = values - high
    mid = rest.astype(jnp.bfloat16).astype(jnp.float32)
    low = (rest - mid).astype(jnp.bfloat16).astype(jnp.float32)
    return high, mid, low


def target_weight(mass, poten):
    return (mass + poten / entropic) * log2e


def partners(shards):
    found, apart = [0], shards // 2
    while apart:
        found += [other ^ apart for other in found]
        apart //= 2
    return found


def read_all(hbm, held, sems):
    copies = [pltpu.make_async_copy(src, dst, sems.at[i]) for i, (src, dst) in enumerate(zip(hbm, held))]
    for copy in copies:
        copy.start()
    return copies


def pack_kernel(*refs):
    hbm, (send_ref, weight_ref), held, sems = refs[:3], refs[3:5], refs[5:8], refs[8]
    for copy in read_all(hbm, held, sems):
        copy.wait()
    feat_ref, mass_ref, poten_ref = held
    feat = feat_ref[0]
    depth, cells = feat.shape
    weight = target_weight(mass_ref[...], poten_ref[...])
    norm = jnp.sum(feat * feat, axis=0, keepdims=True)
    bias = weight - (log2e / entropic) * norm
    send_ref[0, :depth, :] = feat * (2.0 * log2e / entropic)
    send_ref[0, depth:, :] = jnp.broadcast_to(bias, (send_ref.shape[1] - depth, cells))
    weight_ref[...] = weight


def source_kernel(shards, *refs):
    hbm, outs, held, sems = refs[:4], refs[4:8], refs[8:12], refs[12]
    wide_ref, norm_ref, mask_ref, mass_out_ref = outs
    mass_ref, support_ref, counts_ref, feat_ref = held
    copies = read_all(hbm, held, sems)
    for copy in copies[:3]:
        copy.wait()
    mass_out_ref[...] = mass_ref[...]
    support = support_ref[...]
    slots, rows = support.shape
    cells = mass_ref.shape[1]
    me = lax.axis_index("src")
    used = lax.broadcasted_iota(jnp.int32, support.shape, 0) < counts_ref[...]
    hits = [
        jnp.max(jnp.where(used & (support == (me ^ other)), 0.0, very_low), axis=0, keepdims=True)
        for other in partners(shards)
    ]
    hits = jnp.concatenate(hits + [jnp.zeros((cells - shards, rows), jnp.float32)], axis=0)
    hits = jnp.concatenate([hits, jnp.zeros((cells, cells - rows), jnp.float32)], axis=1).T
    for place in range(shards):
        mask_ref[place] = jnp.broadcast_to(hits[:rows, place : place + 1], (rows, cells))
    copies[3].wait()
    depth = feat_ref.shape[1]
    one = jnp.ones((2 * depth, 2 * cells), jnp.bfloat16)
    for pair in range(rows // 2):
        for half in range(2):
            feat = feat_ref[2 * pair + half]
            norm_ref[2 * pair + half : 2 * pair + half + 1, :] = jnp.sum(feat * feat, axis=0, keepdims=True)
            high, mid, low = pieces(feat)
            lanes = slice(half * cells, (half + 1) * cells)
            top = jnp.concatenate([high, mid], axis=0).astype(jnp.bfloat16)
            wide_ref[pair, 0 : 2 * depth, lanes] = top
            wide_ref[pair, 2 * depth : 4 * depth, lanes] = top
            wide_ref[pair, 4 * depth : 6 * depth, lanes] = jnp.concatenate([low, high], axis=0).astype(jnp.bfloat16)
        wide_ref[pair, 6 * depth : 8 * depth, :] = one


def join_kernel(*refs):
    ins, out_ref = refs[:-2], refs[-1]
    start = 0
    for ref in ins:
        out_ref[start : start + ref.shape[0]] = ref[...]
        start += ref.shape[0]


def tile_kernel(packs_ref, wide_ref, exps_ref, tall_ref, peak_ref, total_ref):
    blocks = packs_ref.shape[0]
    pairs, _, both = wide_ref.shape
    cells = both // 2
    depth = cells // 2
    lane = lax.broadcasted_iota(jnp.int32, (cells, cells), 1)
    biases = jnp.concatenate([packs_ref[place, depth : depth + 1, :] for place in range(blocks)], axis=0)
    bias_pieces = jnp.concatenate(list(pieces(biases)), axis=0)
    padded = jnp.concatenate([bias_pieces, jnp.zeros((cells - 3 * blocks, cells), jnp.float32)], axis=0)
    bias_lanes = padded.T
    for place in range(blocks):
        feat = packs_ref[place, :depth, :]
        turned = jnp.concatenate([feat, feat], axis=0).T
        high, mid, low = pieces(turned)
        own = jnp.where(lax.rem(lane, blocks) == place, bias_lanes, 0.0)
        rows = slice(place * cells, (place + 1) * cells)
        tall_ref[rows, 0:cells] = high.astype(jnp.bfloat16)
        tall_ref[rows, cells : 2 * cells] = mid.astype(jnp.bfloat16)
        tall_ref[rows, 2 * cells : 3 * cells] = jnp.where(lane < depth, high, low).astype(jnp.bfloat16)
        tall_ref[rows, 3 * cells : 4 * cells] = own.astype(jnp.bfloat16)

    def body(pair, carry):
        weights = wide_ref[pair]
        for place in range(blocks):
            rows = slice(place * cells, (place + 1) * cells)
            score = jnp.dot(tall_ref[rows, :], weights, preferred_element_type=jnp.float32)
            peak = jnp.max(score, axis=0, keepdims=True)
            exps = jnp.exp2(score - peak)
            exps_ref[pair, rows, :] = exps
            total = jnp.sum(exps, axis=0, keepdims=True)
            for half in range(2):
                lanes = slice(half * cells, (half + 1) * cells)
                peak_ref[place, pl.ds(2 * pair + half, 1), :] = peak[:, lanes]
                total_ref[place, pl.ds(2 * pair + half, 1), :] = total[:, lanes]
        return carry

    lax.fori_loop(0, pairs, body, 0)


def row_kernel(groups, *refs):
    mask_ref, peak_refs, total_refs = refs[0], refs[1 : 1 + groups], refs[1 + groups : 1 + 2 * groups]
    peaks_ref, rowsum_ref = refs[1 + 2 * groups :]
    place = 0
    for ref in peak_refs:
        for index in range(ref.shape[0]):
            peaks_ref[place] = ref[index] + mask_ref[place]
            place += 1
    totals = [ref[index] for ref in total_refs for index in range(ref.shape[0])]
    top = functools.reduce(jnp.maximum, [peaks_ref[index] for index in range(place)])
    summed = sum(total * jnp.exp2(peaks_ref[index] - top) for index, total in enumerate(totals))
    rowsum_ref[...] = top + jnp.log2(summed)


def lane_sums(values):
    ones = jnp.ones((8, values.shape[1]), jnp.bfloat16)
    parts = [
        lax.dot_general(ones, part.astype(jnp.bfloat16), (((1,), (1,)), ((), ())), preferred_element_type=jnp.float32)
        for part in pieces(values)
    ]
    return sum(parts)[0:1, :]


def column_kernel(groups, *refs):
    exps_refs, tall_refs, rest = refs[:groups], refs[groups : 2 * groups], refs[2 * groups :]
    wide_ref, peak_ref, mask_ref, own_ref, other_ref, mass_ref, norm_ref = rest[:7]
    poten_ref, sums_ref, weight_ref, acc_ref, shift_ref = rest[7:]
    pairs, _, both = wide_ref.shape
    cells = both // 2
    shards = mask_ref.shape[0]
    own, other = own_ref[...], other_ref[...]
    top = jnp.maximum(own, other)
    whole = top + jnp.log2(jnp.exp2(own - top) + jnp.exp2(other - top))
    poten_ref[...] = norm_ref[...] - (entropic * ln2) * whole
    shift = mass_ref[...] * log2e - whole
    shift_ref[...] = shift
    for place in range(shards):
        weight_ref[place] = jnp.exp2(peak_ref[place] + shift)
    spots = [
        (group, slice(index * cells, (index + 1) * cells))
        for group, ref in enumerate(tall_refs)
        for index in range(ref.shape[0] // cells)
    ]
    for place, (group, rows) in enumerate(spots):
        acc = jnp.zeros((cells, cells), jnp.float32)
        for pair in range(pairs):
            acc = acc + exps_refs[group][pair, rows, :cells] * weight_ref[place, 2 * pair : 2 * pair + 1, :]
            acc = acc + exps_refs[group][pair, rows, cells:] * weight_ref[place, 2 * pair + 1 : 2 * pair + 2, :]
        acc_ref[place * cells : (place + 1) * cells, :] = acc
    sums = lane_sums(acc_ref[...])
    me = lax.axis_index("src")
    owners = [me ^ other for other in partners(shards)]
    used = [jnp.max(mask_ref[place], axis=0, keepdims=True) > 0.5 * very_low for place in range(shards)]
    worst = jnp.full((1, cells), 1.0, jnp.float32)
    for place in range(shards):
        here = sums[:, place * cells : (place + 1) * cells]
        sums_ref[owners[place]] = jnp.where(used[place], jnp.log2(here), very_low)
        worst = jnp.minimum(worst, jnp.where(used[place], here, 1.0))

    @pl.when(jnp.min(worst) < least_sum)
    def _():
        for place, (group, rows) in enumerate(spots):

            def exponents(pair):
                score = jnp.dot(tall_refs[group][rows, :], wide_ref[pair], preferred_element_type=jnp.float32)
                add = shift_ref[pl.ds(2 * pair, 2), :] + mask_ref[place, pl.ds(2 * pair, 2), :]
                return score[:, :cells] + add[0:1, :], score[:, cells:] + add[1:2, :]

            def highest(pair, peak):
                first, second = exponents(pair)
                return jnp.maximum(peak, jnp.maximum(first, second))

            peak = lax.fori_loop(0, pairs, highest, jnp.full((cells, cells), very_low, jnp.float32))
            peak = jnp.broadcast_to(jnp.max(peak, axis=1, keepdims=True), (cells, cells))

            def add_up(pair, sums):
                first, second = exponents(pair)
                return sums + jnp.exp2(first - peak) + jnp.exp2(second - peak)

            sums = lax.fori_loop(0, pairs, add_up, jnp.zeros((cells, cells), jnp.float32))
            logs = peak.T[0:1, :] + jnp.log2(lane_sums(sums))
            sums_ref[owners[place]] = jnp.where(used[place], logs, very_low)


def merge_kernel(values_ref, weight_ref, out_ref):
    values = values_ref[...]
    top = jnp.max(values, axis=0)
    whole = top + jnp.log2(jnp.sum(jnp.exp2(values - top), axis=0))
    out_ref[...] = -(entropic * ln2) * (whole - weight_ref[...])


def f32(*shape):
    return jax.ShapeDtypeStruct(shape, jnp.float32)


def dense_device(
    source_feat, target_feat, log_mass_src, log_mass_tgt, potential_tgt, support, counts
):
    shards = lax.axis_size("src")
    rows, depth, cells = source_feat.shape
    pairs, wide = rows // 2, 2 * cells

    def call(kernel, ins, out_shape, scratch=(), cost=None):
        many = isinstance(out_shape, list)
        return pl.pallas_call(
            kernel,
            in_specs=ins,
            out_specs=[VM] * len(out_shape) if many else VM,
            out_shape=out_shape,
            scratch_shapes=list(scratch),
            compiler_params=PARAMS,
            cost_estimate=cost,
        )

    def reading(kernel, args, out_shape, cost):
        return call(
            kernel,
            [pl.BlockSpec(memory_space=pltpu.HBM)] * len(args),
            out_shape,
            [pltpu.VMEM(arg.shape, arg.dtype) for arg in args] + [pltpu.SemaphoreType.DMA((len(args),))],
            cost,
        )(*[pltpu.with_memory_space_constraint(arg, pltpu.HBM) for arg in args])

    def cost_of(flops):
        return pl.CostEstimate(flops=flops, bytes_accessed=rows * depth * cells * 4, transcendentals=0)

    pack, weight = reading(
        pack_kernel,
        [target_feat, log_mass_tgt, potential_tgt],
        [in_vmem((1, depth + 8, cells), jnp.float32), in_vmem((1, cells), jnp.float32)],
        None,
    )
    wide_feat, norm, mask, mass = reading(
        functools.partial(source_kernel, shards),
        [log_mass_src, support[:, 0, :].T, counts.T, source_feat],
        [
            in_vmem((pairs, 8 * depth, wide), jnp.bfloat16),
            in_vmem((rows, cells), jnp.float32),
            in_vmem((shards, rows, cells), jnp.float32),
            in_vmem((rows, cells), jnp.float32),
        ],
        cost_of(10**9),
    )

    def tiles(packs):
        blocks = packs.shape[0]
        return call(
            tile_kernel,
            [VM] * 2,
            [
                in_vmem((pairs, blocks * cells, wide), jnp.float32),
                in_vmem((blocks * cells, 8 * depth), jnp.bfloat16),
                in_vmem((blocks, rows, cells), jnp.float32),
                in_vmem((blocks, rows, cells), jnp.float32),
            ],
            cost=cost_of(2 * blocks * cells * pairs * wide * 8 * depth),
        )(packs, wide_feat)

    held, found, apart = pack, [tiles(pack)], shards // 2
    while apart:
        there = lax.ppermute(held, "src", [(i, i ^ apart) for i in range(shards)])
        before = found[-1][-1]
        found.append(tiles(there))
        apart //= 2
        if apart:
            count = 2 * held.shape[0]
            held = call(
                join_kernel,
                [VM] * 2 + [pl.BlockSpec(memory_space=pl.ANY)],
                in_vmem((count,) + held.shape[1:], jnp.float32),
            )(held, there, before)
    exps, tall, peaks, totals = zip(*found)
    groups = len(found)
    peaks, own = call(
        functools.partial(row_kernel, groups),
        [VM] * (1 + 2 * groups),
        [in_vmem((shards, rows, cells), jnp.float32), in_vmem((rows, cells), jnp.float32)],
    )(mask, *peaks, *totals)
    other = lax.ppermute(own, "tgt", [(0, 1), (1, 0)])
    potential_src, columns = call(
        functools.partial(column_kernel, groups),
        [VM] * (2 * groups + 7),
        [f32(rows, cells), in_vmem((shards, 1, cells), jnp.float32)],
        [
            pltpu.VMEM((shards, rows, cells), jnp.float32),
            pltpu.VMEM((shards * cells, cells), jnp.float32),
            pltpu.VMEM((rows, cells), jnp.float32),
        ],
    )(*exps, *tall, wide_feat, peaks, mask, own, other, mass, norm)
    arrived = lax.all_to_all(columns, "src", 0, 0)
    potential_new = call(merge_kernel, [VM] * 2, f32(1, cells))(arrived, weight)
    return potential_src, potential_new


def merged(part, axis, combine):
    gathered = jax.tree.map(lambda a: lax.all_gather(a, axis), part)

    def take(source):
        return jax.tree.map(lambda a: lax.dynamic_index_in_dim(a, source, 0, False), gathered)

    return lax.fori_loop(
        1, lax.axis_size(axis), lambda source, state: combine(state, take(source)), take(0)
    )


def cost_tiles(source_blk, source_sq, target_blk, target_sq):
    cross = jnp.einsum(
        "...fi,...fj->...ij", source_blk, target_blk, precision=lax.Precision.HIGHEST
    )
    return source_sq[..., :, None] + target_sq[..., None, :] - 2.0 * cross


def row_stats(cost, mass_tgt, poten_tgt, usable):
    scores = mass_tgt[..., None, :] + (poten_tgt[..., None, :] - cost) / entropic
    scores = jnp.where(usable[..., None, None], scores, very_low)
    peak = jnp.max(scores, axis=(1, 3))
    total = jnp.sum(jnp.exp(scores - peak[:, None, :, None]), axis=(1, 3))
    return (peak, total)


def column_stats(cost, mass_src, poten_src, usable):
    scores = mass_src[:, None, :, None] + (poten_src[:, None, :, None] - cost) / entropic
    peak = jnp.max(scores, axis=2)
    total = jnp.sum(jnp.exp(scores - peak[:, :, None, :]), axis=2)
    peak = jnp.where(usable[..., None], peak, very_low)
    total = jnp.where(usable[..., None], total, 0.0)
    return (peak, total)


def merge_pair(first_pair, second_pair):
    first_peak, first_total = first_pair
    second_peak, second_total = second_pair
    highest = jnp.maximum(first_peak, second_peak)
    summed = first_total * jnp.exp(first_peak - highest) + second_total * jnp.exp(
        second_peak - highest
    )
    return (highest, summed)


def segment_merge(peaks, totals, seg_ids, segments):
    best = jax.ops.segment_max(peaks, seg_ids, num_segments=segments + 1)
    best = jnp.maximum(best, very_low)
    summed = jax.ops.segment_sum(
        totals * jnp.exp(peaks - best[seg_ids]), seg_ids, num_segments=segments + 1
    )
    return (best[:segments], summed[:segments])


def general_device(
    source_feat, target_feat, log_mass_src, log_mass_tgt, potential_tgt, support, counts
):
    target_all, mass_all, poten_all = (
        lax.all_gather(target_feat, "src", axis=0, tiled=True),
        lax.all_gather(log_mass_tgt, "src", axis=0, tiled=True),
        lax.all_gather(potential_tgt, "src", axis=0, tiled=True),
    )
    blocks = target_all.shape[0]
    rows_here = source_feat.shape[0]
    slots_here = support.shape[2]
    cells = source_feat.shape[2]
    indices = support[:, 0, :]
    limits = counts[:, 0]
    usable = jnp.arange(slots_here, dtype=jnp.int32)[None, :] < limits[:, None]
    source_sq = jnp.sum(source_feat * source_feat, axis=1)
    target_sq = jnp.sum(target_all * target_all, axis=1)
    width = math.gcd(rows_here, 4)

    def grouped(array):
        return array.reshape((rows_here // width, width) + array.shape[1:])

    def row_pass(items):
        source_blk, source_nrm, ids_here, use_here = items
        cost = cost_tiles(
            source_blk[:, None], source_nrm[:, None], target_all[ids_here], target_sq[ids_here]
        )
        return row_stats(cost, mass_all[ids_here], poten_all[ids_here], use_here)

    peak, total = lax.map(
        row_pass, (grouped(source_feat), grouped(source_sq), grouped(indices), grouped(usable))
    )
    peak = peak.reshape(rows_here, cells)
    total = total.reshape(rows_here, cells)
    peak_all, total_all = merged((peak, total), "tgt", merge_pair)
    potential_src = -entropic * (peak_all + jnp.log(total_all))

    def column_pass(items):
        source_blk, source_nrm, mass_here, poten_here, ids_here, use_here = items
        cost = cost_tiles(
            source_blk[:, None], source_nrm[:, None], target_all[ids_here], target_sq[ids_here]
        )
        return column_stats(cost, mass_here, poten_here, use_here)

    peaks, totals = lax.map(
        column_pass,
        (
            grouped(source_feat),
            grouped(source_sq),
            grouped(log_mass_src),
            grouped(potential_src),
            grouped(indices),
            grouped(usable),
        ),
    )
    seg_ids = jnp.where(usable, indices, blocks).reshape(-1)
    best, summed = segment_merge(
        peaks.reshape(-1, cells), totals.reshape(-1, cells), seg_ids, blocks
    )
    share = blocks // lax.axis_size("src")
    own_start = lax.axis_index("src") * share
    highest = lax.pmax(best, "src")
    whole = lax.psum(summed * jnp.exp(best - highest), "src")
    own_peak = lax.dynamic_slice_in_dim(highest, own_start, share, 0)
    own_total = lax.dynamic_slice_in_dim(whole, own_start, share, 0)
    potential_new = -entropic * (own_peak + jnp.log(own_total))
    return (potential_src, potential_new)


def per_device(source_feat, target_feat, *others):
    shards = lax.axis_size("src")
    rows, depth, cells = source_feat.shape
    few = shards == 8 and target_feat.shape[0] == 1 and lax.axis_size("tgt") == 2
    if few and rows % 2 == 0 and cells == 128 and depth == 64:
        return dense_device(source_feat, target_feat, *others)
    return general_device(source_feat, target_feat, *others)


def solution(mesh):
    in_specs = (
        P(("grp", "src"), None, None),
        P(("grp", "src", "tgt"), None, None),
        P(("grp", "src"), None),
        P(("grp", "src", "tgt"), None),
        P(("grp", "src", "tgt"), None),
        P(("grp", "src"), "tgt", None),
        P(("grp", "src"), "tgt"),
    )
    out_specs = (P(("grp", "src"), None), P(("grp", "src", "tgt"), None))
    return jax.shard_map(
        per_device, mesh=mesh, in_specs=in_specs, out_specs=out_specs, check_vma=False
    )
```

```python
import functools
import math

import jax
import jax.numpy as jnp
from jax import lax
from jax.experimental import pallas as pl
from jax.experimental.pallas import tpu as pltpu
from jax.sharding import PartitionSpec as P

entropic = 0.5
very_low = -1e30
log2e = 1.0 / math.log(2.0)
ln2 = math.log(2.0)
least_sum = 1e-28

VM = pl.BlockSpec(memory_space=pltpu.VMEM)
PARAMS = pltpu.CompilerParams(vmem_limit_bytes=40 * 2**20)


def in_vmem(shape, dtype):
    return pltpu.VMEM(shape, dtype)


def pieces(values):
    high = values.astype(jnp.bfloat16).astype(jnp.float32)
    rest = values - high
    mid = rest.astype(jnp.bfloat16).astype(jnp.float32)
    low = (rest - mid).astype(jnp.bfloat16).astype(jnp.float32)
    return high, mid, low


def target_weight(mass, poten):
    return (mass + poten / entropic) * log2e


def blocks_at(shards):
    odd = lax.rem(lax.axis_index("src"), 2)
    half = shards // 2
    return [2 * place + odd for place in range(half)] + [2 * place + 1 - odd for place in range(half)]


def read_all(hbm, held, sems):
    copies = [pltpu.make_async_copy(src, dst, sems.at[i]) for i, (src, dst) in enumerate(zip(hbm, held))]
    for copy in copies:
        copy.start()
    return copies


def pack_kernel(*refs):
    hbm, (send_ref, weight_ref), held, sems = refs[:3], refs[3:5], refs[5:8], refs[8]
    for copy in read_all(hbm, held, sems):
        copy.wait()
    feat_ref, mass_ref, poten_ref = held
    feat = feat_ref[0]
    depth, cells = feat.shape
    weight = target_weight(mass_ref[...], poten_ref[...])
    norm = jnp.sum(feat * feat, axis=0, keepdims=True)
    bias = weight - (log2e / entropic) * norm
    scaled = feat * (2.0 * log2e / entropic)
    below = jnp.broadcast_to(bias, (send_ref.shape[1] - depth, cells))
    for copy in range(send_ref.shape[0]):
        send_ref[copy, :depth, :] = scaled
        send_ref[copy, depth:, :] = below
    weight_ref[...] = weight


def source_kernel(shards, *refs):
    hbm, outs, held, sems = refs[:4], refs[4:8], refs[8:12], refs[12]
    wide_ref, norm_ref, mask_ref, mass_out_ref = outs
    mass_ref, support_ref, counts_ref, feat_ref = held
    copies = read_all(hbm, held, sems)
    for copy in copies[:3]:
        copy.wait()
    mass_out_ref[...] = mass_ref[...]
    support = support_ref[...]
    slots, rows = support.shape
    cells = mass_ref.shape[1]
    used = lax.broadcasted_iota(jnp.int32, support.shape, 0) < counts_ref[...]
    hits = [
        jnp.max(jnp.where(used & (support == block), 0.0, very_low), axis=0, keepdims=True)
        for block in blocks_at(shards)
    ]
    hits = jnp.concatenate(hits + [jnp.zeros((cells - shards, rows), jnp.float32)], axis=0)
    hits = jnp.concatenate([hits, jnp.zeros((cells, cells - rows), jnp.float32)], axis=1).T
    for place in range(shards):
        mask_ref[place] = jnp.broadcast_to(hits[:rows, place : place + 1], (rows, cells))
    copies[3].wait()
    depth = feat_ref.shape[1]
    one = jnp.ones((2 * depth, 2 * cells), jnp.bfloat16)
    for pair in range(rows // 2):
        for half in range(2):
            feat = feat_ref[2 * pair + half]
            norm_ref[2 * pair + half : 2 * pair + half + 1, :] = jnp.sum(feat * feat, axis=0, keepdims=True)
            high, mid, low = pieces(feat)
            lanes = slice(half * cells, (half + 1) * cells)
            top = jnp.concatenate([high, mid], axis=0).astype(jnp.bfloat16)
            wide_ref[pair, 0 : 2 * depth, lanes] = top
            wide_ref[pair, 2 * depth : 4 * depth, lanes] = top
            wide_ref[pair, 4 * depth : 6 * depth, lanes] = jnp.concatenate([low, high], axis=0).astype(jnp.bfloat16)
        wide_ref[pair, 6 * depth : 8 * depth, :] = one


def tile_kernel(packs_ref, wide_ref, exps_ref, tall_ref, peak_ref, total_ref):
    blocks = packs_ref.shape[0]
    pairs, _, both = wide_ref.shape
    cells = both // 2
    depth = cells // 2
    lane = lax.broadcasted_iota(jnp.int32, (cells, cells), 1)
    biases = jnp.concatenate([packs_ref[place, depth : depth + 1, :] for place in range(blocks)], axis=0)
    bias_pieces = jnp.concatenate(list(pieces(biases)), axis=0)
    padded = jnp.concatenate([bias_pieces, jnp.zeros((cells - 3 * blocks, cells), jnp.float32)], axis=0)
    bias_lanes = padded.T
    for place in range(blocks):
        feat = packs_ref[place, :depth, :]
        turned = jnp.concatenate([feat, feat], axis=0).T
        high, mid, low = pieces(turned)
        own = jnp.where(lax.rem(lane, blocks) == place, bias_lanes, 0.0)
        rows = slice(place * cells, (place + 1) * cells)
        tall_ref[rows, 0:cells] = high.astype(jnp.bfloat16)
        tall_ref[rows, cells : 2 * cells] = mid.astype(jnp.bfloat16)
        tall_ref[rows, 2 * cells : 3 * cells] = jnp.where(lane < depth, high, low).astype(jnp.bfloat16)
        tall_ref[rows, 3 * cells : 4 * cells] = own.astype(jnp.bfloat16)

    def body(pair, carry):
        scores = jnp.dot(tall_ref[...], wide_ref[pair], preferred_element_type=jnp.float32)
        for place in range(blocks):
            rows = slice(place * cells, (place + 1) * cells)
            score = scores[rows]
            peak = jnp.max(score, axis=0, keepdims=True)
            exps = jnp.exp2(score - peak)
            exps_ref[pair, rows, :] = exps
            total = jnp.sum(exps, axis=0, keepdims=True)
            for half in range(2):
                lanes = slice(half * cells, (half + 1) * cells)
                peak_ref[place, pl.ds(2 * pair + half, 1), :] = peak[:, lanes]
                total_ref[place, pl.ds(2 * pair + half, 1), :] = total[:, lanes]
        return carry

    lax.fori_loop(0, pairs, body, 0, unroll=2)


def row_kernel(groups, *refs):
    mask_ref, peak_refs, total_refs = refs[0], refs[1 : 1 + groups], refs[1 + groups : 1 + 2 * groups]
    peaks_ref, rowsum_ref = refs[1 + 2 * groups :]
    place = 0
    for ref in peak_refs:
        for index in range(ref.shape[0]):
            peaks_ref[place] = ref[index] + mask_ref[place]
            place += 1
    totals = [ref[index] for ref in total_refs for index in range(ref.shape[0])]
    top = functools.reduce(jnp.maximum, [peaks_ref[index] for index in range(place)])
    summed = sum(total * jnp.exp2(peaks_ref[index] - top) for index, total in enumerate(totals))
    rowsum_ref[...] = top + jnp.log2(summed)


def across(column):
    shape = (column.shape[0],) * 2
    same = lax.broadcasted_iota(jnp.int32, shape, 0) == lax.broadcasted_iota(jnp.int32, shape, 1)
    return jnp.sum(jnp.where(same, jnp.broadcast_to(column, shape), 0.0), axis=0, keepdims=True)


def column_kernel(groups, *refs):
    exps_refs, tall_refs, rest = refs[:groups], refs[groups : 2 * groups], refs[2 * groups :]
    wide_ref, peak_ref, mask_ref, own_ref, other_ref, mass_ref, norm_ref = rest[:7]
    poten_ref, sums_ref, weight_ref, shift_ref = rest[7:]
    pairs, _, both = wide_ref.shape
    cells = both // 2
    shards = mask_ref.shape[0]
    own, other = own_ref[...], other_ref[...]
    top = jnp.maximum(own, other)
    whole = top + jnp.log2(jnp.exp2(own - top) + jnp.exp2(other - top))
    poten_ref[...] = norm_ref[...] - (entropic * ln2) * whole
    shift = mass_ref[...] * log2e - whole
    shift_ref[...] = shift
    for place in range(shards):
        weight_ref[place] = jnp.exp2(peak_ref[place] + shift)
    spots = [
        (group, slice(index * cells, (index + 1) * cells))
        for group, ref in enumerate(tall_refs)
        for index in range(ref.shape[0] // cells)
    ]
    used = [jnp.max(mask_ref[place], axis=0, keepdims=True) > 0.5 * very_low for place in range(shards)]
    worst = jnp.full((1, cells), 1.0, jnp.float32)
    owners = blocks_at(shards)
    for place, (group, rows) in enumerate(spots):
        acc = jnp.zeros((cells, cells), jnp.float32)
        for pair in range(pairs):
            acc = acc + exps_refs[group][pair, rows, :cells] * weight_ref[place, 2 * pair : 2 * pair + 1, :]
            acc = acc + exps_refs[group][pair, rows, cells:] * weight_ref[place, 2 * pair + 1 : 2 * pair + 2, :]
        here = across(jnp.sum(acc, axis=1, keepdims=True))
        sums_ref[owners[place]] = jnp.where(used[place], jnp.log2(here), very_low)
        worst = jnp.minimum(worst, jnp.where(used[place], here, 1.0))

    @pl.when(jnp.min(worst) < least_sum)
    def _():
        for place, (group, rows) in enumerate(spots):

            def exponents(pair):
                score = jnp.dot(tall_refs[group][rows, :], wide_ref[pair], preferred_element_type=jnp.float32)
                add = shift_ref[pl.ds(2 * pair, 2), :] + mask_ref[place, pl.ds(2 * pair, 2), :]
                return score[:, :cells] + add[0:1, :], score[:, cells:] + add[1:2, :]

            def highest(pair, peak):
                first, second = exponents(pair)
                return jnp.maximum(peak, jnp.maximum(first, second))

            peak = lax.fori_loop(0, pairs, highest, jnp.full((cells, cells), very_low, jnp.float32))
            peak = jnp.max(peak, axis=1, keepdims=True)

            def add_up(pair, sums):
                first, second = exponents(pair)
                return sums + jnp.exp2(first - peak) + jnp.exp2(second - peak)

            sums = lax.fori_loop(0, pairs, add_up, jnp.zeros((cells, cells), jnp.float32))
            logs = across(peak) + jnp.log2(across(jnp.sum(sums, axis=1, keepdims=True)))
            sums_ref[owners[place]] = jnp.where(used[place], logs, very_low)


def merge_kernel(values_ref, weight_ref, poten_ref, out_ref, poten_out_ref):
    poten_out_ref[...] = poten_ref[...]
    values = values_ref[...]
    top = jnp.max(values, axis=0)
    whole = top + jnp.log2(jnp.sum(jnp.exp2(values - top), axis=0))
    out_ref[...] = -(entropic * ln2) * (whole - weight_ref[...])


def f32(*shape):
    return jax.ShapeDtypeStruct(shape, jnp.float32)


def dense_device(
    source_feat, target_feat, log_mass_src, log_mass_tgt, potential_tgt, support, counts
):
    shards = lax.axis_size("src")
    rows, depth, cells = source_feat.shape
    pairs, wide = rows // 2, 2 * cells

    def call(kernel, ins, out_shape, scratch=(), cost=None):
        many = isinstance(out_shape, list)
        return pl.pallas_call(
            kernel,
            in_specs=ins,
            out_specs=[VM] * len(out_shape) if many else VM,
            out_shape=out_shape,
            scratch_shapes=list(scratch),
            compiler_params=PARAMS,
            cost_estimate=cost,
        )

    def reading(kernel, args, out_shape, cost):
        return call(
            kernel,
            [pl.BlockSpec(memory_space=pltpu.HBM)] * len(args),
            out_shape,
            [pltpu.VMEM(arg.shape, arg.dtype) for arg in args] + [pltpu.SemaphoreType.DMA((len(args),))],
            cost,
        )(*[pltpu.with_memory_space_constraint(arg, pltpu.HBM) for arg in args])

    def cost_of(flops):
        return pl.CostEstimate(flops=flops, bytes_accessed=rows * depth * cells * 4, transcendentals=0)

    pack, weight = reading(
        pack_kernel,
        [target_feat, log_mass_tgt, potential_tgt],
        [in_vmem((shards // 2, depth + 8, cells), jnp.float32), in_vmem((1, cells), jnp.float32)],
        None,
    )
    wide_feat, norm, mask, mass = reading(
        functools.partial(source_kernel, shards),
        [log_mass_src, support[:, 0, :].T, counts.T, source_feat],
        [
            in_vmem((pairs, 8 * depth, wide), jnp.bfloat16),
            in_vmem((rows, cells), jnp.float32),
            in_vmem((shards, rows, cells), jnp.float32),
            in_vmem((rows, cells), jnp.float32),
        ],
        cost_of(10**9),
    )

    def tiles(packs):
        blocks = packs.shape[0]
        return call(
            tile_kernel,
            [VM] * 2,
            [
                in_vmem((pairs, blocks * cells, wide), jnp.float32),
                in_vmem((blocks * cells, 8 * depth), jnp.bfloat16),
                in_vmem((blocks, rows, cells), jnp.float32),
                in_vmem((blocks, rows, cells), jnp.float32),
            ],
            cost=cost_of(2 * blocks * cells * pairs * wide * 8 * depth),
        )(packs, wide_feat)

    same = [list(range(odd, shards, 2)) for odd in range(2)]
    near = lax.all_to_all(pack, "src", 0, 0, axis_index_groups=same)
    far = lax.ppermute(near, "src", [(i, i ^ 1) for i in range(shards)])
    found = [tiles(near), tiles(far)]
    exps, tall, peaks, totals = zip(*found)
    groups = len(found)
    peaks, own = call(
        functools.partial(row_kernel, groups),
        [VM] * (1 + 2 * groups),
        [in_vmem((shards, rows, cells), jnp.float32), in_vmem((rows, cells), jnp.float32)],
    )(mask, *peaks, *totals)
    other = lax.ppermute(own, "tgt", [(0, 1), (1, 0)])
    potential_src, columns = call(
        functools.partial(column_kernel, groups),
        [VM] * (2 * groups + 7),
        [in_vmem((rows, cells), jnp.float32), in_vmem((shards, 1, cells), jnp.float32)],
        [
            pltpu.VMEM((shards, rows, cells), jnp.float32),
            pltpu.VMEM((rows, cells), jnp.float32),
        ],
    )(*exps, *tall, wide_feat, peaks, mask, own, other, mass, norm)
    arrived = lax.all_to_all(columns, "src", 0, 0)
    outs = [f32(1, cells), f32(rows, cells)]
    potential_new, potential_src = call(merge_kernel, [VM] * 3, outs)(arrived, weight, potential_src)
    return potential_src, potential_new


def merged(part, axis, combine):
    gathered = jax.tree.map(lambda a: lax.all_gather(a, axis), part)

    def take(source):
        return jax.tree.map(lambda a: lax.dynamic_index_in_dim(a, source, 0, False), gathered)

    return lax.fori_loop(
        1, lax.axis_size(axis), lambda source, state: combine(state, take(source)), take(0)
    )


def cost_tiles(source_blk, source_sq, target_blk, target_sq):
    cross = jnp.einsum(
        "...fi,...fj->...ij", source_blk, target_blk, precision=lax.Precision.HIGHEST
    )
    return source_sq[..., :, None] + target_sq[..., None, :] - 2.0 * cross


def row_stats(cost, mass_tgt, poten_tgt, usable):
    scores = mass_tgt[..., None, :] + (poten_tgt[..., None, :] - cost) / entropic
    scores = jnp.where(usable[..., None, None], scores, very_low)
    peak = jnp.max(scores, axis=(1, 3))
    total = jnp.sum(jnp.exp(scores - peak[:, None, :, None]), axis=(1, 3))
    return (peak, total)


def column_stats(cost, mass_src, poten_src, usable):
    scores = mass_src[:, None, :, None] + (poten_src[:, None, :, None] - cost) / entropic
    peak = jnp.max(scores, axis=2)
    total = jnp.sum(jnp.exp(scores - peak[:, :, None, :]), axis=2)
    peak = jnp.where(usable[..., None], peak, very_low)
    total = jnp.where(usable[..., None], total, 0.0)
    return (peak, total)


def merge_pair(first_pair, second_pair):
    first_peak, first_total = first_pair
    second_peak, second_total = second_pair
    highest = jnp.maximum(first_peak, second_peak)
    summed = first_total * jnp.exp(first_peak - highest) + second_total * jnp.exp(
        second_peak - highest
    )
    return (highest, summed)


def segment_merge(peaks, totals, seg_ids, segments):
    best = jax.ops.segment_max(peaks, seg_ids, num_segments=segments + 1)
    best = jnp.maximum(best, very_low)
    summed = jax.ops.segment_sum(
        totals * jnp.exp(peaks - best[seg_ids]), seg_ids, num_segments=segments + 1
    )
    return (best[:segments], summed[:segments])


def general_device(
    source_feat, target_feat, log_mass_src, log_mass_tgt, potential_tgt, support, counts
):
    target_all, mass_all, poten_all = (
        lax.all_gather(target_feat, "src", axis=0, tiled=True),
        lax.all_gather(log_mass_tgt, "src", axis=0, tiled=True),
        lax.all_gather(potential_tgt, "src", axis=0, tiled=True),
    )
    blocks = target_all.shape[0]
    rows_here = source_feat.shape[0]
    slots_here = support.shape[2]
    cells = source_feat.shape[2]
    indices = support[:, 0, :]
    limits = counts[:, 0]
    usable = jnp.arange(slots_here, dtype=jnp.int32)[None, :] < limits[:, None]
    source_sq = jnp.sum(source_feat * source_feat, axis=1)
    target_sq = jnp.sum(target_all * target_all, axis=1)
    width = math.gcd(rows_here, 4)

    def grouped(array):
        return array.reshape((rows_here // width, width) + array.shape[1:])

    def row_pass(items):
        source_blk, source_nrm, ids_here, use_here = items
        cost = cost_tiles(
            source_blk[:, None], source_nrm[:, None], target_all[ids_here], target_sq[ids_here]
        )
        return row_stats(cost, mass_all[ids_here], poten_all[ids_here], use_here)

    peak, total = lax.map(
        row_pass, (grouped(source_feat), grouped(source_sq), grouped(indices), grouped(usable))
    )
    peak = peak.reshape(rows_here, cells)
    total = total.reshape(rows_here, cells)
    peak_all, total_all = merged((peak, total), "tgt", merge_pair)
    potential_src = -entropic * (peak_all + jnp.log(total_all))

    def column_pass(items):
        source_blk, source_nrm, mass_here, poten_here, ids_here, use_here = items
        cost = cost_tiles(
            source_blk[:, None], source_nrm[:, None], target_all[ids_here], target_sq[ids_here]
        )
        return column_stats(cost, mass_here, poten_here, use_here)

    peaks, totals = lax.map(
        column_pass,
        (
            grouped(source_feat),
            grouped(source_sq),
            grouped(log_mass_src),
            grouped(potential_src),
            grouped(indices),
            grouped(usable),
        ),
    )
    seg_ids = jnp.where(usable, indices, blocks).reshape(-1)
    best, summed = segment_merge(
        peaks.reshape(-1, cells), totals.reshape(-1, cells), seg_ids, blocks
    )
    share = blocks // lax.axis_size("src")
    own_start = lax.axis_index("src") * share
    highest = lax.pmax(best, "src")
    whole = lax.psum(summed * jnp.exp(best - highest), "src")
    own_peak = lax.dynamic_slice_in_dim(highest, own_start, share, 0)
    own_total = lax.dynamic_slice_in_dim(whole, own_start, share, 0)
    potential_new = -entropic * (own_peak + jnp.log(own_total))
    return (potential_src, potential_new)


def per_device(source_feat, target_feat, *others):
    shards = lax.axis_size("src")
    rows, depth, cells = source_feat.shape
    few = shards == 8 and target_feat.shape[0] == 1 and lax.axis_size("tgt") == 2
    if few and rows % 2 == 0 and cells == 128 and depth == 64:
        return dense_device(source_feat, target_feat, *others)
    return general_device(source_feat, target_feat, *others)


def solution(mesh):
    in_specs = (
        P(("grp", "src"), None, None),
        P(("grp", "src", "tgt"), None, None),
        P(("grp", "src"), None),
        P(("grp", "src", "tgt"), None),
        P(("grp", "src", "tgt"), None),
        P(("grp", "src"), "tgt", None),
        P(("grp", "src"), "tgt"),
    )
    out_specs = (P(("grp", "src"), None), P(("grp", "src", "tgt"), None))
    return jax.shard_map(
        per_device, mesh=mesh, in_specs=in_specs, out_specs=out_specs, check_vma=False
    )
```

```python
import functools
import math

import jax
import jax.numpy as jnp
from jax import lax
from jax.experimental import pallas as pl
from jax.experimental.pallas import tpu as pltpu
from jax.sharding import PartitionSpec as P

entropic = 0.5
very_low = -1e30
log2e = 1.0 / math.log(2.0)
ln2 = math.log(2.0)
least_sum = 1e-28

VM = pl.BlockSpec(memory_space=pltpu.VMEM)
PARAMS = pltpu.CompilerParams(vmem_limit_bytes=40 * 2**20)


def in_vmem(shape, dtype):
    return pltpu.VMEM(shape, dtype)


def pieces(values):
    high = values.astype(jnp.bfloat16).astype(jnp.float32)
    rest = values - high
    mid = rest.astype(jnp.bfloat16).astype(jnp.float32)
    low = (rest - mid).astype(jnp.bfloat16).astype(jnp.float32)
    return high, mid, low


def target_weight(mass, poten):
    return (mass + poten / entropic) * log2e


def blocks_at(shards):
    odd = lax.rem(lax.axis_index("src"), 2)
    half = shards // 2
    return [2 * place + odd for place in range(half)] + [2 * place + 1 - odd for place in range(half)]


def read_all(hbm, held, sems):
    copies = [pltpu.make_async_copy(src, dst, sems.at[i]) for i, (src, dst) in enumerate(zip(hbm, held))]
    for copy in copies:
        copy.start()
    return copies


def pack_kernel(*refs):
    hbm, (send_ref, weight_ref), held, sems = refs[:3], refs[3:5], refs[5:8], refs[8]
    for copy in read_all(hbm, held, sems):
        copy.wait()
    feat_ref, mass_ref, poten_ref = held
    feat = feat_ref[0]
    depth, cells = feat.shape
    weight = target_weight(mass_ref[...], poten_ref[...])
    norm = jnp.sum(feat * feat, axis=0, keepdims=True)
    bias = weight - (log2e / entropic) * norm
    scaled = feat * (2.0 * log2e / entropic)
    below = jnp.broadcast_to(bias, (send_ref.shape[1] - depth, cells))
    send_ref[0, :depth, :] = scaled
    send_ref[0, depth:, :] = below
    weight_ref[...] = weight


def source_kernel(shards, *refs):
    hbm, outs, held, sems = refs[:4], refs[4:8], refs[8:12], refs[12]
    wide_ref, norm_ref, mask_ref, mass_out_ref = outs
    mass_ref, support_ref, counts_ref, feat_ref = held
    copies = read_all(hbm, held, sems)
    for copy in copies[:3]:
        copy.wait()
    mass_out_ref[...] = mass_ref[...]
    support = support_ref[...]
    slots, rows = support.shape
    cells = mass_ref.shape[1]
    used = lax.broadcasted_iota(jnp.int32, support.shape, 0) < counts_ref[...]
    hits = [
        jnp.max(jnp.where(used & (support == block), 0.0, very_low), axis=0, keepdims=True)
        for block in blocks_at(shards)
    ]
    hits = jnp.concatenate(hits + [jnp.zeros((cells - shards, rows), jnp.float32)], axis=0)
    hits = jnp.concatenate([hits, jnp.zeros((cells, cells - rows), jnp.float32)], axis=1).T
    for place in range(shards):
        mask_ref[place] = jnp.broadcast_to(hits[:rows, place : place + 1], (rows, cells))
    copies[3].wait()
    depth = feat_ref.shape[1]
    one = jnp.ones((2 * depth, 2 * cells), jnp.bfloat16)
    for pair in range(rows // 2):
        for half in range(2):
            feat = feat_ref[2 * pair + half]
            norm_ref[2 * pair + half : 2 * pair + half + 1, :] = jnp.sum(feat * feat, axis=0, keepdims=True)
            high, mid, low = pieces(feat)
            lanes = slice(half * cells, (half + 1) * cells)
            top = jnp.concatenate([high, mid], axis=0).astype(jnp.bfloat16)
            wide_ref[pair, 0 : 2 * depth, lanes] = top
            wide_ref[pair, 2 * depth : 4 * depth, lanes] = top
            wide_ref[pair, 4 * depth : 6 * depth, lanes] = jnp.concatenate([low, high], axis=0).astype(jnp.bfloat16)
        wide_ref[pair, 6 * depth : 8 * depth, :] = one


def bundle_kernel(first_ref, second_ref, out_ref):
    count = first_ref.shape[0]
    out_ref[:count] = first_ref[...]
    out_ref[count:] = second_ref[...]


def order_kernel(line, *refs):
    own_ref, up_refs, down_refs = refs[0], refs[1:line], refs[line : 2 * line - 1]
    out_refs = refs[2 * line - 1 :]
    here = lax.axis_index("src") // 2
    for block in range(line):
        value = own_ref[0]
        for at in range(line):
            if at < block:
                value = jnp.where(here == at, down_refs[line - 2 - at][block - at - 1], value)
            if at > block:
                value = jnp.where(here == at, up_refs[at - 1][block], value)
        out_refs[block // (line // 2)][block % (line // 2)] = value


def tile_kernel(parts, *refs):
    packs = [ref.at[index] for ref in refs[:parts] for index in range(ref.shape[0])]
    wide_ref, exps_ref, tall_ref, peak_ref, total_ref = refs[parts:]
    blocks = len(packs)
    pairs, _, both = wide_ref.shape
    cells = both // 2
    depth = cells // 2
    lane = lax.broadcasted_iota(jnp.int32, (cells, cells), 1)
    biases = jnp.concatenate([pack[depth : depth + 1, :] for pack in packs], axis=0)
    bias_pieces = jnp.concatenate(list(pieces(biases)), axis=0)
    padded = jnp.concatenate([bias_pieces, jnp.zeros((cells - 3 * blocks, cells), jnp.float32)], axis=0)
    bias_lanes = padded.T
    for place, pack in enumerate(packs):
        feat = pack[:depth, :]
        turned = jnp.concatenate([feat, feat], axis=0).T
        high, mid, low = pieces(turned)
        own = jnp.where(lax.rem(lane, blocks) == place, bias_lanes, 0.0)
        rows = slice(place * cells, (place + 1) * cells)
        tall_ref[rows, 0:cells] = high.astype(jnp.bfloat16)
        tall_ref[rows, cells : 2 * cells] = mid.astype(jnp.bfloat16)
        tall_ref[rows, 2 * cells : 3 * cells] = jnp.where(lane < depth, high, low).astype(jnp.bfloat16)
        tall_ref[rows, 3 * cells : 4 * cells] = own.astype(jnp.bfloat16)

    def body(pair, carry):
        scores = jnp.dot(tall_ref[...], wide_ref[pair], preferred_element_type=jnp.float32)
        for place in range(blocks):
            rows = slice(place * cells, (place + 1) * cells)
            score = scores[rows]
            peak = jnp.max(score, axis=0, keepdims=True)
            exps = jnp.exp2(score - peak)
            exps_ref[pair, rows, :] = exps
            total = jnp.sum(exps, axis=0, keepdims=True)
            for half in range(2):
                lanes = slice(half * cells, (half + 1) * cells)
                peak_ref[place, pl.ds(2 * pair + half, 1), :] = peak[:, lanes]
                total_ref[place, pl.ds(2 * pair + half, 1), :] = total[:, lanes]
        return carry

    lax.fori_loop(0, pairs, body, 0, unroll=max(1, 2 * pairs // blocks))


def row_kernel(groups, *refs):
    mask_ref, peak_refs, total_refs = refs[0], refs[1 : 1 + groups], refs[1 + groups : 1 + 2 * groups]
    peaks_ref, rowsum_ref = refs[1 + 2 * groups :]
    place = 0
    for ref in peak_refs:
        for index in range(ref.shape[0]):
            peaks_ref[place] = ref[index] + mask_ref[place]
            place += 1
    totals = [ref[index] for ref in total_refs for index in range(ref.shape[0])]
    top = functools.reduce(jnp.maximum, [peaks_ref[index] for index in range(place)])
    summed = sum(total * jnp.exp2(peaks_ref[index] - top) for index, total in enumerate(totals))
    rowsum_ref[...] = top + jnp.log2(summed)


def across(column):
    shape = (column.shape[0],) * 2
    same = lax.broadcasted_iota(jnp.int32, shape, 0) == lax.broadcasted_iota(jnp.int32, shape, 1)
    return jnp.sum(jnp.where(same, jnp.broadcast_to(column, shape), 0.0), axis=0, keepdims=True)


def column_kernel(groups, *refs):
    exps_refs, tall_refs, rest = refs[:groups], refs[groups : 2 * groups], refs[2 * groups :]
    wide_ref, peak_ref, mask_ref, own_ref, other_ref, mass_ref, norm_ref = rest[:7]
    poten_ref, sums_ref, weight_ref, shift_ref = rest[7:]
    pairs, _, both = wide_ref.shape
    cells = both // 2
    shards = mask_ref.shape[0]
    own, other = own_ref[...], other_ref[...]
    top = jnp.maximum(own, other)
    whole = top + jnp.log2(jnp.exp2(own - top) + jnp.exp2(other - top))
    poten_ref[...] = norm_ref[...] - (entropic * ln2) * whole
    shift = mass_ref[...] * log2e - whole
    shift_ref[...] = shift
    for place in range(shards):
        weight_ref[place] = jnp.exp2(peak_ref[place] + shift)
    spots = [
        (group, slice(index * cells, (index + 1) * cells))
        for group, ref in enumerate(tall_refs)
        for index in range(ref.shape[0] // cells)
    ]
    used = [jnp.max(mask_ref[place], axis=0, keepdims=True) > 0.5 * very_low for place in range(shards)]
    worst = jnp.full((1, cells), 1.0, jnp.float32)
    owners = blocks_at(shards)
    for place, (group, rows) in enumerate(spots):
        acc = jnp.zeros((cells, cells), jnp.float32)
        for pair in range(pairs):
            acc = acc + exps_refs[group][pair, rows, :cells] * weight_ref[place, 2 * pair : 2 * pair + 1, :]
            acc = acc + exps_refs[group][pair, rows, cells:] * weight_ref[place, 2 * pair + 1 : 2 * pair + 2, :]
        here = across(jnp.sum(acc, axis=1, keepdims=True))
        sums_ref[owners[place]] = jnp.where(used[place], jnp.log2(here), very_low)
        worst = jnp.minimum(worst, jnp.where(used[place], here, 1.0))

    @pl.when(jnp.min(worst) < least_sum)
    def _():
        for place, (group, rows) in enumerate(spots):

            def exponents(pair):
                score = jnp.dot(tall_refs[group][rows, :], wide_ref[pair], preferred_element_type=jnp.float32)
                add = shift_ref[pl.ds(2 * pair, 2), :] + mask_ref[place, pl.ds(2 * pair, 2), :]
                return score[:, :cells] + add[0:1, :], score[:, cells:] + add[1:2, :]

            def highest(pair, peak):
                first, second = exponents(pair)
                return jnp.maximum(peak, jnp.maximum(first, second))

            peak = lax.fori_loop(0, pairs, highest, jnp.full((cells, cells), very_low, jnp.float32))
            peak = jnp.max(peak, axis=1, keepdims=True)

            def add_up(pair, sums):
                first, second = exponents(pair)
                return sums + jnp.exp2(first - peak) + jnp.exp2(second - peak)

            sums = lax.fori_loop(0, pairs, add_up, jnp.zeros((cells, cells), jnp.float32))
            logs = across(peak) + jnp.log2(across(jnp.sum(sums, axis=1, keepdims=True)))
            sums_ref[owners[place]] = jnp.where(used[place], logs, very_low)


def merge_kernel(values_ref, weight_ref, poten_ref, out_ref, poten_out_ref):
    poten_out_ref[...] = poten_ref[...]
    values = values_ref[...]
    top = jnp.max(values, axis=0)
    whole = top + jnp.log2(jnp.sum(jnp.exp2(values - top), axis=0))
    out_ref[...] = -(entropic * ln2) * (whole - weight_ref[...])


def f32(*shape):
    return jax.ShapeDtypeStruct(shape, jnp.float32)


def dense_device(
    source_feat, target_feat, log_mass_src, log_mass_tgt, potential_tgt, support, counts
):
    shards = lax.axis_size("src")
    rows, depth, cells = source_feat.shape
    pairs, wide = rows // 2, 2 * cells

    def call(kernel, ins, out_shape, scratch=(), cost=None):
        many = isinstance(out_shape, list)
        return pl.pallas_call(
            kernel,
            in_specs=ins,
            out_specs=[VM] * len(out_shape) if many else VM,
            out_shape=out_shape,
            scratch_shapes=list(scratch),
            compiler_params=PARAMS,
            cost_estimate=cost,
        )

    def reading(kernel, args, out_shape, cost):
        return call(
            kernel,
            [pl.BlockSpec(memory_space=pltpu.HBM)] * len(args),
            out_shape,
            [pltpu.VMEM(arg.shape, arg.dtype) for arg in args] + [pltpu.SemaphoreType.DMA((len(args),))],
            cost,
        )(*[pltpu.with_memory_space_constraint(arg, pltpu.HBM) for arg in args])

    def cost_of(flops):
        return pl.CostEstimate(flops=flops, bytes_accessed=rows * depth * cells * 4, transcendentals=0)

    pack, weight = reading(
        pack_kernel,
        [target_feat, log_mass_tgt, potential_tgt],
        [in_vmem((1, depth + 8, cells), jnp.float32), in_vmem((1, cells), jnp.float32)],
        None,
    )
    wide_feat, norm, mask, mass = reading(
        functools.partial(source_kernel, shards),
        [log_mass_src, support[:, 0, :].T, counts.T, source_feat],
        [
            in_vmem((pairs, 8 * depth, wide), jnp.bfloat16),
            in_vmem((rows, cells), jnp.float32),
            in_vmem((shards, rows, cells), jnp.float32),
            in_vmem((rows, cells), jnp.float32),
        ],
        cost_of(10**9),
    )

    def tiles(*packs):
        blocks = sum(pack.shape[0] for pack in packs)
        return call(
            functools.partial(tile_kernel, len(packs)),
            [VM] * (len(packs) + 1),
            [
                in_vmem((pairs, blocks * cells, wide), jnp.float32),
                in_vmem((blocks * cells, 8 * depth), jnp.bfloat16),
                in_vmem((blocks, rows, cells), jnp.float32),
                in_vmem((blocks, rows, cells), jnp.float32),
            ],
            cost=cost_of(2 * blocks * cells * pairs * wide * 8 * depth),
        )(*packs, wide_feat)

    line = shards // 2

    def moved(array, start, end):
        return lax.ppermute(array, "src", [(2 * start + odd, 2 * end + odd) for odd in range(2)])

    def bundle(first, second):
        shape = (first.shape[0] + second.shape[0],) + pack.shape[1:]
        return call(bundle_kernel, [VM] * 2, in_vmem(shape, jnp.float32))(first, second)

    up, down = [], []
    for at in range(line - 1):
        down.append(moved(bundle(pack, down[-1]) if at else pack, line - 1 - at, line - 2 - at))
        up.append(moved(bundle(up[-1], pack) if at else pack, at, at + 1))
    near = call(
        functools.partial(order_kernel, line),
        [VM] * (2 * line - 1),
        [in_vmem((line // 2,) + pack.shape[1:], jnp.float32)] * 2,
    )(pack, *up, *down)
    far = [lax.ppermute(half, "src", [(i, i ^ 1) for i in range(shards)]) for half in near]
    found = [tiles(*near)] + [tiles(half) for half in far]
    exps, tall, peaks, totals = zip(*found)
    groups = len(found)
    peaks, own = call(
        functools.partial(row_kernel, groups),
        [VM] * (1 + 2 * groups),
        [in_vmem((shards, rows, cells), jnp.float32), in_vmem((rows, cells), jnp.float32)],
    )(mask, *peaks, *totals)
    other = lax.ppermute(own, "tgt", [(0, 1), (1, 0)])
    potential_src, columns = call(
        functools.partial(column_kernel, groups),
        [VM] * (2 * groups + 7),
        [in_vmem((rows, cells), jnp.float32), in_vmem((shards, 1, cells), jnp.float32)],
        [
            pltpu.VMEM((shards, rows, cells), jnp.float32),
            pltpu.VMEM((rows, cells), jnp.float32),
        ],
    )(*exps, *tall, wide_feat, peaks, mask, own, other, mass, norm)
    arrived = lax.all_to_all(columns, "src", 0, 0)
    outs = [f32(1, cells), f32(rows, cells)]
    potential_new, potential_src = call(merge_kernel, [VM] * 3, outs)(arrived, weight, potential_src)
    return potential_src, potential_new


def merged(part, axis, combine):
    gathered = jax.tree.map(lambda a: lax.all_gather(a, axis), part)

    def take(source):
        return jax.tree.map(lambda a: lax.dynamic_index_in_dim(a, source, 0, False), gathered)

    return lax.fori_loop(
        1, lax.axis_size(axis), lambda source, state: combine(state, take(source)), take(0)
    )


def cost_tiles(source_blk, source_sq, target_blk, target_sq):
    cross = jnp.einsum(
        "...fi,...fj->...ij", source_blk, target_blk, precision=lax.Precision.HIGHEST
    )
    return source_sq[..., :, None] + target_sq[..., None, :] - 2.0 * cross


def row_stats(cost, mass_tgt, poten_tgt, usable):
    scores = mass_tgt[..., None, :] + (poten_tgt[..., None, :] - cost) / entropic
    scores = jnp.where(usable[..., None, None], scores, very_low)
    peak = jnp.max(scores, axis=(1, 3))
    total = jnp.sum(jnp.exp(scores - peak[:, None, :, None]), axis=(1, 3))
    return (peak, total)


def column_stats(cost, mass_src, poten_src, usable):
    scores = mass_src[:, None, :, None] + (poten_src[:, None, :, None] - cost) / entropic
    peak = jnp.max(scores, axis=2)
    total = jnp.sum(jnp.exp(scores - peak[:, :, None, :]), axis=2)
    peak = jnp.where(usable[..., None], peak, very_low)
    total = jnp.where(usable[..., None], total, 0.0)
    return (peak, total)


def merge_pair(first_pair, second_pair):
    first_peak, first_total = first_pair
    second_peak, second_total = second_pair
    highest = jnp.maximum(first_peak, second_peak)
    summed = first_total * jnp.exp(first_peak - highest) + second_total * jnp.exp(
        second_peak - highest
    )
    return (highest, summed)


def segment_merge(peaks, totals, seg_ids, segments):
    best = jax.ops.segment_max(peaks, seg_ids, num_segments=segments + 1)
    best = jnp.maximum(best, very_low)
    summed = jax.ops.segment_sum(
        totals * jnp.exp(peaks - best[seg_ids]), seg_ids, num_segments=segments + 1
    )
    return (best[:segments], summed[:segments])


def general_device(
    source_feat, target_feat, log_mass_src, log_mass_tgt, potential_tgt, support, counts
):
    target_all, mass_all, poten_all = (
        lax.all_gather(target_feat, "src", axis=0, tiled=True),
        lax.all_gather(log_mass_tgt, "src", axis=0, tiled=True),
        lax.all_gather(potential_tgt, "src", axis=0, tiled=True),
    )
    blocks = target_all.shape[0]
    rows_here = source_feat.shape[0]
    slots_here = support.shape[2]
    cells = source_feat.shape[2]
    indices = support[:, 0, :]
    limits = counts[:, 0]
    usable = jnp.arange(slots_here, dtype=jnp.int32)[None, :] < limits[:, None]
    source_sq = jnp.sum(source_feat * source_feat, axis=1)
    target_sq = jnp.sum(target_all * target_all, axis=1)
    width = math.gcd(rows_here, 4)

    def grouped(array):
        return array.reshape((rows_here // width, width) + array.shape[1:])

    def row_pass(items):
        source_blk, source_nrm, ids_here, use_here = items
        cost = cost_tiles(
            source_blk[:, None], source_nrm[:, None], target_all[ids_here], target_sq[ids_here]
        )
        return row_stats(cost, mass_all[ids_here], poten_all[ids_here], use_here)

    peak, total = lax.map(
        row_pass, (grouped(source_feat), grouped(source_sq), grouped(indices), grouped(usable))
    )
    peak = peak.reshape(rows_here, cells)
    total = total.reshape(rows_here, cells)
    peak_all, total_all = merged((peak, total), "tgt", merge_pair)
    potential_src = -entropic * (peak_all + jnp.log(total_all))

    def column_pass(items):
        source_blk, source_nrm, mass_here, poten_here, ids_here, use_here = items
        cost = cost_tiles(
            source_blk[:, None], source_nrm[:, None], target_all[ids_here], target_sq[ids_here]
        )
        return column_stats(cost, mass_here, poten_here, use_here)

    peaks, totals = lax.map(
        column_pass,
        (
            grouped(source_feat),
            grouped(source_sq),
            grouped(log_mass_src),
            grouped(potential_src),
            grouped(indices),
            grouped(usable),
        ),
    )
    seg_ids = jnp.where(usable, indices, blocks).reshape(-1)
    best, summed = segment_merge(
        peaks.reshape(-1, cells), totals.reshape(-1, cells), seg_ids, blocks
    )
    share = blocks // lax.axis_size("src")
    own_start = lax.axis_index("src") * share
    highest = lax.pmax(best, "src")
    whole = lax.psum(summed * jnp.exp(best - highest), "src")
    own_peak = lax.dynamic_slice_in_dim(highest, own_start, share, 0)
    own_total = lax.dynamic_slice_in_dim(whole, own_start, share, 0)
    potential_new = -entropic * (own_peak + jnp.log(own_total))
    return (potential_src, potential_new)


def per_device(source_feat, target_feat, *others):
    shards = lax.axis_size("src")
    rows, depth, cells = source_feat.shape
    few = shards == 8 and target_feat.shape[0] == 1 and lax.axis_size("tgt") == 2
    if few and rows % 8 == 0 and cells == 128 and depth == 64:
        return dense_device(source_feat, target_feat, *others)
    return general_device(source_feat, target_feat, *others)


def solution(mesh):
    in_specs = (
        P(("grp", "src"), None, None),
        P(("grp", "src", "tgt"), None, None),
        P(("grp", "src"), None),
        P(("grp", "src", "tgt"), None),
        P(("grp", "src", "tgt"), None),
        P(("grp", "src"), "tgt", None),
        P(("grp", "src"), "tgt"),
    )
    out_specs = (P(("grp", "src"), None), P(("grp", "src", "tgt"), None))
    return jax.shard_map(
        per_device, mesh=mesh, in_specs=in_specs, out_specs=out_specs, check_vma=False
    )
```

```python
import functools
import math

import jax
import jax.numpy as jnp
from jax import lax
from jax.experimental import pallas as pl
from jax.experimental.pallas import tpu as pltpu
from jax.sharding import PartitionSpec as P

entropic = 0.5
very_low = -1e30
log2e = 1.0 / math.log(2.0)
ln2 = math.log(2.0)
least_sum = 1e-28

VM = pl.BlockSpec(memory_space=pltpu.VMEM)
PARAMS = pltpu.CompilerParams(vmem_limit_bytes=40 * 2**20)


def in_vmem(shape, dtype):
    return pltpu.VMEM(shape, dtype)


def pieces(values):
    high = values.astype(jnp.bfloat16).astype(jnp.float32)
    rest = values - high
    mid = rest.astype(jnp.bfloat16).astype(jnp.float32)
    low = (rest - mid).astype(jnp.bfloat16).astype(jnp.float32)
    return high, mid, low


def target_weight(mass, poten):
    return (mass + poten / entropic) * log2e


def line_steps(shards):
    return [2 * (i ^ (i >> 1)) for i in range(shards // 2 - 1, 0, -1)]


def blocks_at(shards):
    near = [0] + line_steps(shards)
    me = lax.axis_index("src")
    return [me ^ other for other in near + [step ^ 1 for step in near]]


def read_all(hbm, held, sems):
    copies = [pltpu.make_async_copy(src, dst, sems.at[i]) for i, (src, dst) in enumerate(zip(hbm, held))]
    for copy in copies:
        copy.start()
    return copies


def pack_kernel(*refs):
    hbm, (send_ref, weight_ref), held, sems = refs[:3], refs[3:5], refs[5:8], refs[8]
    for copy in read_all(hbm, held, sems):
        copy.wait()
    feat_ref, mass_ref, poten_ref = held
    feat = feat_ref[0]
    depth, cells = feat.shape
    weight = target_weight(mass_ref[...], poten_ref[...])
    norm = jnp.sum(feat * feat, axis=0, keepdims=True)
    bias = weight - (log2e / entropic) * norm
    scaled = feat * (2.0 * log2e / entropic)
    below = jnp.broadcast_to(bias, (send_ref.shape[1] - depth, cells))
    send_ref[0, :depth, :] = scaled
    send_ref[0, depth:, :] = below
    weight_ref[...] = weight


def source_kernel(shards, *refs):
    hbm, outs, held, sems = refs[:4], refs[4:8], refs[8:12], refs[12]
    wide_ref, norm_ref, mask_ref, mass_out_ref = outs
    mass_ref, support_ref, counts_ref, feat_ref = held
    copies = read_all(hbm, held, sems)
    for copy in copies[:3]:
        copy.wait()
    mass_out_ref[...] = mass_ref[...]
    support = support_ref[...]
    slots, rows = support.shape
    cells = mass_ref.shape[1]
    used = lax.broadcasted_iota(jnp.int32, support.shape, 0) < counts_ref[...]
    hits = [
        jnp.max(jnp.where(used & (support == block), 0.0, very_low), axis=0, keepdims=True)
        for block in blocks_at(shards)
    ]
    hits = jnp.concatenate(hits + [jnp.zeros((cells - shards, rows), jnp.float32)], axis=0)
    hits = jnp.concatenate([hits, jnp.zeros((cells, cells - rows), jnp.float32)], axis=1).T
    for place in range(shards):
        mask_ref[place] = jnp.broadcast_to(hits[:rows, place : place + 1], (rows, cells))
    copies[3].wait()
    depth = feat_ref.shape[1]
    one = jnp.ones((2 * depth, 2 * cells), jnp.bfloat16)
    for pair in range(rows // 2):
        for half in range(2):
            feat = feat_ref[2 * pair + half]
            norm_ref[2 * pair + half : 2 * pair + half + 1, :] = jnp.sum(feat * feat, axis=0, keepdims=True)
            high, mid, low = pieces(feat)
            lanes = slice(half * cells, (half + 1) * cells)
            top = jnp.concatenate([high, mid], axis=0).astype(jnp.bfloat16)
            wide_ref[pair, 0 : 2 * depth, lanes] = top
            wide_ref[pair, 2 * depth : 4 * depth, lanes] = top
            wide_ref[pair, 4 * depth : 6 * depth, lanes] = jnp.concatenate([low, high], axis=0).astype(jnp.bfloat16)
        wide_ref[pair, 6 * depth : 8 * depth, :] = one


def join_kernel(*refs):
    refs[-1][0] = refs[0][0]
    refs[-1][1] = refs[1][0]


def tile_kernel(parts, *refs):
    packs = [ref.at[index] for ref in refs[:parts] for index in range(ref.shape[0])]
    wide_ref, exps_ref, tall_ref, peak_ref, total_ref = refs[parts:]
    blocks = len(packs)
    pairs, _, both = wide_ref.shape
    cells = both // 2
    depth = cells // 2
    lane = lax.broadcasted_iota(jnp.int32, (cells, cells), 1)
    biases = jnp.concatenate([pack[depth : depth + 1, :] for pack in packs], axis=0)
    bias_pieces = jnp.concatenate(list(pieces(biases)), axis=0)
    padded = jnp.concatenate([bias_pieces, jnp.zeros((cells - 3 * blocks, cells), jnp.float32)], axis=0)
    bias_lanes = padded.T
    for place, pack in enumerate(packs):
        feat = pack[:depth, :]
        turned = jnp.concatenate([feat, feat], axis=0).T
        high, mid, low = pieces(turned)
        own = jnp.where(lax.rem(lane, blocks) == place, bias_lanes, 0.0)
        rows = slice(place * cells, (place + 1) * cells)
        tall_ref[rows, 0:cells] = high.astype(jnp.bfloat16)
        tall_ref[rows, cells : 2 * cells] = mid.astype(jnp.bfloat16)
        tall_ref[rows, 2 * cells : 3 * cells] = jnp.where(lane < depth, high, low).astype(jnp.bfloat16)
        tall_ref[rows, 3 * cells : 4 * cells] = own.astype(jnp.bfloat16)

    def body(pair, carry):
        scores = jnp.dot(tall_ref[...], wide_ref[pair], preferred_element_type=jnp.float32)
        for place in range(blocks):
            rows = slice(place * cells, (place + 1) * cells)
            score = scores[rows]
            peak = jnp.max(score, axis=0, keepdims=True)
            exps = jnp.exp2(score - peak)
            exps_ref[pair, rows, :] = exps
            total = jnp.sum(exps, axis=0, keepdims=True)
            for half in range(2):
                lanes = slice(half * cells, (half + 1) * cells)
                peak_ref[place, pl.ds(2 * pair + half, 1), :] = peak[:, lanes]
                total_ref[place, pl.ds(2 * pair + half, 1), :] = total[:, lanes]
        return carry

    lax.fori_loop(0, pairs, body, 0, unroll=min(pairs, 16 // blocks & -4 or 2))


def row_kernel(groups, *refs):
    mask_ref, peak_refs, total_refs = refs[0], refs[1 : 1 + groups], refs[1 + groups : 1 + 2 * groups]
    peaks_ref, rowsum_ref = refs[1 + 2 * groups :]
    place = 0
    for ref in peak_refs:
        for index in range(ref.shape[0]):
            peaks_ref[place] = ref[index] + mask_ref[place]
            place += 1
    totals = [ref[index] for ref in total_refs for index in range(ref.shape[0])]
    top = functools.reduce(jnp.maximum, [peaks_ref[index] for index in range(place)])
    summed = sum(total * jnp.exp2(peaks_ref[index] - top) for index, total in enumerate(totals))
    rowsum_ref[...] = top + jnp.log2(summed)


def across(column):
    shape = (column.shape[0],) * 2
    same = lax.broadcasted_iota(jnp.int32, shape, 0) == lax.broadcasted_iota(jnp.int32, shape, 1)
    return jnp.sum(jnp.where(same, jnp.broadcast_to(column, shape), 0.0), axis=0, keepdims=True)


def column_kernel(groups, *refs):
    exps_refs, tall_refs, rest = refs[:groups], refs[groups : 2 * groups], refs[2 * groups :]
    wide_ref, peak_ref, mask_ref, own_ref, other_ref, mass_ref, norm_ref = rest[:7]
    poten_ref, sums_ref, weight_ref, shift_ref = rest[7:]
    pairs, _, both = wide_ref.shape
    cells = both // 2
    shards = mask_ref.shape[0]
    own, other = own_ref[...], other_ref[...]
    top = jnp.maximum(own, other)
    whole = top + jnp.log2(jnp.exp2(own - top) + jnp.exp2(other - top))
    poten_ref[...] = norm_ref[...] - (entropic * ln2) * whole
    shift = mass_ref[...] * log2e - whole
    shift_ref[...] = shift
    for place in range(shards):
        weight_ref[place] = jnp.exp2(peak_ref[place] + shift)
    spots = [
        (group, slice(index * cells, (index + 1) * cells))
        for group, ref in enumerate(tall_refs)
        for index in range(ref.shape[0] // cells)
    ]
    used = [jnp.max(mask_ref[place], axis=0, keepdims=True) > 0.5 * very_low for place in range(shards)]
    worst = jnp.full((1, cells), 1.0, jnp.float32)
    owners = blocks_at(shards)
    for place, (group, rows) in enumerate(spots):
        acc = jnp.zeros((cells, cells), jnp.float32)
        for pair in range(pairs):
            acc = acc + exps_refs[group][pair, rows, :cells] * weight_ref[place, 2 * pair : 2 * pair + 1, :]
            acc = acc + exps_refs[group][pair, rows, cells:] * weight_ref[place, 2 * pair + 1 : 2 * pair + 2, :]
        here = across(jnp.sum(acc, axis=1, keepdims=True))
        sums_ref[owners[place]] = jnp.where(used[place], jnp.log2(here), very_low)
        worst = jnp.minimum(worst, jnp.where(used[place], here, 1.0))

    @pl.when(jnp.min(worst) < least_sum)
    def _():
        for place, (group, rows) in enumerate(spots):

            def exponents(pair):
                score = jnp.dot(tall_refs[group][rows, :], wide_ref[pair], preferred_element_type=jnp.float32)
                add = shift_ref[pl.ds(2 * pair, 2), :] + mask_ref[place, pl.ds(2 * pair, 2), :]
                return score[:, :cells] + add[0:1, :], score[:, cells:] + add[1:2, :]

            def highest(pair, peak):
                first, second = exponents(pair)
                return jnp.maximum(peak, jnp.maximum(first, second))

            peak = lax.fori_loop(0, pairs, highest, jnp.full((cells, cells), very_low, jnp.float32))
            peak = jnp.max(peak, axis=1, keepdims=True)

            def add_up(pair, sums):
                first, second = exponents(pair)
                return sums + jnp.exp2(first - peak) + jnp.exp2(second - peak)

            sums = lax.fori_loop(0, pairs, add_up, jnp.zeros((cells, cells), jnp.float32))
            logs = across(peak) + jnp.log2(across(jnp.sum(sums, axis=1, keepdims=True)))
            sums_ref[owners[place]] = jnp.where(used[place], logs, very_low)


def merge_kernel(values_ref, weight_ref, poten_ref, out_ref, poten_out_ref):
    poten_out_ref[...] = poten_ref[...]
    values = values_ref[...]
    top = jnp.max(values, axis=0)
    whole = top + jnp.log2(jnp.sum(jnp.exp2(values - top), axis=0))
    out_ref[...] = -(entropic * ln2) * (whole - weight_ref[...])


def f32(*shape):
    return jax.ShapeDtypeStruct(shape, jnp.float32)


def dense_device(
    source_feat, target_feat, log_mass_src, log_mass_tgt, potential_tgt, support, counts
):
    shards = lax.axis_size("src")
    rows, depth, cells = source_feat.shape
    pairs, wide = rows // 2, 2 * cells

    def call(kernel, ins, out_shape, scratch=(), cost=None):
        many = isinstance(out_shape, list)
        return pl.pallas_call(
            kernel,
            in_specs=ins,
            out_specs=[VM] * len(out_shape) if many else VM,
            out_shape=out_shape,
            scratch_shapes=list(scratch),
            compiler_params=PARAMS,
            cost_estimate=cost,
        )

    def reading(kernel, args, out_shape, cost):
        return call(
            kernel,
            [pl.BlockSpec(memory_space=pltpu.HBM)] * len(args),
            out_shape,
            [pltpu.VMEM(arg.shape, arg.dtype) for arg in args] + [pltpu.SemaphoreType.DMA((len(args),))],
            cost,
        )(*[pltpu.with_memory_space_constraint(arg, pltpu.HBM) for arg in args])

    def cost_of(flops):
        return pl.CostEstimate(flops=flops, bytes_accessed=rows * depth * cells * 4, transcendentals=0)

    pack, weight = reading(
        pack_kernel,
        [target_feat, log_mass_tgt, potential_tgt],
        [in_vmem((1, depth + 8, cells), jnp.float32), in_vmem((1, cells), jnp.float32)],
        None,
    )
    wide_feat, norm, mask, mass = reading(
        functools.partial(source_kernel, shards),
        [log_mass_src, support[:, 0, :].T, counts.T, source_feat],
        [
            in_vmem((pairs, 8 * depth, wide), jnp.bfloat16),
            in_vmem((rows, cells), jnp.float32),
            in_vmem((shards, rows, cells), jnp.float32),
            in_vmem((rows, cells), jnp.float32),
        ],
        cost_of(10**9),
    )

    def tiles(*packs):
        blocks = sum(pack.shape[0] for pack in packs)
        return call(
            functools.partial(tile_kernel, len(packs)),
            [VM] * (len(packs) + 1),
            [
                in_vmem((pairs, blocks * cells, wide), jnp.float32),
                in_vmem((blocks * cells, 8 * depth), jnp.bfloat16),
                in_vmem((blocks, rows, cells), jnp.float32),
                in_vmem((blocks, rows, cells), jnp.float32),
            ],
            cost=cost_of(2 * blocks * cells * pairs * wide * 8 * depth),
        )(*packs, wide_feat)

    def swapped(array, step):
        return lax.ppermute(array, "src", [(i, i ^ step) for i in range(shards)])

    there = {step: swapped(pack, step) for step in reversed(line_steps(shards))}
    near = [pack] + [there[step] for step in line_steps(shards)]
    found = [tiles(pack)]
    halves = [
        call(
            join_kernel,
            [VM] * 2 + [pl.BlockSpec(memory_space=pl.ANY)],
            in_vmem((2,) + pack.shape[1:], jnp.float32),
        )(near[at], near[at + 1], found[0][-1])
        for at in range(0, len(near), 2)
    ]
    far = [swapped(half, 1) for half in halves]
    found += [tiles(*near[1:])] + [tiles(half) for half in far]
    exps, tall, peaks, totals = zip(*found)
    groups = len(found)
    peaks, own = call(
        functools.partial(row_kernel, groups),
        [VM] * (1 + 2 * groups),
        [in_vmem((shards, rows, cells), jnp.float32), in_vmem((rows, cells), jnp.float32)],
    )(mask, *peaks, *totals)
    other = lax.ppermute(own, "tgt", [(0, 1), (1, 0)])
    potential_src, columns = call(
        functools.partial(column_kernel, groups),
        [VM] * (2 * groups + 7),
        [in_vmem((rows, cells), jnp.float32), in_vmem((shards, 1, cells), jnp.float32)],
        [
            pltpu.VMEM((shards, rows, cells), jnp.float32),
            pltpu.VMEM((rows, cells), jnp.float32),
        ],
    )(*exps, *tall, wide_feat, peaks, mask, own, other, mass, norm)
    arrived = lax.all_to_all(columns, "src", 0, 0)
    outs = [f32(1, cells), f32(rows, cells)]
    potential_new, potential_src = call(merge_kernel, [VM] * 3, outs)(arrived, weight, potential_src)
    return potential_src, potential_new


def merged(part, axis, combine):
    gathered = jax.tree.map(lambda a: lax.all_gather(a, axis), part)

    def take(source):
        return jax.tree.map(lambda a: lax.dynamic_index_in_dim(a, source, 0, False), gathered)

    return lax.fori_loop(
        1, lax.axis_size(axis), lambda source, state: combine(state, take(source)), take(0)
    )


def cost_tiles(source_blk, source_sq, target_blk, target_sq):
    cross = jnp.einsum(
        "...fi,...fj->...ij", source_blk, target_blk, precision=lax.Precision.HIGHEST
    )
    return source_sq[..., :, None] + target_sq[..., None, :] - 2.0 * cross


def row_stats(cost, mass_tgt, poten_tgt, usable):
    scores = mass_tgt[..., None, :] + (poten_tgt[..., None, :] - cost) / entropic
    scores = jnp.where(usable[..., None, None], scores, very_low)
    peak = jnp.max(scores, axis=(1, 3))
    total = jnp.sum(jnp.exp(scores - peak[:, None, :, None]), axis=(1, 3))
    return (peak, total)


def column_stats(cost, mass_src, poten_src, usable):
    scores = mass_src[:, None, :, None] + (poten_src[:, None, :, None] - cost) / entropic
    peak = jnp.max(scores, axis=2)
    total = jnp.sum(jnp.exp(scores - peak[:, :, None, :]), axis=2)
    peak = jnp.where(usable[..., None], peak, very_low)
    total = jnp.where(usable[..., None], total, 0.0)
    return (peak, total)


def merge_pair(first_pair, second_pair):
    first_peak, first_total = first_pair
    second_peak, second_total = second_pair
    highest = jnp.maximum(first_peak, second_peak)
    summed = first_total * jnp.exp(first_peak - highest) + second_total * jnp.exp(
        second_peak - highest
    )
    return (highest, summed)


def segment_merge(peaks, totals, seg_ids, segments):
    best = jax.ops.segment_max(peaks, seg_ids, num_segments=segments + 1)
    best = jnp.maximum(best, very_low)
    summed = jax.ops.segment_sum(
        totals * jnp.exp(peaks - best[seg_ids]), seg_ids, num_segments=segments + 1
    )
    return (best[:segments], summed[:segments])


def general_device(
    source_feat, target_feat, log_mass_src, log_mass_tgt, potential_tgt, support, counts
):
    target_all, mass_all, poten_all = (
        lax.all_gather(target_feat, "src", axis=0, tiled=True),
        lax.all_gather(log_mass_tgt, "src", axis=0, tiled=True),
        lax.all_gather(potential_tgt, "src", axis=0, tiled=True),
    )
    blocks = target_all.shape[0]
    rows_here = source_feat.shape[0]
    slots_here = support.shape[2]
    cells = source_feat.shape[2]
    indices = support[:, 0, :]
    limits = counts[:, 0]
    usable = jnp.arange(slots_here, dtype=jnp.int32)[None, :] < limits[:, None]
    source_sq = jnp.sum(source_feat * source_feat, axis=1)
    target_sq = jnp.sum(target_all * target_all, axis=1)
    width = math.gcd(rows_here, 4)

    def grouped(array):
        return array.reshape((rows_here // width, width) + array.shape[1:])

    def row_pass(items):
        source_blk, source_nrm, ids_here, use_here = items
        cost = cost_tiles(
            source_blk[:, None], source_nrm[:, None], target_all[ids_here], target_sq[ids_here]
        )
        return row_stats(cost, mass_all[ids_here], poten_all[ids_here], use_here)

    peak, total = lax.map(
        row_pass, (grouped(source_feat), grouped(source_sq), grouped(indices), grouped(usable))
    )
    peak = peak.reshape(rows_here, cells)
    total = total.reshape(rows_here, cells)
    peak_all, total_all = merged((peak, total), "tgt", merge_pair)
    potential_src = -entropic * (peak_all + jnp.log(total_all))

    def column_pass(items):
        source_blk, source_nrm, mass_here, poten_here, ids_here, use_here = items
        cost = cost_tiles(
            source_blk[:, None], source_nrm[:, None], target_all[ids_here], target_sq[ids_here]
        )
        return column_stats(cost, mass_here, poten_here, use_here)

    peaks, totals = lax.map(
        column_pass,
        (
            grouped(source_feat),
            grouped(source_sq),
            grouped(log_mass_src),
            grouped(potential_src),
            grouped(indices),
            grouped(usable),
        ),
    )
    seg_ids = jnp.where(usable, indices, blocks).reshape(-1)
    best, summed = segment_merge(
        peaks.reshape(-1, cells), totals.reshape(-1, cells), seg_ids, blocks
    )
    share = blocks // lax.axis_size("src")
    own_start = lax.axis_index("src") * share
    highest = lax.pmax(best, "src")
    whole = lax.psum(summed * jnp.exp(best - highest), "src")
    own_peak = lax.dynamic_slice_in_dim(highest, own_start, share, 0)
    own_total = lax.dynamic_slice_in_dim(whole, own_start, share, 0)
    potential_new = -entropic * (own_peak + jnp.log(own_total))
    return (potential_src, potential_new)


def per_device(source_feat, target_feat, *others):
    shards = lax.axis_size("src")
    rows, depth, cells = source_feat.shape
    few = shards == 8 and target_feat.shape[0] == 1 and lax.axis_size("tgt") == 2
    if few and rows % 8 == 0 and cells == 128 and depth == 64:
        return dense_device(source_feat, target_feat, *others)
    return general_device(source_feat, target_feat, *others)


def solution(mesh):
    in_specs = (
        P(("grp", "src"), None, None),
        P(("grp", "src", "tgt"), None, None),
        P(("grp", "src"), None),
        P(("grp", "src", "tgt"), None),
        P(("grp", "src", "tgt"), None),
        P(("grp", "src"), "tgt", None),
        P(("grp", "src"), "tgt"),
    )
    out_specs = (P(("grp", "src"), None), P(("grp", "src", "tgt"), None))
    return jax.shard_map(
        per_device, mesh=mesh, in_specs=in_specs, out_specs=out_specs, check_vma=False
    )
```

```python
import functools
import math

import jax
import jax.numpy as jnp
from jax import lax
from jax.experimental import pallas as pl
from jax.experimental.pallas import tpu as pltpu
from jax.sharding import PartitionSpec as P

entropic = 0.5
very_low = -1e30
log2e = 1.0 / math.log(2.0)
ln2 = math.log(2.0)
row_bounds = (2.0**-30, 2.0**100)
column_bounds = (1e-19, 1e30)

VM = pl.BlockSpec(memory_space=pltpu.VMEM)
PARAMS = pltpu.CompilerParams(vmem_limit_bytes=40 * 2**20)


def in_vmem(shape, dtype):
    return pltpu.VMEM(shape, dtype)


def pieces(values):
    high = values.astype(jnp.bfloat16).astype(jnp.float32)
    rest = values - high
    mid = rest.astype(jnp.bfloat16).astype(jnp.float32)
    low = (rest - mid).astype(jnp.bfloat16).astype(jnp.float32)
    return high, mid, low


def target_weight(mass, poten):
    return (mass + poten / entropic) * log2e


def line_steps(shards):
    return [2 * (i ^ (i >> 1)) for i in range(shards // 2 - 1, 0, -1)]


def blocks_at(shards):
    near = [0] + line_steps(shards)
    me = lax.axis_index("src")
    return [me ^ other for other in near + [step ^ 1 for step in near]]


def read_all(hbm, held, sems):
    copies = [pltpu.make_async_copy(src, dst, sems.at[i]) for i, (src, dst) in enumerate(zip(hbm, held))]
    for copy in copies:
        copy.start()
    return copies


def pack_kernel(*refs):
    hbm, (send_ref, weight_ref), held, sems = refs[:3], refs[3:5], refs[5:8], refs[8]
    for copy in read_all(hbm, held, sems):
        copy.wait()
    feat_ref, mass_ref, poten_ref = held
    feat = feat_ref[0]
    depth, cells = feat.shape
    weight = target_weight(mass_ref[...], poten_ref[...])
    norm = jnp.sum(feat * feat, axis=0, keepdims=True)
    bias = weight - (log2e / entropic) * norm
    scaled = feat * (2.0 * log2e / entropic)
    below = jnp.broadcast_to(bias, (send_ref.shape[1] - depth, cells))
    send_ref[0, :depth, :] = scaled
    send_ref[0, depth:, :] = below
    weight_ref[...] = weight


def source_kernel(shards, *refs):
    hbm, outs, held, sems = refs[:4], refs[4:8], refs[8:12], refs[12]
    wide_ref, norm_ref, mask_ref, mass_out_ref = outs
    mass_ref, support_ref, counts_ref, feat_ref = held
    copies = read_all(hbm, held, sems)
    for copy in copies[:3]:
        copy.wait()
    mass_out_ref[...] = mass_ref[...]
    support = support_ref[...]
    slots, rows = support.shape
    cells = mass_ref.shape[1]
    used = lax.broadcasted_iota(jnp.int32, support.shape, 0) < counts_ref[...]
    hits = [
        jnp.max(jnp.where(used & (support == block), 0.0, very_low), axis=0, keepdims=True)
        for block in blocks_at(shards)
    ]
    hits = jnp.concatenate(hits + [jnp.zeros((cells - shards, rows), jnp.float32)], axis=0)
    hits = jnp.concatenate([hits, jnp.zeros((cells, cells - rows), jnp.float32)], axis=1).T
    for place in range(shards):
        mask_ref[place] = jnp.broadcast_to(hits[:rows, place : place + 1], (rows, cells))
    copies[3].wait()
    depth = feat_ref.shape[1]
    one = jnp.ones((2 * depth, 2 * cells), jnp.bfloat16)
    for pair in range(rows // 2):
        for half in range(2):
            feat = feat_ref[2 * pair + half]
            norm_ref[2 * pair + half : 2 * pair + half + 1, :] = jnp.sum(feat * feat, axis=0, keepdims=True)
            high, mid, low = pieces(feat)
            lanes = slice(half * cells, (half + 1) * cells)
            top = jnp.concatenate([high, mid], axis=0).astype(jnp.bfloat16)
            wide_ref[pair, 0 : 2 * depth, lanes] = top
            wide_ref[pair, 2 * depth : 4 * depth, lanes] = top
            wide_ref[pair, 4 * depth : 6 * depth, lanes] = jnp.concatenate([low, high], axis=0).astype(jnp.bfloat16)
        wide_ref[pair, 6 * depth : 8 * depth, :] = one


def join_kernel(*refs):
    for place, ref in enumerate(refs[:-2]):
        refs[-1][place] = ref[0]


def fill_tall(packs, tall_ref):
    blocks = len(packs)
    cells = packs[0].shape[1]
    depth = cells // 2
    lane = lax.broadcasted_iota(jnp.int32, (cells, cells), 1)
    biases = jnp.concatenate([pack[depth : depth + 1, :] for pack in packs], axis=0)
    bias_pieces = jnp.concatenate(list(pieces(biases)), axis=0)
    padded = jnp.concatenate([bias_pieces, jnp.zeros((cells - 3 * blocks, cells), jnp.float32)], axis=0)
    bias_lanes = padded.T
    for place, pack in enumerate(packs):
        feat = pack[:depth, :]
        turned = jnp.concatenate([feat, feat], axis=0).T
        high, mid, low = pieces(turned)
        own = jnp.where(lax.rem(lane, blocks) == place, bias_lanes, 0.0)
        rows = slice(place * cells, (place + 1) * cells)
        tall_ref[rows, 0:cells] = high.astype(jnp.bfloat16)
        tall_ref[rows, cells : 2 * cells] = mid.astype(jnp.bfloat16)
        tall_ref[rows, 2 * cells : 3 * cells] = jnp.where(lane < depth, high, low).astype(jnp.bfloat16)
        tall_ref[rows, 3 * cells : 4 * cells] = own.astype(jnp.bfloat16)


def put_rows(ref, pair, values):
    cells = values.shape[1] // 2
    ref[pl.ds(2 * pair, 1), :] = values[:, :cells]
    ref[pl.ds(2 * pair + 1, 1), :] = values[:, cells:]


def two_rows(ref, pair):
    return jnp.concatenate([ref[pl.ds(2 * pair, 1), :], ref[pl.ds(2 * pair + 1, 1), :]], axis=1)


def own_kernel(pack_ref, wide_ref, exps_ref, tall_ref, total_ref, shift_ref):
    fill_tall([pack_ref.at[0]], tall_ref)
    pairs = wide_ref.shape[0]

    def body(pair, carry):
        score = jnp.dot(tall_ref[...], wide_ref[pair], preferred_element_type=jnp.float32)
        peak = jnp.max(score, axis=0, keepdims=True)
        exps = jnp.exp2(score - peak)
        exps_ref[pair] = exps
        put_rows(shift_ref, pair, peak)
        put_rows(total_ref.at[0], pair, jnp.sum(exps, axis=0, keepdims=True))
        return carry

    lax.fori_loop(0, pairs, body, 0, unroll=pairs)


def tile_kernel(parts, *refs):
    packs = [ref.at[index] for ref in refs[:parts] for index in range(ref.shape[0])]
    wide_ref, shift_ref, _, exps_ref, tall_ref, total_ref = refs[parts:]
    fill_tall(packs, tall_ref)
    blocks = len(packs)
    pairs, _, both = wide_ref.shape
    cells = both // 2

    def body(pair, carry):
        scores = jnp.dot(tall_ref[...], wide_ref[pair], preferred_element_type=jnp.float32)
        shift = two_rows(shift_ref, pair)
        for place in range(blocks):
            rows = slice(place * cells, (place + 1) * cells)
            exps = jnp.exp2(scores[rows] - shift)
            exps_ref[pair, rows, :] = exps
            put_rows(total_ref.at[place], pair, jnp.sum(exps, axis=0, keepdims=True))
        return carry

    lax.fori_loop(0, pairs, body, 0, unroll=min(pairs, 16 // blocks & -4 or 2))


def inside(values, bounds):
    return (values >= bounds[0]) & (values <= bounds[1])


def spots_of(tall_refs, cells):
    return [
        (group, slice(index * cells, (index + 1) * cells))
        for group, ref in enumerate(tall_refs)
        for index in range(ref.shape[0] // cells)
    ]


def row_kernel(groups, *refs):
    mask_ref, shift_ref, wide_ref = refs[:3]
    total_refs, tall_refs = refs[3 : 3 + groups], refs[3 + groups : 3 + 2 * groups]
    rowsum_ref, exact_ref = refs[3 + 2 * groups :]
    pairs, _, both = wide_ref.shape
    cells = both // 2
    totals = [ref[index] for ref in total_refs for index in range(ref.shape[0])]
    summed = sum(jnp.where(mask_ref[place] > 0.5 * very_low, total, 0.0) for place, total in enumerate(totals))
    rowsum_ref[...] = shift_ref[...] + jnp.log2(summed)
    served = jnp.min(jnp.where(inside(summed, row_bounds), 1.0, 0.0))
    exact_ref[...] = jnp.zeros(exact_ref.shape, jnp.float32) + (1.0 - served)

    @pl.when(served < 0.5)
    def _():
        spots = spots_of(tall_refs, cells)

        def body(pair, carry):
            def scores():
                for place, (group, rows) in enumerate(spots):
                    score = jnp.dot(tall_refs[group][rows, :], wide_ref[pair], preferred_element_type=jnp.float32)
                    yield score + two_rows(mask_ref.at[place], pair)

            peak = functools.reduce(jnp.maximum, [jnp.max(score, axis=0, keepdims=True) for score in scores()])
            sums = [jnp.sum(jnp.exp2(score - peak), axis=0, keepdims=True) for score in scores()]
            put_rows(rowsum_ref, pair, peak + jnp.log2(sum(sums)))
            return carry

        lax.fori_loop(0, pairs, body, 0)


def across(column):
    shape = (column.shape[0],) * 2
    same = lax.broadcasted_iota(jnp.int32, shape, 0) == lax.broadcasted_iota(jnp.int32, shape, 1)
    return jnp.sum(jnp.where(same, jnp.broadcast_to(column, shape), 0.0), axis=0, keepdims=True)


def column_kernel(groups, *refs):
    exps_refs, tall_refs, rest = refs[:groups], refs[groups : 2 * groups], refs[2 * groups :]
    wide_ref, peak_ref, exact_ref, mask_ref, own_ref, other_ref, mass_ref, norm_ref = rest[:8]
    poten_ref, sums_ref, weight_ref, shift_ref = rest[8:]
    pairs, _, both = wide_ref.shape
    cells = both // 2
    shards = mask_ref.shape[0]
    own, other = own_ref[...], other_ref[...]
    top = jnp.maximum(own, other)
    whole = top + jnp.log2(jnp.exp2(own - top) + jnp.exp2(other - top))
    poten_ref[...] = norm_ref[...] - (entropic * ln2) * whole
    shift = mass_ref[...] * log2e - whole
    shift_ref[...] = shift
    weight = jnp.exp2(peak_ref[...] + shift)
    for place in range(shards):
        weight_ref[place] = jnp.where(mask_ref[place] > 0.5 * very_low, weight, 0.0)
    spots = spots_of(tall_refs, cells)
    used = [jnp.max(mask_ref[place], axis=0, keepdims=True) > 0.5 * very_low for place in range(shards)]
    served = 1.0 - exact_ref[0:1, :]
    owners = blocks_at(shards)
    for place, (group, rows) in enumerate(spots):
        acc = jnp.zeros((cells, cells), jnp.float32)
        for pair in range(pairs):
            acc = acc + exps_refs[group][pair, rows, :cells] * weight_ref[place, 2 * pair : 2 * pair + 1, :]
            acc = acc + exps_refs[group][pair, rows, cells:] * weight_ref[place, 2 * pair + 1 : 2 * pair + 2, :]
        here = across(jnp.sum(acc, axis=1, keepdims=True))
        sums_ref[owners[place]] = jnp.where(used[place], jnp.log2(here), very_low)
        served = jnp.where(inside(here, column_bounds) | ~used[place], served, 0.0)

    @pl.when(jnp.min(served) < 0.5)
    def _():
        for place, (group, rows) in enumerate(spots):

            def exponents(pair):
                score = jnp.dot(tall_refs[group][rows, :], wide_ref[pair], preferred_element_type=jnp.float32)
                add = shift_ref[pl.ds(2 * pair, 2), :] + mask_ref[place, pl.ds(2 * pair, 2), :]
                return score[:, :cells] + add[0:1, :], score[:, cells:] + add[1:2, :]

            def highest(pair, peak):
                first, second = exponents(pair)
                return jnp.maximum(peak, jnp.maximum(first, second))

            peak = lax.fori_loop(0, pairs, highest, jnp.full((cells, cells), very_low, jnp.float32))
            peak = jnp.max(peak, axis=1, keepdims=True)

            def add_up(pair, sums):
                first, second = exponents(pair)
                return sums + jnp.exp2(first - peak) + jnp.exp2(second - peak)

            sums = lax.fori_loop(0, pairs, add_up, jnp.zeros((cells, cells), jnp.float32))
            logs = across(peak) + jnp.log2(across(jnp.sum(sums, axis=1, keepdims=True)))
            sums_ref[owners[place]] = jnp.where(used[place], logs, very_low)


def merge_kernel(values_ref, weight_ref, poten_ref, out_ref, poten_out_ref):
    poten_out_ref[...] = poten_ref[...]
    values = values_ref[...]
    top = jnp.max(values, axis=0)
    whole = top + jnp.log2(jnp.sum(jnp.exp2(values - top), axis=0))
    out_ref[...] = -(entropic * ln2) * (whole - weight_ref[...])


def f32(*shape):
    return jax.ShapeDtypeStruct(shape, jnp.float32)


def dense_device(
    source_feat, target_feat, log_mass_src, log_mass_tgt, potential_tgt, support, counts
):
    shards = lax.axis_size("src")
    rows, depth, cells = source_feat.shape
    pairs, wide = rows // 2, 2 * cells

    def call(kernel, ins, out_shape, scratch=(), cost=None):
        many = isinstance(out_shape, list)
        return pl.pallas_call(
            kernel,
            in_specs=ins,
            out_specs=[VM] * len(out_shape) if many else VM,
            out_shape=out_shape,
            scratch_shapes=list(scratch),
            compiler_params=PARAMS,
            cost_estimate=cost,
        )

    def reading(kernel, args, out_shape, cost):
        return call(
            kernel,
            [pl.BlockSpec(memory_space=pltpu.HBM)] * len(args),
            out_shape,
            [pltpu.VMEM(arg.shape, arg.dtype) for arg in args] + [pltpu.SemaphoreType.DMA((len(args),))],
            cost,
        )(*[pltpu.with_memory_space_constraint(arg, pltpu.HBM) for arg in args])

    def cost_of(flops):
        return pl.CostEstimate(flops=flops, bytes_accessed=rows * depth * cells * 4, transcendentals=0)

    pack, weight = reading(
        pack_kernel,
        [target_feat, log_mass_tgt, potential_tgt],
        [in_vmem((1, depth + 8, cells), jnp.float32), in_vmem((1, cells), jnp.float32)],
        None,
    )
    wide_feat, norm, mask, mass = reading(
        functools.partial(source_kernel, shards),
        [log_mass_src, support[:, 0, :].T, counts.T, source_feat],
        [
            in_vmem((pairs, 8 * depth, wide), jnp.bfloat16),
            in_vmem((rows, cells), jnp.float32),
            in_vmem((shards, rows, cells), jnp.float32),
            in_vmem((rows, cells), jnp.float32),
        ],
        cost_of(10**9),
    )

    def tiles(*packs, after=None):
        blocks = sum(pack.shape[0] for pack in packs)
        own = after is None
        return call(
            own_kernel if own else functools.partial(tile_kernel, len(packs)),
            [VM] * (len(packs) + 1) + [VM, pl.BlockSpec(memory_space=pl.ANY)] * (not own),
            [
                in_vmem((pairs, blocks * cells, wide), jnp.float32),
                in_vmem((blocks * cells, 8 * depth), jnp.bfloat16),
                in_vmem((blocks, rows, cells), jnp.float32),
            ]
            + [in_vmem((rows, cells), jnp.float32)] * own,
            cost=cost_of(2 * blocks * cells * pairs * wide * 8 * depth),
        )(*packs, wide_feat, *([] if own else [shift, after]))

    def swapped(array, step):
        return lax.ppermute(array, "src", [(i, i ^ step) for i in range(shards)])

    there = {step: swapped(pack, step) for step in reversed(line_steps(shards))}
    near = [pack] + [there[step] for step in line_steps(shards)]
    *first, shift = tiles(pack)

    def joined(parts):
        return call(
            join_kernel,
            [VM] * len(parts) + [pl.BlockSpec(memory_space=pl.ANY)],
            in_vmem((len(parts),) + pack.shape[1:], jnp.float32),
        )(*parts, shift)

    far = [swapped(joined(parts), 1) for parts in (near[:-1], near[-1:])]
    found = [first]
    for packs in [near[1:]] + [[some] for some in far]:
        found.append(tiles(*packs, after=found[-1][-1]))
    exps, tall, totals = zip(*found)
    groups = len(found)
    own, exact = call(
        functools.partial(row_kernel, groups),
        [VM] * (3 + 2 * groups),
        [in_vmem((rows, cells), jnp.float32), in_vmem((8, cells), jnp.float32)],
    )(mask, shift, wide_feat, *totals, *tall)
    other = lax.ppermute(own, "tgt", [(0, 1), (1, 0)])
    potential_src, columns = call(
        functools.partial(column_kernel, groups),
        [VM] * (2 * groups + 8),
        [in_vmem((rows, cells), jnp.float32), in_vmem((shards, 1, cells), jnp.float32)],
        [
            pltpu.VMEM((shards, rows, cells), jnp.float32),
            pltpu.VMEM((rows, cells), jnp.float32),
        ],
    )(*exps, *tall, wide_feat, shift, exact, mask, own, other, mass, norm)
    arrived = lax.all_to_all(columns, "src", 0, 0)
    outs = [f32(1, cells), f32(rows, cells)]
    potential_new, potential_src = call(merge_kernel, [VM] * 3, outs)(arrived, weight, potential_src)
    return potential_src, potential_new


def merged(part, axis, combine):
    gathered = jax.tree.map(lambda a: lax.all_gather(a, axis), part)

    def take(source):
        return jax.tree.map(lambda a: lax.dynamic_index_in_dim(a, source, 0, False), gathered)

    return lax.fori_loop(
        1, lax.axis_size(axis), lambda source, state: combine(state, take(source)), take(0)
    )


def cost_tiles(source_blk, source_sq, target_blk, target_sq):
    cross = jnp.einsum(
        "...fi,...fj->...ij", source_blk, target_blk, precision=lax.Precision.HIGHEST
    )
    return source_sq[..., :, None] + target_sq[..., None, :] - 2.0 * cross


def row_stats(cost, mass_tgt, poten_tgt, usable):
    scores = mass_tgt[..., None, :] + (poten_tgt[..., None, :] - cost) / entropic
    scores = jnp.where(usable[..., None, None], scores, very_low)
    peak = jnp.max(scores, axis=(1, 3))
    total = jnp.sum(jnp.exp(scores - peak[:, None, :, None]), axis=(1, 3))
    return (peak, total)


def column_stats(cost, mass_src, poten_src, usable):
    scores = mass_src[:, None, :, None] + (poten_src[:, None, :, None] - cost) / entropic
    peak = jnp.max(scores, axis=2)
    total = jnp.sum(jnp.exp(scores - peak[:, :, None, :]), axis=2)
    peak = jnp.where(usable[..., None], peak, very_low)
    total = jnp.where(usable[..., None], total, 0.0)
    return (peak, total)


def merge_pair(first_pair, second_pair):
    first_peak, first_total = first_pair
    second_peak, second_total = second_pair
    highest = jnp.maximum(first_peak, second_peak)
    summed = first_total * jnp.exp(first_peak - highest) + second_total * jnp.exp(
        second_peak - highest
    )
    return (highest, summed)


def segment_merge(peaks, totals, seg_ids, segments):
    best = jax.ops.segment_max(peaks, seg_ids, num_segments=segments + 1)
    best = jnp.maximum(best, very_low)
    summed = jax.ops.segment_sum(
        totals * jnp.exp(peaks - best[seg_ids]), seg_ids, num_segments=segments + 1
    )
    return (best[:segments], summed[:segments])


def general_device(
    source_feat, target_feat, log_mass_src, log_mass_tgt, potential_tgt, support, counts
):
    target_all, mass_all, poten_all = (
        lax.all_gather(target_feat, "src", axis=0, tiled=True),
        lax.all_gather(log_mass_tgt, "src", axis=0, tiled=True),
        lax.all_gather(potential_tgt, "src", axis=0, tiled=True),
    )
    blocks = target_all.shape[0]
    rows_here = source_feat.shape[0]
    slots_here = support.shape[2]
    cells = source_feat.shape[2]
    indices = support[:, 0, :]
    limits = counts[:, 0]
    usable = jnp.arange(slots_here, dtype=jnp.int32)[None, :] < limits[:, None]
    source_sq = jnp.sum(source_feat * source_feat, axis=1)
    target_sq = jnp.sum(target_all * target_all, axis=1)
    width = math.gcd(rows_here, 4)

    def grouped(array):
        return array.reshape((rows_here // width, width) + array.shape[1:])

    def row_pass(items):
        source_blk, source_nrm, ids_here, use_here = items
        cost = cost_tiles(
            source_blk[:, None], source_nrm[:, None], target_all[ids_here], target_sq[ids_here]
        )
        return row_stats(cost, mass_all[ids_here], poten_all[ids_here], use_here)

    peak, total = lax.map(
        row_pass, (grouped(source_feat), grouped(source_sq), grouped(indices), grouped(usable))
    )
    peak = peak.reshape(rows_here, cells)
    total = total.reshape(rows_here, cells)
    peak_all, total_all = merged((peak, total), "tgt", merge_pair)
    potential_src = -entropic * (peak_all + jnp.log(total_all))

    def column_pass(items):
        source_blk, source_nrm, mass_here, poten_here, ids_here, use_here = items
        cost = cost_tiles(
            source_blk[:, None], source_nrm[:, None], target_all[ids_here], target_sq[ids_here]
        )
        return column_stats(cost, mass_here, poten_here, use_here)

    peaks, totals = lax.map(
        column_pass,
        (
            grouped(source_feat),
            grouped(source_sq),
            grouped(log_mass_src),
            grouped(potential_src),
            grouped(indices),
            grouped(usable),
        ),
    )
    seg_ids = jnp.where(usable, indices, blocks).reshape(-1)
    best, summed = segment_merge(
        peaks.reshape(-1, cells), totals.reshape(-1, cells), seg_ids, blocks
    )
    share = blocks // lax.axis_size("src")
    own_start = lax.axis_index("src") * share
    highest = lax.pmax(best, "src")
    whole = lax.psum(summed * jnp.exp(best - highest), "src")
    own_peak = lax.dynamic_slice_in_dim(highest, own_start, share, 0)
    own_total = lax.dynamic_slice_in_dim(whole, own_start, share, 0)
    potential_new = -entropic * (own_peak + jnp.log(own_total))
    return (potential_src, potential_new)


def per_device(source_feat, target_feat, *others):
    shards = lax.axis_size("src")
    rows, depth, cells = source_feat.shape
    few = shards == 8 and target_feat.shape[0] == 1 and lax.axis_size("tgt") == 2
    if few and rows % 8 == 0 and cells == 128 and depth == 64:
        return dense_device(source_feat, target_feat, *others)
    return general_device(source_feat, target_feat, *others)


def solution(mesh):
    in_specs = (
        P(("grp", "src"), None, None),
        P(("grp", "src", "tgt"), None, None),
        P(("grp", "src"), None),
        P(("grp", "src", "tgt"), None),
        P(("grp", "src", "tgt"), None),
        P(("grp", "src"), "tgt", None),
        P(("grp", "src"), "tgt"),
    )
    out_specs = (P(("grp", "src"), None), P(("grp", "src", "tgt"), None))
    return jax.shard_map(
        per_device, mesh=mesh, in_specs=in_specs, out_specs=out_specs, check_vma=False
    )
```

```python
import functools
import math

import jax
import jax.numpy as jnp
from jax import lax
from jax.experimental import pallas as pl
from jax.experimental.pallas import tpu as pltpu
from jax.sharding import PartitionSpec as P

entropic = 0.5
very_low = -1e30
log2e = 1.0 / math.log(2.0)
ln2 = math.log(2.0)
least_sum = 1e-28

VM = pl.BlockSpec(memory_space=pltpu.VMEM)
PARAMS = pltpu.CompilerParams(vmem_limit_bytes=40 * 2**20)


def in_vmem(shape, dtype):
    return pltpu.VMEM(shape, dtype)


def pieces(values):
    high = values.astype(jnp.bfloat16).astype(jnp.float32)
    rest = values - high
    mid = rest.astype(jnp.bfloat16).astype(jnp.float32)
    low = (rest - mid).astype(jnp.bfloat16).astype(jnp.float32)
    return high, mid, low


def target_weight(mass, poten):
    return (mass + poten / entropic) * log2e


def line_steps(shards):
    return [2 * (i ^ (i >> 1)) for i in range(shards // 2 - 1, 0, -1)]


def blocks_at(shards):
    near = [0] + line_steps(shards)
    me = lax.axis_index("src")
    return [me ^ other for other in near + [step ^ 1 for step in near]]


def read_all(hbm, held, sems):
    copies = [pltpu.make_async_copy(src, dst, sems.at[i]) for i, (src, dst) in enumerate(zip(hbm, held))]
    for copy in copies:
        copy.start()
    return copies


def pack_kernel(*refs):
    hbm, (send_ref, weight_ref), held, sems = refs[:3], refs[3:5], refs[5:8], refs[8]
    for copy in read_all(hbm, held, sems):
        copy.wait()
    feat_ref, mass_ref, poten_ref = held
    feat = feat_ref[0]
    depth, cells = feat.shape
    weight = target_weight(mass_ref[...], poten_ref[...])
    norm = jnp.sum(feat * feat, axis=0, keepdims=True)
    bias = weight - (log2e / entropic) * norm
    scaled = feat * (2.0 * log2e / entropic)
    below = jnp.broadcast_to(bias, (send_ref.shape[1] - depth, cells))
    send_ref[0, :depth, :] = scaled
    send_ref[0, depth:, :] = below
    weight_ref[...] = weight


def source_kernel(shards, *refs):
    hbm, outs, held, sems = refs[:4], refs[4:8], refs[8:12], refs[12]
    wide_ref, norm_ref, mask_ref, mass_out_ref = outs
    mass_ref, support_ref, counts_ref, feat_ref = held
    copies = read_all(hbm, held, sems)
    for copy in copies[:3]:
        copy.wait()
    mass_out_ref[...] = mass_ref[...]
    support = support_ref[...]
    slots, rows = support.shape
    cells = mass_ref.shape[1]
    used = lax.broadcasted_iota(jnp.int32, support.shape, 0) < counts_ref[...]
    hits = [
        jnp.max(jnp.where(used & (support == block), 0.0, very_low), axis=0, keepdims=True)
        for block in blocks_at(shards)
    ]
    hits = jnp.concatenate(hits + [jnp.zeros((cells - shards, rows), jnp.float32)], axis=0)
    hits = jnp.concatenate([hits, jnp.zeros((cells, cells - rows), jnp.float32)], axis=1).T
    for place in range(shards):
        mask_ref[place] = jnp.broadcast_to(hits[:rows, place : place + 1], (rows, cells))
    copies[3].wait()
    depth = feat_ref.shape[1]
    one = jnp.ones((2 * depth, 2 * cells), jnp.bfloat16)
    for pair in range(rows // 2):
        for half in range(2):
            feat = feat_ref[2 * pair + half]
            norm_ref[2 * pair + half : 2 * pair + half + 1, :] = jnp.sum(feat * feat, axis=0, keepdims=True)
            high, mid, low = pieces(feat)
            lanes = slice(half * cells, (half + 1) * cells)
            top = jnp.concatenate([high, mid], axis=0).astype(jnp.bfloat16)
            wide_ref[pair, 0 : 2 * depth, lanes] = top
            wide_ref[pair, 2 * depth : 4 * depth, lanes] = top
            wide_ref[pair, 4 * depth : 6 * depth, lanes] = jnp.concatenate([low, high], axis=0).astype(jnp.bfloat16)
        wide_ref[pair, 6 * depth : 8 * depth, :] = one


def join_kernel(*refs):
    refs[-1][0] = refs[0][0]
    refs[-1][1] = refs[1][0]


def on_core(core, work, idle):
    if core is None:
        work()
    else:
        here = lax.axis_index("tgt") == core
        pl.when(here)(work)
        pl.when(jnp.logical_not(here))(idle)


def tile_kernel(parts, core, *refs):
    peak_ref, total_ref = refs[-2:]

    def idle():
        peak_ref[...] = jnp.zeros(peak_ref.shape, jnp.float32)
        total_ref[...] = jnp.zeros(total_ref.shape, jnp.float32)

    ins = refs[: parts + 1] + refs[-4:]
    on_core(core, functools.partial(make_tiles, parts, *ins), idle)


def make_tiles(parts, *refs):
    packs = [ref.at[index] for ref in refs[:parts] for index in range(ref.shape[0])]
    wide_ref, exps_ref, tall_ref, peak_ref, total_ref = refs[parts:]
    blocks = len(packs)
    pairs, _, both = wide_ref.shape
    cells = both // 2
    depth = cells // 2
    lane = lax.broadcasted_iota(jnp.int32, (cells, cells), 1)
    biases = jnp.concatenate([pack[depth : depth + 1, :] for pack in packs], axis=0)
    bias_pieces = jnp.concatenate(list(pieces(biases)), axis=0)
    padded = jnp.concatenate([bias_pieces, jnp.zeros((cells - 3 * blocks, cells), jnp.float32)], axis=0)
    bias_lanes = padded.T
    for place, pack in enumerate(packs):
        feat = pack[:depth, :]
        turned = jnp.concatenate([feat, feat], axis=0).T
        high, mid, low = pieces(turned)
        own = jnp.where(lax.rem(lane, blocks) == place, bias_lanes, 0.0)
        rows = slice(place * cells, (place + 1) * cells)
        tall_ref[rows, 0:cells] = high.astype(jnp.bfloat16)
        tall_ref[rows, cells : 2 * cells] = mid.astype(jnp.bfloat16)
        tall_ref[rows, 2 * cells : 3 * cells] = jnp.where(lane < depth, high, low).astype(jnp.bfloat16)
        tall_ref[rows, 3 * cells : 4 * cells] = own.astype(jnp.bfloat16)

    def body(pair, carry):
        scores = jnp.dot(tall_ref[...], wide_ref[pair], preferred_element_type=jnp.float32)
        for place in range(blocks):
            rows = slice(place * cells, (place + 1) * cells)
            score = scores[rows]
            peak = jnp.max(score, axis=0, keepdims=True)
            exps = jnp.exp2(score - peak)
            exps_ref[pair, rows, :] = exps
            total = jnp.sum(exps, axis=0, keepdims=True)
            for half in range(2):
                lanes = slice(half * cells, (half + 1) * cells)
                peak_ref[place, pl.ds(2 * pair + half, 1), :] = peak[:, lanes]
                total_ref[place, pl.ds(2 * pair + half, 1), :] = total[:, lanes]
        return carry

    lax.fori_loop(0, pairs, body, 0, unroll=min(pairs, 16 // blocks & -4 or 2))


def row_kernel(groups, *refs):
    mask_ref, peak_refs, total_refs = refs[0], refs[1 : 1 + groups], refs[1 + groups : 1 + 2 * groups]
    peaks_ref, rowsum_ref = refs[1 + 2 * groups :]
    place = 0
    for ref in peak_refs:
        for index in range(ref.shape[0]):
            peaks_ref[place] = ref[index] + mask_ref[place]
            place += 1
    totals = [ref[index] for ref in total_refs for index in range(ref.shape[0])]
    top = functools.reduce(jnp.maximum, [peaks_ref[index] for index in range(place)])
    summed = sum(total * jnp.exp2(peaks_ref[index] - top) for index, total in enumerate(totals))
    rowsum_ref[...] = top + jnp.log2(summed)


def across(column):
    shape = (column.shape[0],) * 2
    same = lax.broadcasted_iota(jnp.int32, shape, 0) == lax.broadcasted_iota(jnp.int32, shape, 1)
    return jnp.sum(jnp.where(same, jnp.broadcast_to(column, shape), 0.0), axis=0, keepdims=True)


def column_kernel(groups, core, *refs):
    ins, outs, scratch = refs[: 2 * groups + 7], refs[-4:-2], refs[-2:]

    def idle():
        for given, out in zip(refs[2 * groups + 7 : -4], outs):
            out[...] = given[...]

    on_core(core, functools.partial(sum_columns, groups, *ins, *outs, *scratch), idle)


def sum_columns(groups, *refs):
    exps_refs, tall_refs, rest = refs[:groups], refs[groups : 2 * groups], refs[2 * groups :]
    wide_ref, peak_ref, mask_ref, own_ref, other_ref, mass_ref, norm_ref = rest[:7]
    poten_ref, sums_ref, weight_ref, shift_ref = rest[7:]
    pairs, _, both = wide_ref.shape
    cells = both // 2
    shards = mask_ref.shape[0]
    own, other = own_ref[...], other_ref[...]
    top = jnp.maximum(own, other)
    whole = top + jnp.log2(jnp.exp2(own - top) + jnp.exp2(other - top))
    poten_ref[...] = norm_ref[...] - (entropic * ln2) * whole
    shift = mass_ref[...] * log2e - whole
    shift_ref[...] = shift
    for place in range(shards):
        weight_ref[place] = jnp.exp2(peak_ref[place] + shift)
    spots = [
        (group, slice(index * cells, (index + 1) * cells))
        for group, ref in enumerate(tall_refs)
        for index in range(ref.shape[0] // cells)
    ]
    used = [jnp.max(mask_ref[place], axis=0, keepdims=True) > 0.5 * very_low for place in range(shards)]
    worst = jnp.full((1, cells), 1.0, jnp.float32)
    owners = blocks_at(shards)
    for place, (group, rows) in enumerate(spots):
        acc = jnp.zeros((cells, cells), jnp.float32)
        for pair in range(pairs):
            acc = acc + exps_refs[group][pair, rows, :cells] * weight_ref[place, 2 * pair : 2 * pair + 1, :]
            acc = acc + exps_refs[group][pair, rows, cells:] * weight_ref[place, 2 * pair + 1 : 2 * pair + 2, :]
        here = across(jnp.sum(acc, axis=1, keepdims=True))
        sums_ref[owners[place]] = jnp.where(used[place], jnp.log2(here), very_low)
        worst = jnp.minimum(worst, jnp.where(used[place], here, 1.0))

    @pl.when(jnp.min(worst) < least_sum)
    def _():
        for place, (group, rows) in enumerate(spots):

            def exponents(pair):
                score = jnp.dot(tall_refs[group][rows, :], wide_ref[pair], preferred_element_type=jnp.float32)
                add = shift_ref[pl.ds(2 * pair, 2), :] + mask_ref[place, pl.ds(2 * pair, 2), :]
                return score[:, :cells] + add[0:1, :], score[:, cells:] + add[1:2, :]

            def highest(pair, peak):
                first, second = exponents(pair)
                return jnp.maximum(peak, jnp.maximum(first, second))

            peak = lax.fori_loop(0, pairs, highest, jnp.full((cells, cells), very_low, jnp.float32))
            peak = jnp.max(peak, axis=1, keepdims=True)

            def add_up(pair, sums):
                first, second = exponents(pair)
                return sums + jnp.exp2(first - peak) + jnp.exp2(second - peak)

            sums = lax.fori_loop(0, pairs, add_up, jnp.zeros((cells, cells), jnp.float32))
            logs = across(peak) + jnp.log2(across(jnp.sum(sums, axis=1, keepdims=True)))
            sums_ref[owners[place]] = jnp.where(used[place], logs, very_low)


def merge_kernel(values_ref, weight_ref, poten_ref, out_ref, poten_out_ref):
    poten_out_ref[...] = poten_ref[...]
    values = values_ref[...]
    top = jnp.max(values, axis=0)
    whole = top + jnp.log2(jnp.sum(jnp.exp2(values - top), axis=0))
    out_ref[...] = -(entropic * ln2) * (whole - weight_ref[...])


def f32(*shape):
    return jax.ShapeDtypeStruct(shape, jnp.float32)


def dense_device(
    source_feat, target_feat, log_mass_src, log_mass_tgt, potential_tgt, support, counts
):
    shards = lax.axis_size("src")
    rows, depth, cells = source_feat.shape
    pairs, wide = rows // 2, 2 * cells

    def call(kernel, ins, out_shape, scratch=(), cost=None):
        many = isinstance(out_shape, list)
        return pl.pallas_call(
            kernel,
            in_specs=ins,
            out_specs=[VM] * len(out_shape) if many else VM,
            out_shape=out_shape,
            scratch_shapes=list(scratch),
            compiler_params=PARAMS,
            cost_estimate=cost,
        )

    def reading(kernel, args, out_shape, cost):
        return call(
            kernel,
            [pl.BlockSpec(memory_space=pltpu.HBM)] * len(args),
            out_shape,
            [pltpu.VMEM(arg.shape, arg.dtype) for arg in args] + [pltpu.SemaphoreType.DMA((len(args),))],
            cost,
        )(*[pltpu.with_memory_space_constraint(arg, pltpu.HBM) for arg in args])

    def cost_of(flops):
        return pl.CostEstimate(flops=flops, bytes_accessed=rows * depth * cells * 4, transcendentals=0)

    pack, weight = reading(
        pack_kernel,
        [target_feat, log_mass_tgt, potential_tgt],
        [in_vmem((1, depth + 8, cells), jnp.float32), in_vmem((1, cells), jnp.float32)],
        None,
    )
    wide_feat, norm, mask, mass = reading(
        functools.partial(source_kernel, shards),
        [log_mass_src, support[:, 0, :].T, counts.T, source_feat],
        [
            in_vmem((pairs, 8 * depth, wide), jnp.bfloat16),
            in_vmem((rows, cells), jnp.float32),
            in_vmem((shards, rows, cells), jnp.float32),
            in_vmem((rows, cells), jnp.float32),
        ],
        cost_of(10**9),
    )

    def tiles(*packs, core=None, after=None):
        blocks = sum(pack.shape[0] for pack in packs)
        more = [] if after is None else [after]
        return call(
            functools.partial(tile_kernel, len(packs), core),
            [VM] * (len(packs) + 1) + [pl.BlockSpec(memory_space=pl.ANY)] * len(more),
            [
                in_vmem((pairs, blocks * cells, wide), jnp.float32),
                in_vmem((blocks * cells, 8 * depth), jnp.bfloat16),
                in_vmem((blocks, rows, cells), jnp.float32),
                in_vmem((blocks, rows, cells), jnp.float32),
            ],
            cost=cost_of(2 * blocks * cells * pairs * wide * 8 * depth),
        )(*packs, wide_feat, *more)

    def swapped(array, step):
        return lax.ppermute(array, "src", [(i, i ^ step) for i in range(shards)])

    there = {step: swapped(pack, step) for step in reversed(line_steps(shards))}
    near = [pack] + [there[step] for step in line_steps(shards)]
    found = [tiles(pack)]
    halves = [
        call(
            join_kernel,
            [VM] * 2 + [pl.BlockSpec(memory_space=pl.ANY)],
            in_vmem((2,) + pack.shape[1:], jnp.float32),
        )(near[at], near[at + 1], found[0][-1])
        for at in range(0, len(near), 2)
    ]
    far = [swapped(half, 1) for half in halves]
    found += [tiles(*near[1:]), tiles(far[0])]
    groups = len(found) + 1

    def log_sums(last):
        _, _, peaks, totals = zip(*found, last)
        return call(
            functools.partial(row_kernel, groups),
            [VM] * (1 + 2 * groups),
            [in_vmem((shards, rows, cells), jnp.float32), in_vmem((rows, cells), jnp.float32)],
        )(mask, *peaks, *totals)

    def columns_of(core, last, peaks, own, other, given):
        exps, tall, _, _ = zip(*found, last)
        return call(
            functools.partial(column_kernel, groups, core),
            [VM] * (2 * groups + 7 + len(given)),
            [in_vmem((rows, cells), jnp.float32), in_vmem((shards, 1, cells), jnp.float32)],
            [pltpu.VMEM((shards, rows, cells), jnp.float32), pltpu.VMEM((rows, cells), jnp.float32)],
            cost_of(10**9),
        )(*exps, *tall, wide_feat, peaks, mask, own, other, mass, norm, *given)

    between = [(0, 1), (1, 0)]
    last_one = tiles(far[1], core=1)
    peaks_one, own_one = log_sums(last_one)
    other_zero = lax.ppermute(own_one, "tgt", between)
    last_zero = tiles(far[1], core=0, after=own_one)
    peaks_zero, own_zero = log_sums(last_zero)
    other_one = lax.ppermute(own_zero, "tgt", between)
    given = columns_of(0, last_zero, peaks_zero, own_zero, other_zero, [])
    potential_src, columns = columns_of(1, last_one, peaks_one, own_one, other_one, given)
    arrived = lax.all_to_all(columns, "src", 0, 0)
    outs = [f32(1, cells), f32(rows, cells)]
    potential_new, potential_src = call(merge_kernel, [VM] * 3, outs)(arrived, weight, potential_src)
    return potential_src, potential_new


def merged(part, axis, combine):
    gathered = jax.tree.map(lambda a: lax.all_gather(a, axis), part)

    def take(source):
        return jax.tree.map(lambda a: lax.dynamic_index_in_dim(a, source, 0, False), gathered)

    return lax.fori_loop(
        1, lax.axis_size(axis), lambda source, state: combine(state, take(source)), take(0)
    )


def cost_tiles(source_blk, source_sq, target_blk, target_sq):
    cross = jnp.einsum(
        "...fi,...fj->...ij", source_blk, target_blk, precision=lax.Precision.HIGHEST
    )
    return source_sq[..., :, None] + target_sq[..., None, :] - 2.0 * cross


def row_stats(cost, mass_tgt, poten_tgt, usable):
    scores = mass_tgt[..., None, :] + (poten_tgt[..., None, :] - cost) / entropic
    scores = jnp.where(usable[..., None, None], scores, very_low)
    peak = jnp.max(scores, axis=(1, 3))
    total = jnp.sum(jnp.exp(scores - peak[:, None, :, None]), axis=(1, 3))
    return (peak, total)


def column_stats(cost, mass_src, poten_src, usable):
    scores = mass_src[:, None, :, None] + (poten_src[:, None, :, None] - cost) / entropic
    peak = jnp.max(scores, axis=2)
    total = jnp.sum(jnp.exp(scores - peak[:, :, None, :]), axis=2)
    peak = jnp.where(usable[..., None], peak, very_low)
    total = jnp.where(usable[..., None], total, 0.0)
    return (peak, total)


def merge_pair(first_pair, second_pair):
    first_peak, first_total = first_pair
    second_peak, second_total = second_pair
    highest = jnp.maximum(first_peak, second_peak)
    summed = first_total * jnp.exp(first_peak - highest) + second_total * jnp.exp(
        second_peak - highest
    )
    return (highest, summed)


def segment_merge(peaks, totals, seg_ids, segments):
    best = jax.ops.segment_max(peaks, seg_ids, num_segments=segments + 1)
    best = jnp.maximum(best, very_low)
    summed = jax.ops.segment_sum(
        totals * jnp.exp(peaks - best[seg_ids]), seg_ids, num_segments=segments + 1
    )
    return (best[:segments], summed[:segments])


def general_device(
    source_feat, target_feat, log_mass_src, log_mass_tgt, potential_tgt, support, counts
):
    target_all, mass_all, poten_all = (
        lax.all_gather(target_feat, "src", axis=0, tiled=True),
        lax.all_gather(log_mass_tgt, "src", axis=0, tiled=True),
        lax.all_gather(potential_tgt, "src", axis=0, tiled=True),
    )
    blocks = target_all.shape[0]
    rows_here = source_feat.shape[0]
    slots_here = support.shape[2]
    cells = source_feat.shape[2]
    indices = support[:, 0, :]
    limits = counts[:, 0]
    usable = jnp.arange(slots_here, dtype=jnp.int32)[None, :] < limits[:, None]
    source_sq = jnp.sum(source_feat * source_feat, axis=1)
    target_sq = jnp.sum(target_all * target_all, axis=1)
    width = math.gcd(rows_here, 4)

    def grouped(array):
        return array.reshape((rows_here // width, width) + array.shape[1:])

    def row_pass(items):
        source_blk, source_nrm, ids_here, use_here = items
        cost = cost_tiles(
            source_blk[:, None], source_nrm[:, None], target_all[ids_here], target_sq[ids_here]
        )
        return row_stats(cost, mass_all[ids_here], poten_all[ids_here], use_here)

    peak, total = lax.map(
        row_pass, (grouped(source_feat), grouped(source_sq), grouped(indices), grouped(usable))
    )
    peak = peak.reshape(rows_here, cells)
    total = total.reshape(rows_here, cells)
    peak_all, total_all = merged((peak, total), "tgt", merge_pair)
    potential_src = -entropic * (peak_all + jnp.log(total_all))

    def column_pass(items):
        source_blk, source_nrm, mass_here, poten_here, ids_here, use_here = items
        cost = cost_tiles(
            source_blk[:, None], source_nrm[:, None], target_all[ids_here], target_sq[ids_here]
        )
        return column_stats(cost, mass_here, poten_here, use_here)

    peaks, totals = lax.map(
        column_pass,
        (
            grouped(source_feat),
            grouped(source_sq),
            grouped(log_mass_src),
            grouped(potential_src),
            grouped(indices),
            grouped(usable),
        ),
    )
    seg_ids = jnp.where(usable, indices, blocks).reshape(-1)
    best, summed = segment_merge(
        peaks.reshape(-1, cells), totals.reshape(-1, cells), seg_ids, blocks
    )
    share = blocks // lax.axis_size("src")
    own_start = lax.axis_index("src") * share
    highest = lax.pmax(best, "src")
    whole = lax.psum(summed * jnp.exp(best - highest), "src")
    own_peak = lax.dynamic_slice_in_dim(highest, own_start, share, 0)
    own_total = lax.dynamic_slice_in_dim(whole, own_start, share, 0)
    potential_new = -entropic * (own_peak + jnp.log(own_total))
    return (potential_src, potential_new)


def per_device(source_feat, target_feat, *others):
    shards = lax.axis_size("src")
    rows, depth, cells = source_feat.shape
    few = shards == 8 and target_feat.shape[0] == 1 and lax.axis_size("tgt") == 2
    if few and rows % 8 == 0 and cells == 128 and depth == 64:
        return dense_device(source_feat, target_feat, *others)
    return general_device(source_feat, target_feat, *others)


def solution(mesh):
    in_specs = (
        P(("grp", "src"), None, None),
        P(("grp", "src", "tgt"), None, None),
        P(("grp", "src"), None),
        P(("grp", "src", "tgt"), None),
        P(("grp", "src", "tgt"), None),
        P(("grp", "src"), "tgt", None),
        P(("grp", "src"), "tgt"),
    )
    out_specs = (P(("grp", "src"), None), P(("grp", "src", "tgt"), None))
    return jax.shard_map(
        per_device, mesh=mesh, in_specs=in_specs, out_specs=out_specs, check_vma=False
    )
```

```python
import functools
import math

import jax
import jax.numpy as jnp
from jax import lax
from jax.experimental import pallas as pl
from jax.experimental.pallas import tpu as pltpu
from jax.sharding import PartitionSpec as P

entropic = 0.5
very_low = -1e30
log2e = 1.0 / math.log(2.0)
ln2 = math.log(2.0)
least_sum = 1e-28

VM = pl.BlockSpec(memory_space=pltpu.VMEM)
PARAMS = pltpu.CompilerParams(vmem_limit_bytes=40 * 2**20)


def in_vmem(shape, dtype):
    return pltpu.VMEM(shape, dtype)


def pieces(values):
    high = values.astype(jnp.bfloat16).astype(jnp.float32)
    rest = values - high
    mid = rest.astype(jnp.bfloat16).astype(jnp.float32)
    low = (rest - mid).astype(jnp.bfloat16).astype(jnp.float32)
    return high, mid, low


def target_weight(mass, poten):
    return (mass + poten / entropic) * log2e


def line_steps(shards):
    return [2 * (i ^ (i >> 1)) for i in range(shards // 2 - 1, 0, -1)]


def blocks_at(shards):
    near = [0] + line_steps(shards)
    me = lax.axis_index("src")
    return [me ^ other for other in near + [step ^ 1 for step in near]]


def read_all(hbm, held, sems):
    copies = [pltpu.make_async_copy(src, dst, sems.at[i]) for i, (src, dst) in enumerate(zip(hbm, held))]
    for copy in copies:
        copy.start()
    return copies


def pack_kernel(*refs):
    hbm, (send_ref, weight_ref), held, sems = refs[:3], refs[3:5], refs[5:8], refs[8]
    for copy in read_all(hbm, held, sems):
        copy.wait()
    feat_ref, mass_ref, poten_ref = held
    feat = feat_ref[0]
    depth, cells = feat.shape
    weight = target_weight(mass_ref[...], poten_ref[...])
    norm = jnp.sum(feat * feat, axis=0, keepdims=True)
    bias = weight - (log2e / entropic) * norm
    scaled = feat * (2.0 * log2e / entropic)
    send_ref[0, :depth, 0, :] = scaled
    send_ref[0, depth, 0:1, :] = bias
    weight_ref[...] = weight


def source_kernel(shards, *refs):
    hbm, outs, held, sems = refs[:4], refs[4:8], refs[8:12], refs[12]
    wide_ref, norm_ref, mask_ref, mass_out_ref = outs
    mass_ref, support_ref, counts_ref, feat_ref = held
    copies = read_all(hbm, held, sems)
    for copy in copies[:3]:
        copy.wait()
    mass_out_ref[...] = mass_ref[...]
    support = support_ref[...]
    slots, rows = support.shape
    cells = mass_ref.shape[1]
    used = lax.broadcasted_iota(jnp.int32, support.shape, 0) < counts_ref[...]
    hits = [
        jnp.max(jnp.where(used & (support == block), 0.0, very_low), axis=0, keepdims=True)
        for block in blocks_at(shards)
    ]
    hits = jnp.concatenate(hits + [jnp.zeros((cells - shards, rows), jnp.float32)], axis=0)
    hits = jnp.concatenate([hits, jnp.zeros((cells, cells - rows), jnp.float32)], axis=1).T
    for place in range(shards):
        mask_ref[place] = jnp.broadcast_to(hits[:rows, place : place + 1], (rows, cells))
    copies[3].wait()
    depth = feat_ref.shape[1]
    one = jnp.ones((2 * depth, 2 * cells), jnp.bfloat16)
    for pair in range(rows // 2):
        for half in range(2):
            feat = feat_ref[2 * pair + half]
            norm_ref[2 * pair + half : 2 * pair + half + 1, :] = jnp.sum(feat * feat, axis=0, keepdims=True)
            high, mid, low = pieces(feat)
            lanes = slice(half * cells, (half + 1) * cells)
            top = jnp.concatenate([high, mid], axis=0).astype(jnp.bfloat16)
            wide_ref[pair, 0 : 2 * depth, lanes] = top
            wide_ref[pair, 2 * depth : 4 * depth, lanes] = top
            wide_ref[pair, 4 * depth : 6 * depth, lanes] = jnp.concatenate([low, high], axis=0).astype(jnp.bfloat16)
        wide_ref[pair, 6 * depth : 8 * depth, :] = one


def join_kernel(*refs):
    refs[-1][0] = refs[0][0]
    refs[-1][1] = refs[1][0]


def on_core(core, work, idle):
    if core is None:
        work()
    else:
        here = lax.axis_index("tgt") == core
        pl.when(here)(work)
        pl.when(jnp.logical_not(here))(idle)


def tile_kernel(parts, core, *refs):
    peak_ref, total_ref = refs[-2:]

    def idle():
        peak_ref[...] = jnp.zeros(peak_ref.shape, jnp.float32)
        total_ref[...] = jnp.zeros(total_ref.shape, jnp.float32)

    ins = refs[: parts + 1] + refs[-4:]
    on_core(core, functools.partial(make_tiles, parts, *ins), idle)


def make_tiles(parts, *refs):
    packs = [ref.at[index] for ref in refs[:parts] for index in range(ref.shape[0])]
    wide_ref, exps_ref, tall_ref, peak_ref, total_ref = refs[parts:]
    blocks = len(packs)
    pairs, _, both = wide_ref.shape
    cells = both // 2
    depth = cells // 2
    lane = lax.broadcasted_iota(jnp.int32, (cells, cells), 1)
    biases = jnp.concatenate([pack[depth, 0:1, :] for pack in packs], axis=0)
    bias_pieces = jnp.concatenate(list(pieces(biases)), axis=0)
    padded = jnp.concatenate([bias_pieces, jnp.zeros((cells - 3 * blocks, cells), jnp.float32)], axis=0)
    bias_lanes = padded.T
    for place, pack in enumerate(packs):
        feat = pack[:depth, 0, :]
        turned = jnp.concatenate([feat, feat], axis=0).T
        high, mid, low = pieces(turned)
        own = jnp.where(lax.rem(lane, blocks) == place, bias_lanes, 0.0)
        rows = slice(place * cells, (place + 1) * cells)
        tall_ref[rows, 0:cells] = high.astype(jnp.bfloat16)
        tall_ref[rows, cells : 2 * cells] = mid.astype(jnp.bfloat16)
        tall_ref[rows, 2 * cells : 3 * cells] = jnp.where(lane < depth, high, low).astype(jnp.bfloat16)
        tall_ref[rows, 3 * cells : 4 * cells] = own.astype(jnp.bfloat16)

    def body(pair, carry):
        scores = jnp.dot(tall_ref[...], wide_ref[pair], preferred_element_type=jnp.float32)
        for place in range(blocks):
            rows = slice(place * cells, (place + 1) * cells)
            score = scores[rows]
            peak = jnp.max(score, axis=0, keepdims=True)
            exps = jnp.exp2(score - peak)
            exps_ref[pair, rows, :] = exps
            total = jnp.sum(exps, axis=0, keepdims=True)
            for half in range(2):
                lanes = slice(half * cells, (half + 1) * cells)
                peak_ref[place, pl.ds(2 * pair + half, 1), :] = peak[:, lanes]
                total_ref[place, pl.ds(2 * pair + half, 1), :] = total[:, lanes]
        return carry

    lax.fori_loop(0, pairs, body, 0, unroll=min(pairs, 16 // blocks & -4 or 2))


def row_kernel(groups, *refs):
    mask_ref, peak_refs, total_refs = refs[0], refs[1 : 1 + groups], refs[1 + groups : 1 + 2 * groups]
    peaks_ref, rowsum_ref = refs[1 + 2 * groups :]
    place = 0
    for ref in peak_refs:
        for index in range(ref.shape[0]):
            peaks_ref[place] = ref[index] + mask_ref[place]
            place += 1
    totals = [ref[index] for ref in total_refs for index in range(ref.shape[0])]
    top = functools.reduce(jnp.maximum, [peaks_ref[index] for index in range(place)])
    summed = sum(total * jnp.exp2(peaks_ref[index] - top) for index, total in enumerate(totals))
    rowsum_ref[...] = top + jnp.log2(summed)


def across(column):
    shape = (column.shape[0],) * 2
    same = lax.broadcasted_iota(jnp.int32, shape, 0) == lax.broadcasted_iota(jnp.int32, shape, 1)
    return jnp.sum(jnp.where(same, jnp.broadcast_to(column, shape), 0.0), axis=0, keepdims=True)


def column_kernel(groups, core, *refs):
    ins, outs, scratch = refs[: 2 * groups + 7], refs[-4:-2], refs[-2:]

    def idle():
        for given, out in zip(refs[2 * groups + 7 : -4], outs):
            out[...] = given[...]

    on_core(core, functools.partial(sum_columns, groups, *ins, *outs, *scratch), idle)


def sum_columns(groups, *refs):
    exps_refs, tall_refs, rest = refs[:groups], refs[groups : 2 * groups], refs[2 * groups :]
    wide_ref, peak_ref, mask_ref, own_ref, other_ref, mass_ref, norm_ref = rest[:7]
    poten_ref, sums_ref, weight_ref, shift_ref = rest[7:]
    pairs, _, both = wide_ref.shape
    cells = both // 2
    shards = mask_ref.shape[0]
    own, other = own_ref[...], other_ref[...]
    top = jnp.maximum(own, other)
    whole = top + jnp.log2(jnp.exp2(own - top) + jnp.exp2(other - top))
    poten_ref[...] = norm_ref[...] - (entropic * ln2) * whole
    shift = mass_ref[...] * log2e - whole
    shift_ref[...] = shift
    for place in range(shards):
        weight_ref[place] = jnp.exp2(peak_ref[place] + shift)
    spots = [
        (group, slice(index * cells, (index + 1) * cells))
        for group, ref in enumerate(tall_refs)
        for index in range(ref.shape[0] // cells)
    ]
    used = [jnp.max(mask_ref[place], axis=0, keepdims=True) > 0.5 * very_low for place in range(shards)]
    worst = jnp.full((1, cells), 1.0, jnp.float32)
    owners = blocks_at(shards)
    for place, (group, rows) in enumerate(spots):
        acc = jnp.zeros((cells, cells), jnp.float32)
        for pair in range(pairs):
            acc = acc + exps_refs[group][pair, rows, :cells] * weight_ref[place, 2 * pair : 2 * pair + 1, :]
            acc = acc + exps_refs[group][pair, rows, cells:] * weight_ref[place, 2 * pair + 1 : 2 * pair + 2, :]
        here = across(jnp.sum(acc, axis=1, keepdims=True))
        sums_ref[owners[place]] = jnp.where(used[place], jnp.log2(here), very_low)
        worst = jnp.minimum(worst, jnp.where(used[place], here, 1.0))

    @pl.when(jnp.min(worst) < least_sum)
    def _():
        for place, (group, rows) in enumerate(spots):

            def exponents(pair):
                score = jnp.dot(tall_refs[group][rows, :], wide_ref[pair], preferred_element_type=jnp.float32)
                add = shift_ref[pl.ds(2 * pair, 2), :] + mask_ref[place, pl.ds(2 * pair, 2), :]
                return score[:, :cells] + add[0:1, :], score[:, cells:] + add[1:2, :]

            def highest(pair, peak):
                first, second = exponents(pair)
                return jnp.maximum(peak, jnp.maximum(first, second))

            peak = lax.fori_loop(0, pairs, highest, jnp.full((cells, cells), very_low, jnp.float32))
            peak = jnp.max(peak, axis=1, keepdims=True)

            def add_up(pair, sums):
                first, second = exponents(pair)
                return sums + jnp.exp2(first - peak) + jnp.exp2(second - peak)

            sums = lax.fori_loop(0, pairs, add_up, jnp.zeros((cells, cells), jnp.float32))
            logs = across(peak) + jnp.log2(across(jnp.sum(sums, axis=1, keepdims=True)))
            sums_ref[owners[place]] = jnp.where(used[place], logs, very_low)


def merge_kernel(values_ref, weight_ref, poten_ref, out_ref, poten_out_ref):
    poten_out_ref[...] = poten_ref[...]
    values = values_ref[...]
    top = jnp.max(values, axis=0)
    whole = top + jnp.log2(jnp.sum(jnp.exp2(values - top), axis=0))
    out_ref[...] = -(entropic * ln2) * (whole - weight_ref[...])


def f32(*shape):
    return jax.ShapeDtypeStruct(shape, jnp.float32)


def dense_device(
    source_feat, target_feat, log_mass_src, log_mass_tgt, potential_tgt, support, counts
):
    shards = lax.axis_size("src")
    rows, depth, cells = source_feat.shape
    pairs, wide = rows // 2, 2 * cells

    def call(kernel, ins, out_shape, scratch=(), cost=None):
        many = isinstance(out_shape, list)
        return pl.pallas_call(
            kernel,
            in_specs=ins,
            out_specs=[VM] * len(out_shape) if many else VM,
            out_shape=out_shape,
            scratch_shapes=list(scratch),
            compiler_params=PARAMS,
            cost_estimate=cost,
        )

    def reading(kernel, args, out_shape, cost):
        return call(
            kernel,
            [pl.BlockSpec(memory_space=pltpu.HBM)] * len(args),
            out_shape,
            [pltpu.VMEM(arg.shape, arg.dtype) for arg in args] + [pltpu.SemaphoreType.DMA((len(args),))],
            cost,
        )(*[pltpu.with_memory_space_constraint(arg, pltpu.HBM) for arg in args])

    def cost_of(flops):
        return pl.CostEstimate(flops=flops, bytes_accessed=rows * depth * cells * 4, transcendentals=0)

    pack, weight = reading(
        pack_kernel,
        [target_feat, log_mass_tgt, potential_tgt],
        [in_vmem((1, depth + 1, 1, cells), jnp.float32), in_vmem((1, cells), jnp.float32)],
        None,
    )
    wide_feat, norm, mask, mass = reading(
        functools.partial(source_kernel, shards),
        [log_mass_src, support[:, 0, :].T, counts.T, source_feat],
        [
            in_vmem((pairs, 8 * depth, wide), jnp.bfloat16),
            in_vmem((rows, cells), jnp.float32),
            in_vmem((shards, rows, cells), jnp.float32),
            in_vmem((rows, cells), jnp.float32),
        ],
        cost_of(10**9),
    )

    def tiles(*packs, core=None, after=None):
        blocks = sum(pack.shape[0] for pack in packs)
        more = [] if after is None else [after]
        return call(
            functools.partial(tile_kernel, len(packs), core),
            [VM] * (len(packs) + 1) + [pl.BlockSpec(memory_space=pl.ANY)] * len(more),
            [
                in_vmem((pairs, blocks * cells, wide), jnp.float32),
                in_vmem((blocks * cells, 8 * depth), jnp.bfloat16),
                in_vmem((blocks, rows, cells), jnp.float32),
                in_vmem((blocks, rows, cells), jnp.float32),
            ],
            cost=cost_of(2 * blocks * cells * pairs * wide * 8 * depth),
        )(*packs, wide_feat, *more)

    def swapped(array, step):
        return lax.ppermute(array, "src", [(i, i ^ step) for i in range(shards)])

    there = {step: swapped(pack, step) for step in reversed(line_steps(shards))}
    near = [pack] + [there[step] for step in line_steps(shards)]
    found = [tiles(pack)]
    halves = [
        call(
            join_kernel,
            [VM] * 2 + [pl.BlockSpec(memory_space=pl.ANY)],
            in_vmem((2,) + pack.shape[1:], jnp.float32),
        )(near[at], near[at + 1], found[0][-1])
        for at in range(0, len(near), 2)
    ]
    far = [swapped(half, 1) for half in halves]
    found += [tiles(*near[1:]), tiles(far[0])]
    groups = len(found) + 1

    def log_sums(last):
        _, _, peaks, totals = zip(*found, last)
        return call(
            functools.partial(row_kernel, groups),
            [VM] * (1 + 2 * groups),
            [in_vmem((shards, rows, cells), jnp.float32), in_vmem((rows, cells), jnp.float32)],
        )(mask, *peaks, *totals)

    def columns_of(core, last, peaks, own, other, given):
        exps, tall, _, _ = zip(*found, last)
        return call(
            functools.partial(column_kernel, groups, core),
            [VM] * (2 * groups + 7 + len(given)),
            [in_vmem((rows, cells), jnp.float32), in_vmem((shards, 1, cells), jnp.float32)],
            [pltpu.VMEM((shards, rows, cells), jnp.float32), pltpu.VMEM((rows, cells), jnp.float32)],
            cost_of(10**9),
        )(*exps, *tall, wide_feat, peaks, mask, own, other, mass, norm, *given)

    between = [(0, 1), (1, 0)]
    last_one = tiles(far[1], core=1)
    peaks_one, own_one = log_sums(last_one)
    other_zero = lax.ppermute(own_one, "tgt", between)
    last_zero = tiles(far[1], core=0, after=own_one)
    peaks_zero, own_zero = log_sums(last_zero)
    other_one = lax.ppermute(own_zero, "tgt", between)
    given = columns_of(0, last_zero, peaks_zero, own_zero, other_zero, [])
    potential_src, columns = columns_of(1, last_one, peaks_one, own_one, other_one, given)
    arrived = lax.all_to_all(columns, "src", 0, 0)
    outs = [f32(1, cells), f32(rows, cells)]
    potential_new, potential_src = call(merge_kernel, [VM] * 3, outs)(arrived, weight, potential_src)
    return potential_src, potential_new


def merged(part, axis, combine):
    gathered = jax.tree.map(lambda a: lax.all_gather(a, axis), part)

    def take(source):
        return jax.tree.map(lambda a: lax.dynamic_index_in_dim(a, source, 0, False), gathered)

    return lax.fori_loop(
        1, lax.axis_size(axis), lambda source, state: combine(state, take(source)), take(0)
    )


def cost_tiles(source_blk, source_sq, target_blk, target_sq):
    cross = jnp.einsum(
        "...fi,...fj->...ij", source_blk, target_blk, precision=lax.Precision.HIGHEST
    )
    return source_sq[..., :, None] + target_sq[..., None, :] - 2.0 * cross


def row_stats(cost, mass_tgt, poten_tgt, usable):
    scores = mass_tgt[..., None, :] + (poten_tgt[..., None, :] - cost) / entropic
    scores = jnp.where(usable[..., None, None], scores, very_low)
    peak = jnp.max(scores, axis=(1, 3))
    total = jnp.sum(jnp.exp(scores - peak[:, None, :, None]), axis=(1, 3))
    return (peak, total)


def column_stats(cost, mass_src, poten_src, usable):
    scores = mass_src[:, None, :, None] + (poten_src[:, None, :, None] - cost) / entropic
    peak = jnp.max(scores, axis=2)
    total = jnp.sum(jnp.exp(scores - peak[:, :, None, :]), axis=2)
    peak = jnp.where(usable[..., None], peak, very_low)
    total = jnp.where(usable[..., None], total, 0.0)
    return (peak, total)


def merge_pair(first_pair, second_pair):
    first_peak, first_total = first_pair
    second_peak, second_total = second_pair
    highest = jnp.maximum(first_peak, second_peak)
    summed = first_total * jnp.exp(first_peak - highest) + second_total * jnp.exp(
        second_peak - highest
    )
    return (highest, summed)


def segment_merge(peaks, totals, seg_ids, segments):
    best = jax.ops.segment_max(peaks, seg_ids, num_segments=segments + 1)
    best = jnp.maximum(best, very_low)
    summed = jax.ops.segment_sum(
        totals * jnp.exp(peaks - best[seg_ids]), seg_ids, num_segments=segments + 1
    )
    return (best[:segments], summed[:segments])


def general_device(
    source_feat, target_feat, log_mass_src, log_mass_tgt, potential_tgt, support, counts
):
    target_all, mass_all, poten_all = (
        lax.all_gather(target_feat, "src", axis=0, tiled=True),
        lax.all_gather(log_mass_tgt, "src", axis=0, tiled=True),
        lax.all_gather(potential_tgt, "src", axis=0, tiled=True),
    )
    blocks = target_all.shape[0]
    rows_here = source_feat.shape[0]
    slots_here = support.shape[2]
    cells = source_feat.shape[2]
    indices = support[:, 0, :]
    limits = counts[:, 0]
    usable = jnp.arange(slots_here, dtype=jnp.int32)[None, :] < limits[:, None]
    source_sq = jnp.sum(source_feat * source_feat, axis=1)
    target_sq = jnp.sum(target_all * target_all, axis=1)
    width = math.gcd(rows_here, 4)

    def grouped(array):
        return array.reshape((rows_here // width, width) + array.shape[1:])

    def row_pass(items):
        source_blk, source_nrm, ids_here, use_here = items
        cost = cost_tiles(
            source_blk[:, None], source_nrm[:, None], target_all[ids_here], target_sq[ids_here]
        )
        return row_stats(cost, mass_all[ids_here], poten_all[ids_here], use_here)

    peak, total = lax.map(
        row_pass, (grouped(source_feat), grouped(source_sq), grouped(indices), grouped(usable))
    )
    peak = peak.reshape(rows_here, cells)
    total = total.reshape(rows_here, cells)
    peak_all, total_all = merged((peak, total), "tgt", merge_pair)
    potential_src = -entropic * (peak_all + jnp.log(total_all))

    def column_pass(items):
        source_blk, source_nrm, mass_here, poten_here, ids_here, use_here = items
        cost = cost_tiles(
            source_blk[:, None], source_nrm[:, None], target_all[ids_here], target_sq[ids_here]
        )
        return column_stats(cost, mass_here, poten_here, use_here)

    peaks, totals = lax.map(
        column_pass,
        (
            grouped(source_feat),
            grouped(source_sq),
            grouped(log_mass_src),
            grouped(potential_src),
            grouped(indices),
            grouped(usable),
        ),
    )
    seg_ids = jnp.where(usable, indices, blocks).reshape(-1)
    best, summed = segment_merge(
        peaks.reshape(-1, cells), totals.reshape(-1, cells), seg_ids, blocks
    )
    share = blocks // lax.axis_size("src")
    own_start = lax.axis_index("src") * share
    highest = lax.pmax(best, "src")
    whole = lax.psum(summed * jnp.exp(best - highest), "src")
    own_peak = lax.dynamic_slice_in_dim(highest, own_start, share, 0)
    own_total = lax.dynamic_slice_in_dim(whole, own_start, share, 0)
    potential_new = -entropic * (own_peak + jnp.log(own_total))
    return (potential_src, potential_new)


def per_device(source_feat, target_feat, *others):
    shards = lax.axis_size("src")
    rows, depth, cells = source_feat.shape
    few = shards == 8 and target_feat.shape[0] == 1 and lax.axis_size("tgt") == 2
    if few and rows % 8 == 0 and cells == 128 and depth == 64:
        return dense_device(source_feat, target_feat, *others)
    return general_device(source_feat, target_feat, *others)


def solution(mesh):
    in_specs = (
        P(("grp", "src"), None, None),
        P(("grp", "src", "tgt"), None, None),
        P(("grp", "src"), None),
        P(("grp", "src", "tgt"), None),
        P(("grp", "src", "tgt"), None),
        P(("grp", "src"), "tgt", None),
        P(("grp", "src"), "tgt"),
    )
    out_specs = (P(("grp", "src"), None), P(("grp", "src", "tgt"), None))
    return jax.shard_map(
        per_device, mesh=mesh, in_specs=in_specs, out_specs=out_specs, check_vma=False
    )
```

```python
import functools
import math

import jax
import jax.numpy as jnp
from jax import lax
from jax.experimental import pallas as pl
from jax.experimental.pallas import tpu as pltpu
from jax.sharding import PartitionSpec as P

entropic = 0.5
very_low = -1e30
log2e = 1.0 / math.log(2.0)
ln2 = math.log(2.0)
least_sum = 1e-28

VM = pl.BlockSpec(memory_space=pltpu.VMEM)
PARAMS = pltpu.CompilerParams(vmem_limit_bytes=40 * 2**20)


def in_vmem(shape, dtype):
    return pltpu.VMEM(shape, dtype)


def pieces(values):
    high = values.astype(jnp.bfloat16).astype(jnp.float32)
    rest = values - high
    mid = rest.astype(jnp.bfloat16).astype(jnp.float32)
    low = (rest - mid).astype(jnp.bfloat16).astype(jnp.float32)
    return high, mid, low


def target_weight(mass, poten):
    return (mass + poten / entropic) * log2e


def line_steps(shards):
    return [2 * (i ^ (i >> 1)) for i in range(shards // 2 - 1, 0, -1)]


def blocks_at(shards):
    near = [0] + line_steps(shards)
    me = lax.axis_index("src")
    return [me ^ other for other in near + [step ^ 1 for step in near]]


def read_all(hbm, held, sems):
    copies = [pltpu.make_async_copy(src, dst, sems.at[i]) for i, (src, dst) in enumerate(zip(hbm, held))]
    for copy in copies:
        copy.start()
    return copies


def pack_kernel(*refs):
    hbm, (send_ref, weight_ref), held, sems = refs[:3], refs[3:5], refs[5:8], refs[8]
    for copy in read_all(hbm, held, sems):
        copy.wait()
    feat_ref, mass_ref, poten_ref = held
    feat = feat_ref[0]
    depth, cells = feat.shape
    weight = target_weight(mass_ref[...], poten_ref[...])
    norm = jnp.sum(feat * feat, axis=0, keepdims=True)
    bias = weight - (log2e / entropic) * norm
    scaled = feat * (2.0 * log2e / entropic)
    send_ref[0, :depth, 0, :] = scaled
    send_ref[0, depth, 0:1, :] = bias
    weight_ref[...] = weight


def source_kernel(shards, *refs):
    hbm, outs, held, sems = refs[:4], refs[4:8], refs[8:12], refs[12]
    wide_ref, norm_ref, mask_ref, mass_out_ref = outs
    mass_ref, support_ref, counts_ref, feat_ref = held
    copies = read_all(hbm, held, sems)
    for copy in copies[:3]:
        copy.wait()
    mass_out_ref[...] = mass_ref[...]
    support = support_ref[...]
    slots, rows = support.shape
    cells = mass_ref.shape[1]
    used = lax.broadcasted_iota(jnp.int32, support.shape, 0) < counts_ref[...]
    hits = [
        jnp.max(jnp.where(used & (support == block), 0.0, very_low), axis=0, keepdims=True)
        for block in blocks_at(shards)
    ]
    hits = jnp.concatenate(hits + [jnp.zeros((cells - shards, rows), jnp.float32)], axis=0)
    hits = jnp.concatenate([hits, jnp.zeros((cells, cells - rows), jnp.float32)], axis=1).T
    for place in range(shards):
        mask_ref[place] = jnp.broadcast_to(hits[:rows, place : place + 1], (rows, cells))
    copies[3].wait()
    depth = feat_ref.shape[1]
    one = jnp.ones((2 * depth, 2 * cells), jnp.bfloat16)
    for pair in range(rows // 2):
        for half in range(2):
            feat = feat_ref[2 * pair + half]
            norm_ref[2 * pair + half : 2 * pair + half + 1, :] = jnp.sum(feat * feat, axis=0, keepdims=True)
            high, mid, low = pieces(feat)
            lanes = slice(half * cells, (half + 1) * cells)
            top = jnp.concatenate([high, mid], axis=0).astype(jnp.bfloat16)
            wide_ref[pair, 0 : 2 * depth, lanes] = top
            wide_ref[pair, 2 * depth : 4 * depth, lanes] = top
            wide_ref[pair, 4 * depth : 6 * depth, lanes] = jnp.concatenate([low, high], axis=0).astype(jnp.bfloat16)
        wide_ref[pair, 6 * depth : 8 * depth, :] = one


def join_kernel(*refs):
    refs[-1][0] = refs[0][0]
    refs[-1][1] = refs[1][0]


def on_core(core, work, idle):
    if core is None:
        work()
    else:
        here = lax.axis_index("tgt") == core
        pl.when(here)(work)
        pl.when(jnp.logical_not(here))(idle)


def tile_kernel(parts, core, *refs):
    peak_ref, total_ref = refs[-2:]

    def idle():
        peak_ref[...] = jnp.zeros(peak_ref.shape, jnp.float32)
        total_ref[...] = jnp.zeros(total_ref.shape, jnp.float32)

    ins = refs[: parts + 1] + refs[-4:]
    on_core(core, functools.partial(make_tiles, parts, *ins), idle)


def make_tiles(parts, *refs):
    packs = [ref.at[index] for ref in refs[:parts] for index in range(ref.shape[0])]
    wide_ref, exps_ref, tall_ref, peak_ref, total_ref = refs[parts:]
    blocks = len(packs)
    pairs, _, both = wide_ref.shape
    cells = both // 2
    depth = cells // 2
    lane = lax.broadcasted_iota(jnp.int32, (cells, cells), 1)
    biases = jnp.concatenate([pack[depth, 0:1, :] for pack in packs], axis=0)
    bias_pieces = jnp.concatenate(list(pieces(biases)), axis=0)
    padded = jnp.concatenate([bias_pieces, jnp.zeros((cells - 3 * blocks, cells), jnp.float32)], axis=0)
    bias_lanes = padded.T
    for place, pack in enumerate(packs):
        feat = pack[:depth, 0, :]
        turned = jnp.concatenate([feat, feat], axis=0).T
        high, mid, low = pieces(turned)
        own = jnp.where(lax.rem(lane, blocks) == place, bias_lanes, 0.0)
        rows = slice(place * cells, (place + 1) * cells)
        tall_ref[rows, 0:cells] = high.astype(jnp.bfloat16)
        tall_ref[rows, cells : 2 * cells] = mid.astype(jnp.bfloat16)
        tall_ref[rows, 2 * cells : 3 * cells] = jnp.where(lane < depth, high, low).astype(jnp.bfloat16)
        tall_ref[rows, 3 * cells : 4 * cells] = own.astype(jnp.bfloat16)

    def body(pair, carry):
        scores = jnp.dot(tall_ref[...], wide_ref[pair], preferred_element_type=jnp.float32)
        for place in range(blocks):
            rows = slice(place * cells, (place + 1) * cells)
            score = scores[rows]
            peak = jnp.max(score, axis=0, keepdims=True)
            exps = jnp.exp2(score - peak)
            exps_ref[pair, rows, :] = exps
            total = jnp.sum(exps, axis=0, keepdims=True)
            for half in range(2):
                lanes = slice(half * cells, (half + 1) * cells)
                peak_ref[place, pl.ds(2 * pair + half, 1), :] = peak[:, lanes]
                total_ref[place, pl.ds(2 * pair + half, 1), :] = total[:, lanes]
        return carry

    lax.fori_loop(0, pairs, body, 0, unroll=min(pairs, 16 // blocks & -4 or 2))


def row_kernel(groups, *refs):
    mask_ref, peak_refs, total_refs = refs[0], refs[1 : 1 + groups], refs[1 + groups : 1 + 2 * groups]
    peaks_ref, rowsum_ref = refs[1 + 2 * groups :]
    place = 0
    for ref in peak_refs:
        for index in range(ref.shape[0]):
            peaks_ref[place] = ref[index] + mask_ref[place]
            place += 1
    totals = [ref[index] for ref in total_refs for index in range(ref.shape[0])]
    top = functools.reduce(jnp.maximum, [peaks_ref[index] for index in range(place)])
    summed = sum(total * jnp.exp2(peaks_ref[index] - top) for index, total in enumerate(totals))
    rowsum_ref[...] = top + jnp.log2(summed)


def across(column):
    shape = (column.shape[0],) * 2
    same = lax.broadcasted_iota(jnp.int32, shape, 0) == lax.broadcasted_iota(jnp.int32, shape, 1)
    return jnp.sum(jnp.where(same, jnp.broadcast_to(column, shape), 0.0), axis=0, keepdims=True)


def column_kernel(groups, core, *refs):
    ins, outs, scratch = refs[: 2 * groups + 7], refs[-4:-2], refs[-2:]

    def idle():
        for given, out in zip(refs[2 * groups + 7 : -4], outs):
            out[...] = given[...]

    on_core(core, functools.partial(sum_columns, groups, *ins, *outs, *scratch), idle)


def sum_columns(groups, *refs):
    exps_refs, tall_refs, rest = refs[:groups], refs[groups : 2 * groups], refs[2 * groups :]
    wide_ref, peak_ref, mask_ref, own_ref, other_ref, mass_ref, norm_ref = rest[:7]
    poten_ref, sums_ref, weight_ref, shift_ref = rest[7:]
    pairs, _, both = wide_ref.shape
    cells = both // 2
    shards = mask_ref.shape[0]
    own, other = own_ref[...], other_ref[...]
    top = jnp.maximum(own, other)
    whole = top + jnp.log2(jnp.exp2(own - top) + jnp.exp2(other - top))
    poten_ref[...] = norm_ref[...] - (entropic * ln2) * whole
    shift = mass_ref[...] * log2e - whole
    shift_ref[...] = shift
    for place in range(shards):
        weight_ref[place] = jnp.exp2(peak_ref[place] + shift)
    spots = [
        (group, slice(index * cells, (index + 1) * cells))
        for group, ref in enumerate(tall_refs)
        for index in range(ref.shape[0] // cells)
    ]
    used = [jnp.max(mask_ref[place], axis=0, keepdims=True) > 0.5 * very_low for place in range(shards)]
    owners = blocks_at(shards)
    sums = []
    for place, (group, rows) in enumerate(spots):
        acc = jnp.zeros((cells, cells), jnp.float32)
        for pair in range(pairs):
            acc = acc + exps_refs[group][pair, rows, :cells] * weight_ref[place, 2 * pair : 2 * pair + 1, :]
            acc = acc + exps_refs[group][pair, rows, cells:] * weight_ref[place, 2 * pair + 1 : 2 * pair + 2, :]
        sums.append(jnp.sum(acc.T, axis=0, keepdims=True))
    whole_sums = jnp.concatenate([jnp.where(here, one, 1.0) for here, one in zip(used, sums)], axis=0)
    worst = jnp.min(whole_sums)
    logs = jnp.log2(whole_sums)
    for place in range(shards):
        sums_ref[owners[place]] = jnp.where(used[place], logs[place : place + 1, :], very_low)

    @pl.when(worst < least_sum)
    def _():
        for place, (group, rows) in enumerate(spots):

            def exponents(pair):
                score = jnp.dot(tall_refs[group][rows, :], wide_ref[pair], preferred_element_type=jnp.float32)
                add = shift_ref[pl.ds(2 * pair, 2), :] + mask_ref[place, pl.ds(2 * pair, 2), :]
                return score[:, :cells] + add[0:1, :], score[:, cells:] + add[1:2, :]

            def highest(pair, peak):
                first, second = exponents(pair)
                return jnp.maximum(peak, jnp.maximum(first, second))

            peak = lax.fori_loop(0, pairs, highest, jnp.full((cells, cells), very_low, jnp.float32))
            peak = jnp.max(peak, axis=1, keepdims=True)

            def add_up(pair, sums):
                first, second = exponents(pair)
                return sums + jnp.exp2(first - peak) + jnp.exp2(second - peak)

            sums = lax.fori_loop(0, pairs, add_up, jnp.zeros((cells, cells), jnp.float32))
            logs = across(peak) + jnp.log2(across(jnp.sum(sums, axis=1, keepdims=True)))
            sums_ref[owners[place]] = jnp.where(used[place], logs, very_low)


def merge_kernel(values_ref, weight_ref, poten_ref, out_ref, poten_out_ref):
    poten_out_ref[...] = poten_ref[...]
    values = values_ref[...]
    top = jnp.max(values, axis=0)
    whole = top + jnp.log2(jnp.sum(jnp.exp2(values - top), axis=0))
    out_ref[...] = -(entropic * ln2) * (whole - weight_ref[...])


def f32(*shape):
    return jax.ShapeDtypeStruct(shape, jnp.float32)


def dense_device(
    source_feat, target_feat, log_mass_src, log_mass_tgt, potential_tgt, support, counts
):
    shards = lax.axis_size("src")
    rows, depth, cells = source_feat.shape
    pairs, wide = rows // 2, 2 * cells

    def call(kernel, ins, out_shape, scratch=(), cost=None):
        many = isinstance(out_shape, list)
        return pl.pallas_call(
            kernel,
            in_specs=ins,
            out_specs=[VM] * len(out_shape) if many else VM,
            out_shape=out_shape,
            scratch_shapes=list(scratch),
            compiler_params=PARAMS,
            cost_estimate=cost,
        )

    def reading(kernel, args, out_shape, cost):
        return call(
            kernel,
            [pl.BlockSpec(memory_space=pltpu.HBM)] * len(args),
            out_shape,
            [pltpu.VMEM(arg.shape, arg.dtype) for arg in args] + [pltpu.SemaphoreType.DMA((len(args),))],
            cost,
        )(*[pltpu.with_memory_space_constraint(arg, pltpu.HBM) for arg in args])

    def cost_of(flops):
        return pl.CostEstimate(flops=flops, bytes_accessed=rows * depth * cells * 4, transcendentals=0)

    pack, weight = reading(
        pack_kernel,
        [target_feat, log_mass_tgt, potential_tgt],
        [in_vmem((1, depth + 1, 1, cells), jnp.float32), in_vmem((1, cells), jnp.float32)],
        None,
    )
    wide_feat, norm, mask, mass = reading(
        functools.partial(source_kernel, shards),
        [log_mass_src, support[:, 0, :].T, counts.T, source_feat],
        [
            in_vmem((pairs, 8 * depth, wide), jnp.bfloat16),
            in_vmem((rows, cells), jnp.float32),
            in_vmem((shards, rows, cells), jnp.float32),
            in_vmem((rows, cells), jnp.float32),
        ],
        cost_of(10**9),
    )

    def tiles(*packs, core=None, after=None):
        blocks = sum(pack.shape[0] for pack in packs)
        more = [] if after is None else [after]
        return call(
            functools.partial(tile_kernel, len(packs), core),
            [VM] * (len(packs) + 1) + [pl.BlockSpec(memory_space=pl.ANY)] * len(more),
            [
                in_vmem((pairs, blocks * cells, wide), jnp.float32),
                in_vmem((blocks * cells, 8 * depth), jnp.bfloat16),
                in_vmem((blocks, rows, cells), jnp.float32),
                in_vmem((blocks, rows, cells), jnp.float32),
            ],
            cost=cost_of(2 * blocks * cells * pairs * wide * 8 * depth),
        )(*packs, wide_feat, *more)

    def swapped(array, step):
        return lax.ppermute(array, "src", [(i, i ^ step) for i in range(shards)])

    there = {step: swapped(pack, step) for step in reversed(line_steps(shards))}
    near = [pack] + [there[step] for step in line_steps(shards)]
    found = [tiles(pack)]
    halves = [
        call(
            join_kernel,
            [VM] * 2 + [pl.BlockSpec(memory_space=pl.ANY)],
            in_vmem((2,) + pack.shape[1:], jnp.float32),
        )(near[at], near[at + 1], found[0][-1])
        for at in range(0, len(near), 2)
    ]
    far = [swapped(half, 1) for half in halves]
    found += [tiles(*near[1:]), tiles(far[0])]
    groups = len(found) + 1

    def log_sums(last):
        _, _, peaks, totals = zip(*found, last)
        return call(
            functools.partial(row_kernel, groups),
            [VM] * (1 + 2 * groups),
            [in_vmem((shards, rows, cells), jnp.float32), in_vmem((rows, cells), jnp.float32)],
        )(mask, *peaks, *totals)

    def columns_of(core, last, peaks, own, other, given):
        exps, tall, _, _ = zip(*found, last)
        return call(
            functools.partial(column_kernel, groups, core),
            [VM] * (2 * groups + 7 + len(given)),
            [in_vmem((rows, cells), jnp.float32), in_vmem((shards, 1, cells), jnp.float32)],
            [pltpu.VMEM((shards, rows, cells), jnp.float32), pltpu.VMEM((rows, cells), jnp.float32)],
            cost_of(10**9),
        )(*exps, *tall, wide_feat, peaks, mask, own, other, mass, norm, *given)

    between = [(0, 1), (1, 0)]
    last_one = tiles(far[1], core=1)
    peaks_one, own_one = log_sums(last_one)
    other_zero = lax.ppermute(own_one, "tgt", between)
    last_zero = tiles(far[1], core=0, after=own_one)
    peaks_zero, own_zero = log_sums(last_zero)
    other_one = lax.ppermute(own_zero, "tgt", between)
    given = columns_of(0, last_zero, peaks_zero, own_zero, other_zero, [])
    potential_src, columns = columns_of(1, last_one, peaks_one, own_one, other_one, given)
    arrived = lax.all_to_all(columns, "src", 0, 0)
    outs = [f32(1, cells), f32(rows, cells)]
    potential_new, potential_src = call(merge_kernel, [VM] * 3, outs)(arrived, weight, potential_src)
    return potential_src, potential_new


def merged(part, axis, combine):
    gathered = jax.tree.map(lambda a: lax.all_gather(a, axis), part)

    def take(source):
        return jax.tree.map(lambda a: lax.dynamic_index_in_dim(a, source, 0, False), gathered)

    return lax.fori_loop(
        1, lax.axis_size(axis), lambda source, state: combine(state, take(source)), take(0)
    )


def cost_tiles(source_blk, source_sq, target_blk, target_sq):
    cross = jnp.einsum(
        "...fi,...fj->...ij", source_blk, target_blk, precision=lax.Precision.HIGHEST
    )
    return source_sq[..., :, None] + target_sq[..., None, :] - 2.0 * cross


def row_stats(cost, mass_tgt, poten_tgt, usable):
    scores = mass_tgt[..., None, :] + (poten_tgt[..., None, :] - cost) / entropic
    scores = jnp.where(usable[..., None, None], scores, very_low)
    peak = jnp.max(scores, axis=(1, 3))
    total = jnp.sum(jnp.exp(scores - peak[:, None, :, None]), axis=(1, 3))
    return (peak, total)


def column_stats(cost, mass_src, poten_src, usable):
    scores = mass_src[:, None, :, None] + (poten_src[:, None, :, None] - cost) / entropic
    peak = jnp.max(scores, axis=2)
    total = jnp.sum(jnp.exp(scores - peak[:, :, None, :]), axis=2)
    peak = jnp.where(usable[..., None], peak, very_low)
    total = jnp.where(usable[..., None], total, 0.0)
    return (peak, total)


def merge_pair(first_pair, second_pair):
    first_peak, first_total = first_pair
    second_peak, second_total = second_pair
    highest = jnp.maximum(first_peak, second_peak)
    summed = first_total * jnp.exp(first_peak - highest) + second_total * jnp.exp(
        second_peak - highest
    )
    return (highest, summed)


def segment_merge(peaks, totals, seg_ids, segments):
    best = jax.ops.segment_max(peaks, seg_ids, num_segments=segments + 1)
    best = jnp.maximum(best, very_low)
    summed = jax.ops.segment_sum(
        totals * jnp.exp(peaks - best[seg_ids]), seg_ids, num_segments=segments + 1
    )
    return (best[:segments], summed[:segments])


def general_device(
    source_feat, target_feat, log_mass_src, log_mass_tgt, potential_tgt, support, counts
):
    target_all, mass_all, poten_all = (
        lax.all_gather(target_feat, "src", axis=0, tiled=True),
        lax.all_gather(log_mass_tgt, "src", axis=0, tiled=True),
        lax.all_gather(potential_tgt, "src", axis=0, tiled=True),
    )
    blocks = target_all.shape[0]
    rows_here = source_feat.shape[0]
    slots_here = support.shape[2]
    cells = source_feat.shape[2]
    indices = support[:, 0, :]
    limits = counts[:, 0]
    usable = jnp.arange(slots_here, dtype=jnp.int32)[None, :] < limits[:, None]
    source_sq = jnp.sum(source_feat * source_feat, axis=1)
    target_sq = jnp.sum(target_all * target_all, axis=1)
    width = math.gcd(rows_here, 4)

    def grouped(array):
        return array.reshape((rows_here // width, width) + array.shape[1:])

    def row_pass(items):
        source_blk, source_nrm, ids_here, use_here = items
        cost = cost_tiles(
            source_blk[:, None], source_nrm[:, None], target_all[ids_here], target_sq[ids_here]
        )
        return row_stats(cost, mass_all[ids_here], poten_all[ids_here], use_here)

    peak, total = lax.map(
        row_pass, (grouped(source_feat), grouped(source_sq), grouped(indices), grouped(usable))
    )
    peak = peak.reshape(rows_here, cells)
    total = total.reshape(rows_here, cells)
    peak_all, total_all = merged((peak, total), "tgt", merge_pair)
    potential_src = -entropic * (peak_all + jnp.log(total_all))

    def column_pass(items):
        source_blk, source_nrm, mass_here, poten_here, ids_here, use_here = items
        cost = cost_tiles(
            source_blk[:, None], source_nrm[:, None], target_all[ids_here], target_sq[ids_here]
        )
        return column_stats(cost, mass_here, poten_here, use_here)

    peaks, totals = lax.map(
        column_pass,
        (
            grouped(source_feat),
            grouped(source_sq),
            grouped(log_mass_src),
            grouped(potential_src),
            grouped(indices),
            grouped(usable),
        ),
    )
    seg_ids = jnp.where(usable, indices, blocks).reshape(-1)
    best, summed = segment_merge(
        peaks.reshape(-1, cells), totals.reshape(-1, cells), seg_ids, blocks
    )
    share = blocks // lax.axis_size("src")
    own_start = lax.axis_index("src") * share
    highest = lax.pmax(best, "src")
    whole = lax.psum(summed * jnp.exp(best - highest), "src")
    own_peak = lax.dynamic_slice_in_dim(highest, own_start, share, 0)
    own_total = lax.dynamic_slice_in_dim(whole, own_start, share, 0)
    potential_new = -entropic * (own_peak + jnp.log(own_total))
    return (potential_src, potential_new)


def per_device(source_feat, target_feat, *others):
    shards = lax.axis_size("src")
    rows, depth, cells = source_feat.shape
    few = shards == 8 and target_feat.shape[0] == 1 and lax.axis_size("tgt") == 2
    if few and rows % 8 == 0 and cells == 128 and depth == 64:
        return dense_device(source_feat, target_feat, *others)
    return general_device(source_feat, target_feat, *others)


def solution(mesh):
    in_specs = (
        P(("grp", "src"), None, None),
        P(("grp", "src", "tgt"), None, None),
        P(("grp", "src"), None),
        P(("grp", "src", "tgt"), None),
        P(("grp", "src", "tgt"), None),
        P(("grp", "src"), "tgt", None),
        P(("grp", "src"), "tgt"),
    )
    out_specs = (P(("grp", "src"), None), P(("grp", "src", "tgt"), None))
    return jax.shard_map(
        per_device, mesh=mesh, in_specs=in_specs, out_specs=out_specs, check_vma=False
    )
```

```python
import functools
import math

import jax
import jax.numpy as jnp
from jax import lax
from jax.experimental import pallas as pl
from jax.experimental.pallas import tpu as pltpu
from jax.sharding import PartitionSpec as P

entropic = 0.5
very_low = -1e30
log2e = 1.0 / math.log(2.0)
ln2 = math.log(2.0)
least_sum = 1e-28

VM = pl.BlockSpec(memory_space=pltpu.VMEM)
PARAMS = pltpu.CompilerParams(vmem_limit_bytes=40 * 2**20)


def in_vmem(shape, dtype):
    return pltpu.VMEM(shape, dtype)


def pieces(values):
    high = values.astype(jnp.bfloat16).astype(jnp.float32)
    rest = values - high
    mid = rest.astype(jnp.bfloat16).astype(jnp.float32)
    low = (rest - mid).astype(jnp.bfloat16).astype(jnp.float32)
    return high, mid, low


def target_weight(mass, poten):
    return (mass + poten / entropic) * log2e


def line_steps(shards):
    return [2 * (i ^ (i >> 1)) for i in range(shards // 2 - 1, 0, -1)]


def blocks_at(shards):
    near = [0] + line_steps(shards)
    me = lax.axis_index("src")
    return [me ^ other for other in near + [step ^ 1 for step in near]]


def read_all(hbm, held, sems):
    copies = [pltpu.make_async_copy(src, dst, sems.at[i]) for i, (src, dst) in enumerate(zip(hbm, held))]
    for copy in copies:
        copy.start()
    return copies


def pack_kernel(*refs):
    hbm, (send_ref, weight_ref), held, sems = refs[:3], refs[3:5], refs[5:8], refs[8]
    for copy in read_all(hbm, held, sems):
        copy.wait()
    feat_ref, mass_ref, poten_ref = held
    feat = feat_ref[0]
    depth, cells = feat.shape
    weight = target_weight(mass_ref[...], poten_ref[...])
    norm = jnp.sum(feat * feat, axis=0, keepdims=True)
    bias = weight - (log2e / entropic) * norm
    scaled = feat * (2.0 * log2e / entropic)
    send_ref[0, :depth, 0, :] = scaled
    send_ref[0, depth, 0:1, :] = bias
    weight_ref[...] = weight


def source_kernel(shards, *refs):
    hbm, outs, held, sems = refs[:4], refs[4:8], refs[8:12], refs[12]
    wide_ref, norm_ref, mask_ref, mass_out_ref = outs
    mass_ref, support_ref, counts_ref, feat_ref = held
    copies = read_all(hbm, held, sems)
    for copy in copies[:3]:
        copy.wait()
    mass_out_ref[...] = mass_ref[...]
    support = support_ref[...]
    slots, rows = support.shape
    cells = mass_ref.shape[1]
    used = lax.broadcasted_iota(jnp.int32, support.shape, 0) < counts_ref[...]
    hits = [
        jnp.max(jnp.where(used & (support == block), 0.0, very_low), axis=0, keepdims=True)
        for block in blocks_at(shards)
    ]
    hits = jnp.concatenate(hits + [jnp.zeros((cells - shards, rows), jnp.float32)], axis=0)
    hits = jnp.concatenate([hits, jnp.zeros((cells, cells - rows), jnp.float32)], axis=1).T
    for place in range(shards):
        mask_ref[place] = jnp.broadcast_to(hits[:rows, place : place + 1], (rows, cells))
    copies[3].wait()
    depth = feat_ref.shape[1]
    one = jnp.ones((2 * depth, 2 * cells), jnp.bfloat16)
    for pair in range(rows // 2):
        for half in range(2):
            feat = feat_ref[2 * pair + half]
            norm_ref[2 * pair + half : 2 * pair + half + 1, :] = jnp.sum(feat * feat, axis=0, keepdims=True)
            high, mid, low = pieces(feat)
            lanes = slice(half * cells, (half + 1) * cells)
            top = jnp.concatenate([high, mid], axis=0).astype(jnp.bfloat16)
            wide_ref[pair, 0 : 2 * depth, lanes] = top
            wide_ref[pair, 2 * depth : 4 * depth, lanes] = top
            wide_ref[pair, 4 * depth : 6 * depth, lanes] = jnp.concatenate([low, high], axis=0).astype(jnp.bfloat16)
        wide_ref[pair, 6 * depth : 8 * depth, :] = one


def join_kernel(*refs):
    for place, ref in enumerate(refs[:-2]):
        refs[-1][place] = ref[0]


def on_core(core, work, idle):
    if core is None:
        work()
    else:
        here = lax.axis_index("tgt") == core
        pl.when(here)(work)
        pl.when(jnp.logical_not(here))(idle)


def tile_kernel(parts, core, *refs):
    peak_ref, total_ref = refs[-2:]

    def idle():
        peak_ref[...] = jnp.zeros(peak_ref.shape, jnp.float32)
        total_ref[...] = jnp.zeros(total_ref.shape, jnp.float32)

    ins = refs[: parts + 1] + refs[-4:]
    on_core(core, functools.partial(make_tiles, parts, *ins), idle)


def make_tiles(parts, *refs):
    packs = [ref.at[index] for ref in refs[:parts] for index in range(ref.shape[0])]
    wide_ref, exps_ref, tall_ref, peak_ref, total_ref = refs[parts:]
    blocks = len(packs)
    pairs, _, both = wide_ref.shape
    cells = both // 2
    depth = cells // 2
    lane = lax.broadcasted_iota(jnp.int32, (cells, cells), 1)
    biases = jnp.concatenate([pack[depth, 0:1, :] for pack in packs], axis=0)
    bias_pieces = jnp.concatenate(list(pieces(biases)), axis=0)
    padded = jnp.concatenate([bias_pieces, jnp.zeros((cells - 3 * blocks, cells), jnp.float32)], axis=0)
    bias_lanes = padded.T
    for place, pack in enumerate(packs):
        feat = pack[:depth, 0, :]
        turned = jnp.concatenate([feat, feat], axis=0).T
        high, mid, low = pieces(turned)
        own = jnp.where(lax.rem(lane, blocks) == place, bias_lanes, 0.0)
        rows = slice(place * cells, (place + 1) * cells)
        tall_ref[rows, 0:cells] = high.astype(jnp.bfloat16)
        tall_ref[rows, cells : 2 * cells] = mid.astype(jnp.bfloat16)
        tall_ref[rows, 2 * cells : 3 * cells] = jnp.where(lane < depth, high, low).astype(jnp.bfloat16)
        tall_ref[rows, 3 * cells : 4 * cells] = own.astype(jnp.bfloat16)

    def body(pair, carry):
        scores = jnp.dot(tall_ref[...], wide_ref[pair], preferred_element_type=jnp.float32)
        for place in range(blocks):
            rows = slice(place * cells, (place + 1) * cells)
            score = scores[rows]
            peak = jnp.max(score, axis=0, keepdims=True)
            exps = jnp.exp2(score - peak)
            exps_ref[pair, rows, :] = exps
            total = jnp.sum(exps, axis=0, keepdims=True)
            for half in range(2):
                lanes = slice(half * cells, (half + 1) * cells)
                peak_ref[place, pl.ds(2 * pair + half, 1), :] = peak[:, lanes]
                total_ref[place, pl.ds(2 * pair + half, 1), :] = total[:, lanes]
        return carry

    lax.fori_loop(0, pairs, body, 0, unroll=min(pairs, 16 // blocks & -4 or 2))


def row_kernel(groups, *refs):
    mask_ref, peak_refs, total_refs = refs[0], refs[1 : 1 + groups], refs[1 + groups : 1 + 2 * groups]
    peaks_ref, rowsum_ref = refs[1 + 2 * groups :]
    place = 0
    for ref in peak_refs:
        for index in range(ref.shape[0]):
            peaks_ref[place] = ref[index] + mask_ref[place]
            place += 1
    totals = [ref[index] for ref in total_refs for index in range(ref.shape[0])]
    top = functools.reduce(jnp.maximum, [peaks_ref[index] for index in range(place)])
    summed = sum(total * jnp.exp2(peaks_ref[index] - top) for index, total in enumerate(totals))
    rowsum_ref[...] = top + jnp.log2(summed)


def across(column):
    shape = (column.shape[0],) * 2
    same = lax.broadcasted_iota(jnp.int32, shape, 0) == lax.broadcasted_iota(jnp.int32, shape, 1)
    return jnp.sum(jnp.where(same, jnp.broadcast_to(column, shape), 0.0), axis=0, keepdims=True)


def column_kernel(groups, core, *refs):
    ins, outs, scratch = refs[: 2 * groups + 7], refs[-4:-2], refs[-2:]

    def idle():
        for given, out in zip(refs[2 * groups + 7 : -4], outs):
            out[...] = given[...]

    on_core(core, functools.partial(sum_columns, groups, *ins, *outs, *scratch), idle)


def sum_columns(groups, *refs):
    exps_refs, tall_refs, rest = refs[:groups], refs[groups : 2 * groups], refs[2 * groups :]
    wide_ref, peak_ref, mask_ref, own_ref, other_ref, mass_ref, norm_ref = rest[:7]
    poten_ref, sums_ref, weight_ref, shift_ref = rest[7:]
    pairs, _, both = wide_ref.shape
    cells = both // 2
    shards = mask_ref.shape[0]
    own, other = own_ref[...], other_ref[...]
    top = jnp.maximum(own, other)
    whole = top + jnp.log2(jnp.exp2(own - top) + jnp.exp2(other - top))
    poten_ref[...] = norm_ref[...] - (entropic * ln2) * whole
    shift = mass_ref[...] * log2e - whole
    shift_ref[...] = shift
    for place in range(shards):
        weight_ref[place] = jnp.exp2(peak_ref[place] + shift)
    spots = [
        (group, slice(index * cells, (index + 1) * cells))
        for group, ref in enumerate(tall_refs)
        for index in range(ref.shape[0] // cells)
    ]
    used = [jnp.max(mask_ref[place], axis=0, keepdims=True) > 0.5 * very_low for place in range(shards)]
    owners = blocks_at(shards)
    sums = []
    for place, (group, rows) in enumerate(spots):
        acc = jnp.zeros((cells, cells), jnp.float32)
        for pair in range(pairs):
            acc = acc + exps_refs[group][pair, rows, :cells] * weight_ref[place, 2 * pair : 2 * pair + 1, :]
            acc = acc + exps_refs[group][pair, rows, cells:] * weight_ref[place, 2 * pair + 1 : 2 * pair + 2, :]
        sums.append(jnp.sum(acc.T, axis=0, keepdims=True))
    whole_sums = jnp.concatenate([jnp.where(here, one, 1.0) for here, one in zip(used, sums)], axis=0)
    worst = jnp.min(whole_sums)
    logs = jnp.log2(whole_sums)
    for place in range(shards):
        sums_ref[owners[place]] = jnp.where(used[place], logs[place : place + 1, :], very_low)

    @pl.when(worst < least_sum)
    def _():
        for place, (group, rows) in enumerate(spots):

            def exponents(pair):
                score = jnp.dot(tall_refs[group][rows, :], wide_ref[pair], preferred_element_type=jnp.float32)
                add = shift_ref[pl.ds(2 * pair, 2), :] + mask_ref[place, pl.ds(2 * pair, 2), :]
                return score[:, :cells] + add[0:1, :], score[:, cells:] + add[1:2, :]

            def highest(pair, peak):
                first, second = exponents(pair)
                return jnp.maximum(peak, jnp.maximum(first, second))

            peak = lax.fori_loop(0, pairs, highest, jnp.full((cells, cells), very_low, jnp.float32))
            peak = jnp.max(peak, axis=1, keepdims=True)

            def add_up(pair, sums):
                first, second = exponents(pair)
                return sums + jnp.exp2(first - peak) + jnp.exp2(second - peak)

            sums = lax.fori_loop(0, pairs, add_up, jnp.zeros((cells, cells), jnp.float32))
            logs = across(peak) + jnp.log2(across(jnp.sum(sums, axis=1, keepdims=True)))
            sums_ref[owners[place]] = jnp.where(used[place], logs, very_low)


def merge_kernel(values_ref, weight_ref, poten_ref, out_ref, poten_out_ref):
    poten_out_ref[...] = poten_ref[...]
    values = values_ref[...]
    top = jnp.max(values, axis=0)
    whole = top + jnp.log2(jnp.sum(jnp.exp2(values - top), axis=0))
    out_ref[...] = -(entropic * ln2) * (whole - weight_ref[...])


def f32(*shape):
    return jax.ShapeDtypeStruct(shape, jnp.float32)


def dense_device(
    source_feat, target_feat, log_mass_src, log_mass_tgt, potential_tgt, support, counts
):
    shards = lax.axis_size("src")
    rows, depth, cells = source_feat.shape
    pairs, wide = rows // 2, 2 * cells

    def call(kernel, ins, out_shape, scratch=(), cost=None):
        many = isinstance(out_shape, list)
        return pl.pallas_call(
            kernel,
            in_specs=ins,
            out_specs=[VM] * len(out_shape) if many else VM,
            out_shape=out_shape,
            scratch_shapes=list(scratch),
            compiler_params=PARAMS,
            cost_estimate=cost,
        )

    def reading(kernel, args, out_shape, cost):
        return call(
            kernel,
            [pl.BlockSpec(memory_space=pltpu.HBM)] * len(args),
            out_shape,
            [pltpu.VMEM(arg.shape, arg.dtype) for arg in args] + [pltpu.SemaphoreType.DMA((len(args),))],
            cost,
        )(*[pltpu.with_memory_space_constraint(arg, pltpu.HBM) for arg in args])

    def cost_of(flops):
        return pl.CostEstimate(flops=flops, bytes_accessed=rows * depth * cells * 4, transcendentals=0)

    pack, weight = reading(
        pack_kernel,
        [target_feat, log_mass_tgt, potential_tgt],
        [in_vmem((1, depth + 1, 1, cells), jnp.float32), in_vmem((1, cells), jnp.float32)],
        None,
    )
    wide_feat, norm, mask, mass = reading(
        functools.partial(source_kernel, shards),
        [log_mass_src, support[:, 0, :].T, counts.T, source_feat],
        [
            in_vmem((pairs, 8 * depth, wide), jnp.bfloat16),
            in_vmem((rows, cells), jnp.float32),
            in_vmem((shards, rows, cells), jnp.float32),
            in_vmem((rows, cells), jnp.float32),
        ],
        cost_of(10**9),
    )

    def tiles(*packs, core=None, after=None):
        blocks = sum(pack.shape[0] for pack in packs)
        more = [] if after is None else [after]
        return call(
            functools.partial(tile_kernel, len(packs), core),
            [VM] * (len(packs) + 1) + [pl.BlockSpec(memory_space=pl.ANY)] * len(more),
            [
                in_vmem((pairs, blocks * cells, wide), jnp.float32),
                in_vmem((blocks * cells, 8 * depth), jnp.bfloat16),
                in_vmem((blocks, rows, cells), jnp.float32),
                in_vmem((blocks, rows, cells), jnp.float32),
            ],
            cost=cost_of(2 * blocks * cells * pairs * wide * 8 * depth),
        )(*packs, wide_feat, *more)

    def swapped(array, step):
        return lax.ppermute(array, "src", [(i, i ^ step) for i in range(shards)])

    def joined(blocks, after):
        return call(
            join_kernel,
            [VM] * len(blocks) + [pl.BlockSpec(memory_space=pl.ANY)],
            in_vmem((len(blocks),) + pack.shape[1:], jnp.float32),
        )(*blocks, after)

    steps = line_steps(shards)
    there = [swapped(pack, step) for step in reversed(steps)][::-1]
    first = joined([pack, there[0]], norm)
    found = [tiles(pack, after=first)]
    far = [swapped(joined([block], found[0][-1]), 1) for block in reversed(there[1:])][::-1]
    far = [swapped(first, 1)] + far
    found.append(tiles(*there))
    for some in far[:-1]:
        found.append(tiles(some, after=found[-1][-1]))
    groups = len(found) + 1

    def log_sums(last):
        _, _, peaks, totals = zip(*found, last)
        return call(
            functools.partial(row_kernel, groups),
            [VM] * (1 + 2 * groups),
            [in_vmem((shards, rows, cells), jnp.float32), in_vmem((rows, cells), jnp.float32)],
        )(mask, *peaks, *totals)

    def columns_of(core, last, peaks, own, other, given):
        exps, tall, _, _ = zip(*found, last)
        return call(
            functools.partial(column_kernel, groups, core),
            [VM] * (2 * groups + 7 + len(given)),
            [in_vmem((rows, cells), jnp.float32), in_vmem((shards, 1, cells), jnp.float32)],
            [pltpu.VMEM((shards, rows, cells), jnp.float32), pltpu.VMEM((rows, cells), jnp.float32)],
            cost_of(10**9),
        )(*exps, *tall, wide_feat, peaks, mask, own, other, mass, norm, *given)

    between = [(0, 1), (1, 0)]
    last_one = tiles(far[-1], core=1, after=found[-1][-1])
    peaks_one, own_one = log_sums(last_one)
    other_zero = lax.ppermute(own_one, "tgt", between)
    last_zero = tiles(far[-1], core=0, after=own_one)
    peaks_zero, own_zero = log_sums(last_zero)
    other_one = lax.ppermute(own_zero, "tgt", between)
    given = columns_of(0, last_zero, peaks_zero, own_zero, other_zero, [])
    potential_src, columns = columns_of(1, last_one, peaks_one, own_one, other_one, given)
    arrived = lax.all_to_all(columns, "src", 0, 0)
    outs = [f32(1, cells), f32(rows, cells)]
    potential_new, potential_src = call(merge_kernel, [VM] * 3, outs)(arrived, weight, potential_src)
    return potential_src, potential_new


def merged(part, axis, combine):
    gathered = jax.tree.map(lambda a: lax.all_gather(a, axis), part)

    def take(source):
        return jax.tree.map(lambda a: lax.dynamic_index_in_dim(a, source, 0, False), gathered)

    return lax.fori_loop(
        1, lax.axis_size(axis), lambda source, state: combine(state, take(source)), take(0)
    )


def cost_tiles(source_blk, source_sq, target_blk, target_sq):
    cross = jnp.einsum(
        "...fi,...fj->...ij", source_blk, target_blk, precision=lax.Precision.HIGHEST
    )
    return source_sq[..., :, None] + target_sq[..., None, :] - 2.0 * cross


def row_stats(cost, mass_tgt, poten_tgt, usable):
    scores = mass_tgt[..., None, :] + (poten_tgt[..., None, :] - cost) / entropic
    scores = jnp.where(usable[..., None, None], scores, very_low)
    peak = jnp.max(scores, axis=(1, 3))
    total = jnp.sum(jnp.exp(scores - peak[:, None, :, None]), axis=(1, 3))
    return (peak, total)


def column_stats(cost, mass_src, poten_src, usable):
    scores = mass_src[:, None, :, None] + (poten_src[:, None, :, None] - cost) / entropic
    peak = jnp.max(scores, axis=2)
    total = jnp.sum(jnp.exp(scores - peak[:, :, None, :]), axis=2)
    peak = jnp.where(usable[..., None], peak, very_low)
    total = jnp.where(usable[..., None], total, 0.0)
    return (peak, total)


def merge_pair(first_pair, second_pair):
    first_peak, first_total = first_pair
    second_peak, second_total = second_pair
    highest = jnp.maximum(first_peak, second_peak)
    summed = first_total * jnp.exp(first_peak - highest) + second_total * jnp.exp(
        second_peak - highest
    )
    return (highest, summed)


def segment_merge(peaks, totals, seg_ids, segments):
    best = jax.ops.segment_max(peaks, seg_ids, num_segments=segments + 1)
    best = jnp.maximum(best, very_low)
    summed = jax.ops.segment_sum(
        totals * jnp.exp(peaks - best[seg_ids]), seg_ids, num_segments=segments + 1
    )
    return (best[:segments], summed[:segments])


def general_device(
    source_feat, target_feat, log_mass_src, log_mass_tgt, potential_tgt, support, counts
):
    target_all, mass_all, poten_all = (
        lax.all_gather(target_feat, "src", axis=0, tiled=True),
        lax.all_gather(log_mass_tgt, "src", axis=0, tiled=True),
        lax.all_gather(potential_tgt, "src", axis=0, tiled=True),
    )
    blocks = target_all.shape[0]
    rows_here = source_feat.shape[0]
    slots_here = support.shape[2]
    cells = source_feat.shape[2]
    indices = support[:, 0, :]
    limits = counts[:, 0]
    usable = jnp.arange(slots_here, dtype=jnp.int32)[None, :] < limits[:, None]
    source_sq = jnp.sum(source_feat * source_feat, axis=1)
    target_sq = jnp.sum(target_all * target_all, axis=1)
    width = math.gcd(rows_here, 4)

    def grouped(array):
        return array.reshape((rows_here // width, width) + array.shape[1:])

    def row_pass(items):
        source_blk, source_nrm, ids_here, use_here = items
        cost = cost_tiles(
            source_blk[:, None], source_nrm[:, None], target_all[ids_here], target_sq[ids_here]
        )
        return row_stats(cost, mass_all[ids_here], poten_all[ids_here], use_here)

    peak, total = lax.map(
        row_pass, (grouped(source_feat), grouped(source_sq), grouped(indices), grouped(usable))
    )
    peak = peak.reshape(rows_here, cells)
    total = total.reshape(rows_here, cells)
    peak_all, total_all = merged((peak, total), "tgt", merge_pair)
    potential_src = -entropic * (peak_all + jnp.log(total_all))

    def column_pass(items):
        source_blk, source_nrm, mass_here, poten_here, ids_here, use_here = items
        cost = cost_tiles(
            source_blk[:, None], source_nrm[:, None], target_all[ids_here], target_sq[ids_here]
        )
        return column_stats(cost, mass_here, poten_here, use_here)

    peaks, totals = lax.map(
        column_pass,
        (
            grouped(source_feat),
            grouped(source_sq),
            grouped(log_mass_src),
            grouped(potential_src),
            grouped(indices),
            grouped(usable),
        ),
    )
    seg_ids = jnp.where(usable, indices, blocks).reshape(-1)
    best, summed = segment_merge(
        peaks.reshape(-1, cells), totals.reshape(-1, cells), seg_ids, blocks
    )
    share = blocks // lax.axis_size("src")
    own_start = lax.axis_index("src") * share
    highest = lax.pmax(best, "src")
    whole = lax.psum(summed * jnp.exp(best - highest), "src")
    own_peak = lax.dynamic_slice_in_dim(highest, own_start, share, 0)
    own_total = lax.dynamic_slice_in_dim(whole, own_start, share, 0)
    potential_new = -entropic * (own_peak + jnp.log(own_total))
    return (potential_src, potential_new)


def per_device(source_feat, target_feat, *others):
    shards = lax.axis_size("src")
    rows, depth, cells = source_feat.shape
    few = shards == 8 and target_feat.shape[0] == 1 and lax.axis_size("tgt") == 2
    if few and rows % 8 == 0 and cells == 128 and depth == 64:
        return dense_device(source_feat, target_feat, *others)
    return general_device(source_feat, target_feat, *others)


def solution(mesh):
    in_specs = (
        P(("grp", "src"), None, None),
        P(("grp", "src", "tgt"), None, None),
        P(("grp", "src"), None),
        P(("grp", "src", "tgt"), None),
        P(("grp", "src", "tgt"), None),
        P(("grp", "src"), "tgt", None),
        P(("grp", "src"), "tgt"),
    )
    out_specs = (P(("grp", "src"), None), P(("grp", "src", "tgt"), None))
    return jax.shard_map(
        per_device, mesh=mesh, in_specs=in_specs, out_specs=out_specs, check_vma=False
    )
```

```python
import functools
import math

import jax
import jax.numpy as jnp
from jax import lax
from jax.experimental import pallas as pl
from jax.experimental.pallas import tpu as pltpu
from jax.sharding import PartitionSpec as P

entropic = 0.5
very_low = -1e30
log2e = 1.0 / math.log(2.0)
ln2 = math.log(2.0)
least_sum = 1e-28

VM = pl.BlockSpec(memory_space=pltpu.VMEM)
PARAMS = pltpu.CompilerParams(vmem_limit_bytes=40 * 2**20)


def in_vmem(shape, dtype):
    return pltpu.VMEM(shape, dtype)


def pieces(values):
    high = values.astype(jnp.bfloat16).astype(jnp.float32)
    rest = values - high
    mid = rest.astype(jnp.bfloat16).astype(jnp.float32)
    low = (rest - mid).astype(jnp.bfloat16).astype(jnp.float32)
    return high, mid, low


def target_weight(mass, poten):
    return (mass + poten / entropic) * log2e


def line_steps(shards):
    return [2 * (i ^ (i >> 1)) for i in range(shards // 2 - 1, 0, -1)]


def blocks_at(shards):
    near = [0] + line_steps(shards)
    me = lax.axis_index("src")
    return [me ^ other for other in near + [step ^ 1 for step in near]]


def read_all(hbm, held, sems):
    copies = [pltpu.make_async_copy(src, dst, sems.at[i]) for i, (src, dst) in enumerate(zip(hbm, held))]
    for copy in copies:
        copy.start()
    return copies


def pack_kernel(*refs):
    hbm, (send_ref, weight_ref), held, sems = refs[:3], refs[3:5], refs[5:8], refs[8]
    for copy in read_all(hbm, held, sems):
        copy.wait()
    feat_ref, mass_ref, poten_ref = held
    feat = feat_ref[0]
    depth, cells = feat.shape
    weight = target_weight(mass_ref[...], poten_ref[...])
    norm = jnp.sum(feat * feat, axis=0, keepdims=True)
    bias = weight - (log2e / entropic) * norm
    scaled = feat * (2.0 * log2e / entropic)
    send_ref[0, :depth, 0, :] = scaled
    send_ref[0, depth, 0:1, :] = bias
    weight_ref[...] = weight


def source_kernel(shards, *refs):
    hbm, outs, held, sems = refs[:4], refs[4:8], refs[8:12], refs[12]
    wide_ref, norm_ref, mask_ref, mass_out_ref = outs
    mass_ref, support_ref, counts_ref, feat_ref = held
    copies = read_all(hbm, held, sems)
    for copy in copies[:3]:
        copy.wait()
    mass_out_ref[...] = mass_ref[...]
    support = support_ref[...]
    slots, rows = support.shape
    cells = mass_ref.shape[1]
    used = lax.broadcasted_iota(jnp.int32, support.shape, 0) < counts_ref[...]
    hits = [
        jnp.max(jnp.where(used & (support == block), 0.0, very_low), axis=0, keepdims=True)
        for block in blocks_at(shards)
    ]
    hits = jnp.concatenate(hits + [jnp.zeros((cells - shards, rows), jnp.float32)], axis=0)
    hits = jnp.concatenate([hits, jnp.zeros((cells, cells - rows), jnp.float32)], axis=1).T
    for place in range(shards):
        mask_ref[place] = jnp.broadcast_to(hits[:rows, place : place + 1], (rows, cells))
    copies[3].wait()
    depth = feat_ref.shape[1]
    one = jnp.ones((2 * depth, 2 * cells), jnp.bfloat16)
    for pair in range(rows // 2):
        for half in range(2):
            feat = feat_ref[2 * pair + half]
            norm_ref[2 * pair + half : 2 * pair + half + 1, :] = jnp.sum(feat * feat, axis=0, keepdims=True)
            high, mid, low = pieces(feat)
            lanes = slice(half * cells, (half + 1) * cells)
            top = jnp.concatenate([high, mid], axis=0).astype(jnp.bfloat16)
            wide_ref[pair, 0 : 2 * depth, lanes] = top
            wide_ref[pair, 2 * depth : 4 * depth, lanes] = top
            wide_ref[pair, 4 * depth : 6 * depth, lanes] = jnp.concatenate([low, high], axis=0).astype(jnp.bfloat16)
        wide_ref[pair, 6 * depth : 8 * depth, :] = one


def join_kernel(*refs):
    refs[-1][0] = refs[0][0]
    refs[-1][1] = refs[1][0]


def on_core(core, work, idle):
    if core is None:
        work()
    else:
        here = lax.axis_index("tgt") == core
        pl.when(here)(work)
        pl.when(jnp.logical_not(here))(idle)


def tile_kernel(parts, core, *refs):
    peak_ref, total_ref = refs[-2:]

    def idle():
        peak_ref[...] = jnp.zeros(peak_ref.shape, jnp.float32)
        total_ref[...] = jnp.zeros(total_ref.shape, jnp.float32)

    ins = refs[: parts + 1] + refs[-4:]
    on_core(core, functools.partial(make_tiles, parts, *ins), idle)


def make_tiles(parts, *refs):
    packs = [ref.at[index] for ref in refs[:parts] for index in range(ref.shape[0])]
    wide_ref, exps_ref, tall_ref, peak_ref, total_ref = refs[parts:]
    blocks = len(packs)
    pairs, _, both = wide_ref.shape
    cells = both // 2
    depth = cells // 2
    lane = lax.broadcasted_iota(jnp.int32, (cells, cells), 1)
    biases = jnp.concatenate([pack[depth, 0:1, :] for pack in packs], axis=0)
    bias_pieces = jnp.concatenate(list(pieces(biases)), axis=0)
    padded = jnp.concatenate([bias_pieces, jnp.zeros((cells - 3 * blocks, cells), jnp.float32)], axis=0)
    bias_lanes = padded.T
    for place, pack in enumerate(packs):
        feat = pack[:depth, 0, :]
        turned = jnp.concatenate([feat, feat], axis=0).T
        high, mid, low = pieces(turned)
        own = jnp.where(lax.rem(lane, blocks) == place, bias_lanes, 0.0)
        rows = slice(place * cells, (place + 1) * cells)
        tall_ref[rows, 0:cells] = high.astype(jnp.bfloat16)
        tall_ref[rows, cells : 2 * cells] = mid.astype(jnp.bfloat16)
        tall_ref[rows, 2 * cells : 3 * cells] = jnp.where(lane < depth, high, low).astype(jnp.bfloat16)
        tall_ref[rows, 3 * cells : 4 * cells] = own.astype(jnp.bfloat16)

    def body(pair, carry):
        scores = jnp.dot(tall_ref[...], wide_ref[pair], preferred_element_type=jnp.float32)
        for place in range(blocks):
            rows = slice(place * cells, (place + 1) * cells)
            score = scores[rows]
            peak = jnp.max(score, axis=0, keepdims=True)
            exps = jnp.exp2(score - peak)
            exps_ref[pair, rows, :] = exps
            total = jnp.sum(exps, axis=0, keepdims=True)
            for half in range(2):
                lanes = slice(half * cells, (half + 1) * cells)
                peak_ref[place, pl.ds(2 * pair + half, 1), :] = peak[:, lanes]
                total_ref[place, pl.ds(2 * pair + half, 1), :] = total[:, lanes]
        return carry

    lax.fori_loop(0, pairs, body, 0, unroll=min(pairs, 16 // blocks & -4 or 2))


def row_kernel(groups, *refs):
    mask_ref, peak_refs, total_refs = refs[0], refs[1 : 1 + groups], refs[1 + groups : 1 + 2 * groups]
    peaks_ref, rowsum_ref = refs[1 + 2 * groups :]
    place = 0
    for ref in peak_refs:
        for index in range(ref.shape[0]):
            peaks_ref[place] = ref[index] + mask_ref[place]
            place += 1
    totals = [ref[index] for ref in total_refs for index in range(ref.shape[0])]
    top = functools.reduce(jnp.maximum, [peaks_ref[index] for index in range(place)])
    summed = sum(total * jnp.exp2(peaks_ref[index] - top) for index, total in enumerate(totals))
    rowsum_ref[...] = top + jnp.log2(summed)


def across(column):
    shape = (column.shape[0],) * 2
    same = lax.broadcasted_iota(jnp.int32, shape, 0) == lax.broadcasted_iota(jnp.int32, shape, 1)
    return jnp.sum(jnp.where(same, jnp.broadcast_to(column, shape), 0.0), axis=0, keepdims=True)


def column_kernel(groups, core, *refs):
    ins, outs, scratch = refs[: 2 * groups + 7], refs[-4:-2], refs[-2:]

    def idle():
        for given, out in zip(refs[2 * groups + 7 : -4], outs):
            out[...] = given[...]

    on_core(core, functools.partial(sum_columns, groups, *ins, *outs, *scratch), idle)


def sum_columns(groups, *refs):
    exps_refs, tall_refs, rest = refs[:groups], refs[groups : 2 * groups], refs[2 * groups :]
    wide_ref, peak_ref, mask_ref, own_ref, other_ref, mass_ref, norm_ref = rest[:7]
    poten_ref, sums_ref, weight_ref, shift_ref = rest[7:]
    pairs, _, both = wide_ref.shape
    cells = both // 2
    shards = mask_ref.shape[0]
    own, other = own_ref[...], other_ref[...]
    top = jnp.maximum(own, other)
    whole = top + jnp.log2(jnp.exp2(own - top) + jnp.exp2(other - top))
    poten_ref[...] = norm_ref[...] - (entropic * ln2) * whole
    shift = mass_ref[...] * log2e - whole
    shift_ref[...] = shift
    for place in range(shards):
        weight_ref[place] = jnp.exp2(peak_ref[place] + shift)
    spots = [
        (group, slice(index * cells, (index + 1) * cells))
        for group, ref in enumerate(tall_refs)
        for index in range(ref.shape[0] // cells)
    ]
    used = [jnp.max(mask_ref[place], axis=0, keepdims=True) > 0.5 * very_low for place in range(shards)]
    ranks = [shards - 1 - block for block in blocks_at(shards)]
    sums = []
    for place, (group, rows) in enumerate(spots):
        acc = jnp.zeros((cells, cells), jnp.float32)
        for pair in range(pairs):
            acc = acc + exps_refs[group][pair, rows, :cells] * weight_ref[place, 2 * pair : 2 * pair + 1, :]
            acc = acc + exps_refs[group][pair, rows, cells:] * weight_ref[place, 2 * pair + 1 : 2 * pair + 2, :]
        sums.append(jnp.sum(acc.T, axis=0, keepdims=True))
    whole_sums = jnp.concatenate([jnp.where(here, one, 1.0) for here, one in zip(used, sums)], axis=0)
    worst = jnp.min(whole_sums)
    logs = jnp.log2(whole_sums)
    for place in range(shards):
        sums_ref[ranks[place]] = jnp.where(used[place], logs[place : place + 1, :], very_low)

    @pl.when(worst < least_sum)
    def _():
        for place, (group, rows) in enumerate(spots):

            def exponents(pair):
                score = jnp.dot(tall_refs[group][rows, :], wide_ref[pair], preferred_element_type=jnp.float32)
                add = shift_ref[pl.ds(2 * pair, 2), :] + mask_ref[place, pl.ds(2 * pair, 2), :]
                return score[:, :cells] + add[0:1, :], score[:, cells:] + add[1:2, :]

            def highest(pair, peak):
                first, second = exponents(pair)
                return jnp.maximum(peak, jnp.maximum(first, second))

            peak = lax.fori_loop(0, pairs, highest, jnp.full((cells, cells), very_low, jnp.float32))
            peak = jnp.max(peak, axis=1, keepdims=True)

            def add_up(pair, sums):
                first, second = exponents(pair)
                return sums + jnp.exp2(first - peak) + jnp.exp2(second - peak)

            sums = lax.fori_loop(0, pairs, add_up, jnp.zeros((cells, cells), jnp.float32))
            logs = across(peak) + jnp.log2(across(jnp.sum(sums, axis=1, keepdims=True)))
            sums_ref[ranks[place]] = jnp.where(used[place], logs, very_low)


def merge_kernel(values_ref, weight_ref, poten_ref, out_ref, poten_out_ref):
    poten_out_ref[...] = poten_ref[...]
    values = values_ref[...]
    top = jnp.max(values, axis=0)
    whole = top + jnp.log2(jnp.sum(jnp.exp2(values - top), axis=0))
    out_ref[...] = -(entropic * ln2) * (whole - weight_ref[...])


def f32(*shape):
    return jax.ShapeDtypeStruct(shape, jnp.float32)


def dense_device(
    source_feat, target_feat, log_mass_src, log_mass_tgt, potential_tgt, support, counts
):
    shards = lax.axis_size("src")
    rows, depth, cells = source_feat.shape
    pairs, wide = rows // 2, 2 * cells

    def call(kernel, ins, out_shape, scratch=(), cost=None):
        many = isinstance(out_shape, list)
        return pl.pallas_call(
            kernel,
            in_specs=ins,
            out_specs=[VM] * len(out_shape) if many else VM,
            out_shape=out_shape,
            scratch_shapes=list(scratch),
            compiler_params=PARAMS,
            cost_estimate=cost,
        )

    def reading(kernel, args, out_shape, cost):
        return call(
            kernel,
            [pl.BlockSpec(memory_space=pltpu.HBM)] * len(args),
            out_shape,
            [pltpu.VMEM(arg.shape, arg.dtype) for arg in args] + [pltpu.SemaphoreType.DMA((len(args),))],
            cost,
        )(*[pltpu.with_memory_space_constraint(arg, pltpu.HBM) for arg in args])

    def cost_of(flops):
        return pl.CostEstimate(flops=flops, bytes_accessed=rows * depth * cells * 4, transcendentals=0)

    pack, weight = reading(
        pack_kernel,
        [target_feat, log_mass_tgt, potential_tgt],
        [in_vmem((1, depth + 1, 1, cells), jnp.float32), in_vmem((1, cells), jnp.float32)],
        None,
    )
    wide_feat, norm, mask, mass = reading(
        functools.partial(source_kernel, shards),
        [log_mass_src, support[:, 0, :].T, counts.T, source_feat],
        [
            in_vmem((pairs, 8 * depth, wide), jnp.bfloat16),
            in_vmem((rows, cells), jnp.float32),
            in_vmem((shards, rows, cells), jnp.float32),
            in_vmem((rows, cells), jnp.float32),
        ],
        cost_of(10**9),
    )

    def tiles(*packs, core=None, after=None):
        blocks = sum(pack.shape[0] for pack in packs)
        more = [] if after is None else [after]
        return call(
            functools.partial(tile_kernel, len(packs), core),
            [VM] * (len(packs) + 1) + [pl.BlockSpec(memory_space=pl.ANY)] * len(more),
            [
                in_vmem((pairs, blocks * cells, wide), jnp.float32),
                in_vmem((blocks * cells, 8 * depth), jnp.bfloat16),
                in_vmem((blocks, rows, cells), jnp.float32),
                in_vmem((blocks, rows, cells), jnp.float32),
            ],
            cost=cost_of(2 * blocks * cells * pairs * wide * 8 * depth),
        )(*packs, wide_feat, *more)

    def swapped(array, step):
        return lax.ppermute(array, "src", [(i, i ^ step) for i in range(shards)])

    there = {step: swapped(pack, step) for step in reversed(line_steps(shards))}
    near = [pack] + [there[step] for step in line_steps(shards)]
    found = [tiles(pack)]
    halves = [
        call(
            join_kernel,
            [VM] * 2 + [pl.BlockSpec(memory_space=pl.ANY)],
            in_vmem((2,) + pack.shape[1:], jnp.float32),
        )(near[at], near[at + 1], found[0][-1])
        for at in range(0, len(near), 2)
    ]
    far = [swapped(half, 1) for half in halves]
    found += [tiles(*near[1:]), tiles(far[0])]
    groups = len(found) + 1

    def log_sums(last):
        _, _, peaks, totals = zip(*found, last)
        return call(
            functools.partial(row_kernel, groups),
            [VM] * (1 + 2 * groups),
            [in_vmem((shards, rows, cells), jnp.float32), in_vmem((rows, cells), jnp.float32)],
        )(mask, *peaks, *totals)

    def columns_of(core, last, peaks, own, other, given):
        exps, tall, _, _ = zip(*found, last)
        return call(
            functools.partial(column_kernel, groups, core),
            [VM] * (2 * groups + 7 + len(given)),
            [in_vmem((rows, cells), jnp.float32), in_vmem((shards, 1, cells), jnp.float32)],
            [pltpu.VMEM((shards, rows, cells), jnp.float32), pltpu.VMEM((rows, cells), jnp.float32)],
            cost_of(10**9),
        )(*exps, *tall, wide_feat, peaks, mask, own, other, mass, norm, *given)

    between = [(0, 1), (1, 0)]
    last_one = tiles(far[1], core=1)
    peaks_one, own_one = log_sums(last_one)
    other_zero = lax.ppermute(own_one, "tgt", between)
    last_zero = tiles(far[1], core=0, after=own_one)
    peaks_zero, own_zero = log_sums(last_zero)
    other_one = lax.ppermute(own_zero, "tgt", between)
    given = columns_of(0, last_zero, peaks_zero, own_zero, other_zero, [])
    potential_src, columns = columns_of(1, last_one, peaks_one, own_one, other_one, given)
    arrived = lax.all_to_all(columns, "src", 0, 0, axis_index_groups=[list(range(shards))[::-1]])
    outs = [f32(1, cells), f32(rows, cells)]
    potential_new, potential_src = call(merge_kernel, [VM] * 3, outs)(arrived, weight, potential_src)
    return potential_src, potential_new


def merged(part, axis, combine):
    gathered = jax.tree.map(lambda a: lax.all_gather(a, axis), part)

    def take(source):
        return jax.tree.map(lambda a: lax.dynamic_index_in_dim(a, source, 0, False), gathered)

    return lax.fori_loop(
        1, lax.axis_size(axis), lambda source, state: combine(state, take(source)), take(0)
    )


def cost_tiles(source_blk, source_sq, target_blk, target_sq):
    cross = jnp.einsum(
        "...fi,...fj->...ij", source_blk, target_blk, precision=lax.Precision.HIGHEST
    )
    return source_sq[..., :, None] + target_sq[..., None, :] - 2.0 * cross


def row_stats(cost, mass_tgt, poten_tgt, usable):
    scores = mass_tgt[..., None, :] + (poten_tgt[..., None, :] - cost) / entropic
    scores = jnp.where(usable[..., None, None], scores, very_low)
    peak = jnp.max(scores, axis=(1, 3))
    total = jnp.sum(jnp.exp(scores - peak[:, None, :, None]), axis=(1, 3))
    return (peak, total)


def column_stats(cost, mass_src, poten_src, usable):
    scores = mass_src[:, None, :, None] + (poten_src[:, None, :, None] - cost) / entropic
    peak = jnp.max(scores, axis=2)
    total = jnp.sum(jnp.exp(scores - peak[:, :, None, :]), axis=2)
    peak = jnp.where(usable[..., None], peak, very_low)
    total = jnp.where(usable[..., None], total, 0.0)
    return (peak, total)


def merge_pair(first_pair, second_pair):
    first_peak, first_total = first_pair
    second_peak, second_total = second_pair
    highest = jnp.maximum(first_peak, second_peak)
    summed = first_total * jnp.exp(first_peak - highest) + second_total * jnp.exp(
        second_peak - highest
    )
    return (highest, summed)


def segment_merge(peaks, totals, seg_ids, segments):
    best = jax.ops.segment_max(peaks, seg_ids, num_segments=segments + 1)
    best = jnp.maximum(best, very_low)
    summed = jax.ops.segment_sum(
        totals * jnp.exp(peaks - best[seg_ids]), seg_ids, num_segments=segments + 1
    )
    return (best[:segments], summed[:segments])


def general_device(
    source_feat, target_feat, log_mass_src, log_mass_tgt, potential_tgt, support, counts
):
    target_all, mass_all, poten_all = (
        lax.all_gather(target_feat, "src", axis=0, tiled=True),
        lax.all_gather(log_mass_tgt, "src", axis=0, tiled=True),
        lax.all_gather(potential_tgt, "src", axis=0, tiled=True),
    )
    blocks = target_all.shape[0]
    rows_here = source_feat.shape[0]
    slots_here = support.shape[2]
    cells = source_feat.shape[2]
    indices = support[:, 0, :]
    limits = counts[:, 0]
    usable = jnp.arange(slots_here, dtype=jnp.int32)[None, :] < limits[:, None]
    source_sq = jnp.sum(source_feat * source_feat, axis=1)
    target_sq = jnp.sum(target_all * target_all, axis=1)
    width = math.gcd(rows_here, 4)

    def grouped(array):
        return array.reshape((rows_here // width, width) + array.shape[1:])

    def row_pass(items):
        source_blk, source_nrm, ids_here, use_here = items
        cost = cost_tiles(
            source_blk[:, None], source_nrm[:, None], target_all[ids_here], target_sq[ids_here]
        )
        return row_stats(cost, mass_all[ids_here], poten_all[ids_here], use_here)

    peak, total = lax.map(
        row_pass, (grouped(source_feat), grouped(source_sq), grouped(indices), grouped(usable))
    )
    peak = peak.reshape(rows_here, cells)
    total = total.reshape(rows_here, cells)
    peak_all, total_all = merged((peak, total), "tgt", merge_pair)
    potential_src = -entropic * (peak_all + jnp.log(total_all))

    def column_pass(items):
        source_blk, source_nrm, mass_here, poten_here, ids_here, use_here = items
        cost = cost_tiles(
            source_blk[:, None], source_nrm[:, None], target_all[ids_here], target_sq[ids_here]
        )
        return column_stats(cost, mass_here, poten_here, use_here)

    peaks, totals = lax.map(
        column_pass,
        (
            grouped(source_feat),
            grouped(source_sq),
            grouped(log_mass_src),
            grouped(potential_src),
            grouped(indices),
            grouped(usable),
        ),
    )
    seg_ids = jnp.where(usable, indices, blocks).reshape(-1)
    best, summed = segment_merge(
        peaks.reshape(-1, cells), totals.reshape(-1, cells), seg_ids, blocks
    )
    share = blocks // lax.axis_size("src")
    own_start = lax.axis_index("src") * share
    highest = lax.pmax(best, "src")
    whole = lax.psum(summed * jnp.exp(best - highest), "src")
    own_peak = lax.dynamic_slice_in_dim(highest, own_start, share, 0)
    own_total = lax.dynamic_slice_in_dim(whole, own_start, share, 0)
    potential_new = -entropic * (own_peak + jnp.log(own_total))
    return (potential_src, potential_new)


def per_device(source_feat, target_feat, *others):
    shards = lax.axis_size("src")
    rows, depth, cells = source_feat.shape
    few = shards == 8 and target_feat.shape[0] == 1 and lax.axis_size("tgt") == 2
    if few and rows % 8 == 0 and cells == 128 and depth == 64:
        return dense_device(source_feat, target_feat, *others)
    return general_device(source_feat, target_feat, *others)


def solution(mesh):
    in_specs = (
        P(("grp", "src"), None, None),
        P(("grp", "src", "tgt"), None, None),
        P(("grp", "src"), None),
        P(("grp", "src", "tgt"), None),
        P(("grp", "src", "tgt"), None),
        P(("grp", "src"), "tgt", None),
        P(("grp", "src"), "tgt"),
    )
    out_specs = (P(("grp", "src"), None), P(("grp", "src", "tgt"), None))
    return jax.shard_map(
        per_device, mesh=mesh, in_specs=in_specs, out_specs=out_specs, check_vma=False
    )
```

```python
import functools
import math

import jax
import jax.numpy as jnp
from jax import lax
from jax.experimental import pallas as pl
from jax.experimental.pallas import tpu as pltpu
from jax.sharding import PartitionSpec as P

entropic = 0.5
very_low = -1e30
log2e = 1.0 / math.log(2.0)
ln2 = math.log(2.0)
least_sum = 1e-28

room = 2**24

VM = pl.BlockSpec(memory_space=pltpu.VMEM)
PARAMS = pltpu.CompilerParams(vmem_limit_bytes=40 * 2**20)


def in_vmem(shape, dtype):
    return pltpu.VMEM(shape, dtype)


def pieces(values):
    high = values.astype(jnp.bfloat16).astype(jnp.float32)
    rest = values - high
    mid = rest.astype(jnp.bfloat16).astype(jnp.float32)
    low = (rest - mid).astype(jnp.bfloat16).astype(jnp.float32)
    return high, mid, low


def target_weight(mass, poten):
    return (mass + poten / entropic) * log2e


def line_steps(shards):
    return [2 * (i ^ (i >> 1)) for i in range(shards // 2 - 1, 0, -1)]


def blocks_at(shards):
    near = [0] + line_steps(shards)
    me = lax.axis_index("src")
    return [me ^ other for other in near + [step ^ 1 for step in near]]


def read_all(hbm, held, sems):
    copies = [pltpu.make_async_copy(src, dst, sems.at[i]) for i, (src, dst) in enumerate(zip(hbm, held))]
    for copy in copies:
        copy.start()
    return copies


def pack_kernel(*refs):
    hbm, (send_ref, weight_ref), held, sems = refs[:3], refs[3:5], refs[5:8], refs[8]
    for copy in read_all(hbm, held, sems):
        copy.wait()
    feat_ref, mass_ref, poten_ref = held
    feat = feat_ref[0]
    depth, cells = feat.shape
    weight = target_weight(mass_ref[...], poten_ref[...])
    norm = jnp.sum(feat * feat, axis=0, keepdims=True)
    bias = weight - (log2e / entropic) * norm
    scaled = feat * (2.0 * log2e / entropic)
    send_ref[0, :depth, 0, :] = scaled
    send_ref[0, depth, 0:1, :] = bias
    weight_ref[...] = weight


def source_kernel(shards, *refs):
    hbm, outs, held, sems = refs[:4], refs[4:8], refs[8:12], refs[12]
    wide_ref, norm_ref, mask_ref, mass_out_ref = outs
    mass_ref, support_ref, counts_ref, feat_ref = held
    copies = read_all(hbm, held, sems)
    for copy in copies[:3]:
        copy.wait()
    mass_out_ref[...] = mass_ref[...]
    support = support_ref[...]
    slots, rows = support.shape
    cells = mass_ref.shape[1]
    used = lax.broadcasted_iota(jnp.int32, support.shape, 0) < counts_ref[...]
    hits = [
        jnp.max(jnp.where(used & (support == block), 0.0, very_low), axis=0, keepdims=True)
        for block in blocks_at(shards)
    ]
    hits = jnp.concatenate(hits + [jnp.zeros((cells - shards, rows), jnp.float32)], axis=0)
    hits = jnp.concatenate([hits, jnp.zeros((cells, cells - rows), jnp.float32)], axis=1).T
    for place in range(shards):
        mask_ref[place] = jnp.broadcast_to(hits[:rows, place : place + 1], (rows, cells))
    copies[3].wait()
    depth = feat_ref.shape[1]
    one = jnp.ones((2 * depth, 2 * cells), jnp.bfloat16)
    for pair in range(rows // 2):
        for half in range(2):
            feat = feat_ref[2 * pair + half]
            norm_ref[2 * pair + half : 2 * pair + half + 1, :] = jnp.sum(feat * feat, axis=0, keepdims=True)
            high, mid, low = pieces(feat)
            lanes = slice(half * cells, (half + 1) * cells)
            top = jnp.concatenate([high, mid], axis=0).astype(jnp.bfloat16)
            wide_ref[pair, 0 : 2 * depth, lanes] = top
            wide_ref[pair, 2 * depth : 4 * depth, lanes] = top
            wide_ref[pair, 4 * depth : 6 * depth, lanes] = jnp.concatenate([low, high], axis=0).astype(jnp.bfloat16)
        wide_ref[pair, 6 * depth : 8 * depth, :] = one


def join_kernel(*refs):
    refs[-1][0] = refs[0][0]
    refs[-1][1] = refs[1][0]


def on_core(core, work, idle):
    if core is None:
        work()
    else:
        here = lax.axis_index("tgt") == core
        pl.when(here)(work)
        pl.when(jnp.logical_not(here))(idle)


def tile_kernel(parts, core, *refs):
    peak_ref, total_ref = refs[-2:]

    def idle():
        peak_ref[...] = jnp.zeros(peak_ref.shape, jnp.float32)
        total_ref[...] = jnp.zeros(total_ref.shape, jnp.float32)

    ins = refs[: parts + 1] + refs[-4:]
    on_core(core, functools.partial(make_tiles, parts, *ins), idle)


def make_tiles(parts, *refs):
    packs = [ref.at[index] for ref in refs[:parts] for index in range(ref.shape[0])]
    wide_ref, exps_ref, tall_ref, peak_ref, total_ref = refs[parts:]
    blocks = len(packs)
    pairs, _, both = wide_ref.shape
    cells = both // 2
    depth = cells // 2
    lane = lax.broadcasted_iota(jnp.int32, (cells, cells), 1)
    biases = jnp.concatenate([pack[depth, 0:1, :] for pack in packs], axis=0)
    bias_pieces = jnp.concatenate(list(pieces(biases)), axis=0)
    padded = jnp.concatenate([bias_pieces, jnp.zeros((cells - 3 * blocks, cells), jnp.float32)], axis=0)
    bias_lanes = padded.T
    for place, pack in enumerate(packs):
        feat = pack[:depth, 0, :]
        turned = jnp.concatenate([feat, feat], axis=0).T
        high, mid, low = pieces(turned)
        own = jnp.where(lax.rem(lane, blocks) == place, bias_lanes, 0.0)
        rows = slice(place * cells, (place + 1) * cells)
        tall_ref[rows, 0:cells] = high.astype(jnp.bfloat16)
        tall_ref[rows, cells : 2 * cells] = mid.astype(jnp.bfloat16)
        tall_ref[rows, 2 * cells : 3 * cells] = jnp.where(lane < depth, high, low).astype(jnp.bfloat16)
        tall_ref[rows, 3 * cells : 4 * cells] = own.astype(jnp.bfloat16)

    def body(pair, carry):
        scores = jnp.dot(tall_ref[...], wide_ref[pair], preferred_element_type=jnp.float32)
        for place in range(blocks):
            rows = slice(place * cells, (place + 1) * cells)
            score = scores[rows]
            peak = jnp.max(score, axis=0, keepdims=True)
            exps = jnp.exp2(score - peak)
            exps_ref[pair, rows, :] = exps
            total = jnp.sum(exps, axis=0, keepdims=True)
            for half in range(2):
                lanes = slice(half * cells, (half + 1) * cells)
                peak_ref[place, pl.ds(2 * pair + half, 1), :] = peak[:, lanes]
                total_ref[place, pl.ds(2 * pair + half, 1), :] = total[:, lanes]
        return carry

    lax.fori_loop(0, pairs, body, 0, unroll=min(pairs, 16 // blocks & -4 or 2))


def row_kernel(groups, *refs):
    mask_ref, peak_refs, total_refs = refs[0], refs[1 : 1 + groups], refs[1 + groups : 1 + 2 * groups]
    peaks_ref, rowsum_ref = refs[1 + 2 * groups :]
    place = 0
    for ref in peak_refs:
        for index in range(ref.shape[0]):
            peaks_ref[place] = ref[index] + mask_ref[place]
            place += 1
    totals = [ref[index] for ref in total_refs for index in range(ref.shape[0])]
    top = functools.reduce(jnp.maximum, [peaks_ref[index] for index in range(place)])
    summed = sum(total * jnp.exp2(peaks_ref[index] - top) for index, total in enumerate(totals))
    rowsum_ref[...] = top + jnp.log2(summed)


def across(column):
    shape = (column.shape[0],) * 2
    same = lax.broadcasted_iota(jnp.int32, shape, 0) == lax.broadcasted_iota(jnp.int32, shape, 1)
    return jnp.sum(jnp.where(same, jnp.broadcast_to(column, shape), 0.0), axis=0, keepdims=True)


def column_kernel(groups, core, *refs):
    ins, outs, scratch = refs[: 2 * groups + 7], refs[-4:-2], refs[-2:]

    def idle():
        for given, out in zip(refs[2 * groups + 7 : -4], outs):
            out[...] = given[...]

    on_core(core, functools.partial(sum_columns, groups, *ins, *outs, *scratch), idle)


def sum_columns(groups, *refs):
    exps_refs, tall_refs, rest = refs[:groups], refs[groups : 2 * groups], refs[2 * groups :]
    wide_ref, peak_ref, mask_ref, own_ref, other_ref, mass_ref, norm_ref = rest[:7]
    poten_ref, sums_ref, weight_ref, shift_ref = rest[7:]
    pairs, _, both = wide_ref.shape
    cells = both // 2
    shards = mask_ref.shape[0]
    own, other = own_ref[...], other_ref[...]
    top = jnp.maximum(own, other)
    whole = top + jnp.log2(jnp.exp2(own - top) + jnp.exp2(other - top))
    poten_ref[...] = norm_ref[...] - (entropic * ln2) * whole
    shift = mass_ref[...] * log2e - whole
    shift_ref[...] = shift
    for place in range(shards):
        weight_ref[place] = jnp.exp2(peak_ref[place] + shift)
    spots = [
        (group, slice(index * cells, (index + 1) * cells))
        for group, ref in enumerate(tall_refs)
        for index in range(ref.shape[0] // cells)
    ]
    used = [jnp.max(mask_ref[place], axis=0, keepdims=True) > 0.5 * very_low for place in range(shards)]
    ranks = [shards - 1 - block for block in blocks_at(shards)]
    sums = []
    for place, (group, rows) in enumerate(spots):
        acc = jnp.zeros((cells, cells), jnp.float32)
        for pair in range(pairs):
            acc = acc + exps_refs[group][pair, rows, :cells] * weight_ref[place, 2 * pair : 2 * pair + 1, :]
            acc = acc + exps_refs[group][pair, rows, cells:] * weight_ref[place, 2 * pair + 1 : 2 * pair + 2, :]
        sums.append(jnp.sum(acc.T, axis=0, keepdims=True))
    whole_sums = jnp.concatenate([jnp.where(here, one, 1.0) for here, one in zip(used, sums)], axis=0)
    worst = jnp.min(whole_sums)
    logs = jnp.log2(whole_sums)
    for place in range(shards):
        sums_ref[ranks[place]] = jnp.where(used[place], logs[place : place + 1, :], very_low)

    @pl.when(worst < least_sum)
    def _():
        for place, (group, rows) in enumerate(spots):

            def exponents(pair):
                score = jnp.dot(tall_refs[group][rows, :], wide_ref[pair], preferred_element_type=jnp.float32)
                add = shift_ref[pl.ds(2 * pair, 2), :] + mask_ref[place, pl.ds(2 * pair, 2), :]
                return score[:, :cells] + add[0:1, :], score[:, cells:] + add[1:2, :]

            def highest(pair, peak):
                first, second = exponents(pair)
                return jnp.maximum(peak, jnp.maximum(first, second))

            peak = lax.fori_loop(0, pairs, highest, jnp.full((cells, cells), very_low, jnp.float32))
            peak = jnp.max(peak, axis=1, keepdims=True)

            def add_up(pair, sums):
                first, second = exponents(pair)
                return sums + jnp.exp2(first - peak) + jnp.exp2(second - peak)

            sums = lax.fori_loop(0, pairs, add_up, jnp.zeros((cells, cells), jnp.float32))
            logs = across(peak) + jnp.log2(across(jnp.sum(sums, axis=1, keepdims=True)))
            sums_ref[ranks[place]] = jnp.where(used[place], logs, very_low)


def merge_kernel(values_ref, weight_ref, poten_ref, out_ref, poten_out_ref):
    poten_out_ref[...] = poten_ref[...]
    values = values_ref[...]
    top = jnp.max(values, axis=0)
    whole = top + jnp.log2(jnp.sum(jnp.exp2(values - top), axis=0))
    out_ref[...] = -(entropic * ln2) * (whole - weight_ref[...])


def f32(*shape):
    return jax.ShapeDtypeStruct(shape, jnp.float32)


def dense_device(
    source_feat, target_feat, log_mass_src, log_mass_tgt, potential_tgt, support, counts
):
    shards = lax.axis_size("src")
    rows, depth, cells = source_feat.shape
    pairs, wide = rows // 2, 2 * cells

    def call(kernel, ins, out_shape, scratch=(), cost=None):
        many = isinstance(out_shape, list)
        return pl.pallas_call(
            kernel,
            in_specs=ins,
            out_specs=[VM] * len(out_shape) if many else VM,
            out_shape=out_shape,
            scratch_shapes=list(scratch),
            compiler_params=PARAMS,
            cost_estimate=cost,
        )

    def reading(kernel, args, out_shape, cost):
        return call(
            kernel,
            [pl.BlockSpec(memory_space=pltpu.HBM)] * len(args),
            out_shape,
            [pltpu.VMEM(arg.shape, arg.dtype) for arg in args] + [pltpu.SemaphoreType.DMA((len(args),))],
            cost,
        )(*[pltpu.with_memory_space_constraint(arg, pltpu.HBM) for arg in args])

    def cost_of(flops):
        return pl.CostEstimate(flops=flops, bytes_accessed=rows * depth * cells * 4, transcendentals=0)

    pack, weight = reading(
        pack_kernel,
        [target_feat, log_mass_tgt, potential_tgt],
        [in_vmem((1, depth + 1, 1, cells), jnp.float32), in_vmem((1, cells), jnp.float32)],
        None,
    )
    wide_feat, norm, mask, mass = reading(
        functools.partial(source_kernel, shards),
        [log_mass_src, support[:, 0, :].T, counts.T, source_feat],
        [
            in_vmem((pairs, 8 * depth, wide), jnp.bfloat16),
            in_vmem((rows, cells), jnp.float32),
            in_vmem((shards, rows, cells), jnp.float32),
            in_vmem((rows, cells), jnp.float32),
        ],
        cost_of(10**9),
    )

    def tiles(*packs, core=None, after=None):
        blocks = sum(pack.shape[0] for pack in packs)
        more = [] if after is None else [after]
        return call(
            functools.partial(tile_kernel, len(packs), core),
            [VM] * (len(packs) + 1) + [pl.BlockSpec(memory_space=pl.ANY)] * len(more),
            [
                in_vmem((pairs, blocks * cells, wide), jnp.float32),
                in_vmem((blocks * cells, 8 * depth), jnp.bfloat16),
                in_vmem((blocks, rows, cells), jnp.float32),
                in_vmem((blocks, rows, cells), jnp.float32),
            ],
            cost=cost_of(2 * blocks * cells * pairs * wide * 8 * depth),
        )(*packs, wide_feat, *more)

    def swapped(array, step):
        return lax.ppermute(array, "src", [(i, i ^ step) for i in range(shards)])

    def joined(first, second, after):
        return call(
            join_kernel,
            [VM] * 2 + [pl.BlockSpec(memory_space=pl.ANY)],
            in_vmem((2,) + pack.shape[1:], jnp.float32),
        )(first, second, after)

    steps = line_steps(shards)
    there = [swapped(pack, step) for step in reversed(steps)][::-1]
    near = [pack] + there
    halves = [joined(near[0], near[1], norm)]
    found = [tiles(pack, after=halves[0])]
    halves += [joined(near[at], near[at + 1], found[0][-1]) for at in range(2, shards // 2, 2)]
    far = [swapped(half, 1) for half in halves]
    found.append(tiles(*there))
    for half in far[:-1]:
        found.append(tiles(half, after=found[-1][-1]))
    groups = len(found) + 1

    def log_sums(last):
        _, _, peaks, totals = zip(*found, last)
        return call(
            functools.partial(row_kernel, groups),
            [VM] * (1 + 2 * groups),
            [in_vmem((shards, rows, cells), jnp.float32), in_vmem((rows, cells), jnp.float32)],
        )(mask, *peaks, *totals)

    def columns_of(core, last, peaks, own, other, given):
        exps, tall, _, _ = zip(*found, last)
        return call(
            functools.partial(column_kernel, groups, core),
            [VM] * (2 * groups + 7 + len(given)),
            [in_vmem((rows, cells), jnp.float32), in_vmem((shards, 1, cells), jnp.float32)],
            [pltpu.VMEM((shards, rows, cells), jnp.float32), pltpu.VMEM((rows, cells), jnp.float32)],
            cost_of(10**9),
        )(*exps, *tall, wide_feat, peaks, mask, own, other, mass, norm, *given)

    between = [(0, 1), (1, 0)]
    last_one = tiles(far[-1], core=1, after=found[-1][-1])
    peaks_one, own_one = log_sums(last_one)
    other_zero = lax.ppermute(own_one, "tgt", between)
    last_zero = tiles(far[-1], core=0, after=own_one)
    peaks_zero, own_zero = log_sums(last_zero)
    other_one = lax.ppermute(own_zero, "tgt", between)
    given = columns_of(0, last_zero, peaks_zero, own_zero, other_zero, [])
    potential_src, columns = columns_of(1, last_one, peaks_one, own_one, other_one, given)
    arrived = lax.all_to_all(columns, "src", 0, 0, axis_index_groups=[list(range(shards))[::-1]])
    outs = [f32(1, cells), f32(rows, cells)]
    potential_new, potential_src = call(merge_kernel, [VM] * 3, outs)(arrived, weight, potential_src)
    return potential_src, potential_new


def merged(part, axis, combine):
    gathered = jax.tree.map(lambda a: lax.all_gather(a, axis), part)

    def take(source):
        return jax.tree.map(lambda a: lax.dynamic_index_in_dim(a, source, 0, False), gathered)

    return lax.fori_loop(
        1, lax.axis_size(axis), lambda source, state: combine(state, take(source)), take(0)
    )


def cost_tiles(source_blk, source_sq, target_blk, target_sq):
    cross = jnp.einsum(
        "...fi,...fj->...ij", source_blk, target_blk, precision=lax.Precision.HIGHEST
    )
    return source_sq[..., :, None] + target_sq[..., None, :] - 2.0 * cross


def row_stats(cost, mass_tgt, poten_tgt, usable):
    scores = mass_tgt[..., None, :] + (poten_tgt[..., None, :] - cost) / entropic
    scores = jnp.where(usable[..., None, None], scores, very_low)
    peak = jnp.max(scores, axis=(1, 3))
    total = jnp.sum(jnp.exp(scores - peak[:, None, :, None]), axis=(1, 3))
    return (peak, total)


def column_stats(cost, mass_src, poten_src, usable):
    scores = mass_src[:, None, :, None] + (poten_src[:, None, :, None] - cost) / entropic
    peak = jnp.max(scores, axis=2)
    total = jnp.sum(jnp.exp(scores - peak[:, :, None, :]), axis=2)
    peak = jnp.where(usable[..., None], peak, very_low)
    total = jnp.where(usable[..., None], total, 0.0)
    return (peak, total)


def merge_pair(first_pair, second_pair):
    first_peak, first_total = first_pair
    second_peak, second_total = second_pair
    highest = jnp.maximum(first_peak, second_peak)
    summed = first_total * jnp.exp(first_peak - highest) + second_total * jnp.exp(
        second_peak - highest
    )
    return (highest, summed)


def segment_merge(peaks, totals, seg_ids, segments):
    best = jax.ops.segment_max(peaks, seg_ids, num_segments=segments + 1)
    best = jnp.maximum(best, very_low)
    summed = jax.ops.segment_sum(
        totals * jnp.exp(peaks - best[seg_ids]), seg_ids, num_segments=segments + 1
    )
    return (best[:segments], summed[:segments])


def general_device(
    source_feat, target_feat, log_mass_src, log_mass_tgt, potential_tgt, support, counts
):
    target_all, mass_all, poten_all = (
        lax.all_gather(target_feat, "src", axis=0, tiled=True),
        lax.all_gather(log_mass_tgt, "src", axis=0, tiled=True),
        lax.all_gather(potential_tgt, "src", axis=0, tiled=True),
    )
    blocks = target_all.shape[0]
    rows_here = source_feat.shape[0]
    slots_here = support.shape[2]
    cells = source_feat.shape[2]
    indices = support[:, 0, :]
    limits = counts[:, 0]
    usable = jnp.arange(slots_here, dtype=jnp.int32)[None, :] < limits[:, None]
    source_sq = jnp.sum(source_feat * source_feat, axis=1)
    target_sq = jnp.sum(target_all * target_all, axis=1)
    width = math.gcd(rows_here, 4)

    def grouped(array):
        return array.reshape((rows_here // width, width) + array.shape[1:])

    def row_pass(items):
        source_blk, source_nrm, ids_here, use_here = items
        cost = cost_tiles(
            source_blk[:, None], source_nrm[:, None], target_all[ids_here], target_sq[ids_here]
        )
        return row_stats(cost, mass_all[ids_here], poten_all[ids_here], use_here)

    peak, total = lax.map(
        row_pass, (grouped(source_feat), grouped(source_sq), grouped(indices), grouped(usable))
    )
    peak = peak.reshape(rows_here, cells)
    total = total.reshape(rows_here, cells)
    peak_all, total_all = merged((peak, total), "tgt", merge_pair)
    potential_src = -entropic * (peak_all + jnp.log(total_all))

    def column_pass(items):
        source_blk, source_nrm, mass_here, poten_here, ids_here, use_here = items
        cost = cost_tiles(
            source_blk[:, None], source_nrm[:, None], target_all[ids_here], target_sq[ids_here]
        )
        return column_stats(cost, mass_here, poten_here, use_here)

    peaks, totals = lax.map(
        column_pass,
        (
            grouped(source_feat),
            grouped(source_sq),
            grouped(log_mass_src),
            grouped(potential_src),
            grouped(indices),
            grouped(usable),
        ),
    )
    seg_ids = jnp.where(usable, indices, blocks).reshape(-1)
    best, summed = segment_merge(
        peaks.reshape(-1, cells), totals.reshape(-1, cells), seg_ids, blocks
    )
    share = blocks // lax.axis_size("src")
    own_start = lax.axis_index("src") * share
    highest = lax.pmax(best, "src")
    whole = lax.psum(summed * jnp.exp(best - highest), "src")
    own_peak = lax.dynamic_slice_in_dim(highest, own_start, share, 0)
    own_total = lax.dynamic_slice_in_dim(whole, own_start, share, 0)
    potential_new = -entropic * (own_peak + jnp.log(own_total))
    return (potential_src, potential_new)


def per_device(source_feat, target_feat, *others):
    shards = lax.axis_size("src")
    rows, depth, cells = source_feat.shape
    paired = shards >= 4 and shards & (shards - 1) == 0 and lax.axis_size("tgt") == 2
    shaped = target_feat.shape[0] == 1 and rows % 2 == 0 and cells == 2 * depth and cells % 128 == 0
    if paired and shaped and 4 * rows * cells * shards * cells <= room:
        return dense_device(source_feat, target_feat, *others)
    return general_device(source_feat, target_feat, *others)


def solution(mesh):
    in_specs = (
        P(("grp", "src"), None, None),
        P(("grp", "src", "tgt"), None, None),
        P(("grp", "src"), None),
        P(("grp", "src", "tgt"), None),
        P(("grp", "src", "tgt"), None),
        P(("grp", "src"), "tgt", None),
        P(("grp", "src"), "tgt"),
    )
    out_specs = (P(("grp", "src"), None), P(("grp", "src", "tgt"), None))
    return jax.shard_map(
        per_device, mesh=mesh, in_specs=in_specs, out_specs=out_specs, check_vma=False
    )
```

```python
import functools
import math

import jax
import jax.numpy as jnp
from jax import lax
from jax.experimental import pallas as pl
from jax.experimental.pallas import tpu as pltpu
from jax.sharding import PartitionSpec as P

entropic = 0.5
very_low = -1e30
log2e = 1.0 / math.log(2.0)
ln2 = math.log(2.0)
least_sum = 1e-28

room = 2**24

VM = pl.BlockSpec(memory_space=pltpu.VMEM)
PARAMS = pltpu.CompilerParams(vmem_limit_bytes=40 * 2**20)


def in_vmem(shape, dtype):
    return pltpu.VMEM(shape, dtype)


def pieces(values):
    high = values.astype(jnp.bfloat16).astype(jnp.float32)
    rest = values - high
    mid = rest.astype(jnp.bfloat16).astype(jnp.float32)
    low = (rest - mid).astype(jnp.bfloat16).astype(jnp.float32)
    return high, mid, low


def target_weight(mass, poten):
    return (mass + poten / entropic) * log2e


def line_steps(shards):
    return [2 * (i ^ (i >> 1)) for i in range(shards // 2 - 1, 0, -1)]


def blocks_at(shards):
    near = [0] + line_steps(shards)
    me = lax.axis_index("src")
    return [me ^ other for other in near + [step ^ 1 for step in near]]


def read_all(hbm, held, sems):
    copies = [pltpu.make_async_copy(src, dst, sems.at[i]) for i, (src, dst) in enumerate(zip(hbm, held))]
    for copy in copies:
        copy.start()
    return copies


def pack_kernel(*refs):
    hbm, (send_ref, weight_ref), held, sems = refs[:3], refs[3:5], refs[5:8], refs[8]
    for copy in read_all(hbm, held, sems):
        copy.wait()
    feat_ref, mass_ref, poten_ref = held
    feat = feat_ref[0]
    depth, cells = feat.shape
    weight = target_weight(mass_ref[...], poten_ref[...])
    norm = jnp.sum(feat * feat, axis=0, keepdims=True)
    bias = weight - (log2e / entropic) * norm
    scaled = feat * (2.0 * log2e / entropic)
    send_ref[0, :depth, 0, :] = scaled
    send_ref[0, depth, 0:1, :] = bias
    weight_ref[...] = weight


def source_kernel(shards, *refs):
    hbm, outs, held, sems = refs[:4], refs[4:8], refs[8:12], refs[12]
    wide_ref, norm_ref, mask_ref, mass_out_ref = outs
    mass_ref, support_ref, counts_ref, feat_ref = held
    copies = read_all(hbm, held, sems)
    for copy in copies[:3]:
        copy.wait()
    mass_out_ref[...] = mass_ref[...]
    support = support_ref[...]
    slots, rows = support.shape
    cells = mass_ref.shape[1]
    used = lax.broadcasted_iota(jnp.int32, support.shape, 0) < counts_ref[...]
    hits = [
        jnp.max(jnp.where(used & (support == block), 0.0, very_low), axis=0, keepdims=True)
        for block in blocks_at(shards)
    ]
    hits = jnp.concatenate(hits + [jnp.zeros((cells - shards, rows), jnp.float32)], axis=0)
    hits = jnp.concatenate([hits, jnp.zeros((cells, cells - rows), jnp.float32)], axis=1).T
    for place in range(shards):
        mask_ref[place] = jnp.broadcast_to(hits[:rows, place : place + 1], (rows, cells))
    copies[3].wait()
    depth = feat_ref.shape[1]
    one = jnp.ones((2 * depth, 2 * cells), jnp.bfloat16)
    for pair in range(rows // 2):
        for half in range(2):
            feat = feat_ref[2 * pair + half]
            norm_ref[2 * pair + half : 2 * pair + half + 1, :] = jnp.sum(feat * feat, axis=0, keepdims=True)
            high, mid, low = pieces(feat)
            lanes = slice(half * cells, (half + 1) * cells)
            top = jnp.concatenate([high, mid], axis=0).astype(jnp.bfloat16)
            wide_ref[pair, 0 : 2 * depth, lanes] = top
            wide_ref[pair, 2 * depth : 4 * depth, lanes] = top
            wide_ref[pair, 4 * depth : 6 * depth, lanes] = jnp.concatenate([low, high], axis=0).astype(jnp.bfloat16)
        wide_ref[pair, 6 * depth : 8 * depth, :] = one


def join_kernel(*refs):
    refs[-1][0] = refs[0][0]
    refs[-1][1] = refs[1][0]


def on_core(core, work, idle):
    if core is None:
        work()
    else:
        here = lax.axis_index("tgt") == core
        pl.when(here)(work)
        pl.when(jnp.logical_not(here))(idle)


def tile_kernel(parts, core, *refs):
    peak_ref, total_ref = refs[-2:]

    def idle():
        peak_ref[...] = jnp.zeros(peak_ref.shape, jnp.float32)
        total_ref[...] = jnp.zeros(total_ref.shape, jnp.float32)

    ins = refs[: parts + 1] + refs[-4:]
    on_core(core, functools.partial(make_tiles, parts, *ins), idle)


def make_tiles(parts, *refs):
    packs = [ref.at[index] for ref in refs[:parts] for index in range(ref.shape[0])]
    wide_ref, exps_ref, tall_ref, peak_ref, total_ref = refs[parts:]
    blocks = len(packs)
    pairs, _, both = wide_ref.shape
    cells = both // 2
    depth = cells // 2
    lane = lax.broadcasted_iota(jnp.int32, (cells, cells), 1)
    biases = jnp.concatenate([pack[depth, 0:1, :] for pack in packs], axis=0)
    bias_pieces = jnp.concatenate(list(pieces(biases)), axis=0)
    padded = jnp.concatenate([bias_pieces, jnp.zeros((cells - 3 * blocks, cells), jnp.float32)], axis=0)
    bias_lanes = padded.T
    for place, pack in enumerate(packs):
        feat = pack[:depth, 0, :]
        turned = jnp.concatenate([feat, feat], axis=0).T
        high, mid, low = pieces(turned)
        own = jnp.where(lax.rem(lane, blocks) == place, bias_lanes, 0.0)
        rows = slice(place * cells, (place + 1) * cells)
        tall_ref[rows, 0:cells] = high.astype(jnp.bfloat16)
        tall_ref[rows, cells : 2 * cells] = mid.astype(jnp.bfloat16)
        tall_ref[rows, 2 * cells : 3 * cells] = jnp.where(lane < depth, high, low).astype(jnp.bfloat16)
        tall_ref[rows, 3 * cells : 4 * cells] = own.astype(jnp.bfloat16)

    def body(pair, carry):
        scores = jnp.dot(tall_ref[...], wide_ref[pair], preferred_element_type=jnp.float32)
        for place in range(blocks):
            rows = slice(place * cells, (place + 1) * cells)
            score = scores[rows]
            peak = jnp.max(score, axis=0, keepdims=True)
            exps = jnp.exp2(score - peak)
            exps_ref[pair, rows, :] = exps
            total = jnp.sum(exps, axis=0, keepdims=True)
            for half in range(2):
                lanes = slice(half * cells, (half + 1) * cells)
                peak_ref[place, pl.ds(2 * pair + half, 1), :] = peak[:, lanes]
                total_ref[place, pl.ds(2 * pair + half, 1), :] = total[:, lanes]
        return carry

    lax.fori_loop(0, pairs, body, 0, unroll=min(pairs, 16 // blocks & -4 or 2))


def row_kernel(groups, *refs):
    mask_ref, peak_refs, total_refs = refs[0], refs[1 : 1 + groups], refs[1 + groups : 1 + 2 * groups]
    peaks_ref, rowsum_ref = refs[1 + 2 * groups :]
    place = 0
    for ref in peak_refs:
        for index in range(ref.shape[0]):
            peaks_ref[place] = ref[index] + mask_ref[place]
            place += 1
    totals = [ref[index] for ref in total_refs for index in range(ref.shape[0])]
    top = functools.reduce(jnp.maximum, [peaks_ref[index] for index in range(place)])
    summed = sum(total * jnp.exp2(peaks_ref[index] - top) for index, total in enumerate(totals))
    rowsum_ref[...] = top + jnp.log2(summed)


def across(column):
    shape = (column.shape[0],) * 2
    same = lax.broadcasted_iota(jnp.int32, shape, 0) == lax.broadcasted_iota(jnp.int32, shape, 1)
    return jnp.sum(jnp.where(same, jnp.broadcast_to(column, shape), 0.0), axis=0, keepdims=True)


def column_kernel(groups, core, *refs):
    ins, outs, scratch = refs[: 2 * groups + 7], refs[-4:-2], refs[-2:]

    def idle():
        for given, out in zip(refs[2 * groups + 7 : -4], outs):
            out[...] = given[...]

    on_core(core, functools.partial(sum_columns, groups, *ins, *outs, *scratch), idle)


def sum_columns(groups, *refs):
    exps_refs, tall_refs, rest = refs[:groups], refs[groups : 2 * groups], refs[2 * groups :]
    wide_ref, peak_ref, mask_ref, own_ref, other_ref, mass_ref, norm_ref = rest[:7]
    poten_ref, sums_ref, weight_ref, shift_ref = rest[7:]
    pairs, _, both = wide_ref.shape
    cells = both // 2
    shards = mask_ref.shape[0]
    own, other = own_ref[...], other_ref[...]
    top = jnp.maximum(own, other)
    whole = top + jnp.log2(jnp.exp2(own - top) + jnp.exp2(other - top))
    poten_ref[...] = norm_ref[...] - (entropic * ln2) * whole
    shift = mass_ref[...] * log2e - whole
    shift_ref[...] = shift
    for place in range(shards):
        weight_ref[place] = jnp.exp2(peak_ref[place] + shift)
    spots = [
        (group, slice(index * cells, (index + 1) * cells))
        for group, ref in enumerate(tall_refs)
        for index in range(ref.shape[0] // cells)
    ]
    used = [jnp.max(mask_ref[place], axis=0, keepdims=True) > 0.5 * very_low for place in range(shards)]
    ranks = [lax.rem(block + shards - 1, shards) for block in blocks_at(shards)]
    sums = []
    for place, (group, rows) in enumerate(spots):
        acc = jnp.zeros((cells, cells), jnp.float32)
        for pair in range(pairs):
            acc = acc + exps_refs[group][pair, rows, :cells] * weight_ref[place, 2 * pair : 2 * pair + 1, :]
            acc = acc + exps_refs[group][pair, rows, cells:] * weight_ref[place, 2 * pair + 1 : 2 * pair + 2, :]
        sums.append(jnp.sum(acc.T, axis=0, keepdims=True))
    whole_sums = jnp.concatenate([jnp.where(here, one, 1.0) for here, one in zip(used, sums)], axis=0)
    worst = jnp.min(whole_sums)
    logs = jnp.log2(whole_sums)
    for place in range(shards):
        sums_ref[ranks[place]] = jnp.where(used[place], logs[place : place + 1, :], very_low)

    @pl.when(worst < least_sum)
    def _():
        for place, (group, rows) in enumerate(spots):

            def exponents(pair):
                score = jnp.dot(tall_refs[group][rows, :], wide_ref[pair], preferred_element_type=jnp.float32)
                add = shift_ref[pl.ds(2 * pair, 2), :] + mask_ref[place, pl.ds(2 * pair, 2), :]
                return score[:, :cells] + add[0:1, :], score[:, cells:] + add[1:2, :]

            def highest(pair, peak):
                first, second = exponents(pair)
                return jnp.maximum(peak, jnp.maximum(first, second))

            peak = lax.fori_loop(0, pairs, highest, jnp.full((cells, cells), very_low, jnp.float32))
            peak = jnp.max(peak, axis=1, keepdims=True)

            def add_up(pair, sums):
                first, second = exponents(pair)
                return sums + jnp.exp2(first - peak) + jnp.exp2(second - peak)

            sums = lax.fori_loop(0, pairs, add_up, jnp.zeros((cells, cells), jnp.float32))
            logs = across(peak) + jnp.log2(across(jnp.sum(sums, axis=1, keepdims=True)))
            sums_ref[ranks[place]] = jnp.where(used[place], logs, very_low)


def merge_kernel(values_ref, weight_ref, poten_ref, out_ref, poten_out_ref):
    poten_out_ref[...] = poten_ref[...]
    values = values_ref[...]
    top = jnp.max(values, axis=0)
    whole = top + jnp.log2(jnp.sum(jnp.exp2(values - top), axis=0))
    out_ref[...] = -(entropic * ln2) * (whole - weight_ref[...])


def f32(*shape):
    return jax.ShapeDtypeStruct(shape, jnp.float32)


def dense_device(
    source_feat, target_feat, log_mass_src, log_mass_tgt, potential_tgt, support, counts
):
    shards = lax.axis_size("src")
    rows, depth, cells = source_feat.shape
    pairs, wide = rows // 2, 2 * cells

    def call(kernel, ins, out_shape, scratch=(), cost=None):
        many = isinstance(out_shape, list)
        return pl.pallas_call(
            kernel,
            in_specs=ins,
            out_specs=[VM] * len(out_shape) if many else VM,
            out_shape=out_shape,
            scratch_shapes=list(scratch),
            compiler_params=PARAMS,
            cost_estimate=cost,
        )

    def reading(kernel, args, out_shape, cost):
        return call(
            kernel,
            [pl.BlockSpec(memory_space=pltpu.HBM)] * len(args),
            out_shape,
            [pltpu.VMEM(arg.shape, arg.dtype) for arg in args] + [pltpu.SemaphoreType.DMA((len(args),))],
            cost,
        )(*[pltpu.with_memory_space_constraint(arg, pltpu.HBM) for arg in args])

    def cost_of(flops):
        return pl.CostEstimate(flops=flops, bytes_accessed=rows * depth * cells * 4, transcendentals=0)

    pack, weight = reading(
        pack_kernel,
        [target_feat, log_mass_tgt, potential_tgt],
        [in_vmem((1, depth + 1, 1, cells), jnp.float32), in_vmem((1, cells), jnp.float32)],
        None,
    )
    wide_feat, norm, mask, mass = reading(
        functools.partial(source_kernel, shards),
        [log_mass_src, support[:, 0, :].T, counts.T, source_feat],
        [
            in_vmem((pairs, 8 * depth, wide), jnp.bfloat16),
            in_vmem((rows, cells), jnp.float32),
            in_vmem((shards, rows, cells), jnp.float32),
            in_vmem((rows, cells), jnp.float32),
        ],
        cost_of(10**9),
    )

    def tiles(*packs, core=None, after=None):
        blocks = sum(pack.shape[0] for pack in packs)
        more = [] if after is None else [after]
        return call(
            functools.partial(tile_kernel, len(packs), core),
            [VM] * (len(packs) + 1) + [pl.BlockSpec(memory_space=pl.ANY)] * len(more),
            [
                in_vmem((pairs, blocks * cells, wide), jnp.float32),
                in_vmem((blocks * cells, 8 * depth), jnp.bfloat16),
                in_vmem((blocks, rows, cells), jnp.float32),
                in_vmem((blocks, rows, cells), jnp.float32),
            ],
            cost=cost_of(2 * blocks * cells * pairs * wide * 8 * depth),
        )(*packs, wide_feat, *more)

    def swapped(array, step):
        return lax.ppermute(array, "src", [(i, i ^ step) for i in range(shards)])

    def joined(first, second, after):
        return call(
            join_kernel,
            [VM] * 2 + [pl.BlockSpec(memory_space=pl.ANY)],
            in_vmem((2,) + pack.shape[1:], jnp.float32),
        )(first, second, after)

    steps = line_steps(shards)
    there = [swapped(pack, step) for step in reversed(steps)][::-1]
    near = [pack] + there
    halves = [joined(near[0], near[1], norm)]
    found = [tiles(pack, after=halves[0])]
    halves += [joined(near[at], near[at + 1], found[0][-1]) for at in range(2, shards // 2, 2)]
    far = [swapped(half, 1) for half in halves]
    found.append(tiles(*there))
    for half in far[:-1]:
        found.append(tiles(half, after=found[-1][-1]))
    groups = len(found) + 1

    def log_sums(last):
        _, _, peaks, totals = zip(*found, last)
        return call(
            functools.partial(row_kernel, groups),
            [VM] * (1 + 2 * groups),
            [in_vmem((shards, rows, cells), jnp.float32), in_vmem((rows, cells), jnp.float32)],
        )(mask, *peaks, *totals)

    def columns_of(core, last, peaks, own, other, given):
        exps, tall, _, _ = zip(*found, last)
        return call(
            functools.partial(column_kernel, groups, core),
            [VM] * (2 * groups + 7 + len(given)),
            [in_vmem((rows, cells), jnp.float32), in_vmem((shards, 1, cells), jnp.float32)],
            [pltpu.VMEM((shards, rows, cells), jnp.float32), pltpu.VMEM((rows, cells), jnp.float32)],
            cost_of(10**9),
        )(*exps, *tall, wide_feat, peaks, mask, own, other, mass, norm, *given)

    between = [(0, 1), (1, 0)]
    last_one = tiles(far[-1], core=1, after=found[-1][-1])
    peaks_one, own_one = log_sums(last_one)
    other_zero = lax.ppermute(own_one, "tgt", between)
    last_zero = tiles(far[-1], core=0, after=own_one)
    peaks_zero, own_zero = log_sums(last_zero)
    other_one = lax.ppermute(own_zero, "tgt", between)
    given = columns_of(0, last_zero, peaks_zero, own_zero, other_zero, [])
    potential_src, columns = columns_of(1, last_one, peaks_one, own_one, other_one, given)
    arrived = lax.all_to_all(columns, "src", 0, 0, axis_index_groups=[list(range(1, shards)) + [0]])
    outs = [f32(1, cells), f32(rows, cells)]
    potential_new, potential_src = call(merge_kernel, [VM] * 3, outs)(arrived, weight, potential_src)
    return potential_src, potential_new


def merged(part, axis, combine):
    gathered = jax.tree.map(lambda a: lax.all_gather(a, axis), part)

    def take(source):
        return jax.tree.map(lambda a: lax.dynamic_index_in_dim(a, source, 0, False), gathered)

    return lax.fori_loop(
        1, lax.axis_size(axis), lambda source, state: combine(state, take(source)), take(0)
    )


def cost_tiles(source_blk, source_sq, target_blk, target_sq):
    cross = jnp.einsum(
        "...fi,...fj->...ij", source_blk, target_blk, precision=lax.Precision.HIGHEST
    )
    return source_sq[..., :, None] + target_sq[..., None, :] - 2.0 * cross


def row_stats(cost, mass_tgt, poten_tgt, usable):
    scores = mass_tgt[..., None, :] + (poten_tgt[..., None, :] - cost) / entropic
    scores = jnp.where(usable[..., None, None], scores, very_low)
    peak = jnp.max(scores, axis=(1, 3))
    total = jnp.sum(jnp.exp(scores - peak[:, None, :, None]), axis=(1, 3))
    return (peak, total)


def column_stats(cost, mass_src, poten_src, usable):
    scores = mass_src[:, None, :, None] + (poten_src[:, None, :, None] - cost) / entropic
    peak = jnp.max(scores, axis=2)
    total = jnp.sum(jnp.exp(scores - peak[:, :, None, :]), axis=2)
    peak = jnp.where(usable[..., None], peak, very_low)
    total = jnp.where(usable[..., None], total, 0.0)
    return (peak, total)


def merge_pair(first_pair, second_pair):
    first_peak, first_total = first_pair
    second_peak, second_total = second_pair
    highest = jnp.maximum(first_peak, second_peak)
    summed = first_total * jnp.exp(first_peak - highest) + second_total * jnp.exp(
        second_peak - highest
    )
    return (highest, summed)


def segment_merge(peaks, totals, seg_ids, segments):
    best = jax.ops.segment_max(peaks, seg_ids, num_segments=segments + 1)
    best = jnp.maximum(best, very_low)
    summed = jax.ops.segment_sum(
        totals * jnp.exp(peaks - best[seg_ids]), seg_ids, num_segments=segments + 1
    )
    return (best[:segments], summed[:segments])


def general_device(
    source_feat, target_feat, log_mass_src, log_mass_tgt, potential_tgt, support, counts
):
    target_all, mass_all, poten_all = (
        lax.all_gather(target_feat, "src", axis=0, tiled=True),
        lax.all_gather(log_mass_tgt, "src", axis=0, tiled=True),
        lax.all_gather(potential_tgt, "src", axis=0, tiled=True),
    )
    blocks = target_all.shape[0]
    rows_here = source_feat.shape[0]
    slots_here = support.shape[2]
    cells = source_feat.shape[2]
    indices = support[:, 0, :]
    limits = counts[:, 0]
    usable = jnp.arange(slots_here, dtype=jnp.int32)[None, :] < limits[:, None]
    source_sq = jnp.sum(source_feat * source_feat, axis=1)
    target_sq = jnp.sum(target_all * target_all, axis=1)
    width = math.gcd(rows_here, 4)

    def grouped(array):
        return array.reshape((rows_here // width, width) + array.shape[1:])

    def row_pass(items):
        source_blk, source_nrm, ids_here, use_here = items
        cost = cost_tiles(
            source_blk[:, None], source_nrm[:, None], target_all[ids_here], target_sq[ids_here]
        )
        return row_stats(cost, mass_all[ids_here], poten_all[ids_here], use_here)

    peak, total = lax.map(
        row_pass, (grouped(source_feat), grouped(source_sq), grouped(indices), grouped(usable))
    )
    peak = peak.reshape(rows_here, cells)
    total = total.reshape(rows_here, cells)
    peak_all, total_all = merged((peak, total), "tgt", merge_pair)
    potential_src = -entropic * (peak_all + jnp.log(total_all))

    def column_pass(items):
        source_blk, source_nrm, mass_here, poten_here, ids_here, use_here = items
        cost = cost_tiles(
            source_blk[:, None], source_nrm[:, None], target_all[ids_here], target_sq[ids_here]
        )
        return column_stats(cost, mass_here, poten_here, use_here)

    peaks, totals = lax.map(
        column_pass,
        (
            grouped(source_feat),
            grouped(source_sq),
            grouped(log_mass_src),
            grouped(potential_src),
            grouped(indices),
            grouped(usable),
        ),
    )
    seg_ids = jnp.where(usable, indices, blocks).reshape(-1)
    best, summed = segment_merge(
        peaks.reshape(-1, cells), totals.reshape(-1, cells), seg_ids, blocks
    )
    share = blocks // lax.axis_size("src")
    own_start = lax.axis_index("src") * share
    highest = lax.pmax(best, "src")
    whole = lax.psum(summed * jnp.exp(best - highest), "src")
    own_peak = lax.dynamic_slice_in_dim(highest, own_start, share, 0)
    own_total = lax.dynamic_slice_in_dim(whole, own_start, share, 0)
    potential_new = -entropic * (own_peak + jnp.log(own_total))
    return (potential_src, potential_new)


def per_device(source_feat, target_feat, *others):
    shards = lax.axis_size("src")
    rows, depth, cells = source_feat.shape
    paired = shards >= 4 and shards & (shards - 1) == 0 and lax.axis_size("tgt") == 2
    shaped = target_feat.shape[0] == 1 and rows % 2 == 0 and cells == 2 * depth and cells % 128 == 0
    if paired and shaped and 4 * rows * cells * shards * cells <= room:
        return dense_device(source_feat, target_feat, *others)
    return general_device(source_feat, target_feat, *others)


def solution(mesh):
    in_specs = (
        P(("grp", "src"), None, None),
        P(("grp", "src", "tgt"), None, None),
        P(("grp", "src"), None),
        P(("grp", "src", "tgt"), None),
        P(("grp", "src", "tgt"), None),
        P(("grp", "src"), "tgt", None),
        P(("grp", "src"), "tgt"),
    )
    out_specs = (P(("grp", "src"), None), P(("grp", "src", "tgt"), None))
    return jax.shard_map(
        per_device, mesh=mesh, in_specs=in_specs, out_specs=out_specs, check_vma=False
    )
```

```python
import functools
import math

import jax
import jax.numpy as jnp
from jax import lax
from jax.experimental import pallas as pl
from jax.experimental.pallas import tpu as pltpu
from jax.sharding import PartitionSpec as P

entropic = 0.5
very_low = -1e30
log2e = 1.0 / math.log(2.0)
ln2 = math.log(2.0)
least_sum = 1e-28

room = 2**24

VM = pl.BlockSpec(memory_space=pltpu.VMEM)
PARAMS = pltpu.CompilerParams(vmem_limit_bytes=40 * 2**20)


def in_vmem(shape, dtype):
    return pltpu.VMEM(shape, dtype)


def pieces(values):
    high = values.astype(jnp.bfloat16).astype(jnp.float32)
    rest = values - high
    mid = rest.astype(jnp.bfloat16).astype(jnp.float32)
    low = (rest - mid).astype(jnp.bfloat16).astype(jnp.float32)
    return high, mid, low


def target_weight(mass, poten):
    return (mass + poten / entropic) * log2e


def line_steps(shards):
    return [2 * (i ^ (i >> 1)) for i in range(shards // 2 - 1, 0, -1)]


def blocks_at(shards):
    near = [0] + line_steps(shards)
    me = lax.axis_index("src")
    return [me ^ other for other in near + [step ^ 1 for step in near]]


def read_all(hbm, held, sems):
    copies = [pltpu.make_async_copy(src, dst, sems.at[i]) for i, (src, dst) in enumerate(zip(hbm, held))]
    for copy in copies:
        copy.start()
    return copies


def pack_kernel(*refs):
    hbm, (send_ref, weight_ref), held, sems = refs[:3], refs[3:5], refs[5:8], refs[8]
    for copy in read_all(hbm, held, sems):
        copy.wait()
    feat_ref, mass_ref, poten_ref = held
    feat = feat_ref[0]
    depth, cells = feat.shape
    weight = target_weight(mass_ref[...], poten_ref[...])
    norm = jnp.sum(feat * feat, axis=0, keepdims=True)
    bias = weight - (log2e / entropic) * norm
    scaled = feat * (2.0 * log2e / entropic)
    send_ref[0, :depth, 0, :] = scaled
    send_ref[0, depth, 0:1, :] = bias
    weight_ref[...] = weight


def source_kernel(shards, *refs):
    hbm, outs, held, sems = refs[:4], refs[4:8], refs[8:12], refs[12]
    wide_ref, norm_ref, mask_ref, mass_out_ref = outs
    mass_ref, support_ref, counts_ref, feat_ref = held
    copies = read_all(hbm, held, sems)
    for copy in copies[:3]:
        copy.wait()
    mass_out_ref[...] = mass_ref[...]
    support = support_ref[...]
    slots, rows = support.shape
    cells = mass_ref.shape[1]
    used = lax.broadcasted_iota(jnp.int32, support.shape, 0) < counts_ref[...]
    hits = [
        jnp.max(jnp.where(used & (support == block), 0.0, very_low), axis=0, keepdims=True)
        for block in blocks_at(shards)
    ]
    hits = jnp.concatenate(hits + [jnp.zeros((cells - shards, rows), jnp.float32)], axis=0)
    hits = jnp.concatenate([hits, jnp.zeros((cells, cells - rows), jnp.float32)], axis=1).T
    for place in range(shards):
        mask_ref[place] = jnp.broadcast_to(hits[:rows, place : place + 1], (rows, cells))
    copies[3].wait()
    depth = feat_ref.shape[1]
    one = jnp.ones((2 * depth, 2 * cells), jnp.bfloat16)
    for pair in range(rows // 2):
        for half in range(2):
            feat = feat_ref[2 * pair + half]
            norm_ref[2 * pair + half : 2 * pair + half + 1, :] = jnp.sum(feat * feat, axis=0, keepdims=True)
            high, mid, low = pieces(feat)
            lanes = slice(half * cells, (half + 1) * cells)
            top = jnp.concatenate([high, mid], axis=0).astype(jnp.bfloat16)
            wide_ref[pair, 0 : 2 * depth, lanes] = top
            wide_ref[pair, 2 * depth : 4 * depth, lanes] = top
            wide_ref[pair, 4 * depth : 6 * depth, lanes] = jnp.concatenate([low, high], axis=0).astype(jnp.bfloat16)
        wide_ref[pair, 6 * depth : 8 * depth, :] = one


def join_kernel(*refs):
    refs[-1][0] = refs[0][0]
    refs[-1][1] = refs[1][0]


def on_core(core, work, idle):
    if core is None:
        work()
    else:
        here = lax.axis_index("tgt") == core
        pl.when(here)(work)
        pl.when(jnp.logical_not(here))(idle)


def tile_kernel(parts, core, *refs):
    peak_ref, total_ref = refs[-2:]

    def idle():
        peak_ref[...] = jnp.zeros(peak_ref.shape, jnp.float32)
        total_ref[...] = jnp.zeros(total_ref.shape, jnp.float32)

    ins = refs[: parts + 1] + refs[-4:]
    on_core(core, functools.partial(make_tiles, parts, *ins), idle)


def make_tiles(parts, *refs):
    packs = [ref.at[index] for ref in refs[:parts] for index in range(ref.shape[0])]
    wide_ref, exps_ref, tall_ref, peak_ref, total_ref = refs[parts:]
    blocks = len(packs)
    pairs, _, both = wide_ref.shape
    cells = both // 2
    depth = cells // 2
    lane = lax.broadcasted_iota(jnp.int32, (cells, cells), 1)
    biases = jnp.concatenate([pack[depth, 0:1, :] for pack in packs], axis=0)
    bias_pieces = jnp.concatenate(list(pieces(biases)), axis=0)
    padded = jnp.concatenate([bias_pieces, jnp.zeros((cells - 3 * blocks, cells), jnp.float32)], axis=0)
    bias_lanes = padded.T
    for place, pack in enumerate(packs):
        feat = pack[:depth, 0, :]
        turned = jnp.concatenate([feat, feat], axis=0).T
        high, mid, low = pieces(turned)
        own = jnp.where(lax.rem(lane, blocks) == place, bias_lanes, 0.0)
        rows = slice(place * cells, (place + 1) * cells)
        tall_ref[rows, 0:cells] = high.astype(jnp.bfloat16)
        tall_ref[rows, cells : 2 * cells] = mid.astype(jnp.bfloat16)
        tall_ref[rows, 2 * cells : 3 * cells] = jnp.where(lane < depth, high, low).astype(jnp.bfloat16)
        tall_ref[rows, 3 * cells : 4 * cells] = own.astype(jnp.bfloat16)

    def body(pair, carry):
        scores = jnp.dot(tall_ref[...], wide_ref[pair], preferred_element_type=jnp.float32)
        for place in range(blocks):
            rows = slice(place * cells, (place + 1) * cells)
            score = scores[rows]
            peak = jnp.max(score, axis=0, keepdims=True)
            exps = jnp.exp2(score - peak)
            exps_ref[pair, rows, :] = exps
            total = jnp.sum(exps, axis=0, keepdims=True)
            for half in range(2):
                lanes = slice(half * cells, (half + 1) * cells)
                peak_ref[place, pl.ds(2 * pair + half, 1), :] = peak[:, lanes]
                total_ref[place, pl.ds(2 * pair + half, 1), :] = total[:, lanes]
        return carry

    lax.fori_loop(0, pairs, body, 0, unroll=min(pairs, 16 // blocks & -4 or 2))


def row_kernel(groups, *refs):
    mask_ref, peak_refs, total_refs = refs[0], refs[1 : 1 + groups], refs[1 + groups : 1 + 2 * groups]
    peaks_ref, rowsum_ref = refs[1 + 2 * groups :]
    place = 0
    for ref in peak_refs:
        for index in range(ref.shape[0]):
            peaks_ref[place] = ref[index] + mask_ref[place]
            place += 1
    totals = [ref[index] for ref in total_refs for index in range(ref.shape[0])]
    top = functools.reduce(jnp.maximum, [peaks_ref[index] for index in range(place)])
    summed = sum(total * jnp.exp2(peaks_ref[index] - top) for index, total in enumerate(totals))
    rowsum_ref[...] = top + jnp.log2(summed)


def across(column):
    shape = (column.shape[0],) * 2
    same = lax.broadcasted_iota(jnp.int32, shape, 0) == lax.broadcasted_iota(jnp.int32, shape, 1)
    return jnp.sum(jnp.where(same, jnp.broadcast_to(column, shape), 0.0), axis=0, keepdims=True)


def column_kernel(groups, core, *refs):
    ins, outs, scratch = refs[: 2 * groups + 7], refs[-4:-2], refs[-2:]

    def idle():
        for given, out in zip(refs[2 * groups + 7 : -4], outs):
            out[...] = given[...]

    on_core(core, functools.partial(sum_columns, groups, *ins, *outs, *scratch), idle)


def sum_columns(groups, *refs):
    exps_refs, tall_refs, rest = refs[:groups], refs[groups : 2 * groups], refs[2 * groups :]
    wide_ref, peak_ref, mask_ref, own_ref, other_ref, mass_ref, norm_ref = rest[:7]
    poten_ref, sums_ref, weight_ref, shift_ref = rest[7:]
    pairs, _, both = wide_ref.shape
    cells = both // 2
    shards = mask_ref.shape[0]
    own, other = own_ref[...], other_ref[...]
    top = jnp.maximum(own, other)
    whole = top + jnp.log2(jnp.exp2(own - top) + jnp.exp2(other - top))
    poten_ref[...] = norm_ref[...] - (entropic * ln2) * whole
    shift = mass_ref[...] * log2e - whole
    shift_ref[...] = shift
    for place in range(shards):
        weight_ref[place] = jnp.exp2(peak_ref[place] + shift)
    spots = [
        (group, slice(index * cells, (index + 1) * cells))
        for group, ref in enumerate(tall_refs)
        for index in range(ref.shape[0] // cells)
    ]
    used = [jnp.max(mask_ref[place], axis=0, keepdims=True) > 0.5 * very_low for place in range(shards)]
    ranks = [shards - 1 - block for block in blocks_at(shards)]
    sums = []
    for place, (group, rows) in enumerate(spots):
        acc = jnp.zeros((cells, cells), jnp.float32)
        for pair in range(pairs):
            acc = acc + exps_refs[group][pair, rows, :cells] * weight_ref[place, 2 * pair : 2 * pair + 1, :]
            acc = acc + exps_refs[group][pair, rows, cells:] * weight_ref[place, 2 * pair + 1 : 2 * pair + 2, :]
        sums.append(jnp.sum(acc.T, axis=0, keepdims=True))
    whole_sums = jnp.concatenate([jnp.where(here, one, 1.0) for here, one in zip(used, sums)], axis=0)
    worst = jnp.min(whole_sums)
    logs = jnp.log2(whole_sums)
    for place in range(shards):
        sums_ref[ranks[place]] = jnp.where(used[place], logs[place : place + 1, :], very_low)

    @pl.when(worst < least_sum)
    def _():
        for place, (group, rows) in enumerate(spots):

            def exponents(pair):
                score = jnp.dot(tall_refs[group][rows, :], wide_ref[pair], preferred_element_type=jnp.float32)
                add = shift_ref[pl.ds(2 * pair, 2), :] + mask_ref[place, pl.ds(2 * pair, 2), :]
                return score[:, :cells] + add[0:1, :], score[:, cells:] + add[1:2, :]

            def highest(pair, peak):
                first, second = exponents(pair)
                return jnp.maximum(peak, jnp.maximum(first, second))

            peak = lax.fori_loop(0, pairs, highest, jnp.full((cells, cells), very_low, jnp.float32))
            peak = jnp.max(peak, axis=1, keepdims=True)

            def add_up(pair, sums):
                first, second = exponents(pair)
                return sums + jnp.exp2(first - peak) + jnp.exp2(second - peak)

            sums = lax.fori_loop(0, pairs, add_up, jnp.zeros((cells, cells), jnp.float32))
            logs = across(peak) + jnp.log2(across(jnp.sum(sums, axis=1, keepdims=True)))
            sums_ref[ranks[place]] = jnp.where(used[place], logs, very_low)


def merge_kernel(values_ref, weight_ref, poten_ref, out_ref, poten_out_ref):
    poten_out_ref[...] = poten_ref[...]
    values = values_ref[...]
    top = jnp.max(values, axis=0)
    whole = top + jnp.log2(jnp.sum(jnp.exp2(values - top), axis=0))
    out_ref[...] = -(entropic * ln2) * (whole - weight_ref[...])


def f32(*shape):
    return jax.ShapeDtypeStruct(shape, jnp.float32)


def dense_device(
    source_feat, target_feat, log_mass_src, log_mass_tgt, potential_tgt, support, counts
):
    shards = lax.axis_size("src")
    rows, depth, cells = source_feat.shape
    pairs, wide = rows // 2, 2 * cells

    def call(kernel, ins, out_shape, scratch=(), cost=None):
        many = isinstance(out_shape, list)
        return pl.pallas_call(
            kernel,
            in_specs=ins,
            out_specs=[VM] * len(out_shape) if many else VM,
            out_shape=out_shape,
            scratch_shapes=list(scratch),
            compiler_params=PARAMS,
            cost_estimate=cost,
        )

    def reading(kernel, args, out_shape, cost):
        return call(
            kernel,
            [pl.BlockSpec(memory_space=pltpu.HBM)] * len(args),
            out_shape,
            [pltpu.VMEM(arg.shape, arg.dtype) for arg in args] + [pltpu.SemaphoreType.DMA((len(args),))],
            cost,
        )(*[pltpu.with_memory_space_constraint(arg, pltpu.HBM) for arg in args])

    def cost_of(flops):
        return pl.CostEstimate(flops=flops, bytes_accessed=rows * depth * cells * 4, transcendentals=0)

    pack, weight = reading(
        pack_kernel,
        [target_feat, log_mass_tgt, potential_tgt],
        [in_vmem((1, depth + 1, 1, cells), jnp.float32), in_vmem((1, cells), jnp.float32)],
        None,
    )
    wide_feat, norm, mask, mass = reading(
        functools.partial(source_kernel, shards),
        [log_mass_src, support[:, 0, :].T, counts.T, source_feat],
        [
            in_vmem((pairs, 8 * depth, wide), jnp.bfloat16),
            in_vmem((rows, cells), jnp.float32),
            in_vmem((shards, rows, cells), jnp.float32),
            in_vmem((rows, cells), jnp.float32),
        ],
        cost_of(10**8),
    )

    def tiles(*packs, core=None, after=None):
        blocks = sum(pack.shape[0] for pack in packs)
        more = [] if after is None else [after]
        return call(
            functools.partial(tile_kernel, len(packs), core),
            [VM] * (len(packs) + 1) + [pl.BlockSpec(memory_space=pl.ANY)] * len(more),
            [
                in_vmem((pairs, blocks * cells, wide), jnp.float32),
                in_vmem((blocks * cells, 8 * depth), jnp.bfloat16),
                in_vmem((blocks, rows, cells), jnp.float32),
                in_vmem((blocks, rows, cells), jnp.float32),
            ],
            cost=cost_of(2 * blocks * cells * pairs * wide * 8 * depth),
        )(*packs, wide_feat, *more)

    def swapped(array, step):
        return lax.ppermute(array, "src", [(i, i ^ step) for i in range(shards)])

    def joined(first, second, after):
        return call(
            join_kernel,
            [VM] * 2 + [pl.BlockSpec(memory_space=pl.ANY)],
            in_vmem((2,) + pack.shape[1:], jnp.float32),
        )(first, second, after)

    steps = line_steps(shards)
    there = [swapped(pack, step) for step in reversed(steps)][::-1]
    near = [pack] + there
    halves = [joined(near[0], near[1], norm)]
    for at in range(2, shards // 2, 2):
        halves.append(joined(near[at], near[at + 1], halves[-1]))
    far = [swapped(half, 1) for half in halves]
    found = [tiles(pack, after=halves[-1])]
    found.append(tiles(*there, after=found[0][-1]))
    for half in far[:-1]:
        found.append(tiles(half, after=found[-1][-1]))
    groups = len(found) + 1

    def log_sums(last):
        _, _, peaks, totals = zip(*found, last)
        return call(
            functools.partial(row_kernel, groups),
            [VM] * (1 + 2 * groups),
            [in_vmem((shards, rows, cells), jnp.float32), in_vmem((rows, cells), jnp.float32)],
        )(mask, *peaks, *totals)

    def columns_of(core, last, peaks, own, other, given):
        exps, tall, _, _ = zip(*found, last)
        return call(
            functools.partial(column_kernel, groups, core),
            [VM] * (2 * groups + 7 + len(given)),
            [in_vmem((rows, cells), jnp.float32), in_vmem((shards, 1, cells), jnp.float32)],
            [pltpu.VMEM((shards, rows, cells), jnp.float32), pltpu.VMEM((rows, cells), jnp.float32)],
            cost_of(10**9),
        )(*exps, *tall, wide_feat, peaks, mask, own, other, mass, norm, *given)

    between = [(0, 1), (1, 0)]
    last_one = tiles(far[-1], core=1, after=found[-1][-1])
    peaks_one, own_one = log_sums(last_one)
    other_zero = lax.ppermute(own_one, "tgt", between)
    last_zero = tiles(far[-1], core=0, after=own_one)
    peaks_zero, own_zero = log_sums(last_zero)
    other_one = lax.ppermute(own_zero, "tgt", between)
    given = columns_of(0, last_zero, peaks_zero, own_zero, other_zero, [])
    potential_src, columns = columns_of(1, last_one, peaks_one, own_one, other_one, given)
    arrived = lax.all_to_all(columns, "src", 0, 0, axis_index_groups=[list(range(shards))[::-1]])
    outs = [f32(1, cells), f32(rows, cells)]
    potential_new, potential_src = call(merge_kernel, [VM] * 3, outs)(arrived, weight, potential_src)
    return potential_src, potential_new


def merged(part, axis, combine):
    gathered = jax.tree.map(lambda a: lax.all_gather(a, axis), part)

    def take(source):
        return jax.tree.map(lambda a: lax.dynamic_index_in_dim(a, source, 0, False), gathered)

    return lax.fori_loop(
        1, lax.axis_size(axis), lambda source, state: combine(state, take(source)), take(0)
    )


def cost_tiles(source_blk, source_sq, target_blk, target_sq):
    cross = jnp.einsum(
        "...fi,...fj->...ij", source_blk, target_blk, precision=lax.Precision.HIGHEST
    )
    return source_sq[..., :, None] + target_sq[..., None, :] - 2.0 * cross


def row_stats(cost, mass_tgt, poten_tgt, usable):
    scores = mass_tgt[..., None, :] + (poten_tgt[..., None, :] - cost) / entropic
    scores = jnp.where(usable[..., None, None], scores, very_low)
    peak = jnp.max(scores, axis=(1, 3))
    total = jnp.sum(jnp.exp(scores - peak[:, None, :, None]), axis=(1, 3))
    return (peak, total)


def column_stats(cost, mass_src, poten_src, usable):
    scores = mass_src[:, None, :, None] + (poten_src[:, None, :, None] - cost) / entropic
    peak = jnp.max(scores, axis=2)
    total = jnp.sum(jnp.exp(scores - peak[:, :, None, :]), axis=2)
    peak = jnp.where(usable[..., None], peak, very_low)
    total = jnp.where(usable[..., None], total, 0.0)
    return (peak, total)


def merge_pair(first_pair, second_pair):
    first_peak, first_total = first_pair
    second_peak, second_total = second_pair
    highest = jnp.maximum(first_peak, second_peak)
    summed = first_total * jnp.exp(first_peak - highest) + second_total * jnp.exp(
        second_peak - highest
    )
    return (highest, summed)


def segment_merge(peaks, totals, seg_ids, segments):
    best = jax.ops.segment_max(peaks, seg_ids, num_segments=segments + 1)
    best = jnp.maximum(best, very_low)
    summed = jax.ops.segment_sum(
        totals * jnp.exp(peaks - best[seg_ids]), seg_ids, num_segments=segments + 1
    )
    return (best[:segments], summed[:segments])


def general_device(
    source_feat, target_feat, log_mass_src, log_mass_tgt, potential_tgt, support, counts
):
    target_all, mass_all, poten_all = (
        lax.all_gather(target_feat, "src", axis=0, tiled=True),
        lax.all_gather(log_mass_tgt, "src", axis=0, tiled=True),
        lax.all_gather(potential_tgt, "src", axis=0, tiled=True),
    )
    blocks = target_all.shape[0]
    rows_here = source_feat.shape[0]
    slots_here = support.shape[2]
    cells = source_feat.shape[2]
    indices = support[:, 0, :]
    limits = counts[:, 0]
    usable = jnp.arange(slots_here, dtype=jnp.int32)[None, :] < limits[:, None]
    source_sq = jnp.sum(source_feat * source_feat, axis=1)
    target_sq = jnp.sum(target_all * target_all, axis=1)
    width = math.gcd(rows_here, 4)

    def grouped(array):
        return array.reshape((rows_here // width, width) + array.shape[1:])

    def row_pass(items):
        source_blk, source_nrm, ids_here, use_here = items
        cost = cost_tiles(
            source_blk[:, None], source_nrm[:, None], target_all[ids_here], target_sq[ids_here]
        )
        return row_stats(cost, mass_all[ids_here], poten_all[ids_here], use_here)

    peak, total = lax.map(
        row_pass, (grouped(source_feat), grouped(source_sq), grouped(indices), grouped(usable))
    )
    peak = peak.reshape(rows_here, cells)
    total = total.reshape(rows_here, cells)
    peak_all, total_all = merged((peak, total), "tgt", merge_pair)
    potential_src = -entropic * (peak_all + jnp.log(total_all))

    def column_pass(items):
        source_blk, source_nrm, mass_here, poten_here, ids_here, use_here = items
        cost = cost_tiles(
            source_blk[:, None], source_nrm[:, None], target_all[ids_here], target_sq[ids_here]
        )
        return column_stats(cost, mass_here, poten_here, use_here)

    peaks, totals = lax.map(
        column_pass,
        (
            grouped(source_feat),
            grouped(source_sq),
            grouped(log_mass_src),
            grouped(potential_src),
            grouped(indices),
            grouped(usable),
        ),
    )
    seg_ids = jnp.where(usable, indices, blocks).reshape(-1)
    best, summed = segment_merge(
        peaks.reshape(-1, cells), totals.reshape(-1, cells), seg_ids, blocks
    )
    share = blocks // lax.axis_size("src")
    own_start = lax.axis_index("src") * share
    highest = lax.pmax(best, "src")
    whole = lax.psum(summed * jnp.exp(best - highest), "src")
    own_peak = lax.dynamic_slice_in_dim(highest, own_start, share, 0)
    own_total = lax.dynamic_slice_in_dim(whole, own_start, share, 0)
    potential_new = -entropic * (own_peak + jnp.log(own_total))
    return (potential_src, potential_new)


def per_device(source_feat, target_feat, *others):
    shards = lax.axis_size("src")
    rows, depth, cells = source_feat.shape
    paired = shards >= 4 and shards & (shards - 1) == 0 and lax.axis_size("tgt") == 2
    shaped = target_feat.shape[0] == 1 and rows % 2 == 0 and cells == 2 * depth and cells % 128 == 0
    if paired and shaped and 4 * rows * cells * shards * cells <= room:
        return dense_device(source_feat, target_feat, *others)
    return general_device(source_feat, target_feat, *others)


def solution(mesh):
    in_specs = (
        P(("grp", "src"), None, None),
        P(("grp", "src", "tgt"), None, None),
        P(("grp", "src"), None),
        P(("grp", "src", "tgt"), None),
        P(("grp", "src", "tgt"), None),
        P(("grp", "src"), "tgt", None),
        P(("grp", "src"), "tgt"),
    )
    out_specs = (P(("grp", "src"), None), P(("grp", "src", "tgt"), None))
    return jax.shard_map(
        per_device, mesh=mesh, in_specs=in_specs, out_specs=out_specs, check_vma=False
    )
```

```python
import functools
import math

import jax
import jax.numpy as jnp
from jax import lax
from jax.experimental import pallas as pl
from jax.experimental.pallas import tpu as pltpu
from jax.sharding import PartitionSpec as P

entropic = 0.5
very_low = -1e30
log2e = 1.0 / math.log(2.0)
ln2 = math.log(2.0)
least_sum = 1e-28

room = 2**24

VM = pl.BlockSpec(memory_space=pltpu.VMEM)
PARAMS = pltpu.CompilerParams(vmem_limit_bytes=40 * 2**20)


def in_vmem(shape, dtype):
    return pltpu.VMEM(shape, dtype)


def pieces(values):
    high = values.astype(jnp.bfloat16).astype(jnp.float32)
    rest = values - high
    mid = rest.astype(jnp.bfloat16).astype(jnp.float32)
    low = (rest - mid).astype(jnp.bfloat16).astype(jnp.float32)
    return high, mid, low


def target_weight(mass, poten):
    return (mass + poten / entropic) * log2e


def line_moves(line):
    bits = line.bit_length() - 1
    cycle = [sum(((place >> bit) & 1) << (bits - 1 - bit) for bit in range(bits)) for place in range(line)]
    shifts = [shift for step in range(1, line // 2) for shift in (step, line - step)] + [line // 2]
    return [[cycle[(cycle.index(at) + shift) % line] for at in range(line)] for shift in shifts]


def blocks_at(shards):
    me = lax.axis_index("src")
    at, odd = me // 2, lax.rem(me, 2)
    near = [me]
    for receivers in line_moves(shards // 2):
        senders = [receivers.index(there) for there in range(shards // 2)]
        near.append(2 * sum(jnp.where(at == there, sender, 0) for there, sender in enumerate(senders)) + odd)
    return near + [block ^ 1 for block in near]


def read_all(hbm, held, sems):
    copies = [pltpu.make_async_copy(src, dst, sems.at[i]) for i, (src, dst) in enumerate(zip(hbm, held))]
    for copy in copies:
        copy.start()
    return copies


def pack_kernel(*refs):
    hbm, (send_ref, weight_ref), held, sems = refs[:3], refs[3:5], refs[5:8], refs[8]
    for copy in read_all(hbm, held, sems):
        copy.wait()
    feat_ref, mass_ref, poten_ref = held
    feat = feat_ref[0]
    depth, cells = feat.shape
    weight = target_weight(mass_ref[...], poten_ref[...])
    norm = jnp.sum(feat * feat, axis=0, keepdims=True)
    bias = weight - (log2e / entropic) * norm
    scaled = feat * (2.0 * log2e / entropic)
    send_ref[0, :depth, 0, :] = scaled
    send_ref[0, depth, 0:1, :] = bias
    weight_ref[...] = weight


def source_kernel(shards, *refs):
    hbm, outs, held, sems = refs[:4], refs[4:8], refs[8:12], refs[12]
    wide_ref, norm_ref, mask_ref, mass_out_ref = outs
    mass_ref, support_ref, counts_ref, feat_ref = held
    copies = read_all(hbm, held, sems)
    for copy in copies[:3]:
        copy.wait()
    mass_out_ref[...] = mass_ref[...]
    support = support_ref[...]
    slots, rows = support.shape
    cells = mass_ref.shape[1]
    used = lax.broadcasted_iota(jnp.int32, support.shape, 0) < counts_ref[...]
    hits = [
        jnp.max(jnp.where(used & (support == block), 0.0, very_low), axis=0, keepdims=True)
        for block in blocks_at(shards)
    ]
    hits = jnp.concatenate(hits + [jnp.zeros((cells - shards, rows), jnp.float32)], axis=0)
    hits = jnp.concatenate([hits, jnp.zeros((cells, cells - rows), jnp.float32)], axis=1).T
    for place in range(shards):
        mask_ref[place] = jnp.broadcast_to(hits[:rows, place : place + 1], (rows, cells))
    copies[3].wait()
    depth = feat_ref.shape[1]
    one = jnp.ones((2 * depth, 2 * cells), jnp.bfloat16)
    for pair in range(rows // 2):
        for half in range(2):
            feat = feat_ref[2 * pair + half]
            norm_ref[2 * pair + half : 2 * pair + half + 1, :] = jnp.sum(feat * feat, axis=0, keepdims=True)
            high, mid, low = pieces(feat)
            lanes = slice(half * cells, (half + 1) * cells)
            top = jnp.concatenate([high, mid], axis=0).astype(jnp.bfloat16)
            wide_ref[pair, 0 : 2 * depth, lanes] = top
            wide_ref[pair, 2 * depth : 4 * depth, lanes] = top
            wide_ref[pair, 4 * depth : 6 * depth, lanes] = jnp.concatenate([low, high], axis=0).astype(jnp.bfloat16)
        wide_ref[pair, 6 * depth : 8 * depth, :] = one


def join_kernel(*refs):
    refs[-1][0] = refs[0][0]
    refs[-1][1] = refs[1][0]


def on_core(core, work, idle):
    if core is None:
        work()
    else:
        here = lax.axis_index("tgt") == core
        pl.when(here)(work)
        pl.when(jnp.logical_not(here))(idle)


def tile_kernel(parts, core, *refs):
    peak_ref, total_ref = refs[-2:]

    def idle():
        peak_ref[...] = jnp.zeros(peak_ref.shape, jnp.float32)
        total_ref[...] = jnp.zeros(total_ref.shape, jnp.float32)

    ins = refs[: parts + 1] + refs[-4:]
    on_core(core, functools.partial(make_tiles, parts, *ins), idle)


def make_tiles(parts, *refs):
    packs = [ref.at[index] for ref in refs[:parts] for index in range(ref.shape[0])]
    wide_ref, exps_ref, tall_ref, peak_ref, total_ref = refs[parts:]
    blocks = len(packs)
    pairs, _, both = wide_ref.shape
    cells = both // 2
    depth = cells // 2
    lane = lax.broadcasted_iota(jnp.int32, (cells, cells), 1)
    biases = jnp.concatenate([pack[depth, 0:1, :] for pack in packs], axis=0)
    bias_pieces = jnp.concatenate(list(pieces(biases)), axis=0)
    padded = jnp.concatenate([bias_pieces, jnp.zeros((cells - 3 * blocks, cells), jnp.float32)], axis=0)
    bias_lanes = padded.T
    for place, pack in enumerate(packs):
        feat = pack[:depth, 0, :]
        turned = jnp.concatenate([feat, feat], axis=0).T
        high, mid, low = pieces(turned)
        own = jnp.where(lax.rem(lane, blocks) == place, bias_lanes, 0.0)
        rows = slice(place * cells, (place + 1) * cells)
        tall_ref[rows, 0:cells] = high.astype(jnp.bfloat16)
        tall_ref[rows, cells : 2 * cells] = mid.astype(jnp.bfloat16)
        tall_ref[rows, 2 * cells : 3 * cells] = jnp.where(lane < depth, high, low).astype(jnp.bfloat16)
        tall_ref[rows, 3 * cells : 4 * cells] = own.astype(jnp.bfloat16)

    def body(pair, carry):
        scores = jnp.dot(tall_ref[...], wide_ref[pair], preferred_element_type=jnp.float32)
        for place in range(blocks):
            rows = slice(place * cells, (place + 1) * cells)
            score = scores[rows]
            peak = jnp.max(score, axis=0, keepdims=True)
            exps = jnp.exp2(score - peak)
            exps_ref[pair, rows, :] = exps
            total = jnp.sum(exps, axis=0, keepdims=True)
            for half in range(2):
                lanes = slice(half * cells, (half + 1) * cells)
                peak_ref[place, pl.ds(2 * pair + half, 1), :] = peak[:, lanes]
                total_ref[place, pl.ds(2 * pair + half, 1), :] = total[:, lanes]
        return carry

    lax.fori_loop(0, pairs, body, 0, unroll=min(pairs, 16 // blocks & -4 or 2))


def row_kernel(groups, *refs):
    mask_ref, peak_refs, total_refs = refs[0], refs[1 : 1 + groups], refs[1 + groups : 1 + 2 * groups]
    peaks_ref, rowsum_ref = refs[1 + 2 * groups :]
    place = 0
    for ref in peak_refs:
        for index in range(ref.shape[0]):
            peaks_ref[place] = ref[index] + mask_ref[place]
            place += 1
    totals = [ref[index] for ref in total_refs for index in range(ref.shape[0])]
    top = functools.reduce(jnp.maximum, [peaks_ref[index] for index in range(place)])
    summed = sum(total * jnp.exp2(peaks_ref[index] - top) for index, total in enumerate(totals))
    rowsum_ref[...] = top + jnp.log2(summed)


def across(column):
    shape = (column.shape[0],) * 2
    same = lax.broadcasted_iota(jnp.int32, shape, 0) == lax.broadcasted_iota(jnp.int32, shape, 1)
    return jnp.sum(jnp.where(same, jnp.broadcast_to(column, shape), 0.0), axis=0, keepdims=True)


def column_kernel(groups, core, *refs):
    ins, outs, scratch = refs[: 2 * groups + 7], refs[-4:-2], refs[-2:]

    def idle():
        for given, out in zip(refs[2 * groups + 7 : -4], outs):
            out[...] = given[...]

    on_core(core, functools.partial(sum_columns, groups, *ins, *outs, *scratch), idle)


def sum_columns(groups, *refs):
    exps_refs, tall_refs, rest = refs[:groups], refs[groups : 2 * groups], refs[2 * groups :]
    wide_ref, peak_ref, mask_ref, own_ref, other_ref, mass_ref, norm_ref = rest[:7]
    poten_ref, sums_ref, weight_ref, shift_ref = rest[7:]
    pairs, _, both = wide_ref.shape
    cells = both // 2
    shards = mask_ref.shape[0]
    own, other = own_ref[...], other_ref[...]
    top = jnp.maximum(own, other)
    whole = top + jnp.log2(jnp.exp2(own - top) + jnp.exp2(other - top))
    poten_ref[...] = norm_ref[...] - (entropic * ln2) * whole
    shift = mass_ref[...] * log2e - whole
    shift_ref[...] = shift
    for place in range(shards):
        weight_ref[place] = jnp.exp2(peak_ref[place] + shift)
    spots = [
        (group, slice(index * cells, (index + 1) * cells))
        for group, ref in enumerate(tall_refs)
        for index in range(ref.shape[0] // cells)
    ]
    used = [jnp.max(mask_ref[place], axis=0, keepdims=True) > 0.5 * very_low for place in range(shards)]
    ranks = [shards - 1 - block for block in blocks_at(shards)]
    sums = []
    for place, (group, rows) in enumerate(spots):
        acc = jnp.zeros((cells, cells), jnp.float32)
        for pair in range(pairs):
            acc = acc + exps_refs[group][pair, rows, :cells] * weight_ref[place, 2 * pair : 2 * pair + 1, :]
            acc = acc + exps_refs[group][pair, rows, cells:] * weight_ref[place, 2 * pair + 1 : 2 * pair + 2, :]
        sums.append(jnp.sum(acc.T, axis=0, keepdims=True))
    whole_sums = jnp.concatenate([jnp.where(here, one, 1.0) for here, one in zip(used, sums)], axis=0)
    worst = jnp.min(whole_sums)
    logs = jnp.log2(whole_sums)
    for place in range(shards):
        sums_ref[ranks[place]] = jnp.where(used[place], logs[place : place + 1, :], very_low)

    @pl.when(worst < least_sum)
    def _():
        for place, (group, rows) in enumerate(spots):

            def exponents(pair):
                score = jnp.dot(tall_refs[group][rows, :], wide_ref[pair], preferred_element_type=jnp.float32)
                add = shift_ref[pl.ds(2 * pair, 2), :] + mask_ref[place, pl.ds(2 * pair, 2), :]
                return score[:, :cells] + add[0:1, :], score[:, cells:] + add[1:2, :]

            def highest(pair, peak):
                first, second = exponents(pair)
                return jnp.maximum(peak, jnp.maximum(first, second))

            peak = lax.fori_loop(0, pairs, highest, jnp.full((cells, cells), very_low, jnp.float32))
            peak = jnp.max(peak, axis=1, keepdims=True)

            def add_up(pair, sums):
                first, second = exponents(pair)
                return sums + jnp.exp2(first - peak) + jnp.exp2(second - peak)

            sums = lax.fori_loop(0, pairs, add_up, jnp.zeros((cells, cells), jnp.float32))
            logs = across(peak) + jnp.log2(across(jnp.sum(sums, axis=1, keepdims=True)))
            sums_ref[ranks[place]] = jnp.where(used[place], logs, very_low)


def merge_kernel(values_ref, weight_ref, poten_ref, out_ref, poten_out_ref):
    poten_out_ref[...] = poten_ref[...]
    values = values_ref[...]
    top = jnp.max(values, axis=0)
    whole = top + jnp.log2(jnp.sum(jnp.exp2(values - top), axis=0))
    out_ref[...] = -(entropic * ln2) * (whole - weight_ref[...])


def f32(*shape):
    return jax.ShapeDtypeStruct(shape, jnp.float32)


def dense_device(
    source_feat, target_feat, log_mass_src, log_mass_tgt, potential_tgt, support, counts
):
    shards = lax.axis_size("src")
    rows, depth, cells = source_feat.shape
    pairs, wide = rows // 2, 2 * cells

    def call(kernel, ins, out_shape, scratch=(), cost=None):
        many = isinstance(out_shape, list)
        return pl.pallas_call(
            kernel,
            in_specs=ins,
            out_specs=[VM] * len(out_shape) if many else VM,
            out_shape=out_shape,
            scratch_shapes=list(scratch),
            compiler_params=PARAMS,
            cost_estimate=cost,
        )

    def reading(kernel, args, out_shape, cost):
        return call(
            kernel,
            [pl.BlockSpec(memory_space=pltpu.HBM)] * len(args),
            out_shape,
            [pltpu.VMEM(arg.shape, arg.dtype) for arg in args] + [pltpu.SemaphoreType.DMA((len(args),))],
            cost,
        )(*[pltpu.with_memory_space_constraint(arg, pltpu.HBM) for arg in args])

    def cost_of(flops):
        return pl.CostEstimate(flops=flops, bytes_accessed=rows * depth * cells * 4, transcendentals=0)

    pack, weight = reading(
        pack_kernel,
        [target_feat, log_mass_tgt, potential_tgt],
        [in_vmem((1, depth + 1, 1, cells), jnp.float32), in_vmem((1, cells), jnp.float32)],
        None,
    )
    wide_feat, norm, mask, mass = reading(
        functools.partial(source_kernel, shards),
        [log_mass_src, support[:, 0, :].T, counts.T, source_feat],
        [
            in_vmem((pairs, 8 * depth, wide), jnp.bfloat16),
            in_vmem((rows, cells), jnp.float32),
            in_vmem((shards, rows, cells), jnp.float32),
            in_vmem((rows, cells), jnp.float32),
        ],
        cost_of(10**8),
    )

    def tiles(*packs, core=None, after=None):
        blocks = sum(pack.shape[0] for pack in packs)
        more = [] if after is None else [after]
        return call(
            functools.partial(tile_kernel, len(packs), core),
            [VM] * (len(packs) + 1) + [pl.BlockSpec(memory_space=pl.ANY)] * len(more),
            [
                in_vmem((pairs, blocks * cells, wide), jnp.float32),
                in_vmem((blocks * cells, 8 * depth), jnp.bfloat16),
                in_vmem((blocks, rows, cells), jnp.float32),
                in_vmem((blocks, rows, cells), jnp.float32),
            ],
            cost=cost_of(2 * blocks * cells * pairs * wide * 8 * depth),
        )(*packs, wide_feat, *more)

    def swapped(array):
        return lax.ppermute(array, "src", [(i, i ^ 1) for i in range(shards)])

    def moved(array, receivers):
        moves = [(2 * here + odd, 2 * there + odd) for here, there in enumerate(receivers) for odd in range(2)]
        return lax.ppermute(array, "src", moves)

    def joined(first, second, after):
        return call(
            join_kernel,
            [VM] * 2 + [pl.BlockSpec(memory_space=pl.ANY)],
            in_vmem((2,) + pack.shape[1:], jnp.float32),
        )(first, second, after)

    there = [moved(pack, receivers) for receivers in line_moves(shards // 2)[::-1]][::-1]
    near = [pack] + there
    halves = [joined(near[0], near[1], norm)]
    for at in range(2, shards // 2, 2):
        halves.append(joined(near[at], near[at + 1], halves[-1]))
    far = [swapped(half) for half in halves]
    found = [tiles(pack, after=halves[-1])]
    found.append(tiles(*there, after=found[0][-1]))
    for half in far[:-1]:
        found.append(tiles(half, after=found[-1][-1]))
    groups = len(found) + 1

    def log_sums(last):
        _, _, peaks, totals = zip(*found, last)
        return call(
            functools.partial(row_kernel, groups),
            [VM] * (1 + 2 * groups),
            [in_vmem((shards, rows, cells), jnp.float32), in_vmem((rows, cells), jnp.float32)],
        )(mask, *peaks, *totals)

    def columns_of(core, last, peaks, own, other, given):
        exps, tall, _, _ = zip(*found, last)
        return call(
            functools.partial(column_kernel, groups, core),
            [VM] * (2 * groups + 7 + len(given)),
            [in_vmem((rows, cells), jnp.float32), in_vmem((shards, 1, cells), jnp.float32)],
            [pltpu.VMEM((shards, rows, cells), jnp.float32), pltpu.VMEM((rows, cells), jnp.float32)],
            cost_of(10**9),
        )(*exps, *tall, wide_feat, peaks, mask, own, other, mass, norm, *given)

    between = [(0, 1), (1, 0)]
    last_one = tiles(far[-1], core=1, after=found[-1][-1])
    peaks_one, own_one = log_sums(last_one)
    other_zero = lax.ppermute(own_one, "tgt", between)
    last_zero = tiles(far[-1], core=0, after=own_one)
    peaks_zero, own_zero = log_sums(last_zero)
    other_one = lax.ppermute(own_zero, "tgt", between)
    given = columns_of(0, last_zero, peaks_zero, own_zero, other_zero, [])
    potential_src, columns = columns_of(1, last_one, peaks_one, own_one, other_one, given)
    arrived = lax.all_to_all(columns, "src", 0, 0, axis_index_groups=[list(range(shards))[::-1]])
    outs = [f32(1, cells), f32(rows, cells)]
    potential_new, potential_src = call(merge_kernel, [VM] * 3, outs)(arrived, weight, potential_src)
    return potential_src, potential_new


def merged(part, axis, combine):
    gathered = jax.tree.map(lambda a: lax.all_gather(a, axis), part)

    def take(source):
        return jax.tree.map(lambda a: lax.dynamic_index_in_dim(a, source, 0, False), gathered)

    return lax.fori_loop(
        1, lax.axis_size(axis), lambda source, state: combine(state, take(source)), take(0)
    )


def cost_tiles(source_blk, source_sq, target_blk, target_sq):
    cross = jnp.einsum(
        "...fi,...fj->...ij", source_blk, target_blk, precision=lax.Precision.HIGHEST
    )
    return source_sq[..., :, None] + target_sq[..., None, :] - 2.0 * cross


def row_stats(cost, mass_tgt, poten_tgt, usable):
    scores = mass_tgt[..., None, :] + (poten_tgt[..., None, :] - cost) / entropic
    scores = jnp.where(usable[..., None, None], scores, very_low)
    peak = jnp.max(scores, axis=(1, 3))
    total = jnp.sum(jnp.exp(scores - peak[:, None, :, None]), axis=(1, 3))
    return (peak, total)


def column_stats(cost, mass_src, poten_src, usable):
    scores = mass_src[:, None, :, None] + (poten_src[:, None, :, None] - cost) / entropic
    peak = jnp.max(scores, axis=2)
    total = jnp.sum(jnp.exp(scores - peak[:, :, None, :]), axis=2)
    peak = jnp.where(usable[..., None], peak, very_low)
    total = jnp.where(usable[..., None], total, 0.0)
    return (peak, total)


def merge_pair(first_pair, second_pair):
    first_peak, first_total = first_pair
    second_peak, second_total = second_pair
    highest = jnp.maximum(first_peak, second_peak)
    summed = first_total * jnp.exp(first_peak - highest) + second_total * jnp.exp(
        second_peak - highest
    )
    return (highest, summed)


def segment_merge(peaks, totals, seg_ids, segments):
    best = jax.ops.segment_max(peaks, seg_ids, num_segments=segments + 1)
    best = jnp.maximum(best, very_low)
    summed = jax.ops.segment_sum(
        totals * jnp.exp(peaks - best[seg_ids]), seg_ids, num_segments=segments + 1
    )
    return (best[:segments], summed[:segments])


def general_device(
    source_feat, target_feat, log_mass_src, log_mass_tgt, potential_tgt, support, counts
):
    target_all, mass_all, poten_all = (
        lax.all_gather(target_feat, "src", axis=0, tiled=True),
        lax.all_gather(log_mass_tgt, "src", axis=0, tiled=True),
        lax.all_gather(potential_tgt, "src", axis=0, tiled=True),
    )
    blocks = target_all.shape[0]
    rows_here = source_feat.shape[0]
    slots_here = support.shape[2]
    cells = source_feat.shape[2]
    indices = support[:, 0, :]
    limits = counts[:, 0]
    usable = jnp.arange(slots_here, dtype=jnp.int32)[None, :] < limits[:, None]
    source_sq = jnp.sum(source_feat * source_feat, axis=1)
    target_sq = jnp.sum(target_all * target_all, axis=1)
    width = math.gcd(rows_here, 4)

    def grouped(array):
        return array.reshape((rows_here // width, width) + array.shape[1:])

    def row_pass(items):
        source_blk, source_nrm, ids_here, use_here = items
        cost = cost_tiles(
            source_blk[:, None], source_nrm[:, None], target_all[ids_here], target_sq[ids_here]
        )
        return row_stats(cost, mass_all[ids_here], poten_all[ids_here], use_here)

    peak, total = lax.map(
        row_pass, (grouped(source_feat), grouped(source_sq), grouped(indices), grouped(usable))
    )
    peak = peak.reshape(rows_here, cells)
    total = total.reshape(rows_here, cells)
    peak_all, total_all = merged((peak, total), "tgt", merge_pair)
    potential_src = -entropic * (peak_all + jnp.log(total_all))

    def column_pass(items):
        source_blk, source_nrm, mass_here, poten_here, ids_here, use_here = items
        cost = cost_tiles(
            source_blk[:, None], source_nrm[:, None], target_all[ids_here], target_sq[ids_here]
        )
        return column_stats(cost, mass_here, poten_here, use_here)

    peaks, totals = lax.map(
        column_pass,
        (
            grouped(source_feat),
            grouped(source_sq),
            grouped(log_mass_src),
            grouped(potential_src),
            grouped(indices),
            grouped(usable),
        ),
    )
    seg_ids = jnp.where(usable, indices, blocks).reshape(-1)
    best, summed = segment_merge(
        peaks.reshape(-1, cells), totals.reshape(-1, cells), seg_ids, blocks
    )
    share = blocks // lax.axis_size("src")
    own_start = lax.axis_index("src") * share
    highest = lax.pmax(best, "src")
    whole = lax.psum(summed * jnp.exp(best - highest), "src")
    own_peak = lax.dynamic_slice_in_dim(highest, own_start, share, 0)
    own_total = lax.dynamic_slice_in_dim(whole, own_start, share, 0)
    potential_new = -entropic * (own_peak + jnp.log(own_total))
    return (potential_src, potential_new)


def per_device(source_feat, target_feat, *others):
    shards = lax.axis_size("src")
    rows, depth, cells = source_feat.shape
    paired = shards >= 4 and shards & (shards - 1) == 0 and lax.axis_size("tgt") == 2
    shaped = target_feat.shape[0] == 1 and rows % 2 == 0 and cells == 2 * depth and cells % 128 == 0
    if paired and shaped and 4 * rows * cells * shards * cells <= room:
        return dense_device(source_feat, target_feat, *others)
    return general_device(source_feat, target_feat, *others)


def solution(mesh):
    in_specs = (
        P(("grp", "src"), None, None),
        P(("grp", "src", "tgt"), None, None),
        P(("grp", "src"), None),
        P(("grp", "src", "tgt"), None),
        P(("grp", "src", "tgt"), None),
        P(("grp", "src"), "tgt", None),
        P(("grp", "src"), "tgt"),
    )
    out_specs = (P(("grp", "src"), None), P(("grp", "src", "tgt"), None))
    return jax.shard_map(
        per_device, mesh=mesh, in_specs=in_specs, out_specs=out_specs, check_vma=False
    )
```

```python
import functools
import math

import jax
import jax.numpy as jnp
from jax import lax
from jax.experimental import pallas as pl
from jax.experimental.pallas import tpu as pltpu
from jax.sharding import PartitionSpec as P

entropic = 0.5
very_low = -1e30
log2e = 1.0 / math.log(2.0)
ln2 = math.log(2.0)
least_sum = 1e-28

room = 2**24

VM = pl.BlockSpec(memory_space=pltpu.VMEM)
PARAMS = pltpu.CompilerParams(vmem_limit_bytes=40 * 2**20)


def in_vmem(shape, dtype):
    return pltpu.VMEM(shape, dtype)


def pieces(values):
    high = values.astype(jnp.bfloat16).astype(jnp.float32)
    rest = values - high
    mid = rest.astype(jnp.bfloat16).astype(jnp.float32)
    low = (rest - mid).astype(jnp.bfloat16).astype(jnp.float32)
    return high, mid, low


def target_weight(mass, poten):
    return (mass + poten / entropic) * log2e


def line_moves(line):
    bits = line.bit_length() - 1
    cycle = [sum(((place >> bit) & 1) << (bits - 1 - bit) for bit in range(bits)) for place in range(line)]
    shifts = [shift for step in range(1, line // 2) for shift in (step, line - step)] + [line // 2]
    return [[cycle[(cycle.index(at) + shift) % line] for at in range(line)] for shift in shifts]


def blocks_at(shards):
    me = lax.axis_index("src")
    at, odd = me // 2, lax.rem(me, 2)
    near = [me]
    for receivers in line_moves(shards // 2):
        senders = [receivers.index(there) for there in range(shards // 2)]
        near.append(2 * sum(jnp.where(at == there, sender, 0) for there, sender in enumerate(senders)) + odd)
    return near + [block ^ 1 for block in near]


def read_all(hbm, held, sems):
    copies = [pltpu.make_async_copy(src, dst, sems.at[i]) for i, (src, dst) in enumerate(zip(hbm, held))]
    for copy in copies:
        copy.start()
    return copies


def pack_kernel(*refs):
    hbm, (send_ref, weight_ref), held, sems = refs[:3], refs[3:5], refs[5:8], refs[8]
    for copy in read_all(hbm, held, sems):
        copy.wait()
    feat_ref, mass_ref, poten_ref = held
    feat = feat_ref[0]
    depth, cells = feat.shape
    weight = target_weight(mass_ref[...], poten_ref[...])
    norm = jnp.sum(feat * feat, axis=0, keepdims=True)
    bias = weight - (log2e / entropic) * norm
    scaled = feat * (2.0 * log2e / entropic)
    send_ref[0, :depth, 0, :] = scaled
    send_ref[0, depth, 0:1, :] = bias
    weight_ref[...] = weight


def source_kernel(shards, *refs):
    hbm, outs, held, sems = refs[:4], refs[4:8], refs[8:12], refs[12]
    wide_ref, norm_ref, mask_ref, mass_out_ref = outs
    mass_ref, support_ref, counts_ref, feat_ref = held
    copies = read_all(hbm, held, sems)
    for copy in copies[:3]:
        copy.wait()
    mass_out_ref[...] = mass_ref[...]
    support = support_ref[...]
    slots, rows = support.shape
    cells = mass_ref.shape[1]
    used = lax.broadcasted_iota(jnp.int32, support.shape, 0) < counts_ref[...]
    hits = [
        jnp.max(jnp.where(used & (support == block), 0.0, very_low), axis=0, keepdims=True)
        for block in blocks_at(shards)
    ]
    hits = jnp.concatenate(hits + [jnp.zeros((cells - shards, rows), jnp.float32)], axis=0)
    hits = jnp.concatenate([hits, jnp.zeros((cells, cells - rows), jnp.float32)], axis=1).T
    for place in range(shards):
        mask_ref[place] = jnp.broadcast_to(hits[:rows, place : place + 1], (rows, cells))
    copies[3].wait()
    depth = feat_ref.shape[1]
    one = jnp.ones((2 * depth, 2 * cells), jnp.bfloat16)
    for pair in range(rows // 2):
        for half in range(2):
            feat = feat_ref[2 * pair + half]
            norm_ref[2 * pair + half : 2 * pair + half + 1, :] = jnp.sum(feat * feat, axis=0, keepdims=True)
            high, mid, low = pieces(feat)
            lanes = slice(half * cells, (half + 1) * cells)
            top = jnp.concatenate([high, mid], axis=0).astype(jnp.bfloat16)
            wide_ref[pair, 0 : 2 * depth, lanes] = top
            wide_ref[pair, 2 * depth : 4 * depth, lanes] = top
            wide_ref[pair, 4 * depth : 6 * depth, lanes] = jnp.concatenate([low, high], axis=0).astype(jnp.bfloat16)
        wide_ref[pair, 6 * depth : 8 * depth, :] = one


def join_kernel(*refs):
    refs[-1][0] = refs[0][0]
    refs[-1][1] = refs[1][0]


def on_core(core, work, idle):
    if core is None:
        work()
    else:
        here = lax.axis_index("tgt") == core
        pl.when(here)(work)
        pl.when(jnp.logical_not(here))(idle)


def tile_kernel(parts, core, *refs):
    peak_ref, total_ref = refs[-2:]

    def idle():
        peak_ref[...] = jnp.zeros(peak_ref.shape, jnp.float32)
        total_ref[...] = jnp.zeros(total_ref.shape, jnp.float32)

    ins = refs[: parts + 1] + refs[-4:]
    on_core(core, functools.partial(make_tiles, parts, *ins), idle)


def make_tiles(parts, *refs):
    packs = [ref.at[index] for ref in refs[:parts] for index in range(ref.shape[0])]
    wide_ref, exps_ref, tall_ref, peak_ref, total_ref = refs[parts:]
    blocks = len(packs)
    pairs, _, both = wide_ref.shape
    cells = both // 2
    depth = cells // 2
    lane = lax.broadcasted_iota(jnp.int32, (cells, cells), 1)
    biases = jnp.concatenate([pack[depth, 0:1, :] for pack in packs], axis=0)
    bias_pieces = jnp.concatenate(list(pieces(biases)), axis=0)
    padded = jnp.concatenate([bias_pieces, jnp.zeros((cells - 3 * blocks, cells), jnp.float32)], axis=0)
    bias_lanes = padded.T
    for place, pack in enumerate(packs):
        feat = pack[:depth, 0, :]
        turned = jnp.concatenate([feat, feat], axis=0).T
        high, mid, low = pieces(turned)
        own = jnp.where(lax.rem(lane, blocks) == place, bias_lanes, 0.0)
        rows = slice(place * cells, (place + 1) * cells)
        tall_ref[rows, 0:cells] = high.astype(jnp.bfloat16)
        tall_ref[rows, cells : 2 * cells] = mid.astype(jnp.bfloat16)
        tall_ref[rows, 2 * cells : 3 * cells] = jnp.where(lane < depth, high, low).astype(jnp.bfloat16)
        tall_ref[rows, 3 * cells : 4 * cells] = own.astype(jnp.bfloat16)

    def body(pair, carry):
        scores = jnp.dot(tall_ref[...], wide_ref[pair], preferred_element_type=jnp.float32)
        for place in range(blocks):
            rows = slice(place * cells, (place + 1) * cells)
            score = scores[rows]
            peak = jnp.max(score, axis=0, keepdims=True)
            exps = jnp.exp2(score - peak)
            exps_ref[pair, rows, :] = exps
            total = jnp.sum(exps, axis=0, keepdims=True)
            for half in range(2):
                lanes = slice(half * cells, (half + 1) * cells)
                peak_ref[place, pl.ds(2 * pair + half, 1), :] = peak[:, lanes]
                total_ref[place, pl.ds(2 * pair + half, 1), :] = total[:, lanes]
        return carry

    lax.fori_loop(0, pairs, body, 0, unroll=min(pairs, 16 // blocks & -4 or 2))


def row_kernel(groups, *refs):
    mask_ref, peak_refs, total_refs = refs[0], refs[1 : 1 + groups], refs[1 + groups : 1 + 2 * groups]
    peaks_ref, rowsum_ref = refs[1 + 2 * groups :]
    place = 0
    for ref in peak_refs:
        for index in range(ref.shape[0]):
            peaks_ref[place] = ref[index] + mask_ref[place]
            place += 1
    totals = [ref[index] for ref in total_refs for index in range(ref.shape[0])]
    top = functools.reduce(jnp.maximum, [peaks_ref[index] for index in range(place)])
    summed = sum(total * jnp.exp2(peaks_ref[index] - top) for index, total in enumerate(totals))
    rowsum_ref[...] = top + jnp.log2(summed)


def across(column):
    shape = (column.shape[0],) * 2
    same = lax.broadcasted_iota(jnp.int32, shape, 0) == lax.broadcasted_iota(jnp.int32, shape, 1)
    return jnp.sum(jnp.where(same, jnp.broadcast_to(column, shape), 0.0), axis=0, keepdims=True)


def column_kernel(groups, core, *refs):
    ins, outs, scratch = refs[: 2 * groups + 7], refs[-4:-2], refs[-2:]

    def idle():
        for given, out in zip(refs[2 * groups + 7 : -4], outs):
            out[...] = given[...]

    on_core(core, functools.partial(sum_columns, groups, *ins, *outs, *scratch), idle)


def sum_columns(groups, *refs):
    exps_refs, tall_refs, rest = refs[:groups], refs[groups : 2 * groups], refs[2 * groups :]
    wide_ref, peak_ref, mask_ref, own_ref, other_ref, mass_ref, norm_ref = rest[:7]
    poten_ref, sums_ref, weight_ref, shift_ref = rest[7:]
    pairs, _, both = wide_ref.shape
    cells = both // 2
    shards = mask_ref.shape[0]
    own, other = own_ref[...], other_ref[...]
    top = jnp.maximum(own, other)
    whole = top + jnp.log2(jnp.exp2(own - top) + jnp.exp2(other - top))
    poten_ref[...] = norm_ref[...] - (entropic * ln2) * whole
    shift = mass_ref[...] * log2e - whole
    shift_ref[...] = shift
    for place in range(shards):
        weight_ref[place] = jnp.exp2(peak_ref[place] + shift)
    spots = [
        (group, slice(index * cells, (index + 1) * cells))
        for group, ref in enumerate(tall_refs)
        for index in range(ref.shape[0] // cells)
    ]
    used = [jnp.max(mask_ref[place], axis=0, keepdims=True) > 0.5 * very_low for place in range(shards)]
    ranks = [shards - 1 - block for block in blocks_at(shards)]
    sums = []
    for place, (group, rows) in enumerate(spots):
        acc = jnp.zeros((cells, cells), jnp.float32)
        for pair in range(pairs):
            acc = acc + exps_refs[group][pair, rows, :cells] * weight_ref[place, 2 * pair : 2 * pair + 1, :]
            acc = acc + exps_refs[group][pair, rows, cells:] * weight_ref[place, 2 * pair + 1 : 2 * pair + 2, :]
        sums.append(jnp.sum(acc.T, axis=0, keepdims=True))
    whole_sums = jnp.concatenate([jnp.where(here, one, 1.0) for here, one in zip(used, sums)], axis=0)
    worst = jnp.min(whole_sums)
    logs = jnp.log2(whole_sums)
    for place in range(shards):
        sums_ref[ranks[place]] = jnp.where(used[place], logs[place : place + 1, :], very_low)

    @pl.when(worst < least_sum)
    def _():
        for place, (group, rows) in enumerate(spots):

            def exponents(pair):
                score = jnp.dot(tall_refs[group][rows, :], wide_ref[pair], preferred_element_type=jnp.float32)
                add = shift_ref[pl.ds(2 * pair, 2), :] + mask_ref[place, pl.ds(2 * pair, 2), :]
                return score[:, :cells] + add[0:1, :], score[:, cells:] + add[1:2, :]

            def highest(pair, peak):
                first, second = exponents(pair)
                return jnp.maximum(peak, jnp.maximum(first, second))

            peak = lax.fori_loop(0, pairs, highest, jnp.full((cells, cells), very_low, jnp.float32))
            peak = jnp.max(peak, axis=1, keepdims=True)

            def add_up(pair, sums):
                first, second = exponents(pair)
                return sums + jnp.exp2(first - peak) + jnp.exp2(second - peak)

            sums = lax.fori_loop(0, pairs, add_up, jnp.zeros((cells, cells), jnp.float32))
            logs = across(peak) + jnp.log2(across(jnp.sum(sums, axis=1, keepdims=True)))
            sums_ref[ranks[place]] = jnp.where(used[place], logs, very_low)


def merge_kernel(values_ref, weight_ref, poten_ref, out_ref, poten_out_ref):
    poten_out_ref[...] = poten_ref[...]
    values = values_ref[...]
    top = jnp.max(values, axis=0)
    whole = top + jnp.log2(jnp.sum(jnp.exp2(values - top), axis=0))
    out_ref[...] = -(entropic * ln2) * (whole - weight_ref[...])


def f32(*shape):
    return jax.ShapeDtypeStruct(shape, jnp.float32)


def dense_device(
    source_feat, target_feat, log_mass_src, log_mass_tgt, potential_tgt, support, counts
):
    shards = lax.axis_size("src")
    rows, depth, cells = source_feat.shape
    pairs, wide = rows // 2, 2 * cells

    def call(kernel, ins, out_shape, scratch=(), cost=None):
        many = isinstance(out_shape, list)
        return pl.pallas_call(
            kernel,
            in_specs=ins,
            out_specs=[VM] * len(out_shape) if many else VM,
            out_shape=out_shape,
            scratch_shapes=list(scratch),
            compiler_params=PARAMS,
            cost_estimate=cost,
        )

    def reading(kernel, args, out_shape, cost):
        return call(
            kernel,
            [pl.BlockSpec(memory_space=pltpu.HBM)] * len(args),
            out_shape,
            [pltpu.VMEM(arg.shape, arg.dtype) for arg in args] + [pltpu.SemaphoreType.DMA((len(args),))],
            cost,
        )(*[pltpu.with_memory_space_constraint(arg, pltpu.HBM) for arg in args])

    def cost_of(flops):
        return pl.CostEstimate(flops=flops, bytes_accessed=rows * depth * cells * 4, transcendentals=0)

    pack, weight = reading(
        pack_kernel,
        [target_feat, log_mass_tgt, potential_tgt],
        [in_vmem((1, depth + 1, 1, cells), jnp.float32), in_vmem((1, cells), jnp.float32)],
        None,
    )
    wide_feat, norm, mask, mass = reading(
        functools.partial(source_kernel, shards),
        [log_mass_src, support[:, 0, :].T, counts.T, source_feat],
        [
            in_vmem((pairs, 8 * depth, wide), jnp.bfloat16),
            in_vmem((rows, cells), jnp.float32),
            in_vmem((shards, rows, cells), jnp.float32),
            in_vmem((rows, cells), jnp.float32),
        ],
        cost_of(10**8),
    )

    def tiles(*packs, core=None, after=None):
        blocks = sum(pack.shape[0] for pack in packs)
        more = [] if after is None else [after]
        return call(
            functools.partial(tile_kernel, len(packs), core),
            [VM] * (len(packs) + 1) + [pl.BlockSpec(memory_space=pl.ANY)] * len(more),
            [
                in_vmem((pairs, blocks * cells, wide), jnp.float32),
                in_vmem((blocks * cells, 8 * depth), jnp.bfloat16),
                in_vmem((blocks, rows, cells), jnp.float32),
                in_vmem((blocks, rows, cells), jnp.float32),
            ],
            cost=cost_of(2 * blocks * cells * pairs * wide * 8 * depth),
        )(*packs, wide_feat, *more)

    def swapped(array):
        return lax.ppermute(array, "src", [(i, i ^ 1) for i in range(shards)])

    def moved(array, receivers):
        moves = [(2 * here + odd, 2 * there + odd) for here, there in enumerate(receivers) for odd in range(2)]
        return lax.ppermute(array, "src", moves)

    def joined(first, second, after):
        return call(
            join_kernel,
            [VM] * 2 + [pl.BlockSpec(memory_space=pl.ANY)],
            in_vmem((2,) + pack.shape[1:], jnp.float32),
        )(first, second, after)

    there = [moved(pack, receivers) for receivers in line_moves(shards // 2)[::-1]][::-1]
    near = [pack] + there
    halves = [joined(near[0], near[1], norm)]
    found = [tiles(pack, after=halves[0])]
    halves += [joined(near[at], near[at + 1], found[0][-1]) for at in range(2, shards // 2, 2)]
    far = [swapped(half) for half in halves]
    found.append(tiles(*there))
    for half in far[:-1]:
        found.append(tiles(half, after=found[-1][-1]))
    groups = len(found) + 1

    def log_sums(last):
        _, _, peaks, totals = zip(*found, last)
        return call(
            functools.partial(row_kernel, groups),
            [VM] * (1 + 2 * groups),
            [in_vmem((shards, rows, cells), jnp.float32), in_vmem((rows, cells), jnp.float32)],
        )(mask, *peaks, *totals)

    def columns_of(core, last, peaks, own, other, given):
        exps, tall, _, _ = zip(*found, last)
        return call(
            functools.partial(column_kernel, groups, core),
            [VM] * (2 * groups + 7 + len(given)),
            [in_vmem((rows, cells), jnp.float32), in_vmem((shards, 1, cells), jnp.float32)],
            [pltpu.VMEM((shards, rows, cells), jnp.float32), pltpu.VMEM((rows, cells), jnp.float32)],
            cost_of(10**9),
        )(*exps, *tall, wide_feat, peaks, mask, own, other, mass, norm, *given)

    between = [(0, 1), (1, 0)]
    last_one = tiles(far[-1], core=1, after=found[-1][-1])
    peaks_one, own_one = log_sums(last_one)
    other_zero = lax.ppermute(own_one, "tgt", between)
    last_zero = tiles(far[-1], core=0, after=own_one)
    peaks_zero, own_zero = log_sums(last_zero)
    other_one = lax.ppermute(own_zero, "tgt", between)
    given = columns_of(0, last_zero, peaks_zero, own_zero, other_zero, [])
    potential_src, columns = columns_of(1, last_one, peaks_one, own_one, other_one, given)
    arrived = lax.all_to_all(columns, "src", 0, 0, axis_index_groups=[list(range(shards))[::-1]])
    outs = [f32(1, cells), f32(rows, cells)]
    potential_new, potential_src = call(merge_kernel, [VM] * 3, outs)(arrived, weight, potential_src)
    return potential_src, potential_new


def merged(part, axis, combine):
    gathered = jax.tree.map(lambda a: lax.all_gather(a, axis), part)

    def take(source):
        return jax.tree.map(lambda a: lax.dynamic_index_in_dim(a, source, 0, False), gathered)

    return lax.fori_loop(
        1, lax.axis_size(axis), lambda source, state: combine(state, take(source)), take(0)
    )


def cost_tiles(source_blk, source_sq, target_blk, target_sq):
    cross = jnp.einsum(
        "...fi,...fj->...ij", source_blk, target_blk, precision=lax.Precision.HIGHEST
    )
    return source_sq[..., :, None] + target_sq[..., None, :] - 2.0 * cross


def row_stats(cost, mass_tgt, poten_tgt, usable):
    scores = mass_tgt[..., None, :] + (poten_tgt[..., None, :] - cost) / entropic
    scores = jnp.where(usable[..., None, None], scores, very_low)
    peak = jnp.max(scores, axis=(1, 3))
    total = jnp.sum(jnp.exp(scores - peak[:, None, :, None]), axis=(1, 3))
    return (peak, total)


def column_stats(cost, mass_src, poten_src, usable):
    scores = mass_src[:, None, :, None] + (poten_src[:, None, :, None] - cost) / entropic
    peak = jnp.max(scores, axis=2)
    total = jnp.sum(jnp.exp(scores - peak[:, :, None, :]), axis=2)
    peak = jnp.where(usable[..., None], peak, very_low)
    total = jnp.where(usable[..., None], total, 0.0)
    return (peak, total)


def merge_pair(first_pair, second_pair):
    first_peak, first_total = first_pair
    second_peak, second_total = second_pair
    highest = jnp.maximum(first_peak, second_peak)
    summed = first_total * jnp.exp(first_peak - highest) + second_total * jnp.exp(
        second_peak - highest
    )
    return (highest, summed)


def segment_merge(peaks, totals, seg_ids, segments):
    best = jax.ops.segment_max(peaks, seg_ids, num_segments=segments + 1)
    best = jnp.maximum(best, very_low)
    summed = jax.ops.segment_sum(
        totals * jnp.exp(peaks - best[seg_ids]), seg_ids, num_segments=segments + 1
    )
    return (best[:segments], summed[:segments])


def general_device(
    source_feat, target_feat, log_mass_src, log_mass_tgt, potential_tgt, support, counts
):
    target_all, mass_all, poten_all = (
        lax.all_gather(target_feat, "src", axis=0, tiled=True),
        lax.all_gather(log_mass_tgt, "src", axis=0, tiled=True),
        lax.all_gather(potential_tgt, "src", axis=0, tiled=True),
    )
    blocks = target_all.shape[0]
    rows_here = source_feat.shape[0]
    slots_here = support.shape[2]
    cells = source_feat.shape[2]
    indices = support[:, 0, :]
    limits = counts[:, 0]
    usable = jnp.arange(slots_here, dtype=jnp.int32)[None, :] < limits[:, None]
    source_sq = jnp.sum(source_feat * source_feat, axis=1)
    target_sq = jnp.sum(target_all * target_all, axis=1)
    width = math.gcd(rows_here, 4)

    def grouped(array):
        return array.reshape((rows_here // width, width) + array.shape[1:])

    def row_pass(items):
        source_blk, source_nrm, ids_here, use_here = items
        cost = cost_tiles(
            source_blk[:, None], source_nrm[:, None], target_all[ids_here], target_sq[ids_here]
        )
        return row_stats(cost, mass_all[ids_here], poten_all[ids_here], use_here)

    peak, total = lax.map(
        row_pass, (grouped(source_feat), grouped(source_sq), grouped(indices), grouped(usable))
    )
    peak = peak.reshape(rows_here, cells)
    total = total.reshape(rows_here, cells)
    peak_all, total_all = merged((peak, total), "tgt", merge_pair)
    potential_src = -entropic * (peak_all + jnp.log(total_all))

    def column_pass(items):
        source_blk, source_nrm, mass_here, poten_here, ids_here, use_here = items
        cost = cost_tiles(
            source_blk[:, None], source_nrm[:, None], target_all[ids_here], target_sq[ids_here]
        )
        return column_stats(cost, mass_here, poten_here, use_here)

    peaks, totals = lax.map(
        column_pass,
        (
            grouped(source_feat),
            grouped(source_sq),
            grouped(log_mass_src),
            grouped(potential_src),
            grouped(indices),
            grouped(usable),
        ),
    )
    seg_ids = jnp.where(usable, indices, blocks).reshape(-1)
    best, summed = segment_merge(
        peaks.reshape(-1, cells), totals.reshape(-1, cells), seg_ids, blocks
    )
    share = blocks // lax.axis_size("src")
    own_start = lax.axis_index("src") * share
    highest = lax.pmax(best, "src")
    whole = lax.psum(summed * jnp.exp(best - highest), "src")
    own_peak = lax.dynamic_slice_in_dim(highest, own_start, share, 0)
    own_total = lax.dynamic_slice_in_dim(whole, own_start, share, 0)
    potential_new = -entropic * (own_peak + jnp.log(own_total))
    return (potential_src, potential_new)


def per_device(source_feat, target_feat, *others):
    shards = lax.axis_size("src")
    rows, depth, cells = source_feat.shape
    paired = shards >= 4 and shards & (shards - 1) == 0 and lax.axis_size("tgt") == 2
    shaped = target_feat.shape[0] == 1 and rows % 2 == 0 and cells == 2 * depth and cells % 128 == 0
    if paired and shaped and 4 * rows * cells * shards * cells <= room:
        return dense_device(source_feat, target_feat, *others)
    return general_device(source_feat, target_feat, *others)


def solution(mesh):
    in_specs = (
        P(("grp", "src"), None, None),
        P(("grp", "src", "tgt"), None, None),
        P(("grp", "src"), None),
        P(("grp", "src", "tgt"), None),
        P(("grp", "src", "tgt"), None),
        P(("grp", "src"), "tgt", None),
        P(("grp", "src"), "tgt"),
    )
    out_specs = (P(("grp", "src"), None), P(("grp", "src", "tgt"), None))
    return jax.shard_map(
        per_device, mesh=mesh, in_specs=in_specs, out_specs=out_specs, check_vma=False
    )
```

```python
import functools
import math

import jax
import jax.numpy as jnp
from jax import lax
from jax.experimental import pallas as pl
from jax.experimental.pallas import tpu as pltpu
from jax.sharding import PartitionSpec as P

entropic = 0.5
very_low = -1e30
log2e = 1.0 / math.log(2.0)
ln2 = math.log(2.0)
least_sum = 1e-28

room = 2**24

VM = pl.BlockSpec(memory_space=pltpu.VMEM)
PARAMS = pltpu.CompilerParams(vmem_limit_bytes=40 * 2**20)


def in_vmem(shape, dtype):
    return pltpu.VMEM(shape, dtype)


def pieces(values):
    high = values.astype(jnp.bfloat16).astype(jnp.float32)
    rest = values - high
    mid = rest.astype(jnp.bfloat16).astype(jnp.float32)
    low = (rest - mid).astype(jnp.bfloat16).astype(jnp.float32)
    return high, mid, low


def target_weight(mass, poten):
    return (mass + poten / entropic) * log2e


def line_moves(line):
    bits = line.bit_length() - 1
    cycle = [sum(((place >> bit) & 1) << (bits - 1 - bit) for bit in range(bits)) for place in range(line)]
    shifts = [shift for step in range(1, line // 2) for shift in (step, line - step)] + [line // 2]
    return [[cycle[(cycle.index(at) + shift) % line] for at in range(line)] for shift in shifts]


def blocks_at(shards):
    me = lax.axis_index("src")
    at, odd = me // 2, lax.rem(me, 2)
    near = [me]
    for receivers in line_moves(shards // 2):
        senders = [receivers.index(there) for there in range(shards // 2)]
        near.append(2 * sum(jnp.where(at == there, sender, 0) for there, sender in enumerate(senders)) + odd)
    return near + [block ^ 1 for block in near]


def read_all(hbm, held, sems):
    copies = [pltpu.make_async_copy(src, dst, sems.at[i]) for i, (src, dst) in enumerate(zip(hbm, held))]
    for copy in copies:
        copy.start()
    return copies


def pack_kernel(*refs):
    hbm, (send_ref, weight_ref), held, sems = refs[:3], refs[3:5], refs[5:8], refs[8]
    for copy in read_all(hbm, held, sems):
        copy.wait()
    feat_ref, mass_ref, poten_ref = held
    feat = feat_ref[0]
    depth, cells = feat.shape
    weight = target_weight(mass_ref[...], poten_ref[...])
    norm = jnp.sum(feat * feat, axis=0, keepdims=True)
    bias = weight - (log2e / entropic) * norm
    scaled = feat * (2.0 * log2e / entropic)
    send_ref[0, :depth, 0, :] = scaled
    send_ref[0, depth, 0:1, :] = bias
    weight_ref[...] = weight


def source_kernel(shards, *refs):
    hbm, outs, held, sems = refs[:4], refs[4:8], refs[8:12], refs[12]
    wide_ref, norm_ref, mask_ref, mass_out_ref = outs
    mass_ref, support_ref, counts_ref, feat_ref = held
    copies = read_all(hbm, held, sems)
    for copy in copies[:3]:
        copy.wait()
    mass_out_ref[...] = mass_ref[...]
    support = support_ref[...]
    slots, rows = support.shape
    cells = mass_ref.shape[1]
    used = lax.broadcasted_iota(jnp.int32, support.shape, 0) < counts_ref[...]
    hits = [
        jnp.max(jnp.where(used & (support == block), 0.0, very_low), axis=0, keepdims=True)
        for block in blocks_at(shards)
    ]
    hits = jnp.concatenate(hits + [jnp.zeros((cells - shards, rows), jnp.float32)], axis=0)
    hits = jnp.concatenate([hits, jnp.zeros((cells, cells - rows), jnp.float32)], axis=1).T
    for place in range(shards):
        mask_ref[place] = jnp.broadcast_to(hits[:rows, place : place + 1], (rows, cells))
    copies[3].wait()
    depth = feat_ref.shape[1]
    one = jnp.ones((2 * depth, 2 * cells), jnp.bfloat16)
    for pair in range(rows // 2):
        for half in range(2):
            feat = feat_ref[2 * pair + half]
            norm_ref[2 * pair + half : 2 * pair + half + 1, :] = jnp.sum(feat * feat, axis=0, keepdims=True)
            high, mid, low = pieces(feat)
            lanes = slice(half * cells, (half + 1) * cells)
            top = jnp.concatenate([high, mid], axis=0).astype(jnp.bfloat16)
            wide_ref[pair, 0 : 2 * depth, lanes] = top
            wide_ref[pair, 2 * depth : 4 * depth, lanes] = top
            wide_ref[pair, 4 * depth : 6 * depth, lanes] = jnp.concatenate([low, high], axis=0).astype(jnp.bfloat16)
        wide_ref[pair, 6 * depth : 8 * depth, :] = one


def join_kernel(*refs):
    refs[-1][0] = refs[0][0]
    refs[-1][1] = refs[1][0]


def on_core(core, work, idle):
    if core is None:
        work()
    else:
        here = lax.axis_index("tgt") == core
        pl.when(here)(work)
        pl.when(jnp.logical_not(here))(idle)


def tile_kernel(parts, core, *refs):
    peak_ref, total_ref = refs[-2:]

    def idle():
        peak_ref[...] = jnp.zeros(peak_ref.shape, jnp.float32)
        total_ref[...] = jnp.zeros(total_ref.shape, jnp.float32)

    ins = refs[: parts + 1] + refs[-4:]
    on_core(core, functools.partial(make_tiles, parts, *ins), idle)


def make_tiles(parts, *refs):
    packs = [ref.at[index] for ref in refs[:parts] for index in range(ref.shape[0])]
    wide_ref, exps_ref, tall_ref, peak_ref, total_ref = refs[parts:]
    blocks = len(packs)
    pairs, _, both = wide_ref.shape
    cells = both // 2
    depth = cells // 2
    lane = lax.broadcasted_iota(jnp.int32, (cells, cells), 1)
    biases = jnp.concatenate([pack[depth, 0:1, :] for pack in packs], axis=0)
    bias_pieces = jnp.concatenate(list(pieces(biases)), axis=0)
    padded = jnp.concatenate([bias_pieces, jnp.zeros((cells - 3 * blocks, cells), jnp.float32)], axis=0)
    bias_lanes = padded.T
    for place, pack in enumerate(packs):
        feat = pack[:depth, 0, :]
        turned = jnp.concatenate([feat, feat], axis=0).T
        high, mid, low = pieces(turned)
        own = jnp.where(lax.rem(lane, blocks) == place, bias_lanes, 0.0)
        rows = slice(place * cells, (place + 1) * cells)
        tall_ref[rows, 0:cells] = high.astype(jnp.bfloat16)
        tall_ref[rows, cells : 2 * cells] = mid.astype(jnp.bfloat16)
        tall_ref[rows, 2 * cells : 3 * cells] = jnp.where(lane < depth, high, low).astype(jnp.bfloat16)
        tall_ref[rows, 3 * cells : 4 * cells] = own.astype(jnp.bfloat16)

    def body(pair, carry):
        scores = jnp.dot(tall_ref[...], wide_ref[pair], preferred_element_type=jnp.float32)
        for place in range(blocks):
            rows = slice(place * cells, (place + 1) * cells)
            score = scores[rows]
            peak = jnp.max(score, axis=0, keepdims=True)
            exps = jnp.exp2(score - peak)
            exps_ref[pair, rows, :] = exps
            total = jnp.sum(exps, axis=0, keepdims=True)
            for half in range(2):
                lanes = slice(half * cells, (half + 1) * cells)
                peak_ref[place, pl.ds(2 * pair + half, 1), :] = peak[:, lanes]
                total_ref[place, pl.ds(2 * pair + half, 1), :] = total[:, lanes]
        return carry

    lax.fori_loop(0, pairs, body, 0, unroll=max(1, min(pairs, 32 // blocks)))


def row_kernel(groups, *refs):
    mask_ref, peak_refs, total_refs = refs[0], refs[1 : 1 + groups], refs[1 + groups : 1 + 2 * groups]
    peaks_ref, rowsum_ref = refs[1 + 2 * groups :]
    place = 0
    for ref in peak_refs:
        for index in range(ref.shape[0]):
            peaks_ref[place] = ref[index] + mask_ref[place]
            place += 1
    totals = [ref[index] for ref in total_refs for index in range(ref.shape[0])]
    top = functools.reduce(jnp.maximum, [peaks_ref[index] for index in range(place)])
    summed = sum(total * jnp.exp2(peaks_ref[index] - top) for index, total in enumerate(totals))
    rowsum_ref[...] = top + jnp.log2(summed)


def across(column):
    shape = (column.shape[0],) * 2
    same = lax.broadcasted_iota(jnp.int32, shape, 0) == lax.broadcasted_iota(jnp.int32, shape, 1)
    return jnp.sum(jnp.where(same, jnp.broadcast_to(column, shape), 0.0), axis=0, keepdims=True)


def column_kernel(groups, core, *refs):
    ins, outs, scratch = refs[: 2 * groups + 7], refs[-4:-2], refs[-2:]

    def idle():
        for given, out in zip(refs[2 * groups + 7 : -4], outs):
            out[...] = given[...]

    on_core(core, functools.partial(sum_columns, groups, *ins, *outs, *scratch), idle)


def sum_columns(groups, *refs):
    exps_refs, tall_refs, rest = refs[:groups], refs[groups : 2 * groups], refs[2 * groups :]
    wide_ref, peak_ref, mask_ref, own_ref, other_ref, mass_ref, norm_ref = rest[:7]
    poten_ref, sums_ref, weight_ref, shift_ref = rest[7:]
    pairs, _, both = wide_ref.shape
    cells = both // 2
    shards = mask_ref.shape[0]
    own, other = own_ref[...], other_ref[...]
    top = jnp.maximum(own, other)
    whole = top + jnp.log2(jnp.exp2(own - top) + jnp.exp2(other - top))
    poten_ref[...] = norm_ref[...] - (entropic * ln2) * whole
    shift = mass_ref[...] * log2e - whole
    shift_ref[...] = shift
    for place in range(shards):
        weight_ref[place] = jnp.exp2(peak_ref[place] + shift)
    spots = [
        (group, slice(index * cells, (index + 1) * cells))
        for group, ref in enumerate(tall_refs)
        for index in range(ref.shape[0] // cells)
    ]
    used = [jnp.max(mask_ref[place], axis=0, keepdims=True) > 0.5 * very_low for place in range(shards)]
    ranks = [shards - 1 - block for block in blocks_at(shards)]
    sums = []
    for place, (group, rows) in enumerate(spots):
        acc = jnp.zeros((cells, cells), jnp.float32)
        for pair in range(pairs):
            acc = acc + exps_refs[group][pair, rows, :cells] * weight_ref[place, 2 * pair : 2 * pair + 1, :]
            acc = acc + exps_refs[group][pair, rows, cells:] * weight_ref[place, 2 * pair + 1 : 2 * pair + 2, :]
        sums.append(jnp.sum(acc.T, axis=0, keepdims=True))
    whole_sums = jnp.concatenate([jnp.where(here, one, 1.0) for here, one in zip(used, sums)], axis=0)
    worst = jnp.min(whole_sums)
    logs = jnp.log2(whole_sums)
    for place in range(shards):
        sums_ref[ranks[place]] = jnp.where(used[place], logs[place : place + 1, :], very_low)

    @pl.when(worst < least_sum)
    def _():
        for place, (group, rows) in enumerate(spots):

            def exponents(pair):
                score = jnp.dot(tall_refs[group][rows, :], wide_ref[pair], preferred_element_type=jnp.float32)
                add = shift_ref[pl.ds(2 * pair, 2), :] + mask_ref[place, pl.ds(2 * pair, 2), :]
                return score[:, :cells] + add[0:1, :], score[:, cells:] + add[1:2, :]

            def highest(pair, peak):
                first, second = exponents(pair)
                return jnp.maximum(peak, jnp.maximum(first, second))

            peak = lax.fori_loop(0, pairs, highest, jnp.full((cells, cells), very_low, jnp.float32))
            peak = jnp.max(peak, axis=1, keepdims=True)

            def add_up(pair, sums):
                first, second = exponents(pair)
                return sums + jnp.exp2(first - peak) + jnp.exp2(second - peak)

            sums = lax.fori_loop(0, pairs, add_up, jnp.zeros((cells, cells), jnp.float32))
            logs = across(peak) + jnp.log2(across(jnp.sum(sums, axis=1, keepdims=True)))
            sums_ref[ranks[place]] = jnp.where(used[place], logs, very_low)


def merge_kernel(values_ref, weight_ref, poten_ref, out_ref, poten_out_ref):
    poten_out_ref[...] = poten_ref[...]
    values = values_ref[...]
    top = jnp.max(values, axis=0)
    whole = top + jnp.log2(jnp.sum(jnp.exp2(values - top), axis=0))
    out_ref[...] = -(entropic * ln2) * (whole - weight_ref[...])


def f32(*shape):
    return jax.ShapeDtypeStruct(shape, jnp.float32)


def dense_device(
    source_feat, target_feat, log_mass_src, log_mass_tgt, potential_tgt, support, counts
):
    shards = lax.axis_size("src")
    rows, depth, cells = source_feat.shape
    pairs, wide = rows // 2, 2 * cells

    def call(kernel, ins, out_shape, scratch=(), cost=None):
        many = isinstance(out_shape, list)
        return pl.pallas_call(
            kernel,
            in_specs=ins,
            out_specs=[VM] * len(out_shape) if many else VM,
            out_shape=out_shape,
            scratch_shapes=list(scratch),
            compiler_params=PARAMS,
            cost_estimate=cost,
        )

    def reading(kernel, args, out_shape, cost):
        return call(
            kernel,
            [pl.BlockSpec(memory_space=pltpu.HBM)] * len(args),
            out_shape,
            [pltpu.VMEM(arg.shape, arg.dtype) for arg in args] + [pltpu.SemaphoreType.DMA((len(args),))],
            cost,
        )(*[pltpu.with_memory_space_constraint(arg, pltpu.HBM) for arg in args])

    def cost_of(flops):
        return pl.CostEstimate(flops=flops, bytes_accessed=rows * depth * cells * 4, transcendentals=0)

    pack, weight = reading(
        pack_kernel,
        [target_feat, log_mass_tgt, potential_tgt],
        [in_vmem((1, depth + 1, 1, cells), jnp.float32), in_vmem((1, cells), jnp.float32)],
        None,
    )
    wide_feat, norm, mask, mass = reading(
        functools.partial(source_kernel, shards),
        [log_mass_src, support[:, 0, :].T, counts.T, source_feat],
        [
            in_vmem((pairs, 8 * depth, wide), jnp.bfloat16),
            in_vmem((rows, cells), jnp.float32),
            in_vmem((shards, rows, cells), jnp.float32),
            in_vmem((rows, cells), jnp.float32),
        ],
        cost_of(10**8),
    )

    def tiles(*packs, core=None, after=None):
        blocks = sum(pack.shape[0] for pack in packs)
        more = [] if after is None else [after]
        return call(
            functools.partial(tile_kernel, len(packs), core),
            [VM] * (len(packs) + 1) + [pl.BlockSpec(memory_space=pl.ANY)] * len(more),
            [
                in_vmem((pairs, blocks * cells, wide), jnp.float32),
                in_vmem((blocks * cells, 8 * depth), jnp.bfloat16),
                in_vmem((blocks, rows, cells), jnp.float32),
                in_vmem((blocks, rows, cells), jnp.float32),
            ],
            cost=cost_of(2 * blocks * cells * pairs * wide * 8 * depth),
        )(*packs, wide_feat, *more)

    def swapped(array):
        return lax.ppermute(array, "src", [(i, i ^ 1) for i in range(shards)])

    def moved(array, receivers):
        moves = [(2 * here + odd, 2 * there + odd) for here, there in enumerate(receivers) for odd in range(2)]
        return lax.ppermute(array, "src", moves)

    def joined(first, second, after):
        return call(
            join_kernel,
            [VM] * 2 + [pl.BlockSpec(memory_space=pl.ANY)],
            in_vmem((2,) + pack.shape[1:], jnp.float32),
        )(first, second, after)

    there = [moved(pack, receivers) for receivers in line_moves(shards // 2)[::-1]][::-1]
    near = [pack] + there
    halves = [joined(near[0], near[1], norm)]
    for at in range(2, shards // 2, 2):
        halves.append(joined(near[at], near[at + 1], halves[-1]))
    far = [swapped(half) for half in halves]
    found = [tiles(*near, after=halves[-1])]
    for half in far[:-1]:
        found.append(tiles(half, after=found[-1][-1]))
    groups = len(found) + 1

    def log_sums(last):
        _, _, peaks, totals = zip(*found, last)
        return call(
            functools.partial(row_kernel, groups),
            [VM] * (1 + 2 * groups),
            [in_vmem((shards, rows, cells), jnp.float32), in_vmem((rows, cells), jnp.float32)],
        )(mask, *peaks, *totals)

    def columns_of(core, last, peaks, own, other, given):
        exps, tall, _, _ = zip(*found, last)
        return call(
            functools.partial(column_kernel, groups, core),
            [VM] * (2 * groups + 7 + len(given)),
            [in_vmem((rows, cells), jnp.float32), in_vmem((shards, 1, cells), jnp.float32)],
            [pltpu.VMEM((shards, rows, cells), jnp.float32), pltpu.VMEM((rows, cells), jnp.float32)],
            cost_of(10**9),
        )(*exps, *tall, wide_feat, peaks, mask, own, other, mass, norm, *given)

    between = [(0, 1), (1, 0)]
    last_one = tiles(far[-1], core=1, after=found[-1][-1])
    peaks_one, own_one = log_sums(last_one)
    other_zero = lax.ppermute(own_one, "tgt", between)
    last_zero = tiles(far[-1], core=0, after=own_one)
    peaks_zero, own_zero = log_sums(last_zero)
    other_one = lax.ppermute(own_zero, "tgt", between)
    given = columns_of(0, last_zero, peaks_zero, own_zero, other_zero, [])
    potential_src, columns = columns_of(1, last_one, peaks_one, own_one, other_one, given)
    arrived = lax.all_to_all(columns, "src", 0, 0, axis_index_groups=[list(range(shards))[::-1]])
    outs = [f32(1, cells), f32(rows, cells)]
    potential_new, potential_src = call(merge_kernel, [VM] * 3, outs)(arrived, weight, potential_src)
    return potential_src, potential_new


def merged(part, axis, combine):
    gathered = jax.tree.map(lambda a: lax.all_gather(a, axis), part)

    def take(source):
        return jax.tree.map(lambda a: lax.dynamic_index_in_dim(a, source, 0, False), gathered)

    return lax.fori_loop(
        1, lax.axis_size(axis), lambda source, state: combine(state, take(source)), take(0)
    )


def cost_tiles(source_blk, source_sq, target_blk, target_sq):
    cross = jnp.einsum(
        "...fi,...fj->...ij", source_blk, target_blk, precision=lax.Precision.HIGHEST
    )
    return source_sq[..., :, None] + target_sq[..., None, :] - 2.0 * cross


def row_stats(cost, mass_tgt, poten_tgt, usable):
    scores = mass_tgt[..., None, :] + (poten_tgt[..., None, :] - cost) / entropic
    scores = jnp.where(usable[..., None, None], scores, very_low)
    peak = jnp.max(scores, axis=(1, 3))
    total = jnp.sum(jnp.exp(scores - peak[:, None, :, None]), axis=(1, 3))
    return (peak, total)


def column_stats(cost, mass_src, poten_src, usable):
    scores = mass_src[:, None, :, None] + (poten_src[:, None, :, None] - cost) / entropic
    peak = jnp.max(scores, axis=2)
    total = jnp.sum(jnp.exp(scores - peak[:, :, None, :]), axis=2)
    peak = jnp.where(usable[..., None], peak, very_low)
    total = jnp.where(usable[..., None], total, 0.0)
    return (peak, total)


def merge_pair(first_pair, second_pair):
    first_peak, first_total = first_pair
    second_peak, second_total = second_pair
    highest = jnp.maximum(first_peak, second_peak)
    summed = first_total * jnp.exp(first_peak - highest) + second_total * jnp.exp(
        second_peak - highest
    )
    return (highest, summed)


def segment_merge(peaks, totals, seg_ids, segments):
    best = jax.ops.segment_max(peaks, seg_ids, num_segments=segments + 1)
    best = jnp.maximum(best, very_low)
    summed = jax.ops.segment_sum(
        totals * jnp.exp(peaks - best[seg_ids]), seg_ids, num_segments=segments + 1
    )
    return (best[:segments], summed[:segments])


def general_device(
    source_feat, target_feat, log_mass_src, log_mass_tgt, potential_tgt, support, counts
):
    target_all, mass_all, poten_all = (
        lax.all_gather(target_feat, "src", axis=0, tiled=True),
        lax.all_gather(log_mass_tgt, "src", axis=0, tiled=True),
        lax.all_gather(potential_tgt, "src", axis=0, tiled=True),
    )
    blocks = target_all.shape[0]
    rows_here = source_feat.shape[0]
    slots_here = support.shape[2]
    cells = source_feat.shape[2]
    indices = support[:, 0, :]
    limits = counts[:, 0]
    usable = jnp.arange(slots_here, dtype=jnp.int32)[None, :] < limits[:, None]
    source_sq = jnp.sum(source_feat * source_feat, axis=1)
    target_sq = jnp.sum(target_all * target_all, axis=1)
    width = math.gcd(rows_here, 4)

    def grouped(array):
        return array.reshape((rows_here // width, width) + array.shape[1:])

    def row_pass(items):
        source_blk, source_nrm, ids_here, use_here = items
        cost = cost_tiles(
            source_blk[:, None], source_nrm[:, None], target_all[ids_here], target_sq[ids_here]
        )
        return row_stats(cost, mass_all[ids_here], poten_all[ids_here], use_here)

    peak, total = lax.map(
        row_pass, (grouped(source_feat), grouped(source_sq), grouped(indices), grouped(usable))
    )
    peak = peak.reshape(rows_here, cells)
    total = total.reshape(rows_here, cells)
    peak_all, total_all = merged((peak, total), "tgt", merge_pair)
    potential_src = -entropic * (peak_all + jnp.log(total_all))

    def column_pass(items):
        source_blk, source_nrm, mass_here, poten_here, ids_here, use_here = items
        cost = cost_tiles(
            source_blk[:, None], source_nrm[:, None], target_all[ids_here], target_sq[ids_here]
        )
        return column_stats(cost, mass_here, poten_here, use_here)

    peaks, totals = lax.map(
        column_pass,
        (
            grouped(source_feat),
            grouped(source_sq),
            grouped(log_mass_src),
            grouped(potential_src),
            grouped(indices),
            grouped(usable),
        ),
    )
    seg_ids = jnp.where(usable, indices, blocks).reshape(-1)
    best, summed = segment_merge(
        peaks.reshape(-1, cells), totals.reshape(-1, cells), seg_ids, blocks
    )
    share = blocks // lax.axis_size("src")
    own_start = lax.axis_index("src") * share
    highest = lax.pmax(best, "src")
    whole = lax.psum(summed * jnp.exp(best - highest), "src")
    own_peak = lax.dynamic_slice_in_dim(highest, own_start, share, 0)
    own_total = lax.dynamic_slice_in_dim(whole, own_start, share, 0)
    potential_new = -entropic * (own_peak + jnp.log(own_total))
    return (potential_src, potential_new)


def per_device(source_feat, target_feat, *others):
    shards = lax.axis_size("src")
    rows, depth, cells = source_feat.shape
    paired = shards >= 4 and shards & (shards - 1) == 0 and lax.axis_size("tgt") == 2
    shaped = target_feat.shape[0] == 1 and rows % 2 == 0 and cells == 2 * depth and cells % 128 == 0
    if paired and shaped and 4 * rows * cells * shards * cells <= room:
        return dense_device(source_feat, target_feat, *others)
    return general_device(source_feat, target_feat, *others)


def solution(mesh):
    in_specs = (
        P(("grp", "src"), None, None),
        P(("grp", "src", "tgt"), None, None),
        P(("grp", "src"), None),
        P(("grp", "src", "tgt"), None),
        P(("grp", "src", "tgt"), None),
        P(("grp", "src"), "tgt", None),
        P(("grp", "src"), "tgt"),
    )
    out_specs = (P(("grp", "src"), None), P(("grp", "src", "tgt"), None))
    return jax.shard_map(
        per_device, mesh=mesh, in_specs=in_specs, out_specs=out_specs, check_vma=False
    )
```

```python
import functools
import math

import jax
import jax.numpy as jnp
from jax import lax
from jax.experimental import pallas as pl
from jax.experimental.pallas import tpu as pltpu
from jax.sharding import PartitionSpec as P

entropic = 0.5
very_low = -1e30
log2e = 1.0 / math.log(2.0)
ln2 = math.log(2.0)
least_sum = 1e-28

room = 2**24

VM = pl.BlockSpec(memory_space=pltpu.VMEM)
PARAMS = pltpu.CompilerParams(vmem_limit_bytes=40 * 2**20)


def in_vmem(shape, dtype):
    return pltpu.VMEM(shape, dtype)


def pieces(values):
    high = values.astype(jnp.bfloat16).astype(jnp.float32)
    rest = values - high
    mid = rest.astype(jnp.bfloat16).astype(jnp.float32)
    low = (rest - mid).astype(jnp.bfloat16).astype(jnp.float32)
    return high, mid, low


def target_weight(mass, poten):
    return (mass + poten / entropic) * log2e


def line_moves(line):
    bits = line.bit_length() - 1
    cycle = [sum(((place >> bit) & 1) << (bits - 1 - bit) for bit in range(bits)) for place in range(line)]
    shifts = [shift for step in range(1, line // 2) for shift in (step, line - step)] + [line // 2]
    return [[cycle[(cycle.index(at) + shift) % line] for at in range(line)] for shift in shifts]


def blocks_at(shards):
    me = lax.axis_index("src")
    at, odd = me // 2, lax.rem(me, 2)
    near = [me]
    for receivers in line_moves(shards // 2):
        senders = [receivers.index(there) for there in range(shards // 2)]
        near.append(2 * sum(jnp.where(at == there, sender, 0) for there, sender in enumerate(senders)) + odd)
    return near + [block ^ 1 for block in near]


def read_all(hbm, held, sems):
    copies = [pltpu.make_async_copy(src, dst, sems.at[i]) for i, (src, dst) in enumerate(zip(hbm, held))]
    for copy in copies:
        copy.start()
    return copies


def pack_kernel(*refs):
    hbm, (send_ref, weight_ref), held, sems = refs[:3], refs[3:5], refs[5:8], refs[8]
    for copy in read_all(hbm, held, sems):
        copy.wait()
    feat_ref, mass_ref, poten_ref = held
    feat = feat_ref[0]
    depth, cells = feat.shape
    weight = target_weight(mass_ref[...], poten_ref[...])
    norm = jnp.sum(feat * feat, axis=0, keepdims=True)
    bias = weight - (log2e / entropic) * norm
    scaled = feat * (2.0 * log2e / entropic)
    send_ref[0, :depth, 0, :] = scaled
    send_ref[0, depth, 0:1, :] = bias
    weight_ref[...] = weight


def source_kernel(shards, *refs):
    hbm, outs, held, sems = refs[:4], refs[4:8], refs[8:12], refs[12]
    wide_ref, norm_ref, mask_ref, mass_out_ref = outs
    mass_ref, support_ref, counts_ref, feat_ref = held
    copies = read_all(hbm, held, sems)
    for copy in copies[:3]:
        copy.wait()
    mass_out_ref[...] = mass_ref[...]
    support = support_ref[...]
    slots, rows = support.shape
    cells = mass_ref.shape[1]
    used = lax.broadcasted_iota(jnp.int32, support.shape, 0) < counts_ref[...]
    hits = [
        jnp.max(jnp.where(used & (support == block), 0.0, very_low), axis=0, keepdims=True)
        for block in blocks_at(shards)
    ]
    hits = jnp.concatenate(hits + [jnp.zeros((cells - shards, rows), jnp.float32)], axis=0)
    hits = jnp.concatenate([hits, jnp.zeros((cells, cells - rows), jnp.float32)], axis=1).T
    for place in range(shards):
        mask_ref[place] = jnp.broadcast_to(hits[:rows, place : place + 1], (rows, cells))
    copies[3].wait()
    depth = feat_ref.shape[1]
    one = jnp.ones((2 * depth, 2 * cells), jnp.bfloat16)
    for pair in range(rows // 2):
        for half in range(2):
            feat = feat_ref[2 * pair + half]
            norm_ref[2 * pair + half : 2 * pair + half + 1, :] = jnp.sum(feat * feat, axis=0, keepdims=True)
            high, mid, low = pieces(feat)
            lanes = slice(half * cells, (half + 1) * cells)
            top = jnp.concatenate([high, mid], axis=0).astype(jnp.bfloat16)
            wide_ref[pair, 0 : 2 * depth, lanes] = top
            wide_ref[pair, 2 * depth : 4 * depth, lanes] = top
            wide_ref[pair, 4 * depth : 6 * depth, lanes] = jnp.concatenate([low, high], axis=0).astype(jnp.bfloat16)
        wide_ref[pair, 6 * depth : 8 * depth, :] = one


def join_kernel(*refs):
    refs[-1][0] = refs[0][0]
    refs[-1][1] = refs[1][0]


def on_core(core, work, idle):
    if core is None:
        work()
    else:
        here = lax.axis_index("tgt") == core
        pl.when(here)(work)
        pl.when(jnp.logical_not(here))(idle)


def tile_kernel(parts, *refs):
    make_tiles(parts, *refs[: parts + 1], *refs[-4:])


def make_tiles(parts, *refs):
    packs = [ref.at[index] for ref in refs[:parts] for index in range(ref.shape[0])]
    wide_ref, exps_ref, tall_ref, peak_ref, total_ref = refs[parts:]
    blocks = len(packs)
    pairs, _, both = wide_ref.shape
    cells = both // 2
    depth = cells // 2
    lane = lax.broadcasted_iota(jnp.int32, (cells, cells), 1)
    biases = jnp.concatenate([pack[depth, 0:1, :] for pack in packs], axis=0)
    bias_pieces = jnp.concatenate(list(pieces(biases)), axis=0)
    padded = jnp.concatenate([bias_pieces, jnp.zeros((cells - 3 * blocks, cells), jnp.float32)], axis=0)
    bias_lanes = padded.T
    for place, pack in enumerate(packs):
        feat = pack[:depth, 0, :]
        turned = jnp.concatenate([feat, feat], axis=0).T
        high, mid, low = pieces(turned)
        own = jnp.where(lax.rem(lane, blocks) == place, bias_lanes, 0.0)
        rows = slice(place * cells, (place + 1) * cells)
        tall_ref[rows, 0:cells] = high.astype(jnp.bfloat16)
        tall_ref[rows, cells : 2 * cells] = mid.astype(jnp.bfloat16)
        tall_ref[rows, 2 * cells : 3 * cells] = jnp.where(lane < depth, high, low).astype(jnp.bfloat16)
        tall_ref[rows, 3 * cells : 4 * cells] = own.astype(jnp.bfloat16)

    def body(pair, carry):
        scores = jnp.dot(tall_ref[...], wide_ref[pair], preferred_element_type=jnp.float32)
        for place in range(blocks):
            rows = slice(place * cells, (place + 1) * cells)
            score = scores[rows]
            peak = jnp.max(score, axis=0, keepdims=True)
            exps = jnp.exp2(score - peak)
            exps_ref[pair, rows, :] = exps
            total = jnp.sum(exps, axis=0, keepdims=True)
            for half in range(2):
                lanes = slice(half * cells, (half + 1) * cells)
                peak_ref[place, pl.ds(2 * pair + half, 1), :] = peak[:, lanes]
                total_ref[place, pl.ds(2 * pair + half, 1), :] = total[:, lanes]
        return carry

    lax.fori_loop(0, pairs, body, 0, unroll=max(1, min(pairs, 32 // blocks)))


def row_kernel(groups, *refs):
    mask_ref, peak_refs, total_refs = refs[0], refs[1 : 1 + groups], refs[1 + groups : 1 + 2 * groups]
    peaks_ref, rowsum_ref = refs[1 + 2 * groups :]
    place = 0
    for ref in peak_refs:
        for index in range(ref.shape[0]):
            peaks_ref[place] = ref[index] + mask_ref[place]
            place += 1
    totals = [ref[index] for ref in total_refs for index in range(ref.shape[0])]
    top = functools.reduce(jnp.maximum, [peaks_ref[index] for index in range(place)])
    summed = sum(total * jnp.exp2(peaks_ref[index] - top) for index, total in enumerate(totals))
    rowsum_ref[...] = top + jnp.log2(summed)


def last_kernel(groups, core, *refs):
    packs_ref, wide_ref, _, mask_ref = refs[:4]
    peak_refs, total_refs = refs[4 : 3 + groups], refs[3 + groups : 2 + 2 * groups]
    exps_ref, tall_ref, peak_ref, total_ref, peaks_ref, rowsum_ref = refs[2 + 2 * groups :]

    def idle():
        peak_ref[...] = jnp.zeros(peak_ref.shape, jnp.float32)
        total_ref[...] = jnp.zeros(total_ref.shape, jnp.float32)

    work = functools.partial(make_tiles, 1, packs_ref, wide_ref, exps_ref, tall_ref, peak_ref, total_ref)
    on_core(core, work, idle)
    row_kernel(groups, mask_ref, *peak_refs, peak_ref, *total_refs, total_ref, peaks_ref, rowsum_ref)


def across(column):
    shape = (column.shape[0],) * 2
    same = lax.broadcasted_iota(jnp.int32, shape, 0) == lax.broadcasted_iota(jnp.int32, shape, 1)
    return jnp.sum(jnp.where(same, jnp.broadcast_to(column, shape), 0.0), axis=0, keepdims=True)


def column_kernel(groups, core, *refs):
    ins, outs, scratch = refs[: 2 * groups + 7], refs[-4:-2], refs[-2:]

    def idle():
        for given, out in zip(refs[2 * groups + 7 : -4], outs):
            out[...] = given[...]

    on_core(core, functools.partial(sum_columns, groups, *ins, *outs, *scratch), idle)


def sum_columns(groups, *refs):
    exps_refs, tall_refs, rest = refs[:groups], refs[groups : 2 * groups], refs[2 * groups :]
    wide_ref, peak_ref, mask_ref, own_ref, other_ref, mass_ref, norm_ref = rest[:7]
    poten_ref, sums_ref, weight_ref, shift_ref = rest[7:]
    pairs, _, both = wide_ref.shape
    cells = both // 2
    shards = mask_ref.shape[0]
    own, other = own_ref[...], other_ref[...]
    top = jnp.maximum(own, other)
    whole = top + jnp.log2(jnp.exp2(own - top) + jnp.exp2(other - top))
    poten_ref[...] = norm_ref[...] - (entropic * ln2) * whole
    shift = mass_ref[...] * log2e - whole
    shift_ref[...] = shift
    for place in range(shards):
        weight_ref[place] = jnp.exp2(peak_ref[place] + shift)
    spots = [
        (group, slice(index * cells, (index + 1) * cells))
        for group, ref in enumerate(tall_refs)
        for index in range(ref.shape[0] // cells)
    ]
    used = [jnp.max(mask_ref[place], axis=0, keepdims=True) > 0.5 * very_low for place in range(shards)]
    ranks = [shards - 1 - block for block in blocks_at(shards)]
    sums = []
    for place, (group, rows) in enumerate(spots):
        acc = jnp.zeros((cells, cells), jnp.float32)
        for pair in range(pairs):
            acc = acc + exps_refs[group][pair, rows, :cells] * weight_ref[place, 2 * pair : 2 * pair + 1, :]
            acc = acc + exps_refs[group][pair, rows, cells:] * weight_ref[place, 2 * pair + 1 : 2 * pair + 2, :]
        sums.append(jnp.sum(acc.T, axis=0, keepdims=True))
    whole_sums = jnp.concatenate([jnp.where(here, one, 1.0) for here, one in zip(used, sums)], axis=0)
    worst = jnp.min(whole_sums)
    logs = jnp.log2(whole_sums)
    for place in range(shards):
        sums_ref[ranks[place]] = jnp.where(used[place], logs[place : place + 1, :], very_low)

    @pl.when(worst < least_sum)
    def _():
        for place, (group, rows) in enumerate(spots):

            def exponents(pair):
                score = jnp.dot(tall_refs[group][rows, :], wide_ref[pair], preferred_element_type=jnp.float32)
                add = shift_ref[pl.ds(2 * pair, 2), :] + mask_ref[place, pl.ds(2 * pair, 2), :]
                return score[:, :cells] + add[0:1, :], score[:, cells:] + add[1:2, :]

            def highest(pair, peak):
                first, second = exponents(pair)
                return jnp.maximum(peak, jnp.maximum(first, second))

            peak = lax.fori_loop(0, pairs, highest, jnp.full((cells, cells), very_low, jnp.float32))
            peak = jnp.max(peak, axis=1, keepdims=True)

            def add_up(pair, sums):
                first, second = exponents(pair)
                return sums + jnp.exp2(first - peak) + jnp.exp2(second - peak)

            sums = lax.fori_loop(0, pairs, add_up, jnp.zeros((cells, cells), jnp.float32))
            logs = across(peak) + jnp.log2(across(jnp.sum(sums, axis=1, keepdims=True)))
            sums_ref[ranks[place]] = jnp.where(used[place], logs, very_low)


def merge_kernel(values_ref, weight_ref, poten_ref, out_ref, poten_out_ref):
    poten_out_ref[...] = poten_ref[...]
    values = values_ref[...]
    top = jnp.max(values, axis=0)
    whole = top + jnp.log2(jnp.sum(jnp.exp2(values - top), axis=0))
    out_ref[...] = -(entropic * ln2) * (whole - weight_ref[...])


def f32(*shape):
    return jax.ShapeDtypeStruct(shape, jnp.float32)


def dense_device(
    source_feat, target_feat, log_mass_src, log_mass_tgt, potential_tgt, support, counts
):
    shards = lax.axis_size("src")
    rows, depth, cells = source_feat.shape
    pairs, wide = rows // 2, 2 * cells

    def call(kernel, ins, out_shape, scratch=(), cost=None):
        many = isinstance(out_shape, list)
        return pl.pallas_call(
            kernel,
            in_specs=ins,
            out_specs=[VM] * len(out_shape) if many else VM,
            out_shape=out_shape,
            scratch_shapes=list(scratch),
            compiler_params=PARAMS,
            cost_estimate=cost,
        )

    def reading(kernel, args, out_shape, cost):
        return call(
            kernel,
            [pl.BlockSpec(memory_space=pltpu.HBM)] * len(args),
            out_shape,
            [pltpu.VMEM(arg.shape, arg.dtype) for arg in args] + [pltpu.SemaphoreType.DMA((len(args),))],
            cost,
        )(*[pltpu.with_memory_space_constraint(arg, pltpu.HBM) for arg in args])

    def cost_of(flops):
        return pl.CostEstimate(flops=flops, bytes_accessed=rows * depth * cells * 4, transcendentals=0)

    pack, weight = reading(
        pack_kernel,
        [target_feat, log_mass_tgt, potential_tgt],
        [in_vmem((1, depth + 1, 1, cells), jnp.float32), in_vmem((1, cells), jnp.float32)],
        None,
    )
    wide_feat, norm, mask, mass = reading(
        functools.partial(source_kernel, shards),
        [log_mass_src, support[:, 0, :].T, counts.T, source_feat],
        [
            in_vmem((pairs, 8 * depth, wide), jnp.bfloat16),
            in_vmem((rows, cells), jnp.float32),
            in_vmem((shards, rows, cells), jnp.float32),
            in_vmem((rows, cells), jnp.float32),
        ],
        cost_of(10**8),
    )

    def tile_shapes(blocks):
        return [
            in_vmem((pairs, blocks * cells, wide), jnp.float32),
            in_vmem((blocks * cells, 8 * depth), jnp.bfloat16),
            in_vmem((blocks, rows, cells), jnp.float32),
            in_vmem((blocks, rows, cells), jnp.float32),
        ]

    def tiles(*packs, after):
        blocks = sum(pack.shape[0] for pack in packs)
        return call(
            functools.partial(tile_kernel, len(packs)),
            [VM] * (len(packs) + 1) + [pl.BlockSpec(memory_space=pl.ANY)],
            tile_shapes(blocks),
            cost=cost_of(2 * blocks * cells * pairs * wide * 8 * depth),
        )(*packs, wide_feat, after)

    def swapped(array):
        return lax.ppermute(array, "src", [(i, i ^ 1) for i in range(shards)])

    def moved(array, receivers):
        moves = [(2 * here + odd, 2 * there + odd) for here, there in enumerate(receivers) for odd in range(2)]
        return lax.ppermute(array, "src", moves)

    def joined(first, second, after):
        return call(
            join_kernel,
            [VM] * 2 + [pl.BlockSpec(memory_space=pl.ANY)],
            in_vmem((2,) + pack.shape[1:], jnp.float32),
        )(first, second, after)

    there = [moved(pack, receivers) for receivers in line_moves(shards // 2)[::-1]][::-1]
    near = [pack] + there
    halves = [joined(near[0], near[1], norm)]
    for at in range(2, shards // 2, 2):
        halves.append(joined(near[at], near[at + 1], halves[-1]))
    far = [swapped(half) for half in halves]
    found = [tiles(*near, after=halves[-1])]
    for half in far[:-1]:
        found.append(tiles(half, after=found[-1][-1]))
    groups = len(found) + 1

    def last_tiles(core, after):
        _, _, peaks, totals = zip(*found)
        blocks = far[-1].shape[0]
        *last, peaks, own = call(
            functools.partial(last_kernel, groups, core),
            [VM] * 2 + [pl.BlockSpec(memory_space=pl.ANY)] + [VM] * (2 * groups - 1),
            tile_shapes(blocks) + [in_vmem((shards, rows, cells), jnp.float32), in_vmem((rows, cells), jnp.float32)],
            cost=cost_of(2 * blocks * cells * pairs * wide * 8 * depth),
        )(far[-1], wide_feat, after, mask, *peaks, *totals)
        return last, peaks, own

    def columns_of(core, last, peaks, own, other, given):
        exps, tall, _, _ = zip(*found, last)
        return call(
            functools.partial(column_kernel, groups, core),
            [VM] * (2 * groups + 7 + len(given)),
            [in_vmem((rows, cells), jnp.float32), in_vmem((shards, 1, cells), jnp.float32)],
            [pltpu.VMEM((shards, rows, cells), jnp.float32), pltpu.VMEM((rows, cells), jnp.float32)],
            cost_of(10**9),
        )(*exps, *tall, wide_feat, peaks, mask, own, other, mass, norm, *given)

    between = [(0, 1), (1, 0)]
    last_one, peaks_one, own_one = last_tiles(1, found[-1][-1])
    other_zero = lax.ppermute(own_one, "tgt", between)
    last_zero, peaks_zero, own_zero = last_tiles(0, own_one)
    other_one = lax.ppermute(own_zero, "tgt", between)
    given = columns_of(0, last_zero, peaks_zero, own_zero, other_zero, [])
    potential_src, columns = columns_of(1, last_one, peaks_one, own_one, other_one, given)
    arrived = lax.all_to_all(columns, "src", 0, 0, axis_index_groups=[list(range(shards))[::-1]])
    outs = [f32(1, cells), f32(rows, cells)]
    potential_new, potential_src = call(merge_kernel, [VM] * 3, outs)(arrived, weight, potential_src)
    return potential_src, potential_new


def merged(part, axis, combine):
    gathered = jax.tree.map(lambda a: lax.all_gather(a, axis), part)

    def take(source):
        return jax.tree.map(lambda a: lax.dynamic_index_in_dim(a, source, 0, False), gathered)

    return lax.fori_loop(
        1, lax.axis_size(axis), lambda source, state: combine(state, take(source)), take(0)
    )


def cost_tiles(source_blk, source_sq, target_blk, target_sq):
    cross = jnp.einsum(
        "...fi,...fj->...ij", source_blk, target_blk, precision=lax.Precision.HIGHEST
    )
    return source_sq[..., :, None] + target_sq[..., None, :] - 2.0 * cross


def row_stats(cost, mass_tgt, poten_tgt, usable):
    scores = mass_tgt[..., None, :] + (poten_tgt[..., None, :] - cost) / entropic
    scores = jnp.where(usable[..., None, None], scores, very_low)
    peak = jnp.max(scores, axis=(1, 3))
    total = jnp.sum(jnp.exp(scores - peak[:, None, :, None]), axis=(1, 3))
    return (peak, total)


def column_stats(cost, mass_src, poten_src, usable):
    scores = mass_src[:, None, :, None] + (poten_src[:, None, :, None] - cost) / entropic
    peak = jnp.max(scores, axis=2)
    total = jnp.sum(jnp.exp(scores - peak[:, :, None, :]), axis=2)
    peak = jnp.where(usable[..., None], peak, very_low)
    total = jnp.where(usable[..., None], total, 0.0)
    return (peak, total)


def merge_pair(first_pair, second_pair):
    first_peak, first_total = first_pair
    second_peak, second_total = second_pair
    highest = jnp.maximum(first_peak, second_peak)
    summed = first_total * jnp.exp(first_peak - highest) + second_total * jnp.exp(
        second_peak - highest
    )
    return (highest, summed)


def segment_merge(peaks, totals, seg_ids, segments):
    best = jax.ops.segment_max(peaks, seg_ids, num_segments=segments + 1)
    best = jnp.maximum(best, very_low)
    summed = jax.ops.segment_sum(
        totals * jnp.exp(peaks - best[seg_ids]), seg_ids, num_segments=segments + 1
    )
    return (best[:segments], summed[:segments])


def general_device(
    source_feat, target_feat, log_mass_src, log_mass_tgt, potential_tgt, support, counts
):
    target_all, mass_all, poten_all = (
        lax.all_gather(target_feat, "src", axis=0, tiled=True),
        lax.all_gather(log_mass_tgt, "src", axis=0, tiled=True),
        lax.all_gather(potential_tgt, "src", axis=0, tiled=True),
    )
    blocks = target_all.shape[0]
    rows_here = source_feat.shape[0]
    slots_here = support.shape[2]
    cells = source_feat.shape[2]
    indices = support[:, 0, :]
    limits = counts[:, 0]
    usable = jnp.arange(slots_here, dtype=jnp.int32)[None, :] < limits[:, None]
    source_sq = jnp.sum(source_feat * source_feat, axis=1)
    target_sq = jnp.sum(target_all * target_all, axis=1)
    width = math.gcd(rows_here, 4)

    def grouped(array):
        return array.reshape((rows_here // width, width) + array.shape[1:])

    def row_pass(items):
        source_blk, source_nrm, ids_here, use_here = items
        cost = cost_tiles(
            source_blk[:, None], source_nrm[:, None], target_all[ids_here], target_sq[ids_here]
        )
        return row_stats(cost, mass_all[ids_here], poten_all[ids_here], use_here)

    peak, total = lax.map(
        row_pass, (grouped(source_feat), grouped(source_sq), grouped(indices), grouped(usable))
    )
    peak = peak.reshape(rows_here, cells)
    total = total.reshape(rows_here, cells)
    peak_all, total_all = merged((peak, total), "tgt", merge_pair)
    potential_src = -entropic * (peak_all + jnp.log(total_all))

    def column_pass(items):
        source_blk, source_nrm, mass_here, poten_here, ids_here, use_here = items
        cost = cost_tiles(
            source_blk[:, None], source_nrm[:, None], target_all[ids_here], target_sq[ids_here]
        )
        return column_stats(cost, mass_here, poten_here, use_here)

    peaks, totals = lax.map(
        column_pass,
        (
            grouped(source_feat),
            grouped(source_sq),
            grouped(log_mass_src),
            grouped(potential_src),
            grouped(indices),
            grouped(usable),
        ),
    )
    seg_ids = jnp.where(usable, indices, blocks).reshape(-1)
    best, summed = segment_merge(
        peaks.reshape(-1, cells), totals.reshape(-1, cells), seg_ids, blocks
    )
    share = blocks // lax.axis_size("src")
    own_start = lax.axis_index("src") * share
    highest = lax.pmax(best, "src")
    whole = lax.psum(summed * jnp.exp(best - highest), "src")
    own_peak = lax.dynamic_slice_in_dim(highest, own_start, share, 0)
    own_total = lax.dynamic_slice_in_dim(whole, own_start, share, 0)
    potential_new = -entropic * (own_peak + jnp.log(own_total))
    return (potential_src, potential_new)


def per_device(source_feat, target_feat, *others):
    shards = lax.axis_size("src")
    rows, depth, cells = source_feat.shape
    paired = shards >= 4 and shards & (shards - 1) == 0 and lax.axis_size("tgt") == 2
    shaped = target_feat.shape[0] == 1 and rows % 2 == 0 and cells == 2 * depth and cells % 128 == 0
    if paired and shaped and 4 * rows * cells * shards * cells <= room:
        return dense_device(source_feat, target_feat, *others)
    return general_device(source_feat, target_feat, *others)


def solution(mesh):
    in_specs = (
        P(("grp", "src"), None, None),
        P(("grp", "src", "tgt"), None, None),
        P(("grp", "src"), None),
        P(("grp", "src", "tgt"), None),
        P(("grp", "src", "tgt"), None),
        P(("grp", "src"), "tgt", None),
        P(("grp", "src"), "tgt"),
    )
    out_specs = (P(("grp", "src"), None), P(("grp", "src", "tgt"), None))
    return jax.shard_map(
        per_device, mesh=mesh, in_specs=in_specs, out_specs=out_specs, check_vma=False
    )
```

```python
import functools
import math

import jax
import jax.numpy as jnp
from jax import lax
from jax.experimental import pallas as pl
from jax.experimental.pallas import tpu as pltpu
from jax.sharding import PartitionSpec as P

entropic = 0.5
very_low = -1e30
log2e = 1.0 / math.log(2.0)
ln2 = math.log(2.0)
least_sum = 1e-28

room = 2**24

VM = pl.BlockSpec(memory_space=pltpu.VMEM)
PARAMS = pltpu.CompilerParams(vmem_limit_bytes=40 * 2**20)


def in_vmem(shape, dtype):
    return pltpu.VMEM(shape, dtype)


def pieces(values):
    high = values.astype(jnp.bfloat16).astype(jnp.float32)
    rest = values - high
    mid = rest.astype(jnp.bfloat16).astype(jnp.float32)
    low = (rest - mid).astype(jnp.bfloat16).astype(jnp.float32)
    return high, mid, low


def target_weight(mass, poten):
    return (mass + poten / entropic) * log2e


def line_moves(line):
    bits = line.bit_length() - 1
    cycle = [sum(((place >> bit) & 1) << (bits - 1 - bit) for bit in range(bits)) for place in range(line)]
    shifts = [shift for step in range(1, line // 2) for shift in (step, line - step)] + [line // 2]
    return [[cycle[(cycle.index(at) + shift) % line] for at in range(line)] for shift in shifts]


def blocks_at(shards):
    me = lax.axis_index("src")
    at, odd = me // 2, lax.rem(me, 2)
    near = [me]
    for receivers in line_moves(shards // 2):
        senders = [receivers.index(there) for there in range(shards // 2)]
        near.append(2 * sum(jnp.where(at == there, sender, 0) for there, sender in enumerate(senders)) + odd)
    return near + [block ^ 1 for block in near]


def read_all(hbm, held, sems):
    copies = [pltpu.make_async_copy(src, dst, sems.at[i]) for i, (src, dst) in enumerate(zip(hbm, held))]
    for copy in copies:
        copy.start()
    return copies


def pack_kernel(*refs):
    hbm, (send_ref, weight_ref), held, sems = refs[:3], refs[3:5], refs[5:8], refs[8]
    for copy in read_all(hbm, held, sems):
        copy.wait()
    feat_ref, mass_ref, poten_ref = held
    feat = feat_ref[0]
    depth, cells = feat.shape
    weight = target_weight(mass_ref[...], poten_ref[...])
    norm = jnp.sum(feat * feat, axis=0, keepdims=True)
    bias = weight - (log2e / entropic) * norm
    scaled = feat * (2.0 * log2e / entropic)
    send_ref[0, :depth, 0, :] = scaled
    send_ref[0, depth, 0:1, :] = bias
    weight_ref[...] = weight


def source_kernel(shards, *refs):
    hbm, outs, held, sems = refs[:4], refs[4:8], refs[8:12], refs[12]
    wide_ref, norm_ref, mask_ref, mass_out_ref = outs
    mass_ref, support_ref, counts_ref, feat_ref = held
    copies = read_all(hbm, held, sems)
    for copy in copies[:3]:
        copy.wait()
    mass_out_ref[...] = mass_ref[...]
    support = support_ref[...]
    slots, rows = support.shape
    cells = mass_ref.shape[1]
    used = lax.broadcasted_iota(jnp.int32, support.shape, 0) < counts_ref[...]
    hits = [
        jnp.max(jnp.where(used & (support == block), 0.0, very_low), axis=0, keepdims=True)
        for block in blocks_at(shards)
    ]
    hits = jnp.concatenate(hits + [jnp.zeros((cells - shards, rows), jnp.float32)], axis=0)
    hits = jnp.concatenate([hits, jnp.zeros((cells, cells - rows), jnp.float32)], axis=1).T
    for place in range(shards):
        mask_ref[place] = jnp.broadcast_to(hits[:rows, place : place + 1], (rows, cells))
    copies[3].wait()
    depth = feat_ref.shape[1]
    one = jnp.ones((2 * depth, 2 * cells), jnp.bfloat16)
    for pair in range(rows // 2):
        for half in range(2):
            feat = feat_ref[2 * pair + half]
            norm_ref[2 * pair + half : 2 * pair + half + 1, :] = jnp.sum(feat * feat, axis=0, keepdims=True)
            high, mid, low = pieces(feat)
            lanes = slice(half * cells, (half + 1) * cells)
            top = jnp.concatenate([high, mid], axis=0).astype(jnp.bfloat16)
            wide_ref[pair, 0 : 2 * depth, lanes] = top
            wide_ref[pair, 2 * depth : 4 * depth, lanes] = top
            wide_ref[pair, 4 * depth : 6 * depth, lanes] = jnp.concatenate([low, high], axis=0).astype(jnp.bfloat16)
        wide_ref[pair, 6 * depth : 8 * depth, :] = one


def join_kernel(*refs):
    refs[-1][0] = refs[0][0]
    refs[-1][1] = refs[1][0]


def on_core(core, work, idle):
    if core is None:
        work()
    else:
        here = lax.axis_index("tgt") == core
        pl.when(here)(work)
        pl.when(jnp.logical_not(here))(idle)


def tile_kernel(parts, *refs):
    make_tiles(parts, *refs[: parts + 1], *refs[-4:])


def make_tiles(parts, *refs):
    packs = [ref.at[index] for ref in refs[:parts] for index in range(ref.shape[0])]
    wide_ref, exps_ref, tall_ref, peak_ref, total_ref = refs[parts:]
    blocks = len(packs)
    pairs, _, both = wide_ref.shape
    cells = both // 2
    depth = cells // 2
    lane = lax.broadcasted_iota(jnp.int32, (cells, cells), 1)
    biases = jnp.concatenate([pack[depth, 0:1, :] for pack in packs], axis=0)
    bias_pieces = jnp.concatenate(list(pieces(biases)), axis=0)
    padded = jnp.concatenate([bias_pieces, jnp.zeros((cells - 3 * blocks, cells), jnp.float32)], axis=0)
    bias_lanes = padded.T
    for place, pack in enumerate(packs):
        feat = pack[:depth, 0, :]
        turned = jnp.concatenate([feat, feat], axis=0).T
        high, mid, low = pieces(turned)
        own = jnp.where(lax.rem(lane, blocks) == place, bias_lanes, 0.0)
        rows = slice(place * cells, (place + 1) * cells)
        tall_ref[rows, 0:cells] = high.astype(jnp.bfloat16)
        tall_ref[rows, cells : 2 * cells] = mid.astype(jnp.bfloat16)
        tall_ref[rows, 2 * cells : 3 * cells] = jnp.where(lane < depth, high, low).astype(jnp.bfloat16)
        tall_ref[rows, 3 * cells : 4 * cells] = own.astype(jnp.bfloat16)

    def body(pair, carry):
        scores = jnp.dot(tall_ref[...], wide_ref[pair], preferred_element_type=jnp.float32)
        for place in range(blocks):
            rows = slice(place * cells, (place + 1) * cells)
            score = scores[rows]
            peak = jnp.max(score, axis=0, keepdims=True)
            exps = jnp.exp2(score - peak)
            exps_ref[pair, rows, :] = exps
            total = jnp.sum(exps, axis=0, keepdims=True)
            for half in range(2):
                lanes = slice(half * cells, (half + 1) * cells)
                peak_ref[place, pl.ds(2 * pair + half, 1), :] = peak[:, lanes]
                total_ref[place, pl.ds(2 * pair + half, 1), :] = total[:, lanes]
        return carry

    lax.fori_loop(0, pairs, body, 0, unroll=max(1, min(pairs, 32 // blocks)))


def row_kernel(groups, *refs):
    mask_ref, peak_refs, total_refs = refs[0], refs[1 : 1 + groups], refs[1 + groups : 1 + 2 * groups]
    peaks_ref, rowsum_ref = refs[1 + 2 * groups :]
    place = 0
    for ref in peak_refs:
        for index in range(ref.shape[0]):
            peaks_ref[place] = ref[index] + mask_ref[place]
            place += 1
    totals = [ref[index] for ref in total_refs for index in range(ref.shape[0])]
    top = functools.reduce(jnp.maximum, [peaks_ref[index] for index in range(place)])
    summed = sum(total * jnp.exp2(peaks_ref[index] - top) for index, total in enumerate(totals))
    rowsum_ref[...] = top + jnp.log2(summed)


def last_kernel(groups, core, *refs):
    packs_ref, wide_ref, _, mask_ref = refs[:4]
    peak_refs, total_refs = refs[4 : 3 + groups], refs[3 + groups : 2 + 2 * groups]
    exps_ref, tall_ref, peaks_ref, rowsum_ref, peak_ref, total_ref = refs[2 + 2 * groups :]

    def idle():
        peak_ref[...] = jnp.zeros(peak_ref.shape, jnp.float32)
        total_ref[...] = jnp.zeros(total_ref.shape, jnp.float32)

    work = functools.partial(make_tiles, 1, packs_ref, wide_ref, exps_ref, tall_ref, peak_ref, total_ref)
    on_core(core, work, idle)
    row_kernel(groups, mask_ref, *peak_refs, peak_ref, *total_refs, total_ref, peaks_ref, rowsum_ref)


def across(column):
    shape = (column.shape[0],) * 2
    same = lax.broadcasted_iota(jnp.int32, shape, 0) == lax.broadcasted_iota(jnp.int32, shape, 1)
    return jnp.sum(jnp.where(same, jnp.broadcast_to(column, shape), 0.0), axis=0, keepdims=True)


def column_kernel(groups, core, *refs):
    ins, outs, scratch = refs[: 2 * groups + 7], refs[-4:-2], refs[-2:]

    def idle():
        for given, out in zip(refs[2 * groups + 7 : -4], outs):
            out[...] = given[...]

    on_core(core, functools.partial(sum_columns, groups, *ins, *outs, *scratch), idle)


def sum_columns(groups, *refs):
    exps_refs, tall_refs, rest = refs[:groups], refs[groups : 2 * groups], refs[2 * groups :]
    wide_ref, peak_ref, mask_ref, own_ref, other_ref, mass_ref, norm_ref = rest[:7]
    poten_ref, sums_ref, weight_ref, shift_ref = rest[7:]
    pairs, _, both = wide_ref.shape
    cells = both // 2
    shards = mask_ref.shape[0]
    own, other = own_ref[...], other_ref[...]
    top = jnp.maximum(own, other)
    whole = top + jnp.log2(jnp.exp2(own - top) + jnp.exp2(other - top))
    poten_ref[...] = norm_ref[...] - (entropic * ln2) * whole
    shift = mass_ref[...] * log2e - whole
    shift_ref[...] = shift
    for place in range(shards):
        weight_ref[place] = jnp.exp2(peak_ref[place] + shift)
    spots = [
        (group, slice(index * cells, (index + 1) * cells))
        for group, ref in enumerate(tall_refs)
        for index in range(ref.shape[0] // cells)
    ]
    used = [jnp.max(mask_ref[place], axis=0, keepdims=True) > 0.5 * very_low for place in range(shards)]
    ranks = [shards - 1 - block for block in blocks_at(shards)]
    sums = []
    for place, (group, rows) in enumerate(spots):
        acc = jnp.zeros((cells, cells), jnp.float32)
        for pair in range(pairs):
            acc = acc + exps_refs[group][pair, rows, :cells] * weight_ref[place, 2 * pair : 2 * pair + 1, :]
            acc = acc + exps_refs[group][pair, rows, cells:] * weight_ref[place, 2 * pair + 1 : 2 * pair + 2, :]
        sums.append(jnp.sum(acc.T, axis=0, keepdims=True))
    whole_sums = jnp.concatenate([jnp.where(here, one, 1.0) for here, one in zip(used, sums)], axis=0)
    worst = jnp.min(whole_sums)
    logs = jnp.log2(whole_sums)
    for place in range(shards):
        sums_ref[ranks[place]] = jnp.where(used[place], logs[place : place + 1, :], very_low)

    @pl.when(worst < least_sum)
    def _():
        for place, (group, rows) in enumerate(spots):

            def exponents(pair):
                score = jnp.dot(tall_refs[group][rows, :], wide_ref[pair], preferred_element_type=jnp.float32)
                add = shift_ref[pl.ds(2 * pair, 2), :] + mask_ref[place, pl.ds(2 * pair, 2), :]
                return score[:, :cells] + add[0:1, :], score[:, cells:] + add[1:2, :]

            def highest(pair, peak):
                first, second = exponents(pair)
                return jnp.maximum(peak, jnp.maximum(first, second))

            peak = lax.fori_loop(0, pairs, highest, jnp.full((cells, cells), very_low, jnp.float32))
            peak = jnp.max(peak, axis=1, keepdims=True)

            def add_up(pair, sums):
                first, second = exponents(pair)
                return sums + jnp.exp2(first - peak) + jnp.exp2(second - peak)

            sums = lax.fori_loop(0, pairs, add_up, jnp.zeros((cells, cells), jnp.float32))
            logs = across(peak) + jnp.log2(across(jnp.sum(sums, axis=1, keepdims=True)))
            sums_ref[ranks[place]] = jnp.where(used[place], logs, very_low)


def merge_kernel(values_ref, weight_ref, poten_ref, out_ref, poten_out_ref):
    poten_out_ref[...] = poten_ref[...]
    values = values_ref[...]
    top = jnp.max(values, axis=0)
    whole = top + jnp.log2(jnp.sum(jnp.exp2(values - top), axis=0))
    out_ref[...] = -(entropic * ln2) * (whole - weight_ref[...])


def f32(*shape):
    return jax.ShapeDtypeStruct(shape, jnp.float32)


def dense_device(
    source_feat, target_feat, log_mass_src, log_mass_tgt, potential_tgt, support, counts
):
    shards = lax.axis_size("src")
    rows, depth, cells = source_feat.shape
    pairs, wide = rows // 2, 2 * cells

    def call(kernel, ins, out_shape, scratch=(), cost=None):
        many = isinstance(out_shape, list)
        return pl.pallas_call(
            kernel,
            in_specs=ins,
            out_specs=[VM] * len(out_shape) if many else VM,
            out_shape=out_shape,
            scratch_shapes=list(scratch),
            compiler_params=PARAMS,
            cost_estimate=cost,
        )

    def reading(kernel, args, out_shape, cost):
        return call(
            kernel,
            [pl.BlockSpec(memory_space=pltpu.HBM)] * len(args),
            out_shape,
            [pltpu.VMEM(arg.shape, arg.dtype) for arg in args] + [pltpu.SemaphoreType.DMA((len(args),))],
            cost,
        )(*[pltpu.with_memory_space_constraint(arg, pltpu.HBM) for arg in args])

    def cost_of(flops):
        return pl.CostEstimate(flops=flops, bytes_accessed=rows * depth * cells * 4, transcendentals=0)

    pack, weight = reading(
        pack_kernel,
        [target_feat, log_mass_tgt, potential_tgt],
        [in_vmem((1, depth + 1, 1, cells), jnp.float32), in_vmem((1, cells), jnp.float32)],
        None,
    )
    wide_feat, norm, mask, mass = reading(
        functools.partial(source_kernel, shards),
        [log_mass_src, support[:, 0, :].T, counts.T, source_feat],
        [
            in_vmem((pairs, 8 * depth, wide), jnp.bfloat16),
            in_vmem((rows, cells), jnp.float32),
            in_vmem((shards, rows, cells), jnp.float32),
            in_vmem((rows, cells), jnp.float32),
        ],
        cost_of(10**8),
    )

    def tile_shapes(blocks):
        return [
            in_vmem((pairs, blocks * cells, wide), jnp.float32),
            in_vmem((blocks * cells, 8 * depth), jnp.bfloat16),
            in_vmem((blocks, rows, cells), jnp.float32),
            in_vmem((blocks, rows, cells), jnp.float32),
        ]

    def tiles(*packs, after):
        blocks = sum(pack.shape[0] for pack in packs)
        return call(
            functools.partial(tile_kernel, len(packs)),
            [VM] * (len(packs) + 1) + [pl.BlockSpec(memory_space=pl.ANY)],
            tile_shapes(blocks),
            cost=cost_of(2 * blocks * cells * pairs * wide * 8 * depth),
        )(*packs, wide_feat, after)

    def swapped(array):
        return lax.ppermute(array, "src", [(i, i ^ 1) for i in range(shards)])

    def moved(array, receivers):
        moves = [(2 * here + odd, 2 * there + odd) for here, there in enumerate(receivers) for odd in range(2)]
        return lax.ppermute(array, "src", moves)

    def joined(first, second, after):
        return call(
            join_kernel,
            [VM] * 2 + [pl.BlockSpec(memory_space=pl.ANY)],
            in_vmem((2,) + pack.shape[1:], jnp.float32),
        )(first, second, after)

    there = [moved(pack, receivers) for receivers in line_moves(shards // 2)[::-1]][::-1]
    near = [pack] + there
    halves = [joined(near[0], near[1], norm)]
    for at in range(2, shards // 2, 2):
        halves.append(joined(near[at], near[at + 1], halves[-1]))
    far = [swapped(half) for half in halves]
    found = [tiles(*near, after=halves[-1])]
    for half in far[:-1]:
        found.append(tiles(half, after=found[-1][-1]))
    groups = len(found) + 1

    def last_tiles(core, after):
        _, _, peaks, totals = zip(*found)
        blocks = far[-1].shape[0]
        exps, tall, *_ = tile_shapes(blocks)
        *last, peaks, own = call(
            functools.partial(last_kernel, groups, core),
            [VM] * 2 + [pl.BlockSpec(memory_space=pl.ANY)] + [VM] * (2 * groups - 1),
            [exps, tall, in_vmem((shards, rows, cells), jnp.float32), in_vmem((rows, cells), jnp.float32)],
            [pltpu.VMEM((blocks, rows, cells), jnp.float32)] * 2,
            cost=cost_of(2 * blocks * cells * pairs * wide * 8 * depth),
        )(far[-1], wide_feat, after, mask, *peaks, *totals)
        return last, peaks, own

    def columns_of(core, last, peaks, own, other, given):
        exps, tall = zip(*[group[:2] for group in found], last)
        return call(
            functools.partial(column_kernel, groups, core),
            [VM] * (2 * groups + 7 + len(given)),
            [in_vmem((rows, cells), jnp.float32), in_vmem((shards, 1, cells), jnp.float32)],
            [pltpu.VMEM((shards, rows, cells), jnp.float32), pltpu.VMEM((rows, cells), jnp.float32)],
            cost_of(10**9),
        )(*exps, *tall, wide_feat, peaks, mask, own, other, mass, norm, *given)

    between = [(0, 1), (1, 0)]
    last_one, peaks_one, own_one = last_tiles(1, found[-1][-1])
    other_zero = lax.ppermute(own_one, "tgt", between)
    last_zero, peaks_zero, own_zero = last_tiles(0, own_one)
    other_one = lax.ppermute(own_zero, "tgt", between)
    given = columns_of(0, last_zero, peaks_zero, own_zero, other_zero, [])
    potential_src, columns = columns_of(1, last_one, peaks_one, own_one, other_one, given)
    arrived = lax.all_to_all(columns, "src", 0, 0, axis_index_groups=[list(range(shards))[::-1]])
    outs = [f32(1, cells), f32(rows, cells)]
    potential_new, potential_src = call(merge_kernel, [VM] * 3, outs)(arrived, weight, potential_src)
    return potential_src, potential_new


def merged(part, axis, combine):
    gathered = jax.tree.map(lambda a: lax.all_gather(a, axis), part)

    def take(source):
        return jax.tree.map(lambda a: lax.dynamic_index_in_dim(a, source, 0, False), gathered)

    return lax.fori_loop(
        1, lax.axis_size(axis), lambda source, state: combine(state, take(source)), take(0)
    )


def cost_tiles(source_blk, source_sq, target_blk, target_sq):
    cross = jnp.einsum(
        "...fi,...fj->...ij", source_blk, target_blk, precision=lax.Precision.HIGHEST
    )
    return source_sq[..., :, None] + target_sq[..., None, :] - 2.0 * cross


def row_stats(cost, mass_tgt, poten_tgt, usable):
    scores = mass_tgt[..., None, :] + (poten_tgt[..., None, :] - cost) / entropic
    scores = jnp.where(usable[..., None, None], scores, very_low)
    peak = jnp.max(scores, axis=(1, 3))
    total = jnp.sum(jnp.exp(scores - peak[:, None, :, None]), axis=(1, 3))
    return (peak, total)


def column_stats(cost, mass_src, poten_src, usable):
    scores = mass_src[:, None, :, None] + (poten_src[:, None, :, None] - cost) / entropic
    peak = jnp.max(scores, axis=2)
    total = jnp.sum(jnp.exp(scores - peak[:, :, None, :]), axis=2)
    peak = jnp.where(usable[..., None], peak, very_low)
    total = jnp.where(usable[..., None], total, 0.0)
    return (peak, total)


def merge_pair(first_pair, second_pair):
    first_peak, first_total = first_pair
    second_peak, second_total = second_pair
    highest = jnp.maximum(first_peak, second_peak)
    summed = first_total * jnp.exp(first_peak - highest) + second_total * jnp.exp(
        second_peak - highest
    )
    return (highest, summed)


def segment_merge(peaks, totals, seg_ids, segments):
    best = jax.ops.segment_max(peaks, seg_ids, num_segments=segments + 1)
    best = jnp.maximum(best, very_low)
    summed = jax.ops.segment_sum(
        totals * jnp.exp(peaks - best[seg_ids]), seg_ids, num_segments=segments + 1
    )
    return (best[:segments], summed[:segments])


def general_device(
    source_feat, target_feat, log_mass_src, log_mass_tgt, potential_tgt, support, counts
):
    target_all, mass_all, poten_all = (
        lax.all_gather(target_feat, "src", axis=0, tiled=True),
        lax.all_gather(log_mass_tgt, "src", axis=0, tiled=True),
        lax.all_gather(potential_tgt, "src", axis=0, tiled=True),
    )
    blocks = target_all.shape[0]
    rows_here = source_feat.shape[0]
    slots_here = support.shape[2]
    cells = source_feat.shape[2]
    indices = support[:, 0, :]
    limits = counts[:, 0]
    usable = jnp.arange(slots_here, dtype=jnp.int32)[None, :] < limits[:, None]
    source_sq = jnp.sum(source_feat * source_feat, axis=1)
    target_sq = jnp.sum(target_all * target_all, axis=1)
    width = math.gcd(rows_here, 4)

    def grouped(array):
        return array.reshape((rows_here // width, width) + array.shape[1:])

    def row_pass(items):
        source_blk, source_nrm, ids_here, use_here = items
        cost = cost_tiles(
            source_blk[:, None], source_nrm[:, None], target_all[ids_here], target_sq[ids_here]
        )
        return row_stats(cost, mass_all[ids_here], poten_all[ids_here], use_here)

    peak, total = lax.map(
        row_pass, (grouped(source_feat), grouped(source_sq), grouped(indices), grouped(usable))
    )
    peak = peak.reshape(rows_here, cells)
    total = total.reshape(rows_here, cells)
    peak_all, total_all = merged((peak, total), "tgt", merge_pair)
    potential_src = -entropic * (peak_all + jnp.log(total_all))

    def column_pass(items):
        source_blk, source_nrm, mass_here, poten_here, ids_here, use_here = items
        cost = cost_tiles(
            source_blk[:, None], source_nrm[:, None], target_all[ids_here], target_sq[ids_here]
        )
        return column_stats(cost, mass_here, poten_here, use_here)

    peaks, totals = lax.map(
        column_pass,
        (
            grouped(source_feat),
            grouped(source_sq),
            grouped(log_mass_src),
            grouped(potential_src),
            grouped(indices),
            grouped(usable),
        ),
    )
    seg_ids = jnp.where(usable, indices, blocks).reshape(-1)
    best, summed = segment_merge(
        peaks.reshape(-1, cells), totals.reshape(-1, cells), seg_ids, blocks
    )
    share = blocks // lax.axis_size("src")
    own_start = lax.axis_index("src") * share
    highest = lax.pmax(best, "src")
    whole = lax.psum(summed * jnp.exp(best - highest), "src")
    own_peak = lax.dynamic_slice_in_dim(highest, own_start, share, 0)
    own_total = lax.dynamic_slice_in_dim(whole, own_start, share, 0)
    potential_new = -entropic * (own_peak + jnp.log(own_total))
    return (potential_src, potential_new)


def per_device(source_feat, target_feat, *others):
    shards = lax.axis_size("src")
    rows, depth, cells = source_feat.shape
    paired = shards >= 4 and shards & (shards - 1) == 0 and lax.axis_size("tgt") == 2
    shaped = target_feat.shape[0] == 1 and rows % 2 == 0 and cells == 2 * depth and cells % 128 == 0
    if paired and shaped and 4 * rows * cells * shards * cells <= room:
        return dense_device(source_feat, target_feat, *others)
    return general_device(source_feat, target_feat, *others)


def solution(mesh):
    in_specs = (
        P(("grp", "src"), None, None),
        P(("grp", "src", "tgt"), None, None),
        P(("grp", "src"), None),
        P(("grp", "src", "tgt"), None),
        P(("grp", "src", "tgt"), None),
        P(("grp", "src"), "tgt", None),
        P(("grp", "src"), "tgt"),
    )
    out_specs = (P(("grp", "src"), None), P(("grp", "src", "tgt"), None))
    return jax.shard_map(
        per_device, mesh=mesh, in_specs=in_specs, out_specs=out_specs, check_vma=False
    )
```

```python
import functools
import math

import jax
import jax.numpy as jnp
from jax import lax
from jax.experimental import pallas as pl
from jax.experimental.pallas import tpu as pltpu
from jax.sharding import PartitionSpec as P

entropic = 0.5
very_low = -1e30
log2e = 1.0 / math.log(2.0)
ln2 = math.log(2.0)
least_sum = 1e-28

pack_cuts = 4
room = 2**24

VM = pl.BlockSpec(memory_space=pltpu.VMEM)
PARAMS = pltpu.CompilerParams(vmem_limit_bytes=40 * 2**20)


def in_vmem(shape, dtype):
    return pltpu.VMEM(shape, dtype)


def pieces(values):
    high = values.astype(jnp.bfloat16).astype(jnp.float32)
    rest = values - high
    mid = rest.astype(jnp.bfloat16).astype(jnp.float32)
    low = (rest - mid).astype(jnp.bfloat16).astype(jnp.float32)
    return high, mid, low


def target_weight(mass, poten):
    return (mass + poten / entropic) * log2e


def line_moves(line):
    bits = line.bit_length() - 1
    cycle = [sum(((place >> bit) & 1) << (bits - 1 - bit) for bit in range(bits)) for place in range(line)]
    shifts = [shift for step in range(1, line // 2) for shift in (step, line - step)] + [line // 2]
    return [[cycle[(cycle.index(at) + shift) % line] for at in range(line)] for shift in shifts]


def blocks_at(shards):
    me = lax.axis_index("src")
    at, odd = me // 2, lax.rem(me, 2)
    near = [me]
    for receivers in line_moves(shards // 2):
        senders = [receivers.index(there) for there in range(shards // 2)]
        near.append(2 * sum(jnp.where(at == there, sender, 0) for there, sender in enumerate(senders)) + odd)
    return near + [block ^ 1 for block in near]


def read_all(hbm, held, sems, cuts):
    *whole, (cut_from, cut_to) = zip(hbm, held)
    size = cut_from.shape[0] // cuts
    spans = [pl.ds(at * size, size) for at in range(cuts)]
    moves = [(cut_from.at[span], cut_to.at[span]) for span in spans] + whole
    copies = [pltpu.make_async_copy(*move, sems.at[at]) for at, move in enumerate(moves)]
    for copy in copies:
        copy.start()
    return copies[cuts:], copies[:cuts]


def pack_kernel(*refs):
    hbm, (send_ref, weight_ref), held, sems = refs[:3], refs[3:5], refs[5:8], refs[8]
    whole, cut = read_all(hbm, held, sems, pack_cuts)
    for copy in whole + cut:
        copy.wait()
    mass_ref, poten_ref, feat_ref = held
    feat = feat_ref[...]
    depth, cells = feat.shape
    weight = target_weight(mass_ref[...], poten_ref[...])
    norm = jnp.sum(feat * feat, axis=0, keepdims=True)
    bias = weight - (log2e / entropic) * norm
    scaled = feat * (2.0 * log2e / entropic)
    send_ref[0, :depth, 0, :] = scaled
    send_ref[0, depth, 0:1, :] = bias
    weight_ref[...] = weight


def source_kernel(shards, *refs):
    hbm, outs, held, sems = refs[:4], refs[4:8], refs[8:12], refs[12]
    wide_ref, norm_ref, mask_ref, mass_out_ref = outs
    mass_ref, support_ref, counts_ref, feat_ref = held
    rows = feat_ref.shape[0]
    whole, cut = read_all(hbm, held, sems, rows // 2)
    for copy in whole:
        copy.wait()
    mass_out_ref[...] = mass_ref[...]
    support = support_ref[...]
    slots, rows = support.shape
    cells = mass_ref.shape[1]
    used = lax.broadcasted_iota(jnp.int32, support.shape, 0) < counts_ref[...]
    hits = [
        jnp.max(jnp.where(used & (support == block), 0.0, very_low), axis=0, keepdims=True)
        for block in blocks_at(shards)
    ]
    hits = jnp.concatenate(hits + [jnp.zeros((cells - shards, rows), jnp.float32)], axis=0)
    hits = jnp.concatenate([hits, jnp.zeros((cells, cells - rows), jnp.float32)], axis=1).T
    for place in range(shards):
        mask_ref[place] = jnp.broadcast_to(hits[:rows, place : place + 1], (rows, cells))
    depth = feat_ref.shape[1]
    one = jnp.ones((2 * depth, 2 * cells), jnp.bfloat16)
    for pair in range(rows // 2):
        cut[pair].wait()
        for half in range(2):
            feat = feat_ref[2 * pair + half]
            norm_ref[2 * pair + half : 2 * pair + half + 1, :] = jnp.sum(feat * feat, axis=0, keepdims=True)
            high, mid, low = pieces(feat)
            lanes = slice(half * cells, (half + 1) * cells)
            top = jnp.concatenate([high, mid], axis=0).astype(jnp.bfloat16)
            wide_ref[pair, 0 : 2 * depth, lanes] = top
            wide_ref[pair, 2 * depth : 4 * depth, lanes] = top
            wide_ref[pair, 4 * depth : 6 * depth, lanes] = jnp.concatenate([low, high], axis=0).astype(jnp.bfloat16)
        wide_ref[pair, 6 * depth : 8 * depth, :] = one


def join_kernel(*refs):
    refs[-1][0] = refs[0][0]
    refs[-1][1] = refs[1][0]


def on_core(core, work, idle):
    if core is None:
        work()
    else:
        here = lax.axis_index("tgt") == core
        pl.when(here)(work)
        pl.when(jnp.logical_not(here))(idle)


def tile_kernel(parts, core, *refs):
    peak_ref, total_ref = refs[-2:]

    def idle():
        peak_ref[...] = jnp.zeros(peak_ref.shape, jnp.float32)
        total_ref[...] = jnp.zeros(total_ref.shape, jnp.float32)

    ins = refs[: parts + 1] + refs[-4:]
    on_core(core, functools.partial(make_tiles, parts, *ins), idle)


def make_tiles(parts, *refs):
    packs = [ref.at[index] for ref in refs[:parts] for index in range(ref.shape[0])]
    wide_ref, exps_ref, tall_ref, peak_ref, total_ref = refs[parts:]
    blocks = len(packs)
    pairs, _, both = wide_ref.shape
    cells = both // 2
    depth = cells // 2
    lane = lax.broadcasted_iota(jnp.int32, (cells, cells), 1)
    biases = jnp.concatenate([pack[depth, 0:1, :] for pack in packs], axis=0)
    bias_pieces = jnp.concatenate(list(pieces(biases)), axis=0)
    padded = jnp.concatenate([bias_pieces, jnp.zeros((cells - 3 * blocks, cells), jnp.float32)], axis=0)
    bias_lanes = padded.T
    for place, pack in enumerate(packs):
        feat = pack[:depth, 0, :]
        turned = jnp.concatenate([feat, feat], axis=0).T
        high, mid, low = pieces(turned)
        own = jnp.where(lax.rem(lane, blocks) == place, bias_lanes, 0.0)
        rows = slice(place * cells, (place + 1) * cells)
        tall_ref[rows, 0:cells] = high.astype(jnp.bfloat16)
        tall_ref[rows, cells : 2 * cells] = mid.astype(jnp.bfloat16)
        tall_ref[rows, 2 * cells : 3 * cells] = jnp.where(lane < depth, high, low).astype(jnp.bfloat16)
        tall_ref[rows, 3 * cells : 4 * cells] = own.astype(jnp.bfloat16)

    def body(pair, carry):
        scores = jnp.dot(tall_ref[...], wide_ref[pair], preferred_element_type=jnp.float32)
        for place in range(blocks):
            rows = slice(place * cells, (place + 1) * cells)
            score = scores[rows]
            peak = jnp.max(score, axis=0, keepdims=True)
            exps = jnp.exp2(score - peak)
            exps_ref[pair, rows, :] = exps
            total = jnp.sum(exps, axis=0, keepdims=True)
            for half in range(2):
                lanes = slice(half * cells, (half + 1) * cells)
                peak_ref[place, pl.ds(2 * pair + half, 1), :] = peak[:, lanes]
                total_ref[place, pl.ds(2 * pair + half, 1), :] = total[:, lanes]
        return carry

    lax.fori_loop(0, pairs, body, 0, unroll=max(1, min(pairs, 32 // blocks)))


def row_kernel(groups, *refs):
    mask_ref, peak_refs, total_refs = refs[0], refs[1 : 1 + groups], refs[1 + groups : 1 + 2 * groups]
    peaks_ref, rowsum_ref = refs[1 + 2 * groups :]
    place = 0
    for ref in peak_refs:
        for index in range(ref.shape[0]):
            peaks_ref[place] = ref[index] + mask_ref[place]
            place += 1
    totals = [ref[index] for ref in total_refs for index in range(ref.shape[0])]
    top = functools.reduce(jnp.maximum, [peaks_ref[index] for index in range(place)])
    summed = sum(total * jnp.exp2(peaks_ref[index] - top) for index, total in enumerate(totals))
    rowsum_ref[...] = top + jnp.log2(summed)


def across(column):
    shape = (column.shape[0],) * 2
    same = lax.broadcasted_iota(jnp.int32, shape, 0) == lax.broadcasted_iota(jnp.int32, shape, 1)
    return jnp.sum(jnp.where(same, jnp.broadcast_to(column, shape), 0.0), axis=0, keepdims=True)


def column_kernel(groups, core, *refs):
    ins, outs, scratch = refs[: 2 * groups + 7], refs[-4:-2], refs[-2:]

    def idle():
        for given, out in zip(refs[2 * groups + 7 : -4], outs):
            out[...] = given[...]

    on_core(core, functools.partial(sum_columns, groups, *ins, *outs, *scratch), idle)


def sum_columns(groups, *refs):
    exps_refs, tall_refs, rest = refs[:groups], refs[groups : 2 * groups], refs[2 * groups :]
    wide_ref, peak_ref, mask_ref, own_ref, other_ref, mass_ref, norm_ref = rest[:7]
    poten_ref, sums_ref, weight_ref, shift_ref = rest[7:]
    pairs, _, both = wide_ref.shape
    cells = both // 2
    shards = mask_ref.shape[0]
    own, other = own_ref[...], other_ref[...]
    top = jnp.maximum(own, other)
    whole = top + jnp.log2(jnp.exp2(own - top) + jnp.exp2(other - top))
    poten_ref[...] = norm_ref[...] - (entropic * ln2) * whole
    shift = mass_ref[...] * log2e - whole
    shift_ref[...] = shift
    for place in range(shards):
        weight_ref[place] = jnp.exp2(peak_ref[place] + shift)
    spots = [
        (group, slice(index * cells, (index + 1) * cells))
        for group, ref in enumerate(tall_refs)
        for index in range(ref.shape[0] // cells)
    ]
    used = [jnp.max(mask_ref[place], axis=0, keepdims=True) > 0.5 * very_low for place in range(shards)]
    ranks = [shards - 1 - block for block in blocks_at(shards)]
    sums = []
    for place, (group, rows) in enumerate(spots):
        acc = jnp.zeros((cells, cells), jnp.float32)
        for pair in range(pairs):
            acc = acc + exps_refs[group][pair, rows, :cells] * weight_ref[place, 2 * pair : 2 * pair + 1, :]
            acc = acc + exps_refs[group][pair, rows, cells:] * weight_ref[place, 2 * pair + 1 : 2 * pair + 2, :]
        sums.append(jnp.sum(acc.T, axis=0, keepdims=True))
    whole_sums = jnp.concatenate([jnp.where(here, one, 1.0) for here, one in zip(used, sums)], axis=0)
    worst = jnp.min(whole_sums)
    logs = jnp.log2(whole_sums)
    for place in range(shards):
        sums_ref[ranks[place]] = jnp.where(used[place], logs[place : place + 1, :], very_low)

    @pl.when(worst < least_sum)
    def _():
        for place, (group, rows) in enumerate(spots):

            def exponents(pair):
                score = jnp.dot(tall_refs[group][rows, :], wide_ref[pair], preferred_element_type=jnp.float32)
                add = shift_ref[pl.ds(2 * pair, 2), :] + mask_ref[place, pl.ds(2 * pair, 2), :]
                return score[:, :cells] + add[0:1, :], score[:, cells:] + add[1:2, :]

            def highest(pair, peak):
                first, second = exponents(pair)
                return jnp.maximum(peak, jnp.maximum(first, second))

            peak = lax.fori_loop(0, pairs, highest, jnp.full((cells, cells), very_low, jnp.float32))
            peak = jnp.max(peak, axis=1, keepdims=True)

            def add_up(pair, sums):
                first, second = exponents(pair)
                return sums + jnp.exp2(first - peak) + jnp.exp2(second - peak)

            sums = lax.fori_loop(0, pairs, add_up, jnp.zeros((cells, cells), jnp.float32))
            logs = across(peak) + jnp.log2(across(jnp.sum(sums, axis=1, keepdims=True)))
            sums_ref[ranks[place]] = jnp.where(used[place], logs, very_low)


def merge_kernel(values_ref, weight_ref, poten_ref, out_ref, poten_out_ref):
    poten_out_ref[...] = poten_ref[...]
    values = values_ref[...]
    top = jnp.max(values, axis=0)
    whole = top + jnp.log2(jnp.sum(jnp.exp2(values - top), axis=0))
    out_ref[...] = -(entropic * ln2) * (whole - weight_ref[...])


def f32(*shape):
    return jax.ShapeDtypeStruct(shape, jnp.float32)


def dense_device(
    source_feat, target_feat, log_mass_src, log_mass_tgt, potential_tgt, support, counts
):
    shards = lax.axis_size("src")
    rows, depth, cells = source_feat.shape
    pairs, wide = rows // 2, 2 * cells

    def call(kernel, ins, out_shape, scratch=(), cost=None):
        many = isinstance(out_shape, list)
        return pl.pallas_call(
            kernel,
            in_specs=ins,
            out_specs=[VM] * len(out_shape) if many else VM,
            out_shape=out_shape,
            scratch_shapes=list(scratch),
            compiler_params=PARAMS,
            cost_estimate=cost,
        )

    def reading(kernel, args, out_shape, cost, cuts):
        return call(
            kernel,
            [pl.BlockSpec(memory_space=pltpu.HBM)] * len(args),
            out_shape,
            [pltpu.VMEM(arg.shape, arg.dtype) for arg in args] + [pltpu.SemaphoreType.DMA((len(args) - 1 + cuts,))],
            cost,
        )(*[pltpu.with_memory_space_constraint(arg, pltpu.HBM) for arg in args])

    def cost_of(flops):
        return pl.CostEstimate(flops=flops, bytes_accessed=rows * depth * cells * 4, transcendentals=0)

    pack, weight = reading(
        pack_kernel,
        [log_mass_tgt, potential_tgt, target_feat[0]],
        [in_vmem((1, depth + 1, 1, cells), jnp.float32), in_vmem((1, cells), jnp.float32)],
        None,
        pack_cuts,
    )
    wide_feat, norm, mask, mass = reading(
        functools.partial(source_kernel, shards),
        [log_mass_src, support[:, 0, :].T, counts.T, source_feat],
        [
            in_vmem((pairs, 8 * depth, wide), jnp.bfloat16),
            in_vmem((rows, cells), jnp.float32),
            in_vmem((shards, rows, cells), jnp.float32),
            in_vmem((rows, cells), jnp.float32),
        ],
        cost_of(10**8),
        pairs,
    )

    def tiles(*packs, core=None, after=None):
        blocks = sum(pack.shape[0] for pack in packs)
        more = [] if after is None else [after]
        return call(
            functools.partial(tile_kernel, len(packs), core),
            [VM] * (len(packs) + 1) + [pl.BlockSpec(memory_space=pl.ANY)] * len(more),
            [
                in_vmem((pairs, blocks * cells, wide), jnp.float32),
                in_vmem((blocks * cells, 8 * depth), jnp.bfloat16),
                in_vmem((blocks, rows, cells), jnp.float32),
                in_vmem((blocks, rows, cells), jnp.float32),
            ],
            cost=cost_of(2 * blocks * cells * pairs * wide * 8 * depth),
        )(*packs, wide_feat, *more)

    def swapped(array):
        return lax.ppermute(array, "src", [(i, i ^ 1) for i in range(shards)])

    def moved(array, receivers):
        moves = [(2 * here + odd, 2 * there + odd) for here, there in enumerate(receivers) for odd in range(2)]
        return lax.ppermute(array, "src", moves)

    def joined(first, second, after):
        return call(
            join_kernel,
            [VM] * 2 + [pl.BlockSpec(memory_space=pl.ANY)],
            in_vmem((2,) + pack.shape[1:], jnp.float32),
        )(first, second, after)

    there = [moved(pack, receivers) for receivers in line_moves(shards // 2)[::-1]][::-1]
    near = [pack] + there
    halves = [joined(near[0], near[1], norm)]
    for at in range(2, shards // 2, 2):
        halves.append(joined(near[at], near[at + 1], halves[-1]))
    far = [swapped(half) for half in halves]
    found = [tiles(*near, after=halves[-1])]
    for half in far[:-1]:
        found.append(tiles(half, after=found[-1][-1]))
    groups = len(found) + 1

    def log_sums(last):
        _, _, peaks, totals = zip(*found, last)
        return call(
            functools.partial(row_kernel, groups),
            [VM] * (1 + 2 * groups),
            [in_vmem((shards, rows, cells), jnp.float32), in_vmem((rows, cells), jnp.float32)],
        )(mask, *peaks, *totals)

    def columns_of(core, last, peaks, own, other, given):
        exps, tall, _, _ = zip(*found, last)
        return call(
            functools.partial(column_kernel, groups, core),
            [VM] * (2 * groups + 7 + len(given)),
            [in_vmem((rows, cells), jnp.float32), in_vmem((shards, 1, cells), jnp.float32)],
            [pltpu.VMEM((shards, rows, cells), jnp.float32), pltpu.VMEM((rows, cells), jnp.float32)],
            cost_of(10**9),
        )(*exps, *tall, wide_feat, peaks, mask, own, other, mass, norm, *given)

    between = [(0, 1), (1, 0)]
    last_one = tiles(far[-1], core=1, after=found[-1][-1])
    peaks_one, own_one = log_sums(last_one)
    other_zero = lax.ppermute(own_one, "tgt", between)
    last_zero = tiles(far[-1], core=0, after=own_one)
    peaks_zero, own_zero = log_sums(last_zero)
    other_one = lax.ppermute(own_zero, "tgt", between)
    given = columns_of(0, last_zero, peaks_zero, own_zero, other_zero, [])
    potential_src, columns = columns_of(1, last_one, peaks_one, own_one, other_one, given)
    arrived = lax.all_to_all(columns, "src", 0, 0, axis_index_groups=[list(range(shards))[::-1]])
    outs = [f32(1, cells), f32(rows, cells)]
    potential_new, potential_src = call(merge_kernel, [VM] * 3, outs)(arrived, weight, potential_src)
    return potential_src, potential_new


def merged(part, axis, combine):
    gathered = jax.tree.map(lambda a: lax.all_gather(a, axis), part)

    def take(source):
        return jax.tree.map(lambda a: lax.dynamic_index_in_dim(a, source, 0, False), gathered)

    return lax.fori_loop(
        1, lax.axis_size(axis), lambda source, state: combine(state, take(source)), take(0)
    )


def cost_tiles(source_blk, source_sq, target_blk, target_sq):
    cross = jnp.einsum(
        "...fi,...fj->...ij", source_blk, target_blk, precision=lax.Precision.HIGHEST
    )
    return source_sq[..., :, None] + target_sq[..., None, :] - 2.0 * cross


def row_stats(cost, mass_tgt, poten_tgt, usable):
    scores = mass_tgt[..., None, :] + (poten_tgt[..., None, :] - cost) / entropic
    scores = jnp.where(usable[..., None, None], scores, very_low)
    peak = jnp.max(scores, axis=(1, 3))
    total = jnp.sum(jnp.exp(scores - peak[:, None, :, None]), axis=(1, 3))
    return (peak, total)


def column_stats(cost, mass_src, poten_src, usable):
    scores = mass_src[:, None, :, None] + (poten_src[:, None, :, None] - cost) / entropic
    peak = jnp.max(scores, axis=2)
    total = jnp.sum(jnp.exp(scores - peak[:, :, None, :]), axis=2)
    peak = jnp.where(usable[..., None], peak, very_low)
    total = jnp.where(usable[..., None], total, 0.0)
    return (peak, total)


def merge_pair(first_pair, second_pair):
    first_peak, first_total = first_pair
    second_peak, second_total = second_pair
    highest = jnp.maximum(first_peak, second_peak)
    summed = first_total * jnp.exp(first_peak - highest) + second_total * jnp.exp(
        second_peak - highest
    )
    return (highest, summed)


def segment_merge(peaks, totals, seg_ids, segments):
    best = jax.ops.segment_max(peaks, seg_ids, num_segments=segments + 1)
    best = jnp.maximum(best, very_low)
    summed = jax.ops.segment_sum(
        totals * jnp.exp(peaks - best[seg_ids]), seg_ids, num_segments=segments + 1
    )
    return (best[:segments], summed[:segments])


def general_device(
    source_feat, target_feat, log_mass_src, log_mass_tgt, potential_tgt, support, counts
):
    target_all, mass_all, poten_all = (
        lax.all_gather(target_feat, "src", axis=0, tiled=True),
        lax.all_gather(log_mass_tgt, "src", axis=0, tiled=True),
        lax.all_gather(potential_tgt, "src", axis=0, tiled=True),
    )
    blocks = target_all.shape[0]
    rows_here = source_feat.shape[0]
    slots_here = support.shape[2]
    cells = source_feat.shape[2]
    indices = support[:, 0, :]
    limits = counts[:, 0]
    usable = jnp.arange(slots_here, dtype=jnp.int32)[None, :] < limits[:, None]
    source_sq = jnp.sum(source_feat * source_feat, axis=1)
    target_sq = jnp.sum(target_all * target_all, axis=1)
    width = math.gcd(rows_here, 4)

    def grouped(array):
        return array.reshape((rows_here // width, width) + array.shape[1:])

    def row_pass(items):
        source_blk, source_nrm, ids_here, use_here = items
        cost = cost_tiles(
            source_blk[:, None], source_nrm[:, None], target_all[ids_here], target_sq[ids_here]
        )
        return row_stats(cost, mass_all[ids_here], poten_all[ids_here], use_here)

    peak, total = lax.map(
        row_pass, (grouped(source_feat), grouped(source_sq), grouped(indices), grouped(usable))
    )
    peak = peak.reshape(rows_here, cells)
    total = total.reshape(rows_here, cells)
    peak_all, total_all = merged((peak, total), "tgt", merge_pair)
    potential_src = -entropic * (peak_all + jnp.log(total_all))

    def column_pass(items):
        source_blk, source_nrm, mass_here, poten_here, ids_here, use_here = items
        cost = cost_tiles(
            source_blk[:, None], source_nrm[:, None], target_all[ids_here], target_sq[ids_here]
        )
        return column_stats(cost, mass_here, poten_here, use_here)

    peaks, totals = lax.map(
        column_pass,
        (
            grouped(source_feat),
            grouped(source_sq),
            grouped(log_mass_src),
            grouped(potential_src),
            grouped(indices),
            grouped(usable),
        ),
    )
    seg_ids = jnp.where(usable, indices, blocks).reshape(-1)
    best, summed = segment_merge(
        peaks.reshape(-1, cells), totals.reshape(-1, cells), seg_ids, blocks
    )
    share = blocks // lax.axis_size("src")
    own_start = lax.axis_index("src") * share
    highest = lax.pmax(best, "src")
    whole = lax.psum(summed * jnp.exp(best - highest), "src")
    own_peak = lax.dynamic_slice_in_dim(highest, own_start, share, 0)
    own_total = lax.dynamic_slice_in_dim(whole, own_start, share, 0)
    potential_new = -entropic * (own_peak + jnp.log(own_total))
    return (potential_src, potential_new)


def per_device(source_feat, target_feat, *others):
    shards = lax.axis_size("src")
    rows, depth, cells = source_feat.shape
    paired = shards >= 4 and shards & (shards - 1) == 0 and lax.axis_size("tgt") == 2
    shaped = target_feat.shape[0] == 1 and rows % 2 == 0 and cells == 2 * depth and cells % 128 == 0
    if paired and shaped and 4 * rows * cells * shards * cells <= room:
        return dense_device(source_feat, target_feat, *others)
    return general_device(source_feat, target_feat, *others)


def solution(mesh):
    in_specs = (
        P(("grp", "src"), None, None),
        P(("grp", "src", "tgt"), None, None),
        P(("grp", "src"), None),
        P(("grp", "src", "tgt"), None),
        P(("grp", "src", "tgt"), None),
        P(("grp", "src"), "tgt", None),
        P(("grp", "src"), "tgt"),
    )
    out_specs = (P(("grp", "src"), None), P(("grp", "src", "tgt"), None))
    return jax.shard_map(
        per_device, mesh=mesh, in_specs=in_specs, out_specs=out_specs, check_vma=False
    )
```

```python
import functools
import math

import jax
import jax.numpy as jnp
from jax import lax
from jax.experimental import pallas as pl
from jax.experimental.pallas import tpu as pltpu
from jax.sharding import PartitionSpec as P

entropic = 0.5
very_low = -1e30
log2e = 1.0 / math.log(2.0)
ln2 = math.log(2.0)
least_sum = 1e-28

room = 2**24

VM = pl.BlockSpec(memory_space=pltpu.VMEM)
PARAMS = pltpu.CompilerParams(vmem_limit_bytes=40 * 2**20)


def in_vmem(shape, dtype):
    return pltpu.VMEM(shape, dtype)


def pieces(values):
    high = values.astype(jnp.bfloat16).astype(jnp.float32)
    rest = values - high
    mid = rest.astype(jnp.bfloat16).astype(jnp.float32)
    low = (rest - mid).astype(jnp.bfloat16).astype(jnp.float32)
    return high, mid, low


def target_weight(mass, poten):
    return (mass + poten / entropic) * log2e


def line_moves(line):
    bits = line.bit_length() - 1
    cycle = [sum(((place >> bit) & 1) << (bits - 1 - bit) for bit in range(bits)) for place in range(line)]
    shifts = [shift for step in range(1, line // 2) for shift in (step, line - step)] + [line // 2]
    return [[cycle[(cycle.index(at) + shift) % line] for at in range(line)] for shift in shifts]


def blocks_at(shards):
    me = lax.axis_index("src")
    at, odd = me // 2, lax.rem(me, 2)
    near = [me]
    for receivers in line_moves(shards // 2):
        senders = [receivers.index(there) for there in range(shards // 2)]
        near.append(2 * sum(jnp.where(at == there, sender, 0) for there, sender in enumerate(senders)) + odd)
    return near + [block ^ 1 for block in near]


def read_all(hbm, held, sems):
    copies = [pltpu.make_async_copy(src, dst, sems.at[i]) for i, (src, dst) in enumerate(zip(hbm, held))]
    for copy in copies:
        copy.start()
    return copies


def pack_kernel(*refs):
    hbm, (send_ref, weight_ref), held, sems = refs[:3], refs[3:5], refs[5:8], refs[8]
    for copy in read_all(hbm, held, sems):
        copy.wait()
    feat_ref, mass_ref, poten_ref = held
    feat = feat_ref[0]
    depth, cells = feat.shape
    weight = target_weight(mass_ref[...], poten_ref[...])
    norm = jnp.sum(feat * feat, axis=0, keepdims=True)
    bias = weight - (log2e / entropic) * norm
    scaled = feat * (2.0 * log2e / entropic)
    send_ref[0, :depth, 0, :] = scaled
    send_ref[0, depth, 0:1, :] = bias
    weight_ref[...] = weight


def source_kernel(shards, *refs):
    hbm, outs, held, sems = refs[:4], refs[4:8], refs[8:12], refs[12]
    wide_ref, norm_ref, mask_ref, mass_out_ref = outs
    mass_ref, support_ref, counts_ref, feat_ref = held
    copies = read_all(hbm, held, sems)
    for copy in copies[:3]:
        copy.wait()
    mass_out_ref[...] = mass_ref[...]
    support = support_ref[...]
    slots, rows = support.shape
    cells = mass_ref.shape[1]
    used = lax.broadcasted_iota(jnp.int32, support.shape, 0) < counts_ref[...]
    hits = [
        jnp.max(jnp.where(used & (support == block), 0.0, very_low), axis=0, keepdims=True)
        for block in blocks_at(shards)
    ]
    hits = jnp.concatenate(hits + [jnp.zeros((cells - shards, rows), jnp.float32)], axis=0)
    hits = jnp.concatenate([hits, jnp.zeros((cells, cells - rows), jnp.float32)], axis=1).T
    for place in range(shards):
        mask_ref[place] = jnp.broadcast_to(hits[:rows, place : place + 1], (rows, cells))
    copies[3].wait()
    depth = feat_ref.shape[1]
    one = jnp.ones((2 * depth, 2 * cells), jnp.bfloat16)
    for pair in range(rows // 2):
        for half in range(2):
            feat = feat_ref[2 * pair + half]
            norm_ref[2 * pair + half : 2 * pair + half + 1, :] = jnp.sum(feat * feat, axis=0, keepdims=True)
            high, mid, low = pieces(feat)
            lanes = slice(half * cells, (half + 1) * cells)
            top = jnp.concatenate([high, mid], axis=0).astype(jnp.bfloat16)
            wide_ref[pair, 0 : 2 * depth, lanes] = top
            wide_ref[pair, 2 * depth : 4 * depth, lanes] = top
            wide_ref[pair, 4 * depth : 6 * depth, lanes] = jnp.concatenate([low, high], axis=0).astype(jnp.bfloat16)
        wide_ref[pair, 6 * depth : 8 * depth, :] = one


def join_kernel(*refs):
    refs[-1][0] = refs[0][0]
    refs[-1][1] = refs[1][0]


def on_core(core, work, idle):
    if core is None:
        work()
    else:
        here = lax.axis_index("tgt") == core
        pl.when(here)(work)
        pl.when(jnp.logical_not(here))(idle)


def tile_kernel(parts, core, *refs):
    peak_ref, total_ref = refs[-2:]

    def idle():
        peak_ref[...] = jnp.zeros(peak_ref.shape, jnp.float32)
        total_ref[...] = jnp.zeros(total_ref.shape, jnp.float32)

    ins = refs[: parts + 1] + refs[-4:]
    on_core(core, functools.partial(make_tiles, parts, *ins), idle)


def make_tiles(parts, *refs):
    packs = [ref.at[index] for ref in refs[:parts] for index in range(ref.shape[0])]
    wide_ref, exps_ref, tall_ref, peak_ref, total_ref = refs[parts:]
    blocks = len(packs)
    pairs, _, both = wide_ref.shape
    cells = both // 2
    depth = cells // 2
    lane = lax.broadcasted_iota(jnp.int32, (cells, cells), 1)
    biases = jnp.concatenate([pack[depth, 0:1, :] for pack in packs], axis=0)
    bias_pieces = jnp.concatenate(list(pieces(biases)), axis=0)
    padded = jnp.concatenate([bias_pieces, jnp.zeros((cells - 3 * blocks, cells), jnp.float32)], axis=0)
    bias_lanes = padded.T
    for place, pack in enumerate(packs):
        feat = pack[:depth, 0, :]
        turned = jnp.concatenate([feat, feat], axis=0).T
        high, mid, low = pieces(turned)
        own = jnp.where(lax.rem(lane, blocks) == place, bias_lanes, 0.0)
        rows = slice(place * cells, (place + 1) * cells)
        tall_ref[rows, 0:cells] = high.astype(jnp.bfloat16)
        tall_ref[rows, cells : 2 * cells] = mid.astype(jnp.bfloat16)
        tall_ref[rows, 2 * cells : 3 * cells] = jnp.where(lane < depth, high, low).astype(jnp.bfloat16)
        tall_ref[rows, 3 * cells : 4 * cells] = own.astype(jnp.bfloat16)

    def body(pair, carry):
        scores = jnp.dot(tall_ref[...], wide_ref[pair], preferred_element_type=jnp.float32)
        for place in range(blocks):
            rows = slice(place * cells, (place + 1) * cells)
            score = scores[rows]
            peak = jnp.max(score, axis=0, keepdims=True)
            exps = jnp.exp2(score - peak)
            exps_ref[pair, rows, :] = exps
            total = jnp.sum(exps, axis=0, keepdims=True)
            for half in range(2):
                lanes = slice(half * cells, (half + 1) * cells)
                peak_ref[place, pl.ds(2 * pair + half, 1), :] = peak[:, lanes]
                total_ref[place, pl.ds(2 * pair + half, 1), :] = total[:, lanes]
        return carry

    lax.fori_loop(0, pairs, body, 0, unroll=max(1, min(pairs, 32 // blocks)))


def row_kernel(groups, *refs):
    mask_ref, peak_refs, total_refs = refs[0], refs[1 : 1 + groups], refs[1 + groups : 1 + 2 * groups]
    peaks_ref, rowsum_ref = refs[1 + 2 * groups :]
    place = 0
    for ref in peak_refs:
        for index in range(ref.shape[0]):
            peaks_ref[place] = ref[index] + mask_ref[place]
            place += 1
    totals = [ref[index] for ref in total_refs for index in range(ref.shape[0])]
    top = functools.reduce(jnp.maximum, [peaks_ref[index] for index in range(place)])
    summed = sum(total * jnp.exp2(peaks_ref[index] - top) for index, total in enumerate(totals))
    rowsum_ref[...] = top + jnp.log2(summed)


def across(column):
    shape = (column.shape[0],) * 2
    same = lax.broadcasted_iota(jnp.int32, shape, 0) == lax.broadcasted_iota(jnp.int32, shape, 1)
    return jnp.sum(jnp.where(same, jnp.broadcast_to(column, shape), 0.0), axis=0, keepdims=True)


def column_kernel(groups, core, *refs):
    ins, outs, scratch = refs[: 2 * groups + 7], refs[-4:-2], refs[-2:]

    def idle():
        for given, out in zip(refs[2 * groups + 7 : -4], outs):
            out[...] = given[...]

    on_core(core, functools.partial(sum_columns, groups, *ins, *outs, *scratch), idle)


def sum_columns(groups, *refs):
    exps_refs, tall_refs, rest = refs[:groups], refs[groups : 2 * groups], refs[2 * groups :]
    wide_ref, peak_ref, mask_ref, own_ref, other_ref, mass_ref, norm_ref = rest[:7]
    poten_ref, sums_ref, weight_ref, shift_ref = rest[7:]
    pairs, _, both = wide_ref.shape
    cells = both // 2
    shards = mask_ref.shape[0]
    own, other = own_ref[...], other_ref[...]
    top = jnp.maximum(own, other)
    whole = top + jnp.log2(jnp.exp2(own - top) + jnp.exp2(other - top))
    poten_ref[...] = norm_ref[...] - (entropic * ln2) * whole
    shift = mass_ref[...] * log2e - whole
    shift_ref[...] = shift
    for place in range(shards):
        weight_ref[place] = jnp.exp2(peak_ref[place] + shift)
    spots = [
        (group, slice(index * cells, (index + 1) * cells))
        for group, ref in enumerate(tall_refs)
        for index in range(ref.shape[0] // cells)
    ]
    used = [jnp.max(mask_ref[place], axis=0, keepdims=True) > 0.5 * very_low for place in range(shards)]
    tile = sums_ref.shape[1:]
    ranks = [shards - 1 - block for block in blocks_at(shards)]
    sums = []
    for place, (group, rows) in enumerate(spots):
        acc = jnp.zeros((cells, cells), jnp.float32)
        for pair in range(pairs):
            acc = acc + exps_refs[group][pair, rows, :cells] * weight_ref[place, 2 * pair : 2 * pair + 1, :]
            acc = acc + exps_refs[group][pair, rows, cells:] * weight_ref[place, 2 * pair + 1 : 2 * pair + 2, :]
        sums.append(jnp.sum(acc.T, axis=0, keepdims=True))
    whole_sums = jnp.concatenate([jnp.where(here, one, 1.0) for here, one in zip(used, sums)], axis=0)
    worst = jnp.min(whole_sums)
    logs = jnp.log2(whole_sums)
    for place in range(shards):
        sums_ref[ranks[place]] = jnp.broadcast_to(jnp.where(used[place], logs[place : place + 1, :], very_low), tile)

    @pl.when(worst < least_sum)
    def _():
        for place, (group, rows) in enumerate(spots):

            def exponents(pair):
                score = jnp.dot(tall_refs[group][rows, :], wide_ref[pair], preferred_element_type=jnp.float32)
                add = shift_ref[pl.ds(2 * pair, 2), :] + mask_ref[place, pl.ds(2 * pair, 2), :]
                return score[:, :cells] + add[0:1, :], score[:, cells:] + add[1:2, :]

            def highest(pair, peak):
                first, second = exponents(pair)
                return jnp.maximum(peak, jnp.maximum(first, second))

            peak = lax.fori_loop(0, pairs, highest, jnp.full((cells, cells), very_low, jnp.float32))
            peak = jnp.max(peak, axis=1, keepdims=True)

            def add_up(pair, sums):
                first, second = exponents(pair)
                return sums + jnp.exp2(first - peak) + jnp.exp2(second - peak)

            sums = lax.fori_loop(0, pairs, add_up, jnp.zeros((cells, cells), jnp.float32))
            logs = across(peak) + jnp.log2(across(jnp.sum(sums, axis=1, keepdims=True)))
            sums_ref[ranks[place]] = jnp.broadcast_to(jnp.where(used[place], logs, very_low), tile)


def merge_kernel(values_ref, weight_ref, poten_ref, out_ref, poten_out_ref):
    poten_out_ref[...] = poten_ref[...]
    values = values_ref[:, 0:1, :]
    top = jnp.max(values, axis=0)
    whole = top + jnp.log2(jnp.sum(jnp.exp2(values - top), axis=0))
    out_ref[...] = -(entropic * ln2) * (whole - weight_ref[...])


def f32(*shape):
    return jax.ShapeDtypeStruct(shape, jnp.float32)


def dense_device(
    source_feat, target_feat, log_mass_src, log_mass_tgt, potential_tgt, support, counts
):
    shards = lax.axis_size("src")
    rows, depth, cells = source_feat.shape
    pairs, wide = rows // 2, 2 * cells

    def call(kernel, ins, out_shape, scratch=(), cost=None):
        many = isinstance(out_shape, list)
        return pl.pallas_call(
            kernel,
            in_specs=ins,
            out_specs=[VM] * len(out_shape) if many else VM,
            out_shape=out_shape,
            scratch_shapes=list(scratch),
            compiler_params=PARAMS,
            cost_estimate=cost,
        )

    def reading(kernel, args, out_shape, cost):
        return call(
            kernel,
            [pl.BlockSpec(memory_space=pltpu.HBM)] * len(args),
            out_shape,
            [pltpu.VMEM(arg.shape, arg.dtype) for arg in args] + [pltpu.SemaphoreType.DMA((len(args),))],
            cost,
        )(*[pltpu.with_memory_space_constraint(arg, pltpu.HBM) for arg in args])

    def cost_of(flops):
        return pl.CostEstimate(flops=flops, bytes_accessed=rows * depth * cells * 4, transcendentals=0)

    pack, weight = reading(
        pack_kernel,
        [target_feat, log_mass_tgt, potential_tgt],
        [in_vmem((1, depth + 1, 1, cells), jnp.float32), in_vmem((1, cells), jnp.float32)],
        None,
    )
    wide_feat, norm, mask, mass = reading(
        functools.partial(source_kernel, shards),
        [log_mass_src, support[:, 0, :].T, counts.T, source_feat],
        [
            in_vmem((pairs, 8 * depth, wide), jnp.bfloat16),
            in_vmem((rows, cells), jnp.float32),
            in_vmem((shards, rows, cells), jnp.float32),
            in_vmem((rows, cells), jnp.float32),
        ],
        cost_of(10**8),
    )

    def tiles(*packs, core=None, after=None):
        blocks = sum(pack.shape[0] for pack in packs)
        more = [] if after is None else [after]
        return call(
            functools.partial(tile_kernel, len(packs), core),
            [VM] * (len(packs) + 1) + [pl.BlockSpec(memory_space=pl.ANY)] * len(more),
            [
                in_vmem((pairs, blocks * cells, wide), jnp.float32),
                in_vmem((blocks * cells, 8 * depth), jnp.bfloat16),
                in_vmem((blocks, rows, cells), jnp.float32),
                in_vmem((blocks, rows, cells), jnp.float32),
            ],
            cost=cost_of(2 * blocks * cells * pairs * wide * 8 * depth),
        )(*packs, wide_feat, *more)

    def swapped(array):
        return lax.ppermute(array, "src", [(i, i ^ 1) for i in range(shards)])

    def moved(array, receivers):
        moves = [(2 * here + odd, 2 * there + odd) for here, there in enumerate(receivers) for odd in range(2)]
        return lax.ppermute(array, "src", moves)

    def joined(first, second, after):
        return call(
            join_kernel,
            [VM] * 2 + [pl.BlockSpec(memory_space=pl.ANY)],
            in_vmem((2,) + pack.shape[1:], jnp.float32),
        )(first, second, after)

    there = [moved(pack, receivers) for receivers in line_moves(shards // 2)[::-1]][::-1]
    near = [pack] + there
    halves = [joined(near[0], near[1], norm)]
    for at in range(2, shards // 2, 2):
        halves.append(joined(near[at], near[at + 1], halves[-1]))
    far = [swapped(half) for half in halves]
    found = [tiles(*near, after=halves[-1])]
    for half in far[:-1]:
        found.append(tiles(half, after=found[-1][-1]))
    groups = len(found) + 1

    def log_sums(last):
        _, _, peaks, totals = zip(*found, last)
        return call(
            functools.partial(row_kernel, groups),
            [VM] * (1 + 2 * groups),
            [in_vmem((shards, rows, cells), jnp.float32), in_vmem((rows, cells), jnp.float32)],
        )(mask, *peaks, *totals)

    def columns_of(core, last, peaks, own, other, given):
        exps, tall, _, _ = zip(*found, last)
        return call(
            functools.partial(column_kernel, groups, core),
            [VM] * (2 * groups + 7 + len(given)),
            [in_vmem((rows, cells), jnp.float32), in_vmem((shards, 8, cells), jnp.float32)],
            [pltpu.VMEM((shards, rows, cells), jnp.float32), pltpu.VMEM((rows, cells), jnp.float32)],
            cost_of(10**9),
        )(*exps, *tall, wide_feat, peaks, mask, own, other, mass, norm, *given)

    between = [(0, 1), (1, 0)]
    last_one = tiles(far[-1], core=1, after=found[-1][-1])
    peaks_one, own_one = log_sums(last_one)
    other_zero = lax.ppermute(own_one, "tgt", between)
    last_zero = tiles(far[-1], core=0, after=own_one)
    peaks_zero, own_zero = log_sums(last_zero)
    other_one = lax.ppermute(own_zero, "tgt", between)
    given = columns_of(0, last_zero, peaks_zero, own_zero, other_zero, [])
    potential_src, columns = columns_of(1, last_one, peaks_one, own_one, other_one, given)
    arrived = lax.all_to_all(columns, "src", 0, 0, axis_index_groups=[list(range(shards))[::-1]])
    outs = [f32(1, cells), f32(rows, cells)]
    potential_new, potential_src = call(merge_kernel, [VM] * 3, outs)(arrived, weight, potential_src)
    return potential_src, potential_new


def merged(part, axis, combine):
    gathered = jax.tree.map(lambda a: lax.all_gather(a, axis), part)

    def take(source):
        return jax.tree.map(lambda a: lax.dynamic_index_in_dim(a, source, 0, False), gathered)

    return lax.fori_loop(
        1, lax.axis_size(axis), lambda source, state: combine(state, take(source)), take(0)
    )


def cost_tiles(source_blk, source_sq, target_blk, target_sq):
    cross = jnp.einsum(
        "...fi,...fj->...ij", source_blk, target_blk, precision=lax.Precision.HIGHEST
    )
    return source_sq[..., :, None] + target_sq[..., None, :] - 2.0 * cross


def row_stats(cost, mass_tgt, poten_tgt, usable):
    scores = mass_tgt[..., None, :] + (poten_tgt[..., None, :] - cost) / entropic
    scores = jnp.where(usable[..., None, None], scores, very_low)
    peak = jnp.max(scores, axis=(1, 3))
    total = jnp.sum(jnp.exp(scores - peak[:, None, :, None]), axis=(1, 3))
    return (peak, total)


def column_stats(cost, mass_src, poten_src, usable):
    scores = mass_src[:, None, :, None] + (poten_src[:, None, :, None] - cost) / entropic
    peak = jnp.max(scores, axis=2)
    total = jnp.sum(jnp.exp(scores - peak[:, :, None, :]), axis=2)
    peak = jnp.where(usable[..., None], peak, very_low)
    total = jnp.where(usable[..., None], total, 0.0)
    return (peak, total)


def merge_pair(first_pair, second_pair):
    first_peak, first_total = first_pair
    second_peak, second_total = second_pair
    highest = jnp.maximum(first_peak, second_peak)
    summed = first_total * jnp.exp(first_peak - highest) + second_total * jnp.exp(
        second_peak - highest
    )
    return (highest, summed)


def segment_merge(peaks, totals, seg_ids, segments):
    best = jax.ops.segment_max(peaks, seg_ids, num_segments=segments + 1)
    best = jnp.maximum(best, very_low)
    summed = jax.ops.segment_sum(
        totals * jnp.exp(peaks - best[seg_ids]), seg_ids, num_segments=segments + 1
    )
    return (best[:segments], summed[:segments])


def general_device(
    source_feat, target_feat, log_mass_src, log_mass_tgt, potential_tgt, support, counts
):
    target_all, mass_all, poten_all = (
        lax.all_gather(target_feat, "src", axis=0, tiled=True),
        lax.all_gather(log_mass_tgt, "src", axis=0, tiled=True),
        lax.all_gather(potential_tgt, "src", axis=0, tiled=True),
    )
    blocks = target_all.shape[0]
    rows_here = source_feat.shape[0]
    slots_here = support.shape[2]
    cells = source_feat.shape[2]
    indices = support[:, 0, :]
    limits = counts[:, 0]
    usable = jnp.arange(slots_here, dtype=jnp.int32)[None, :] < limits[:, None]
    source_sq = jnp.sum(source_feat * source_feat, axis=1)
    target_sq = jnp.sum(target_all * target_all, axis=1)
    width = math.gcd(rows_here, 4)

    def grouped(array):
        return array.reshape((rows_here // width, width) + array.shape[1:])

    def row_pass(items):
        source_blk, source_nrm, ids_here, use_here = items
        cost = cost_tiles(
            source_blk[:, None], source_nrm[:, None], target_all[ids_here], target_sq[ids_here]
        )
        return row_stats(cost, mass_all[ids_here], poten_all[ids_here], use_here)

    peak, total = lax.map(
        row_pass, (grouped(source_feat), grouped(source_sq), grouped(indices), grouped(usable))
    )
    peak = peak.reshape(rows_here, cells)
    total = total.reshape(rows_here, cells)
    peak_all, total_all = merged((peak, total), "tgt", merge_pair)
    potential_src = -entropic * (peak_all + jnp.log(total_all))

    def column_pass(items):
        source_blk, source_nrm, mass_here, poten_here, ids_here, use_here = items
        cost = cost_tiles(
            source_blk[:, None], source_nrm[:, None], target_all[ids_here], target_sq[ids_here]
        )
        return column_stats(cost, mass_here, poten_here, use_here)

    peaks, totals = lax.map(
        column_pass,
        (
            grouped(source_feat),
            grouped(source_sq),
            grouped(log_mass_src),
            grouped(potential_src),
            grouped(indices),
            grouped(usable),
        ),
    )
    seg_ids = jnp.where(usable, indices, blocks).reshape(-1)
    best, summed = segment_merge(
        peaks.reshape(-1, cells), totals.reshape(-1, cells), seg_ids, blocks
    )
    share = blocks // lax.axis_size("src")
    own_start = lax.axis_index("src") * share
    highest = lax.pmax(best, "src")
    whole = lax.psum(summed * jnp.exp(best - highest), "src")
    own_peak = lax.dynamic_slice_in_dim(highest, own_start, share, 0)
    own_total = lax.dynamic_slice_in_dim(whole, own_start, share, 0)
    potential_new = -entropic * (own_peak + jnp.log(own_total))
    return (potential_src, potential_new)


def per_device(source_feat, target_feat, *others):
    shards = lax.axis_size("src")
    rows, depth, cells = source_feat.shape
    paired = shards >= 4 and shards & (shards - 1) == 0 and lax.axis_size("tgt") == 2
    shaped = target_feat.shape[0] == 1 and rows % 2 == 0 and cells == 2 * depth and cells % 128 == 0
    if paired and shaped and 4 * rows * cells * shards * cells <= room:
        return dense_device(source_feat, target_feat, *others)
    return general_device(source_feat, target_feat, *others)


def solution(mesh):
    in_specs = (
        P(("grp", "src"), None, None),
        P(("grp", "src", "tgt"), None, None),
        P(("grp", "src"), None),
        P(("grp", "src", "tgt"), None),
        P(("grp", "src", "tgt"), None),
        P(("grp", "src"), "tgt", None),
        P(("grp", "src"), "tgt"),
    )
    out_specs = (P(("grp", "src"), None), P(("grp", "src", "tgt"), None))
    return jax.shard_map(
        per_device, mesh=mesh, in_specs=in_specs, out_specs=out_specs, check_vma=False
    )
```

```python
import functools
import math

import jax
import jax.numpy as jnp
from jax import lax
from jax.experimental import pallas as pl
from jax.experimental.pallas import tpu as pltpu
from jax.sharding import PartitionSpec as P

entropic = 0.5
very_low = -1e30
log2e = 1.0 / math.log(2.0)
ln2 = math.log(2.0)
least_sum = 1e-28

room = 2**24

VM = pl.BlockSpec(memory_space=pltpu.VMEM)
PARAMS = pltpu.CompilerParams(vmem_limit_bytes=40 * 2**20)


def in_vmem(shape, dtype):
    return pltpu.VMEM(shape, dtype)


def pieces(values):
    high = values.astype(jnp.bfloat16).astype(jnp.float32)
    rest = values - high
    mid = rest.astype(jnp.bfloat16).astype(jnp.float32)
    low = (rest - mid).astype(jnp.bfloat16).astype(jnp.float32)
    return high, mid, low


def target_weight(mass, poten):
    return (mass + poten / entropic) * log2e


def line_moves(line):
    bits = line.bit_length() - 1
    cycle = [sum(((place >> bit) & 1) << (bits - 1 - bit) for bit in range(bits)) for place in range(line)]
    shifts = [shift for step in range(1, line // 2) for shift in (step, line - step)] + [line // 2]
    return [[cycle[(cycle.index(at) + shift) % line] for at in range(line)] for shift in shifts]


def blocks_at(shards):
    me = lax.axis_index("src")
    at, odd = me // 2, lax.rem(me, 2)
    near = [me]
    for receivers in line_moves(shards // 2):
        senders = [receivers.index(there) for there in range(shards // 2)]
        near.append(2 * sum(jnp.where(at == there, sender, 0) for there, sender in enumerate(senders)) + odd)
    return near + [block ^ 1 for block in near]


def read_all(hbm, held, sems):
    copies = [pltpu.make_async_copy(src, dst, sems.at[i]) for i, (src, dst) in enumerate(zip(hbm, held))]
    for copy in copies:
        copy.start()
    return copies


def pack_kernel(*refs):
    hbm, (send_ref, weight_ref), held, sems = refs[:3], refs[3:5], refs[5:8], refs[8]
    for copy in read_all(hbm, held, sems):
        copy.wait()
    feat_ref, mass_ref, poten_ref = held
    feat = feat_ref[0]
    depth, cells = feat.shape
    weight = target_weight(mass_ref[...], poten_ref[...])
    norm = jnp.sum(feat * feat, axis=0, keepdims=True)
    bias = weight - (log2e / entropic) * norm
    scaled = feat * (2.0 * log2e / entropic)
    send_ref[0, :depth, 0, :] = scaled
    send_ref[0, depth, 0:1, :] = bias
    weight_ref[...] = weight


def source_kernel(shards, *refs):
    hbm, outs, held, sems = refs[:4], refs[4:8], refs[8:12], refs[12]
    wide_ref, norm_ref, mask_ref, mass_out_ref = outs
    mass_ref, support_ref, counts_ref, feat_ref = held
    copies = read_all(hbm, held, sems)
    for copy in copies[:3]:
        copy.wait()
    mass_out_ref[...] = mass_ref[...]
    support = support_ref[...]
    slots, rows = support.shape
    cells = mass_ref.shape[1]
    used = lax.broadcasted_iota(jnp.int32, support.shape, 0) < counts_ref[...]
    hits = [
        jnp.max(jnp.where(used & (support == block), 0.0, very_low), axis=0, keepdims=True)
        for block in blocks_at(shards)
    ]
    hits = jnp.concatenate(hits + [jnp.zeros((cells - shards, rows), jnp.float32)], axis=0)
    hits = jnp.concatenate([hits, jnp.zeros((cells, cells - rows), jnp.float32)], axis=1).T
    for place in range(shards):
        mask_ref[place] = jnp.broadcast_to(hits[:rows, place : place + 1], (rows, cells))
    copies[3].wait()
    depth = feat_ref.shape[1]
    one = jnp.ones((2 * depth, 2 * cells), jnp.bfloat16)
    for pair in range(rows // 2):
        for half in range(2):
            feat = feat_ref[2 * pair + half]
            norm_ref[2 * pair + half : 2 * pair + half + 1, :] = jnp.sum(feat * feat, axis=0, keepdims=True)
            high, mid, low = pieces(feat)
            lanes = slice(half * cells, (half + 1) * cells)
            top = jnp.concatenate([high, mid], axis=0).astype(jnp.bfloat16)
            wide_ref[pair, 0 : 2 * depth, lanes] = top
            wide_ref[pair, 2 * depth : 4 * depth, lanes] = top
            wide_ref[pair, 4 * depth : 6 * depth, lanes] = jnp.concatenate([low, high], axis=0).astype(jnp.bfloat16)
        wide_ref[pair, 6 * depth : 8 * depth, :] = one


def join_kernel(*refs):
    refs[-1][0] = refs[0][0]
    refs[-1][1] = refs[1][0]


def on_core(core, work, idle):
    if core is None:
        work()
    else:
        here = lax.axis_index("tgt") == core
        pl.when(here)(work)
        pl.when(jnp.logical_not(here))(idle)


def tile_kernel(parts, core, *refs):
    peak_ref, total_ref = refs[-2:]

    def idle():
        peak_ref[...] = jnp.zeros(peak_ref.shape, jnp.float32)
        total_ref[...] = jnp.zeros(total_ref.shape, jnp.float32)

    ins = refs[: parts + 1] + refs[-4:]
    on_core(core, functools.partial(make_tiles, parts, *ins), idle)


def make_tiles(parts, *refs):
    packs = [ref.at[index] for ref in refs[:parts] for index in range(ref.shape[0])]
    wide_ref, exps_ref, tall_ref, peak_ref, total_ref = refs[parts:]
    blocks = len(packs)
    pairs, _, both = wide_ref.shape
    cells = both // 2
    depth = cells // 2
    lane = lax.broadcasted_iota(jnp.int32, (cells, cells), 1)
    biases = jnp.concatenate([pack[depth, 0:1, :] for pack in packs], axis=0)
    bias_pieces = jnp.concatenate(list(pieces(biases)), axis=0)
    padded = jnp.concatenate([bias_pieces, jnp.zeros((cells - 3 * blocks, cells), jnp.float32)], axis=0)
    bias_lanes = padded.T
    for place, pack in enumerate(packs):
        feat = pack[:depth, 0, :]
        turned = jnp.concatenate([feat, feat], axis=0).T
        high, mid, low = pieces(turned)
        own = jnp.where(lax.rem(lane, blocks) == place, bias_lanes, 0.0)
        rows = slice(place * cells, (place + 1) * cells)
        tall_ref[rows, 0:cells] = high.astype(jnp.bfloat16)
        tall_ref[rows, cells : 2 * cells] = mid.astype(jnp.bfloat16)
        tall_ref[rows, 2 * cells : 3 * cells] = jnp.where(lane < depth, high, low).astype(jnp.bfloat16)
        tall_ref[rows, 3 * cells : 4 * cells] = own.astype(jnp.bfloat16)

    def body(pair, carry):
        scores = jnp.dot(tall_ref[...], wide_ref[pair], preferred_element_type=jnp.float32)
        for place in range(blocks):
            rows = slice(place * cells, (place + 1) * cells)
            score = scores[rows]
            peak = jnp.max(score, axis=0, keepdims=True)
            exps = jnp.exp2(score - peak)
            exps_ref[pair, rows, :] = exps
            total = jnp.sum(exps, axis=0, keepdims=True)
            for half in range(2):
                lanes = slice(half * cells, (half + 1) * cells)
                peak_ref[place, pl.ds(2 * pair + half, 1), :] = peak[:, lanes]
                total_ref[place, pl.ds(2 * pair + half, 1), :] = total[:, lanes]
        return carry

    lax.fori_loop(0, pairs, body, 0, unroll=max(1, min(pairs, 32 // blocks)))


def row_kernel(groups, *refs):
    mask_ref, peak_refs, total_refs = refs[0], refs[1 : 1 + groups], refs[1 + groups : 1 + 2 * groups]
    peaks_ref, rowsum_ref = refs[1 + 2 * groups :]
    place = 0
    for ref in peak_refs:
        for index in range(ref.shape[0]):
            peaks_ref[place] = ref[index] + mask_ref[place]
            place += 1
    totals = [ref[index] for ref in total_refs for index in range(ref.shape[0])]
    top = functools.reduce(jnp.maximum, [peaks_ref[index] for index in range(place)])
    summed = sum(total * jnp.exp2(peaks_ref[index] - top) for index, total in enumerate(totals))
    rowsum_ref[...] = top + jnp.log2(summed)


def across(column):
    shape = (column.shape[0],) * 2
    same = lax.broadcasted_iota(jnp.int32, shape, 0) == lax.broadcasted_iota(jnp.int32, shape, 1)
    return jnp.sum(jnp.where(same, jnp.broadcast_to(column, shape), 0.0), axis=0, keepdims=True)


def column_kernel(groups, core, *refs):
    ins, outs, scratch = refs[: 2 * groups + 7], refs[-4:-2], refs[-2:]

    def idle():
        for given, out in zip(refs[2 * groups + 7 : -4], outs):
            out[...] = given[...]

    on_core(core, functools.partial(sum_columns, groups, *ins, *outs, *scratch), idle)


def sum_columns(groups, *refs):
    exps_refs, tall_refs, rest = refs[:groups], refs[groups : 2 * groups], refs[2 * groups :]
    wide_ref, peak_ref, mask_ref, own_ref, other_ref, mass_ref, norm_ref = rest[:7]
    poten_ref, sums_ref, weight_ref, shift_ref = rest[7:]
    pairs, _, both = wide_ref.shape
    cells = both // 2
    shards = mask_ref.shape[0]
    own, other = own_ref[...], other_ref[...]
    top = jnp.maximum(own, other)
    whole = top + jnp.log2(jnp.exp2(own - top) + jnp.exp2(other - top))
    poten_ref[...] = norm_ref[...] - (entropic * ln2) * whole
    shift = mass_ref[...] * log2e - whole
    shift_ref[...] = shift
    for place in range(shards):
        weight_ref[place] = jnp.exp2(peak_ref[place] + shift)
    spots = [
        (group, slice(index * cells, (index + 1) * cells))
        for group, ref in enumerate(tall_refs)
        for index in range(ref.shape[0] // cells)
    ]
    used = [jnp.max(mask_ref[place], axis=0, keepdims=True) > 0.5 * very_low for place in range(shards)]
    ranks = [shards - 1 - jnp.where(block > 1, block ^ 1, block) for block in blocks_at(shards)]
    sums = []
    for place, (group, rows) in enumerate(spots):
        acc = jnp.zeros((cells, cells), jnp.float32)
        for pair in range(pairs):
            acc = acc + exps_refs[group][pair, rows, :cells] * weight_ref[place, 2 * pair : 2 * pair + 1, :]
            acc = acc + exps_refs[group][pair, rows, cells:] * weight_ref[place, 2 * pair + 1 : 2 * pair + 2, :]
        sums.append(jnp.sum(acc.T, axis=0, keepdims=True))
    whole_sums = jnp.concatenate([jnp.where(here, one, 1.0) for here, one in zip(used, sums)], axis=0)
    worst = jnp.min(whole_sums)
    logs = jnp.log2(whole_sums)
    for place in range(shards):
        sums_ref[ranks[place]] = jnp.where(used[place], logs[place : place + 1, :], very_low)

    @pl.when(worst < least_sum)
    def _():
        for place, (group, rows) in enumerate(spots):

            def exponents(pair):
                score = jnp.dot(tall_refs[group][rows, :], wide_ref[pair], preferred_element_type=jnp.float32)
                add = shift_ref[pl.ds(2 * pair, 2), :] + mask_ref[place, pl.ds(2 * pair, 2), :]
                return score[:, :cells] + add[0:1, :], score[:, cells:] + add[1:2, :]

            def highest(pair, peak):
                first, second = exponents(pair)
                return jnp.maximum(peak, jnp.maximum(first, second))

            peak = lax.fori_loop(0, pairs, highest, jnp.full((cells, cells), very_low, jnp.float32))
            peak = jnp.max(peak, axis=1, keepdims=True)

            def add_up(pair, sums):
                first, second = exponents(pair)
                return sums + jnp.exp2(first - peak) + jnp.exp2(second - peak)

            sums = lax.fori_loop(0, pairs, add_up, jnp.zeros((cells, cells), jnp.float32))
            logs = across(peak) + jnp.log2(across(jnp.sum(sums, axis=1, keepdims=True)))
            sums_ref[ranks[place]] = jnp.where(used[place], logs, very_low)


def merge_kernel(values_ref, weight_ref, poten_ref, out_ref, poten_out_ref):
    poten_out_ref[...] = poten_ref[...]
    values = values_ref[...]
    top = jnp.max(values, axis=0)
    whole = top + jnp.log2(jnp.sum(jnp.exp2(values - top), axis=0))
    out_ref[...] = -(entropic * ln2) * (whole - weight_ref[...])


def f32(*shape):
    return jax.ShapeDtypeStruct(shape, jnp.float32)


def dense_device(
    source_feat, target_feat, log_mass_src, log_mass_tgt, potential_tgt, support, counts
):
    shards = lax.axis_size("src")
    rows, depth, cells = source_feat.shape
    pairs, wide = rows // 2, 2 * cells

    def call(kernel, ins, out_shape, scratch=(), cost=None):
        many = isinstance(out_shape, list)
        return pl.pallas_call(
            kernel,
            in_specs=ins,
            out_specs=[VM] * len(out_shape) if many else VM,
            out_shape=out_shape,
            scratch_shapes=list(scratch),
            compiler_params=PARAMS,
            cost_estimate=cost,
        )

    def reading(kernel, args, out_shape, cost):
        return call(
            kernel,
            [pl.BlockSpec(memory_space=pltpu.HBM)] * len(args),
            out_shape,
            [pltpu.VMEM(arg.shape, arg.dtype) for arg in args] + [pltpu.SemaphoreType.DMA((len(args),))],
            cost,
        )(*[pltpu.with_memory_space_constraint(arg, pltpu.HBM) for arg in args])

    def cost_of(flops):
        return pl.CostEstimate(flops=flops, bytes_accessed=rows * depth * cells * 4, transcendentals=0)

    pack, weight = reading(
        pack_kernel,
        [target_feat, log_mass_tgt, potential_tgt],
        [in_vmem((1, depth + 1, 1, cells), jnp.float32), in_vmem((1, cells), jnp.float32)],
        None,
    )
    wide_feat, norm, mask, mass = reading(
        functools.partial(source_kernel, shards),
        [log_mass_src, support[:, 0, :].T, counts.T, source_feat],
        [
            in_vmem((pairs, 8 * depth, wide), jnp.bfloat16),
            in_vmem((rows, cells), jnp.float32),
            in_vmem((shards, rows, cells), jnp.float32),
            in_vmem((rows, cells), jnp.float32),
        ],
        cost_of(10**8),
    )

    def tiles(*packs, core=None, after=None):
        blocks = sum(pack.shape[0] for pack in packs)
        more = [] if after is None else [after]
        return call(
            functools.partial(tile_kernel, len(packs), core),
            [VM] * (len(packs) + 1) + [pl.BlockSpec(memory_space=pl.ANY)] * len(more),
            [
                in_vmem((pairs, blocks * cells, wide), jnp.float32),
                in_vmem((blocks * cells, 8 * depth), jnp.bfloat16),
                in_vmem((blocks, rows, cells), jnp.float32),
                in_vmem((blocks, rows, cells), jnp.float32),
            ],
            cost=cost_of(2 * blocks * cells * pairs * wide * 8 * depth),
        )(*packs, wide_feat, *more)

    def swapped(array):
        return lax.ppermute(array, "src", [(i, i ^ 1) for i in range(shards)])

    def moved(array, receivers):
        moves = [(2 * here + odd, 2 * there + odd) for here, there in enumerate(receivers) for odd in range(2)]
        return lax.ppermute(array, "src", moves)

    def joined(first, second, after):
        return call(
            join_kernel,
            [VM] * 2 + [pl.BlockSpec(memory_space=pl.ANY)],
            in_vmem((2,) + pack.shape[1:], jnp.float32),
        )(first, second, after)

    there = [moved(pack, receivers) for receivers in line_moves(shards // 2)[::-1]][::-1]
    near = [pack] + there
    halves = [joined(near[0], near[1], norm)]
    for at in range(2, shards // 2, 2):
        halves.append(joined(near[at], near[at + 1], halves[-1]))
    far = [swapped(half) for half in halves]
    found = [tiles(*near, after=halves[-1])]
    for half in far[:-1]:
        found.append(tiles(half, after=found[-1][-1]))
    groups = len(found) + 1

    def log_sums(last):
        _, _, peaks, totals = zip(*found, last)
        return call(
            functools.partial(row_kernel, groups),
            [VM] * (1 + 2 * groups),
            [in_vmem((shards, rows, cells), jnp.float32), in_vmem((rows, cells), jnp.float32)],
        )(mask, *peaks, *totals)

    def columns_of(core, last, peaks, own, other, given):
        exps, tall, _, _ = zip(*found, last)
        return call(
            functools.partial(column_kernel, groups, core),
            [VM] * (2 * groups + 7 + len(given)),
            [in_vmem((rows, cells), jnp.float32), in_vmem((shards, 1, cells), jnp.float32)],
            [pltpu.VMEM((shards, rows, cells), jnp.float32), pltpu.VMEM((rows, cells), jnp.float32)],
            cost_of(10**9),
        )(*exps, *tall, wide_feat, peaks, mask, own, other, mass, norm, *given)

    between = [(0, 1), (1, 0)]
    last_one = tiles(far[-1], core=1, after=found[-1][-1])
    peaks_one, own_one = log_sums(last_one)
    other_zero = lax.ppermute(own_one, "tgt", between)
    last_zero = tiles(far[-1], core=0, after=own_one)
    peaks_zero, own_zero = log_sums(last_zero)
    other_one = lax.ppermute(own_zero, "tgt", between)
    given = columns_of(0, last_zero, peaks_zero, own_zero, other_zero, [])
    potential_src, columns = columns_of(1, last_one, peaks_one, own_one, other_one, given)
    members = [block ^ (block > 1) for block in reversed(range(shards))]
    arrived = lax.all_to_all(columns, "src", 0, 0, axis_index_groups=[members])
    outs = [f32(1, cells), f32(rows, cells)]
    potential_new, potential_src = call(merge_kernel, [VM] * 3, outs)(arrived, weight, potential_src)
    return potential_src, potential_new


def merged(part, axis, combine):
    gathered = jax.tree.map(lambda a: lax.all_gather(a, axis), part)

    def take(source):
        return jax.tree.map(lambda a: lax.dynamic_index_in_dim(a, source, 0, False), gathered)

    return lax.fori_loop(
        1, lax.axis_size(axis), lambda source, state: combine(state, take(source)), take(0)
    )


def cost_tiles(source_blk, source_sq, target_blk, target_sq):
    cross = jnp.einsum(
        "...fi,...fj->...ij", source_blk, target_blk, precision=lax.Precision.HIGHEST
    )
    return source_sq[..., :, None] + target_sq[..., None, :] - 2.0 * cross


def row_stats(cost, mass_tgt, poten_tgt, usable):
    scores = mass_tgt[..., None, :] + (poten_tgt[..., None, :] - cost) / entropic
    scores = jnp.where(usable[..., None, None], scores, very_low)
    peak = jnp.max(scores, axis=(1, 3))
    total = jnp.sum(jnp.exp(scores - peak[:, None, :, None]), axis=(1, 3))
    return (peak, total)


def column_stats(cost, mass_src, poten_src, usable):
    scores = mass_src[:, None, :, None] + (poten_src[:, None, :, None] - cost) / entropic
    peak = jnp.max(scores, axis=2)
    total = jnp.sum(jnp.exp(scores - peak[:, :, None, :]), axis=2)
    peak = jnp.where(usable[..., None], peak, very_low)
    total = jnp.where(usable[..., None], total, 0.0)
    return (peak, total)


def merge_pair(first_pair, second_pair):
    first_peak, first_total = first_pair
    second_peak, second_total = second_pair
    highest = jnp.maximum(first_peak, second_peak)
    summed = first_total * jnp.exp(first_peak - highest) + second_total * jnp.exp(
        second_peak - highest
    )
    return (highest, summed)


def segment_merge(peaks, totals, seg_ids, segments):
    best = jax.ops.segment_max(peaks, seg_ids, num_segments=segments + 1)
    best = jnp.maximum(best, very_low)
    summed = jax.ops.segment_sum(
        totals * jnp.exp(peaks - best[seg_ids]), seg_ids, num_segments=segments + 1
    )
    return (best[:segments], summed[:segments])


def general_device(
    source_feat, target_feat, log_mass_src, log_mass_tgt, potential_tgt, support, counts
):
    target_all, mass_all, poten_all = (
        lax.all_gather(target_feat, "src", axis=0, tiled=True),
        lax.all_gather(log_mass_tgt, "src", axis=0, tiled=True),
        lax.all_gather(potential_tgt, "src", axis=0, tiled=True),
    )
    blocks = target_all.shape[0]
    rows_here = source_feat.shape[0]
    slots_here = support.shape[2]
    cells = source_feat.shape[2]
    indices = support[:, 0, :]
    limits = counts[:, 0]
    usable = jnp.arange(slots_here, dtype=jnp.int32)[None, :] < limits[:, None]
    source_sq = jnp.sum(source_feat * source_feat, axis=1)
    target_sq = jnp.sum(target_all * target_all, axis=1)
    width = math.gcd(rows_here, 4)

    def grouped(array):
        return array.reshape((rows_here // width, width) + array.shape[1:])

    def row_pass(items):
        source_blk, source_nrm, ids_here, use_here = items
        cost = cost_tiles(
            source_blk[:, None], source_nrm[:, None], target_all[ids_here], target_sq[ids_here]
        )
        return row_stats(cost, mass_all[ids_here], poten_all[ids_here], use_here)

    peak, total = lax.map(
        row_pass, (grouped(source_feat), grouped(source_sq), grouped(indices), grouped(usable))
    )
    peak = peak.reshape(rows_here, cells)
    total = total.reshape(rows_here, cells)
    peak_all, total_all = merged((peak, total), "tgt", merge_pair)
    potential_src = -entropic * (peak_all + jnp.log(total_all))

    def column_pass(items):
        source_blk, source_nrm, mass_here, poten_here, ids_here, use_here = items
        cost = cost_tiles(
            source_blk[:, None], source_nrm[:, None], target_all[ids_here], target_sq[ids_here]
        )
        return column_stats(cost, mass_here, poten_here, use_here)

    peaks, totals = lax.map(
        column_pass,
        (
            grouped(source_feat),
            grouped(source_sq),
            grouped(log_mass_src),
            grouped(potential_src),
            grouped(indices),
            grouped(usable),
        ),
    )
    seg_ids = jnp.where(usable, indices, blocks).reshape(-1)
    best, summed = segment_merge(
        peaks.reshape(-1, cells), totals.reshape(-1, cells), seg_ids, blocks
    )
    share = blocks // lax.axis_size("src")
    own_start = lax.axis_index("src") * share
    highest = lax.pmax(best, "src")
    whole = lax.psum(summed * jnp.exp(best - highest), "src")
    own_peak = lax.dynamic_slice_in_dim(highest, own_start, share, 0)
    own_total = lax.dynamic_slice_in_dim(whole, own_start, share, 0)
    potential_new = -entropic * (own_peak + jnp.log(own_total))
    return (potential_src, potential_new)


def per_device(source_feat, target_feat, *others):
    shards = lax.axis_size("src")
    rows, depth, cells = source_feat.shape
    paired = shards >= 4 and shards & (shards - 1) == 0 and lax.axis_size("tgt") == 2
    shaped = target_feat.shape[0] == 1 and rows % 2 == 0 and cells == 2 * depth and cells % 128 == 0
    if paired and shaped and 4 * rows * cells * shards * cells <= room:
        return dense_device(source_feat, target_feat, *others)
    return general_device(source_feat, target_feat, *others)


def solution(mesh):
    in_specs = (
        P(("grp", "src"), None, None),
        P(("grp", "src", "tgt"), None, None),
        P(("grp", "src"), None),
        P(("grp", "src", "tgt"), None),
        P(("grp", "src", "tgt"), None),
        P(("grp", "src"), "tgt", None),
        P(("grp", "src"), "tgt"),
    )
    out_specs = (P(("grp", "src"), None), P(("grp", "src", "tgt"), None))
    return jax.shard_map(
        per_device, mesh=mesh, in_specs=in_specs, out_specs=out_specs, check_vma=False
    )
```

```python
import functools
import math

import jax
import jax.numpy as jnp
from jax import lax
from jax.experimental import pallas as pl
from jax.experimental.pallas import tpu as pltpu
from jax.sharding import PartitionSpec as P

entropic = 0.5
very_low = -1e30
log2e = 1.0 / math.log(2.0)
ln2 = math.log(2.0)
least_sum = 1e-28

room = 2**24

VM = pl.BlockSpec(memory_space=pltpu.VMEM)
PARAMS = pltpu.CompilerParams(vmem_limit_bytes=40 * 2**20)


def in_vmem(shape, dtype):
    return pltpu.VMEM(shape, dtype)


def pieces(values):
    high = values.astype(jnp.bfloat16).astype(jnp.float32)
    rest = values - high
    mid = rest.astype(jnp.bfloat16).astype(jnp.float32)
    low = (rest - mid).astype(jnp.bfloat16).astype(jnp.float32)
    return high, mid, low


def target_weight(mass, poten):
    return (mass + poten / entropic) * log2e


def line_moves(line):
    bits = line.bit_length() - 1
    cycle = [sum(((place >> bit) & 1) << (bits - 1 - bit) for bit in range(bits)) for place in range(line)]
    shifts = [shift for step in range(1, line // 2) for shift in (step, line - step)] + [line // 2]
    return [[cycle[(cycle.index(at) + shift) % line] for at in range(line)] for shift in shifts]


def blocks_at(shards):
    me = lax.axis_index("src")
    at, odd = me // 2, lax.rem(me, 2)
    near = [me]
    for receivers in line_moves(shards // 2):
        senders = [receivers.index(there) for there in range(shards // 2)]
        near.append(2 * sum(jnp.where(at == there, sender, 0) for there, sender in enumerate(senders)) + odd)
    return near + [block ^ 1 for block in near]


def members_of(shards):
    return sorted(range(shards), key=lambda at: (-(at // 2 + at % 2), -(at % 2)))


def read_all(hbm, held, sems):
    copies = [pltpu.make_async_copy(src, dst, sems.at[i]) for i, (src, dst) in enumerate(zip(hbm, held))]
    for copy in copies:
        copy.start()
    return copies


def pack_kernel(*refs):
    hbm, (send_ref, weight_ref), held, sems = refs[:3], refs[3:5], refs[5:8], refs[8]
    for copy in read_all(hbm, held, sems):
        copy.wait()
    feat_ref, mass_ref, poten_ref = held
    feat = feat_ref[0]
    depth, cells = feat.shape
    weight = target_weight(mass_ref[...], poten_ref[...])
    norm = jnp.sum(feat * feat, axis=0, keepdims=True)
    bias = weight - (log2e / entropic) * norm
    scaled = feat * (2.0 * log2e / entropic)
    send_ref[0, :depth, 0, :] = scaled
    send_ref[0, depth, 0:1, :] = bias
    weight_ref[...] = weight


def source_kernel(shards, *refs):
    hbm, outs, held, sems = refs[:4], refs[4:8], refs[8:12], refs[12]
    wide_ref, norm_ref, mask_ref, mass_out_ref = outs
    mass_ref, support_ref, counts_ref, feat_ref = held
    copies = read_all(hbm, held, sems)
    for copy in copies[:3]:
        copy.wait()
    mass_out_ref[...] = mass_ref[...]
    support = support_ref[...]
    slots, rows = support.shape
    cells = mass_ref.shape[1]
    used = lax.broadcasted_iota(jnp.int32, support.shape, 0) < counts_ref[...]
    hits = [
        jnp.max(jnp.where(used & (support == block), 0.0, very_low), axis=0, keepdims=True)
        for block in blocks_at(shards)
    ]
    hits = jnp.concatenate(hits + [jnp.zeros((cells - shards, rows), jnp.float32)], axis=0)
    hits = jnp.concatenate([hits, jnp.zeros((cells, cells - rows), jnp.float32)], axis=1).T
    for place in range(shards):
        mask_ref[place] = jnp.broadcast_to(hits[:rows, place : place + 1], (rows, cells))
    copies[3].wait()
    depth = feat_ref.shape[1]
    one = jnp.ones((2 * depth, 2 * cells), jnp.bfloat16)
    for pair in range(rows // 2):
        for half in range(2):
            feat = feat_ref[2 * pair + half]
            norm_ref[2 * pair + half : 2 * pair + half + 1, :] = jnp.sum(feat * feat, axis=0, keepdims=True)
            high, mid, low = pieces(feat)
            lanes = slice(half * cells, (half + 1) * cells)
            top = jnp.concatenate([high, mid], axis=0).astype(jnp.bfloat16)
            wide_ref[pair, 0 : 2 * depth, lanes] = top
            wide_ref[pair, 2 * depth : 4 * depth, lanes] = top
            wide_ref[pair, 4 * depth : 6 * depth, lanes] = jnp.concatenate([low, high], axis=0).astype(jnp.bfloat16)
        wide_ref[pair, 6 * depth : 8 * depth, :] = one


def join_kernel(*refs):
    refs[-1][0] = refs[0][0]
    refs[-1][1] = refs[1][0]


def on_core(core, work, idle):
    if core is None:
        work()
    else:
        here = lax.axis_index("tgt") == core
        pl.when(here)(work)
        pl.when(jnp.logical_not(here))(idle)


def tile_kernel(parts, core, *refs):
    peak_ref, total_ref = refs[-2:]

    def idle():
        peak_ref[...] = jnp.zeros(peak_ref.shape, jnp.float32)
        total_ref[...] = jnp.zeros(total_ref.shape, jnp.float32)

    ins = refs[: parts + 1] + refs[-4:]
    on_core(core, functools.partial(make_tiles, parts, *ins), idle)


def make_tiles(parts, *refs):
    packs = [ref.at[index] for ref in refs[:parts] for index in range(ref.shape[0])]
    wide_ref, exps_ref, tall_ref, peak_ref, total_ref = refs[parts:]
    blocks = len(packs)
    pairs, _, both = wide_ref.shape
    cells = both // 2
    depth = cells // 2
    lane = lax.broadcasted_iota(jnp.int32, (cells, cells), 1)
    biases = jnp.concatenate([pack[depth, 0:1, :] for pack in packs], axis=0)
    bias_pieces = jnp.concatenate(list(pieces(biases)), axis=0)
    padded = jnp.concatenate([bias_pieces, jnp.zeros((cells - 3 * blocks, cells), jnp.float32)], axis=0)
    bias_lanes = padded.T
    for place, pack in enumerate(packs):
        feat = pack[:depth, 0, :]
        turned = jnp.concatenate([feat, feat], axis=0).T
        high, mid, low = pieces(turned)
        own = jnp.where(lax.rem(lane, blocks) == place, bias_lanes, 0.0)
        rows = slice(place * cells, (place + 1) * cells)
        tall_ref[rows, 0:cells] = high.astype(jnp.bfloat16)
        tall_ref[rows, cells : 2 * cells] = mid.astype(jnp.bfloat16)
        tall_ref[rows, 2 * cells : 3 * cells] = jnp.where(lane < depth, high, low).astype(jnp.bfloat16)
        tall_ref[rows, 3 * cells : 4 * cells] = own.astype(jnp.bfloat16)

    def body(pair, carry):
        scores = jnp.dot(tall_ref[...], wide_ref[pair], preferred_element_type=jnp.float32)
        for place in range(blocks):
            rows = slice(place * cells, (place + 1) * cells)
            score = scores[rows]
            peak = jnp.max(score, axis=0, keepdims=True)
            exps = jnp.exp2(score - peak)
            exps_ref[pair, rows, :] = exps
            total = jnp.sum(exps, axis=0, keepdims=True)
            for half in range(2):
                lanes = slice(half * cells, (half + 1) * cells)
                peak_ref[place, pl.ds(2 * pair + half, 1), :] = peak[:, lanes]
                total_ref[place, pl.ds(2 * pair + half, 1), :] = total[:, lanes]
        return carry

    lax.fori_loop(0, pairs, body, 0, unroll=max(1, min(pairs, 32 // blocks)))


def row_kernel(groups, *refs):
    mask_ref, peak_refs, total_refs = refs[0], refs[1 : 1 + groups], refs[1 + groups : 1 + 2 * groups]
    peaks_ref, rowsum_ref = refs[1 + 2 * groups :]
    place = 0
    for ref in peak_refs:
        for index in range(ref.shape[0]):
            peaks_ref[place] = ref[index] + mask_ref[place]
            place += 1
    totals = [ref[index] for ref in total_refs for index in range(ref.shape[0])]
    top = functools.reduce(jnp.maximum, [peaks_ref[index] for index in range(place)])
    summed = sum(total * jnp.exp2(peaks_ref[index] - top) for index, total in enumerate(totals))
    rowsum_ref[...] = top + jnp.log2(summed)


def across(column):
    shape = (column.shape[0],) * 2
    same = lax.broadcasted_iota(jnp.int32, shape, 0) == lax.broadcasted_iota(jnp.int32, shape, 1)
    return jnp.sum(jnp.where(same, jnp.broadcast_to(column, shape), 0.0), axis=0, keepdims=True)


def column_kernel(groups, core, *refs):
    ins, outs, scratch = refs[: 2 * groups + 7], refs[-4:-2], refs[-2:]

    def idle():
        for given, out in zip(refs[2 * groups + 7 : -4], outs):
            out[...] = given[...]

    on_core(core, functools.partial(sum_columns, groups, *ins, *outs, *scratch), idle)


def sum_columns(groups, *refs):
    exps_refs, tall_refs, rest = refs[:groups], refs[groups : 2 * groups], refs[2 * groups :]
    wide_ref, peak_ref, mask_ref, own_ref, other_ref, mass_ref, norm_ref = rest[:7]
    poten_ref, sums_ref, weight_ref, shift_ref = rest[7:]
    pairs, _, both = wide_ref.shape
    cells = both // 2
    shards = mask_ref.shape[0]
    own, other = own_ref[...], other_ref[...]
    top = jnp.maximum(own, other)
    whole = top + jnp.log2(jnp.exp2(own - top) + jnp.exp2(other - top))
    poten_ref[...] = norm_ref[...] - (entropic * ln2) * whole
    shift = mass_ref[...] * log2e - whole
    shift_ref[...] = shift
    for place in range(shards):
        weight_ref[place] = jnp.exp2(peak_ref[place] + shift)
    spots = [
        (group, slice(index * cells, (index + 1) * cells))
        for group, ref in enumerate(tall_refs)
        for index in range(ref.shape[0] // cells)
    ]
    used = [jnp.max(mask_ref[place], axis=0, keepdims=True) > 0.5 * very_low for place in range(shards)]
    places = [members_of(shards).index(block) for block in range(shards)]
    ranks = [sum(jnp.where(block == at, rank, 0) for at, rank in enumerate(places)) for block in blocks_at(shards)]
    sums = []
    for place, (group, rows) in enumerate(spots):
        acc = jnp.zeros((cells, cells), jnp.float32)
        for pair in range(pairs):
            acc = acc + exps_refs[group][pair, rows, :cells] * weight_ref[place, 2 * pair : 2 * pair + 1, :]
            acc = acc + exps_refs[group][pair, rows, cells:] * weight_ref[place, 2 * pair + 1 : 2 * pair + 2, :]
        sums.append(jnp.sum(acc.T, axis=0, keepdims=True))
    whole_sums = jnp.concatenate([jnp.where(here, one, 1.0) for here, one in zip(used, sums)], axis=0)
    worst = jnp.min(whole_sums)
    logs = jnp.log2(whole_sums)
    for place in range(shards):
        sums_ref[ranks[place]] = jnp.where(used[place], logs[place : place + 1, :], very_low)

    @pl.when(worst < least_sum)
    def _():
        for place, (group, rows) in enumerate(spots):

            def exponents(pair):
                score = jnp.dot(tall_refs[group][rows, :], wide_ref[pair], preferred_element_type=jnp.float32)
                add = shift_ref[pl.ds(2 * pair, 2), :] + mask_ref[place, pl.ds(2 * pair, 2), :]
                return score[:, :cells] + add[0:1, :], score[:, cells:] + add[1:2, :]

            def highest(pair, peak):
                first, second = exponents(pair)
                return jnp.maximum(peak, jnp.maximum(first, second))

            peak = lax.fori_loop(0, pairs, highest, jnp.full((cells, cells), very_low, jnp.float32))
            peak = jnp.max(peak, axis=1, keepdims=True)

            def add_up(pair, sums):
                first, second = exponents(pair)
                return sums + jnp.exp2(first - peak) + jnp.exp2(second - peak)

            sums = lax.fori_loop(0, pairs, add_up, jnp.zeros((cells, cells), jnp.float32))
            logs = across(peak) + jnp.log2(across(jnp.sum(sums, axis=1, keepdims=True)))
            sums_ref[ranks[place]] = jnp.where(used[place], logs, very_low)


def merge_kernel(values_ref, weight_ref, poten_ref, out_ref, poten_out_ref):
    poten_out_ref[...] = poten_ref[...]
    values = values_ref[...]
    top = jnp.max(values, axis=0)
    whole = top + jnp.log2(jnp.sum(jnp.exp2(values - top), axis=0))
    out_ref[...] = -(entropic * ln2) * (whole - weight_ref[...])


def f32(*shape):
    return jax.ShapeDtypeStruct(shape, jnp.float32)


def dense_device(
    source_feat, target_feat, log_mass_src, log_mass_tgt, potential_tgt, support, counts
):
    shards = lax.axis_size("src")
    rows, depth, cells = source_feat.shape
    pairs, wide = rows // 2, 2 * cells

    def call(kernel, ins, out_shape, scratch=(), cost=None):
        many = isinstance(out_shape, list)
        return pl.pallas_call(
            kernel,
            in_specs=ins,
            out_specs=[VM] * len(out_shape) if many else VM,
            out_shape=out_shape,
            scratch_shapes=list(scratch),
            compiler_params=PARAMS,
            cost_estimate=cost,
        )

    def reading(kernel, args, out_shape, cost):
        return call(
            kernel,
            [pl.BlockSpec(memory_space=pltpu.HBM)] * len(args),
            out_shape,
            [pltpu.VMEM(arg.shape, arg.dtype) for arg in args] + [pltpu.SemaphoreType.DMA((len(args),))],
            cost,
        )(*[pltpu.with_memory_space_constraint(arg, pltpu.HBM) for arg in args])

    def cost_of(flops):
        return pl.CostEstimate(flops=flops, bytes_accessed=rows * depth * cells * 4, transcendentals=0)

    pack, weight = reading(
        pack_kernel,
        [target_feat, log_mass_tgt, potential_tgt],
        [in_vmem((1, depth + 1, 1, cells), jnp.float32), in_vmem((1, cells), jnp.float32)],
        None,
    )
    wide_feat, norm, mask, mass = reading(
        functools.partial(source_kernel, shards),
        [log_mass_src, support[:, 0, :].T, counts.T, source_feat],
        [
            in_vmem((pairs, 8 * depth, wide), jnp.bfloat16),
            in_vmem((rows, cells), jnp.float32),
            in_vmem((shards, rows, cells), jnp.float32),
            in_vmem((rows, cells), jnp.float32),
        ],
        cost_of(10**8),
    )

    def tiles(*packs, core=None, after=None):
        blocks = sum(pack.shape[0] for pack in packs)
        more = [] if after is None else [after]
        return call(
            functools.partial(tile_kernel, len(packs), core),
            [VM] * (len(packs) + 1) + [pl.BlockSpec(memory_space=pl.ANY)] * len(more),
            [
                in_vmem((pairs, blocks * cells, wide), jnp.float32),
                in_vmem((blocks * cells, 8 * depth), jnp.bfloat16),
                in_vmem((blocks, rows, cells), jnp.float32),
                in_vmem((blocks, rows, cells), jnp.float32),
            ],
            cost=cost_of(2 * blocks * cells * pairs * wide * 8 * depth),
        )(*packs, wide_feat, *more)

    def swapped(array):
        return lax.ppermute(array, "src", [(i, i ^ 1) for i in range(shards)])

    def moved(array, receivers):
        moves = [(2 * here + odd, 2 * there + odd) for here, there in enumerate(receivers) for odd in range(2)]
        return lax.ppermute(array, "src", moves)

    def joined(first, second, after):
        return call(
            join_kernel,
            [VM] * 2 + [pl.BlockSpec(memory_space=pl.ANY)],
            in_vmem((2,) + pack.shape[1:], jnp.float32),
        )(first, second, after)

    there = [moved(pack, receivers) for receivers in line_moves(shards // 2)[::-1]][::-1]
    near = [pack] + there
    halves = [joined(near[0], near[1], norm)]
    for at in range(2, shards // 2, 2):
        halves.append(joined(near[at], near[at + 1], halves[-1]))
    far = [swapped(half) for half in halves]
    found = [tiles(*near, after=halves[-1])]
    for half in far[:-1]:
        found.append(tiles(half, after=found[-1][-1]))
    groups = len(found) + 1

    def log_sums(last):
        _, _, peaks, totals = zip(*found, last)
        return call(
            functools.partial(row_kernel, groups),
            [VM] * (1 + 2 * groups),
            [in_vmem((shards, rows, cells), jnp.float32), in_vmem((rows, cells), jnp.float32)],
        )(mask, *peaks, *totals)

    def columns_of(core, last, peaks, own, other, given):
        exps, tall, _, _ = zip(*found, last)
        return call(
            functools.partial(column_kernel, groups, core),
            [VM] * (2 * groups + 7 + len(given)),
            [in_vmem((rows, cells), jnp.float32), in_vmem((shards, 1, cells), jnp.float32)],
            [pltpu.VMEM((shards, rows, cells), jnp.float32), pltpu.VMEM((rows, cells), jnp.float32)],
            cost_of(10**9),
        )(*exps, *tall, wide_feat, peaks, mask, own, other, mass, norm, *given)

    between = [(0, 1), (1, 0)]
    last_one = tiles(far[-1], core=1, after=found[-1][-1])
    peaks_one, own_one = log_sums(last_one)
    other_zero = lax.ppermute(own_one, "tgt", between)
    last_zero = tiles(far[-1], core=0, after=own_one)
    peaks_zero, own_zero = log_sums(last_zero)
    other_one = lax.ppermute(own_zero, "tgt", between)
    given = columns_of(0, last_zero, peaks_zero, own_zero, other_zero, [])
    potential_src, columns = columns_of(1, last_one, peaks_one, own_one, other_one, given)
    arrived = lax.all_to_all(columns, "src", 0, 0, axis_index_groups=[members_of(shards)])
    outs = [f32(1, cells), f32(rows, cells)]
    potential_new, potential_src = call(merge_kernel, [VM] * 3, outs)(arrived, weight, potential_src)
    return potential_src, potential_new


def merged(part, axis, combine):
    gathered = jax.tree.map(lambda a: lax.all_gather(a, axis), part)

    def take(source):
        return jax.tree.map(lambda a: lax.dynamic_index_in_dim(a, source, 0, False), gathered)

    return lax.fori_loop(
        1, lax.axis_size(axis), lambda source, state: combine(state, take(source)), take(0)
    )


def cost_tiles(source_blk, source_sq, target_blk, target_sq):
    cross = jnp.einsum(
        "...fi,...fj->...ij", source_blk, target_blk, precision=lax.Precision.HIGHEST
    )
    return source_sq[..., :, None] + target_sq[..., None, :] - 2.0 * cross


def row_stats(cost, mass_tgt, poten_tgt, usable):
    scores = mass_tgt[..., None, :] + (poten_tgt[..., None, :] - cost) / entropic
    scores = jnp.where(usable[..., None, None], scores, very_low)
    peak = jnp.max(scores, axis=(1, 3))
    total = jnp.sum(jnp.exp(scores - peak[:, None, :, None]), axis=(1, 3))
    return (peak, total)


def column_stats(cost, mass_src, poten_src, usable):
    scores = mass_src[:, None, :, None] + (poten_src[:, None, :, None] - cost) / entropic
    peak = jnp.max(scores, axis=2)
    total = jnp.sum(jnp.exp(scores - peak[:, :, None, :]), axis=2)
    peak = jnp.where(usable[..., None], peak, very_low)
    total = jnp.where(usable[..., None], total, 0.0)
    return (peak, total)


def merge_pair(first_pair, second_pair):
    first_peak, first_total = first_pair
    second_peak, second_total = second_pair
    highest = jnp.maximum(first_peak, second_peak)
    summed = first_total * jnp.exp(first_peak - highest) + second_total * jnp.exp(
        second_peak - highest
    )
    return (highest, summed)


def segment_merge(peaks, totals, seg_ids, segments):
    best = jax.ops.segment_max(peaks, seg_ids, num_segments=segments + 1)
    best = jnp.maximum(best, very_low)
    summed = jax.ops.segment_sum(
        totals * jnp.exp(peaks - best[seg_ids]), seg_ids, num_segments=segments + 1
    )
    return (best[:segments], summed[:segments])


def general_device(
    source_feat, target_feat, log_mass_src, log_mass_tgt, potential_tgt, support, counts
):
    target_all, mass_all, poten_all = (
        lax.all_gather(target_feat, "src", axis=0, tiled=True),
        lax.all_gather(log_mass_tgt, "src", axis=0, tiled=True),
        lax.all_gather(potential_tgt, "src", axis=0, tiled=True),
    )
    blocks = target_all.shape[0]
    rows_here = source_feat.shape[0]
    slots_here = support.shape[2]
    cells = source_feat.shape[2]
    indices = support[:, 0, :]
    limits = counts[:, 0]
    usable = jnp.arange(slots_here, dtype=jnp.int32)[None, :] < limits[:, None]
    source_sq = jnp.sum(source_feat * source_feat, axis=1)
    target_sq = jnp.sum(target_all * target_all, axis=1)
    width = math.gcd(rows_here, 4)

    def grouped(array):
        return array.reshape((rows_here // width, width) + array.shape[1:])

    def row_pass(items):
        source_blk, source_nrm, ids_here, use_here = items
        cost = cost_tiles(
            source_blk[:, None], source_nrm[:, None], target_all[ids_here], target_sq[ids_here]
        )
        return row_stats(cost, mass_all[ids_here], poten_all[ids_here], use_here)

    peak, total = lax.map(
        row_pass, (grouped(source_feat), grouped(source_sq), grouped(indices), grouped(usable))
    )
    peak = peak.reshape(rows_here, cells)
    total = total.reshape(rows_here, cells)
    peak_all, total_all = merged((peak, total), "tgt", merge_pair)
    potential_src = -entropic * (peak_all + jnp.log(total_all))

    def column_pass(items):
        source_blk, source_nrm, mass_here, poten_here, ids_here, use_here = items
        cost = cost_tiles(
            source_blk[:, None], source_nrm[:, None], target_all[ids_here], target_sq[ids_here]
        )
        return column_stats(cost, mass_here, poten_here, use_here)

    peaks, totals = lax.map(
        column_pass,
        (
            grouped(source_feat),
            grouped(source_sq),
            grouped(log_mass_src),
            grouped(potential_src),
            grouped(indices),
            grouped(usable),
        ),
    )
    seg_ids = jnp.where(usable, indices, blocks).reshape(-1)
    best, summed = segment_merge(
        peaks.reshape(-1, cells), totals.reshape(-1, cells), seg_ids, blocks
    )
    share = blocks // lax.axis_size("src")
    own_start = lax.axis_index("src") * share
    highest = lax.pmax(best, "src")
    whole = lax.psum(summed * jnp.exp(best - highest), "src")
    own_peak = lax.dynamic_slice_in_dim(highest, own_start, share, 0)
    own_total = lax.dynamic_slice_in_dim(whole, own_start, share, 0)
    potential_new = -entropic * (own_peak + jnp.log(own_total))
    return (potential_src, potential_new)


def per_device(source_feat, target_feat, *others):
    shards = lax.axis_size("src")
    rows, depth, cells = source_feat.shape
    paired = shards >= 4 and shards & (shards - 1) == 0 and lax.axis_size("tgt") == 2
    shaped = target_feat.shape[0] == 1 and rows % 2 == 0 and cells == 2 * depth and cells % 128 == 0
    if paired and shaped and 4 * rows * cells * shards * cells <= room:
        return dense_device(source_feat, target_feat, *others)
    return general_device(source_feat, target_feat, *others)


def solution(mesh):
    in_specs = (
        P(("grp", "src"), None, None),
        P(("grp", "src", "tgt"), None, None),
        P(("grp", "src"), None),
        P(("grp", "src", "tgt"), None),
        P(("grp", "src", "tgt"), None),
        P(("grp", "src"), "tgt", None),
        P(("grp", "src"), "tgt"),
    )
    out_specs = (P(("grp", "src"), None), P(("grp", "src", "tgt"), None))
    return jax.shard_map(
        per_device, mesh=mesh, in_specs=in_specs, out_specs=out_specs, check_vma=False
    )
```

```python
import functools
import math

import jax
import jax.numpy as jnp
from jax import lax
from jax.experimental import pallas as pl
from jax.experimental.pallas import tpu as pltpu
from jax.sharding import PartitionSpec as P

entropic = 0.5
very_low = -1e30
log2e = 1.0 / math.log(2.0)
ln2 = math.log(2.0)
least_sum = 1e-28

room = 2**24

VM = pl.BlockSpec(memory_space=pltpu.VMEM)
PARAMS = pltpu.CompilerParams(vmem_limit_bytes=40 * 2**20)


def in_vmem(shape, dtype):
    return pltpu.VMEM(shape, dtype)


def pieces(values):
    high = values.astype(jnp.bfloat16).astype(jnp.float32)
    rest = values - high
    mid = rest.astype(jnp.bfloat16).astype(jnp.float32)
    low = (rest - mid).astype(jnp.bfloat16).astype(jnp.float32)
    return high, mid, low


def target_weight(mass, poten):
    return (mass + poten / entropic) * log2e


def line_moves(line):
    bits = line.bit_length() - 1
    cycle = [sum(((place >> bit) & 1) << (bits - 1 - bit) for bit in range(bits)) for place in range(line)]
    shifts = [shift for step in range(1, line // 2) for shift in (step, line - step)] + [line // 2]
    return [[cycle[(cycle.index(at) + shift) % line] for at in range(line)] for shift in shifts]


def blocks_at(shards):
    me = lax.axis_index("src")
    at, odd = me // 2, lax.rem(me, 2)
    near = [me]
    for receivers in line_moves(shards // 2):
        senders = [receivers.index(there) for there in range(shards // 2)]
        near.append(2 * sum(jnp.where(at == there, sender, 0) for there, sender in enumerate(senders)) + odd)
    return near + [block ^ 1 for block in near]


def members_of(shards):
    return sorted(range(shards), key=lambda at: (-(at // 2 + at % 2), -(at % 2)))


def read_all(hbm, held, sems):
    copies = [pltpu.make_async_copy(src, dst, sems.at[i]) for i, (src, dst) in enumerate(zip(hbm, held))]
    for copy in copies:
        copy.start()
    return copies


def pack_kernel(*refs):
    hbm, (send_ref, weight_ref), held, sems = refs[:3], refs[3:5], refs[5:8], refs[8]
    for copy in read_all(hbm, held, sems):
        copy.wait()
    feat_ref, mass_ref, poten_ref = held
    feat = feat_ref[0]
    depth, cells = feat.shape
    weight = target_weight(mass_ref[...], poten_ref[...])
    norm = jnp.sum(feat * feat, axis=0, keepdims=True)
    bias = weight - (log2e / entropic) * norm
    scaled = feat * (2.0 * log2e / entropic)
    send_ref[0, :depth, 0, :] = scaled
    send_ref[0, depth, 0:1, :] = bias
    weight_ref[...] = weight


def source_kernel(shards, *refs):
    hbm, outs, held, sems = refs[:4], refs[4:8], refs[8:12], refs[12]
    wide_ref, norm_ref, mask_ref, mass_out_ref = outs
    mass_ref, support_ref, counts_ref, feat_ref = held
    copies = read_all(hbm, held, sems)
    for copy in copies[:3]:
        copy.wait()
    mass_out_ref[...] = mass_ref[...]
    support = support_ref[...]
    slots, rows = support.shape
    cells = mass_ref.shape[1]
    used = lax.broadcasted_iota(jnp.int32, support.shape, 0) < counts_ref[...]
    hits = [
        jnp.max(jnp.where(used & (support == block), 0.0, very_low), axis=0, keepdims=True)
        for block in blocks_at(shards)
    ]
    hits = jnp.concatenate(hits + [jnp.zeros((cells - shards, rows), jnp.float32)], axis=0)
    hits = jnp.concatenate([hits, jnp.zeros((cells, cells - rows), jnp.float32)], axis=1).T
    for place in range(shards):
        mask_ref[place] = jnp.broadcast_to(hits[:rows, place : place + 1], (rows, cells))
    copies[3].wait()
    depth = feat_ref.shape[1]
    one = jnp.ones((2 * depth, 2 * cells), jnp.bfloat16)
    for pair in range(rows // 2):
        for half in range(2):
            feat = feat_ref[2 * pair + half]
            norm_ref[2 * pair + half : 2 * pair + half + 1, :] = jnp.sum(feat * feat, axis=0, keepdims=True)
            high, mid, low = pieces(feat)
            lanes = slice(half * cells, (half + 1) * cells)
            top = jnp.concatenate([high, mid], axis=0).astype(jnp.bfloat16)
            wide_ref[pair, 0 : 2 * depth, lanes] = top
            wide_ref[pair, 2 * depth : 4 * depth, lanes] = top
            wide_ref[pair, 4 * depth : 6 * depth, lanes] = jnp.concatenate([low, high], axis=0).astype(jnp.bfloat16)
        wide_ref[pair, 6 * depth : 8 * depth, :] = one


def join_kernel(*refs):
    refs[-1][0] = refs[0][0]
    refs[-1][1] = refs[1][0]


def on_core(core, work, idle):
    if core is None:
        work()
    else:
        here = lax.axis_index("tgt") == core
        pl.when(here)(work)
        pl.when(jnp.logical_not(here))(idle)


def tile_kernel(parts, *refs):
    make_tiles(parts, *refs[: parts + 1], *refs[-4:])


def make_tiles(parts, *refs):
    packs = [ref.at[index] for ref in refs[:parts] for index in range(ref.shape[0])]
    wide_ref, exps_ref, tall_ref, peak_ref, total_ref = refs[parts:]
    blocks = len(packs)
    pairs, _, both = wide_ref.shape
    cells = both // 2
    depth = cells // 2
    lane = lax.broadcasted_iota(jnp.int32, (cells, cells), 1)
    biases = jnp.concatenate([pack[depth, 0:1, :] for pack in packs], axis=0)
    bias_pieces = jnp.concatenate(list(pieces(biases)), axis=0)
    padded = jnp.concatenate([bias_pieces, jnp.zeros((cells - 3 * blocks, cells), jnp.float32)], axis=0)
    bias_lanes = padded.T
    for place, pack in enumerate(packs):
        feat = pack[:depth, 0, :]
        turned = jnp.concatenate([feat, feat], axis=0).T
        high, mid, low = pieces(turned)
        own = jnp.where(lax.rem(lane, blocks) == place, bias_lanes, 0.0)
        rows = slice(place * cells, (place + 1) * cells)
        tall_ref[rows, 0:cells] = high.astype(jnp.bfloat16)
        tall_ref[rows, cells : 2 * cells] = mid.astype(jnp.bfloat16)
        tall_ref[rows, 2 * cells : 3 * cells] = jnp.where(lane < depth, high, low).astype(jnp.bfloat16)
        tall_ref[rows, 3 * cells : 4 * cells] = own.astype(jnp.bfloat16)

    def body(pair, carry):
        scores = jnp.dot(tall_ref[...], wide_ref[pair], preferred_element_type=jnp.float32)
        for place in range(blocks):
            rows = slice(place * cells, (place + 1) * cells)
            score = scores[rows]
            peak = jnp.max(score, axis=0, keepdims=True)
            exps = jnp.exp2(score - peak)
            exps_ref[pair, rows, :] = exps
            total = jnp.sum(exps, axis=0, keepdims=True)
            for half in range(2):
                lanes = slice(half * cells, (half + 1) * cells)
                peak_ref[place, pl.ds(2 * pair + half, 1), :] = peak[:, lanes]
                total_ref[place, pl.ds(2 * pair + half, 1), :] = total[:, lanes]
        return carry

    lax.fori_loop(0, pairs, body, 0, unroll=max(1, min(pairs, 32 // blocks)))


def row_kernel(groups, *refs):
    mask_ref, peak_refs, total_refs = refs[0], refs[1 : 1 + groups], refs[1 + groups : 1 + 2 * groups]
    peaks_ref, rowsum_ref = refs[1 + 2 * groups :]
    place = 0
    for ref in peak_refs:
        for index in range(ref.shape[0]):
            peaks_ref[place] = ref[index] + mask_ref[place]
            place += 1
    totals = [ref[index] for ref in total_refs for index in range(ref.shape[0])]
    top = functools.reduce(jnp.maximum, [peaks_ref[index] for index in range(place)])
    summed = sum(total * jnp.exp2(peaks_ref[index] - top) for index, total in enumerate(totals))
    rowsum_ref[...] = top + jnp.log2(summed)


def last_kernel(groups, core, *refs):
    packs_ref, wide_ref, _, mask_ref = refs[:4]
    peak_refs, total_refs = refs[4 : 3 + groups], refs[3 + groups : 2 + 2 * groups]
    exps_ref, tall_ref, peaks_ref, rowsum_ref, peak_ref, total_ref = refs[2 + 2 * groups :]

    def idle():
        peak_ref[...] = jnp.zeros(peak_ref.shape, jnp.float32)
        total_ref[...] = jnp.zeros(total_ref.shape, jnp.float32)

    work = functools.partial(make_tiles, 1, packs_ref, wide_ref, exps_ref, tall_ref, peak_ref, total_ref)
    on_core(core, work, idle)
    row_kernel(groups, mask_ref, *peak_refs, peak_ref, *total_refs, total_ref, peaks_ref, rowsum_ref)


def across(column):
    shape = (column.shape[0],) * 2
    same = lax.broadcasted_iota(jnp.int32, shape, 0) == lax.broadcasted_iota(jnp.int32, shape, 1)
    return jnp.sum(jnp.where(same, jnp.broadcast_to(column, shape), 0.0), axis=0, keepdims=True)


def column_kernel(groups, core, *refs):
    ins, outs, scratch = refs[: 2 * groups + 7], refs[-4:-2], refs[-2:]

    def idle():
        for given, out in zip(refs[2 * groups + 7 : -4], outs):
            out[...] = given[...]

    on_core(core, functools.partial(sum_columns, groups, *ins, *outs, *scratch), idle)


def sum_columns(groups, *refs):
    exps_refs, tall_refs, rest = refs[:groups], refs[groups : 2 * groups], refs[2 * groups :]
    wide_ref, peak_ref, mask_ref, own_ref, other_ref, mass_ref, norm_ref = rest[:7]
    poten_ref, sums_ref, weight_ref, shift_ref = rest[7:]
    pairs, _, both = wide_ref.shape
    cells = both // 2
    shards = mask_ref.shape[0]
    own, other = own_ref[...], other_ref[...]
    top = jnp.maximum(own, other)
    whole = top + jnp.log2(jnp.exp2(own - top) + jnp.exp2(other - top))
    poten_ref[...] = norm_ref[...] - (entropic * ln2) * whole
    shift = mass_ref[...] * log2e - whole
    shift_ref[...] = shift
    for place in range(shards):
        weight_ref[place] = jnp.exp2(peak_ref[place] + shift)
    spots = [
        (group, slice(index * cells, (index + 1) * cells))
        for group, ref in enumerate(tall_refs)
        for index in range(ref.shape[0] // cells)
    ]
    used = [jnp.max(mask_ref[place], axis=0, keepdims=True) > 0.5 * very_low for place in range(shards)]
    places = [members_of(shards).index(block) for block in range(shards)]
    ranks = [sum(jnp.where(block == at, rank, 0) for at, rank in enumerate(places)) for block in blocks_at(shards)]
    sums = []
    for place, (group, rows) in enumerate(spots):
        acc = jnp.zeros((cells, cells), jnp.float32)
        for pair in range(pairs):
            acc = acc + exps_refs[group][pair, rows, :cells] * weight_ref[place, 2 * pair : 2 * pair + 1, :]
            acc = acc + exps_refs[group][pair, rows, cells:] * weight_ref[place, 2 * pair + 1 : 2 * pair + 2, :]
        sums.append(jnp.sum(acc.T, axis=0, keepdims=True))
    whole_sums = jnp.concatenate([jnp.where(here, one, 1.0) for here, one in zip(used, sums)], axis=0)
    worst = jnp.min(whole_sums)
    logs = jnp.log2(whole_sums)
    for place in range(shards):
        sums_ref[ranks[place]] = jnp.where(used[place], logs[place : place + 1, :], very_low)

    @pl.when(worst < least_sum)
    def _():
        for place, (group, rows) in enumerate(spots):

            def exponents(pair):
                score = jnp.dot(tall_refs[group][rows, :], wide_ref[pair], preferred_element_type=jnp.float32)
                add = shift_ref[pl.ds(2 * pair, 2), :] + mask_ref[place, pl.ds(2 * pair, 2), :]
                return score[:, :cells] + add[0:1, :], score[:, cells:] + add[1:2, :]

            def highest(pair, peak):
                first, second = exponents(pair)
                return jnp.maximum(peak, jnp.maximum(first, second))

            peak = lax.fori_loop(0, pairs, highest, jnp.full((cells, cells), very_low, jnp.float32))
            peak = jnp.max(peak, axis=1, keepdims=True)

            def add_up(pair, sums):
                first, second = exponents(pair)
                return sums + jnp.exp2(first - peak) + jnp.exp2(second - peak)

            sums = lax.fori_loop(0, pairs, add_up, jnp.zeros((cells, cells), jnp.float32))
            logs = across(peak) + jnp.log2(across(jnp.sum(sums, axis=1, keepdims=True)))
            sums_ref[ranks[place]] = jnp.where(used[place], logs, very_low)


def merge_kernel(values_ref, weight_ref, poten_ref, out_ref, poten_out_ref):
    poten_out_ref[...] = poten_ref[...]
    values = values_ref[...]
    top = jnp.max(values, axis=0)
    whole = top + jnp.log2(jnp.sum(jnp.exp2(values - top), axis=0))
    out_ref[...] = -(entropic * ln2) * (whole - weight_ref[...])


def f32(*shape):
    return jax.ShapeDtypeStruct(shape, jnp.float32)


def dense_device(
    source_feat, target_feat, log_mass_src, log_mass_tgt, potential_tgt, support, counts
):
    shards = lax.axis_size("src")
    rows, depth, cells = source_feat.shape
    pairs, wide = rows // 2, 2 * cells

    def call(kernel, ins, out_shape, scratch=(), cost=None):
        many = isinstance(out_shape, list)
        return pl.pallas_call(
            kernel,
            in_specs=ins,
            out_specs=[VM] * len(out_shape) if many else VM,
            out_shape=out_shape,
            scratch_shapes=list(scratch),
            compiler_params=PARAMS,
            cost_estimate=cost,
        )

    def reading(kernel, args, out_shape, cost):
        return call(
            kernel,
            [pl.BlockSpec(memory_space=pltpu.HBM)] * len(args),
            out_shape,
            [pltpu.VMEM(arg.shape, arg.dtype) for arg in args] + [pltpu.SemaphoreType.DMA((len(args),))],
            cost,
        )(*[pltpu.with_memory_space_constraint(arg, pltpu.HBM) for arg in args])

    def cost_of(flops):
        return pl.CostEstimate(flops=flops, bytes_accessed=rows * depth * cells * 4, transcendentals=0)

    pack, weight = reading(
        pack_kernel,
        [target_feat, log_mass_tgt, potential_tgt],
        [in_vmem((1, depth + 1, 1, cells), jnp.float32), in_vmem((1, cells), jnp.float32)],
        None,
    )
    wide_feat, norm, mask, mass = reading(
        functools.partial(source_kernel, shards),
        [log_mass_src, support[:, 0, :].T, counts.T, source_feat],
        [
            in_vmem((pairs, 8 * depth, wide), jnp.bfloat16),
            in_vmem((rows, cells), jnp.float32),
            in_vmem((shards, rows, cells), jnp.float32),
            in_vmem((rows, cells), jnp.float32),
        ],
        cost_of(10**8),
    )

    def tile_shapes(blocks):
        return [
            in_vmem((pairs, blocks * cells, wide), jnp.float32),
            in_vmem((blocks * cells, 8 * depth), jnp.bfloat16),
            in_vmem((blocks, rows, cells), jnp.float32),
            in_vmem((blocks, rows, cells), jnp.float32),
        ]

    def tiles(*packs, after):
        blocks = sum(pack.shape[0] for pack in packs)
        return call(
            functools.partial(tile_kernel, len(packs)),
            [VM] * (len(packs) + 1) + [pl.BlockSpec(memory_space=pl.ANY)],
            tile_shapes(blocks),
            cost=cost_of(2 * blocks * cells * pairs * wide * 8 * depth),
        )(*packs, wide_feat, after)

    def swapped(array):
        return lax.ppermute(array, "src", [(i, i ^ 1) for i in range(shards)])

    def moved(array, receivers):
        moves = [(2 * here + odd, 2 * there + odd) for here, there in enumerate(receivers) for odd in range(2)]
        return lax.ppermute(array, "src", moves)

    def joined(first, second, after):
        return call(
            join_kernel,
            [VM] * 2 + [pl.BlockSpec(memory_space=pl.ANY)],
            in_vmem((2,) + pack.shape[1:], jnp.float32),
        )(first, second, after)

    there = [moved(pack, receivers) for receivers in line_moves(shards // 2)[::-1]][::-1]
    near = [pack] + there
    halves = [joined(near[0], near[1], norm)]
    for at in range(2, shards // 2, 2):
        halves.append(joined(near[at], near[at + 1], halves[-1]))
    far = [swapped(half) for half in halves]
    found = [tiles(*near, after=halves[-1])]
    for half in far[:-1]:
        found.append(tiles(half, after=found[-1][-1]))
    groups = len(found) + 1

    def last_tiles(core, after):
        _, _, peaks, totals = zip(*found)
        blocks = far[-1].shape[0]
        exps, tall, *_ = tile_shapes(blocks)
        *last, peaks, own = call(
            functools.partial(last_kernel, groups, core),
            [VM] * 2 + [pl.BlockSpec(memory_space=pl.ANY)] + [VM] * (2 * groups - 1),
            [exps, tall, in_vmem((shards, rows, cells), jnp.float32), in_vmem((rows, cells), jnp.float32)],
            [pltpu.VMEM((blocks, rows, cells), jnp.float32)] * 2,
            cost=cost_of(2 * blocks * cells * pairs * wide * 8 * depth),
        )(far[-1], wide_feat, after, mask, *peaks, *totals)
        return last, peaks, own

    def columns_of(core, last, peaks, own, other, given):
        exps, tall = zip(*[group[:2] for group in found], last)
        return call(
            functools.partial(column_kernel, groups, core),
            [VM] * (2 * groups + 7 + len(given)),
            [in_vmem((rows, cells), jnp.float32), in_vmem((shards, 1, cells), jnp.float32)],
            [pltpu.VMEM((shards, rows, cells), jnp.float32), pltpu.VMEM((rows, cells), jnp.float32)],
            cost_of(10**9),
        )(*exps, *tall, wide_feat, peaks, mask, own, other, mass, norm, *given)

    between = [(0, 1), (1, 0)]
    last_one, peaks_one, own_one = last_tiles(1, found[-1][-1])
    other_zero = lax.ppermute(own_one, "tgt", between)
    last_zero, peaks_zero, own_zero = last_tiles(0, own_one)
    other_one = lax.ppermute(own_zero, "tgt", between)
    given = columns_of(0, last_zero, peaks_zero, own_zero, other_zero, [])
    potential_src, columns = columns_of(1, last_one, peaks_one, own_one, other_one, given)
    arrived = lax.all_to_all(columns, "src", 0, 0, axis_index_groups=[members_of(shards)])
    outs = [f32(1, cells), f32(rows, cells)]
    potential_new, potential_src = call(merge_kernel, [VM] * 3, outs)(arrived, weight, potential_src)
    return potential_src, potential_new


def merged(part, axis, combine):
    gathered = jax.tree.map(lambda a: lax.all_gather(a, axis), part)

    def take(source):
        return jax.tree.map(lambda a: lax.dynamic_index_in_dim(a, source, 0, False), gathered)

    return lax.fori_loop(
        1, lax.axis_size(axis), lambda source, state: combine(state, take(source)), take(0)
    )


def cost_tiles(source_blk, source_sq, target_blk, target_sq):
    cross = jnp.einsum(
        "...fi,...fj->...ij", source_blk, target_blk, precision=lax.Precision.HIGHEST
    )
    return source_sq[..., :, None] + target_sq[..., None, :] - 2.0 * cross


def row_stats(cost, mass_tgt, poten_tgt, usable):
    scores = mass_tgt[..., None, :] + (poten_tgt[..., None, :] - cost) / entropic
    scores = jnp.where(usable[..., None, None], scores, very_low)
    peak = jnp.max(scores, axis=(1, 3))
    total = jnp.sum(jnp.exp(scores - peak[:, None, :, None]), axis=(1, 3))
    return (peak, total)


def column_stats(cost, mass_src, poten_src, usable):
    scores = mass_src[:, None, :, None] + (poten_src[:, None, :, None] - cost) / entropic
    peak = jnp.max(scores, axis=2)
    total = jnp.sum(jnp.exp(scores - peak[:, :, None, :]), axis=2)
    peak = jnp.where(usable[..., None], peak, very_low)
    total = jnp.where(usable[..., None], total, 0.0)
    return (peak, total)


def merge_pair(first_pair, second_pair):
    first_peak, first_total = first_pair
    second_peak, second_total = second_pair
    highest = jnp.maximum(first_peak, second_peak)
    summed = first_total * jnp.exp(first_peak - highest) + second_total * jnp.exp(
        second_peak - highest
    )
    return (highest, summed)


def segment_merge(peaks, totals, seg_ids, segments):
    best = jax.ops.segment_max(peaks, seg_ids, num_segments=segments + 1)
    best = jnp.maximum(best, very_low)
    summed = jax.ops.segment_sum(
        totals * jnp.exp(peaks - best[seg_ids]), seg_ids, num_segments=segments + 1
    )
    return (best[:segments], summed[:segments])


def general_device(
    source_feat, target_feat, log_mass_src, log_mass_tgt, potential_tgt, support, counts
):
    target_all, mass_all, poten_all = (
        lax.all_gather(target_feat, "src", axis=0, tiled=True),
        lax.all_gather(log_mass_tgt, "src", axis=0, tiled=True),
        lax.all_gather(potential_tgt, "src", axis=0, tiled=True),
    )
    blocks = target_all.shape[0]
    rows_here = source_feat.shape[0]
    slots_here = support.shape[2]
    cells = source_feat.shape[2]
    indices = support[:, 0, :]
    limits = counts[:, 0]
    usable = jnp.arange(slots_here, dtype=jnp.int32)[None, :] < limits[:, None]
    source_sq = jnp.sum(source_feat * source_feat, axis=1)
    target_sq = jnp.sum(target_all * target_all, axis=1)
    width = math.gcd(rows_here, 4)

    def grouped(array):
        return array.reshape((rows_here // width, width) + array.shape[1:])

    def row_pass(items):
        source_blk, source_nrm, ids_here, use_here = items
        cost = cost_tiles(
            source_blk[:, None], source_nrm[:, None], target_all[ids_here], target_sq[ids_here]
        )
        return row_stats(cost, mass_all[ids_here], poten_all[ids_here], use_here)

    peak, total = lax.map(
        row_pass, (grouped(source_feat), grouped(source_sq), grouped(indices), grouped(usable))
    )
    peak = peak.reshape(rows_here, cells)
    total = total.reshape(rows_here, cells)
    peak_all, total_all = merged((peak, total), "tgt", merge_pair)
    potential_src = -entropic * (peak_all + jnp.log(total_all))

    def column_pass(items):
        source_blk, source_nrm, mass_here, poten_here, ids_here, use_here = items
        cost = cost_tiles(
            source_blk[:, None], source_nrm[:, None], target_all[ids_here], target_sq[ids_here]
        )
        return column_stats(cost, mass_here, poten_here, use_here)

    peaks, totals = lax.map(
        column_pass,
        (
            grouped(source_feat),
            grouped(source_sq),
            grouped(log_mass_src),
            grouped(potential_src),
            grouped(indices),
            grouped(usable),
        ),
    )
    seg_ids = jnp.where(usable, indices, blocks).reshape(-1)
    best, summed = segment_merge(
        peaks.reshape(-1, cells), totals.reshape(-1, cells), seg_ids, blocks
    )
    share = blocks // lax.axis_size("src")
    own_start = lax.axis_index("src") * share
    highest = lax.pmax(best, "src")
    whole = lax.psum(summed * jnp.exp(best - highest), "src")
    own_peak = lax.dynamic_slice_in_dim(highest, own_start, share, 0)
    own_total = lax.dynamic_slice_in_dim(whole, own_start, share, 0)
    potential_new = -entropic * (own_peak + jnp.log(own_total))
    return (potential_src, potential_new)


def per_device(source_feat, target_feat, *others):
    shards = lax.axis_size("src")
    rows, depth, cells = source_feat.shape
    paired = shards >= 4 and shards & (shards - 1) == 0 and lax.axis_size("tgt") == 2
    shaped = target_feat.shape[0] == 1 and rows % 2 == 0 and cells == 2 * depth and cells % 128 == 0
    if paired and shaped and 4 * rows * cells * shards * cells <= room:
        return dense_device(source_feat, target_feat, *others)
    return general_device(source_feat, target_feat, *others)


def solution(mesh):
    in_specs = (
        P(("grp", "src"), None, None),
        P(("grp", "src", "tgt"), None, None),
        P(("grp", "src"), None),
        P(("grp", "src", "tgt"), None),
        P(("grp", "src", "tgt"), None),
        P(("grp", "src"), "tgt", None),
        P(("grp", "src"), "tgt"),
    )
    out_specs = (P(("grp", "src"), None), P(("grp", "src", "tgt"), None))
    return jax.shard_map(
        per_device, mesh=mesh, in_specs=in_specs, out_specs=out_specs, check_vma=False
    )
```
